32 devices in a mesh: dp: 8 (over y, x, core), mp: 4 (over z).
Axes of the slice: x: 2, y: 2, z: 4, core: 2. Of those that a mesh axis runs over, the one named last changes fastest.
Arguments:
- latents: bfloat16 [24, 1024, 1152], P('dp'), may hold values from -6 to 6
- condition: float32 [24, 1152], P('dp'), may hold values from -6 to 6
- cotangent: bfloat16 [24, 1024, 1152], P('dp'), may hold values from -6 to 6
- qkv_weight: bfloat16 [1152, 3, 1152], P(None, None, 'mp'), may hold values from -1 to 1
- qv_bias: bfloat16 [2, 1152], P(None, 'mp'), may hold values from -3 to 3
- proj_weight: bfloat16 [1152, 1152], P('mp'), may hold values from -6 to 6
- proj_bias: bfloat16 [1152], replicated, may hold values from -3 to 3
- fc1_weight: bfloat16 [1152, 4608], P(None, 'mp'), may hold values from -0.1875 to 0.1875
- fc1_bias: bfloat16 [4608], P('mp'), may hold values from -3 to 3
- fc2_weight: bfloat16 [4608, 1152], P('mp'), may hold values from -0.09375 to 0.09375
- fc2_bias: bfloat16 [1152], replicated, may hold values from -3 to 3
- ada_weight: bfloat16 [1152, 6912], P(None, 'mp'), may hold values from -0.1875 to 0.1875
- ada_bias: bfloat16 [6912], P('mp'), may hold values from -3 to 3
Outputs:
- block_out: bfloat16 [24, 1024, 1152], P('dp')
- latents_grad: bfloat16 [24, 1024, 1152], P('dp')
- condition_grad: float32 [24, 1152], P('dp')
- qkv_weight_grad: float32 [1152, 3, 1152], P(None, None, 'mp')
- qv_bias_grad: float32 [2, 1152], P(None, 'mp')
- proj_weight_grad: float32 [1152, 1152], P('mp')
- proj_bias_grad: float32 [1152], replicated
- fc1_weight_grad: float32 [1152, 4608], P(None, 'mp')
- fc1_bias_grad: float32 [4608], P('mp')
- fc2_weight_grad: float32 [4608, 1152], P('mp')
- fc2_bias_grad: float32 [1152], replicated
- ada_weight_grad: float32 [1152, 6912], P(None, 'mp')
- ada_bias_grad: float32 [6912], P('mp')
The draws below stay inside these ranges and needn't reach their ends.
All inputs are finite; a program needn't handle non-finite values.
Results may differ from the reference program's by a relative error of at most 0.025.
Values may be sent and summed in bfloat16 or wider, within the bound.
A program may use at most 448 MiB of HBM per device.

```python
import math
import jax
import jax.numpy as jnp
from jax import lax

D = 1152
HEADS = 16
HEAD_DIM = 72
FF = 4608
SEQ = 1024
LATENTS = 24
N_MP = 4


def draw_latents(key, part):
    key = jax.random.fold_in(key, 11)
    values = jnp.clip(jax.random.normal(key, (LATENTS, SEQ, D), jnp.float32), -6.0, 6.0)
    return values.astype(jnp.bfloat16)


def draw_qkv_weight(key, part):
    key = jax.random.fold_in(key, 21)
    base = jnp.clip(jax.random.normal(key, (D, 3, D), jnp.float32), -6.0, 6.0)
    base = base / math.sqrt(D)
    return jnp.clip(base, -1.0, 1.0).astype(jnp.bfloat16)


def draw_fc1_weight(key, part):
    key = jax.random.fold_in(key, 31)
    limit = 0.1875
    spread = min(2.75 / math.sqrt(D), 0.09)
    base = jnp.clip(jax.random.normal(key, (D, FF), jnp.float32) * spread, -limit, limit)
    return base.astype(jnp.bfloat16)


def draw_fc2_weight(key, part):
    key = jax.random.fold_in(key, 41)
    limit = 0.09375
    spread = min(2.75 / math.sqrt(FF), 0.045)
    base = jnp.clip(jax.random.normal(key, (FF, D), jnp.float32) * spread, -limit, limit)
    return base.astype(jnp.bfloat16)


def shard_levels(own_key, extent, split, low, top_value):
    level = 1.0
    for dim, blocks in split:
        draws = jax.random.uniform(jax.random.fold_in(jax.random.fold_in(own_key, 6), dim), (blocks,), jnp.float32, low / len(split), top_value / len(split))
        level = level * jnp.repeat(jnp.exp(draws), extent[dim] // blocks).reshape((-1,) + (1,) * (len(extent) - 1 - dim))
    return level


def gaussian(own_key, extent, scale, most, shards=(), held_as=jnp.bfloat16):
    loudness = shard_levels(own_key, extent, shards, -0.22, 0.18) if shards else 1.0
    values = jax.random.normal(own_key, extent, jnp.float32) * scale * loudness
    return jnp.minimum(jnp.maximum(values, -most), most).astype(held_as)


def setup_inputs(seed: int = 0) -> dict:
    streams_of = jax.random.split(jax.random.key(seed), 14)
    return {
        "latents": draw_latents(jax.random.fold_in(streams_of[13], 71), 0),
        "condition": gaussian(streams_of[1], (LATENTS, D), 1.0, 6.0, ((0, 8),), jnp.float32),
        "cotangent": gaussian(streams_of[2], (LATENTS, SEQ, D), 1.0, 6.0, ((0, 8),)),
        "qkv_weight": draw_qkv_weight(jax.random.fold_in(streams_of[13], 71), 0),
        "qv_bias": gaussian(streams_of[4], (2, D), 0.5, 3.0, ((1, 4),)),
        "proj_weight": gaussian(streams_of[5], (D, D), (max(D // SEQ, 1)) ** -0.5, 6.0, ((0, 4),)),
        "proj_bias": gaussian(streams_of[6], (D,), 0.5, 3.0),
        "fc1_weight": draw_fc1_weight(jax.random.fold_in(streams_of[13], 71), 0),
        "fc1_bias": gaussian(streams_of[8], (FF,), 0.5, 3.0, ((0, 4),)),
        "fc2_weight": draw_fc2_weight(jax.random.fold_in(streams_of[13], 71), 0),
        "fc2_bias": gaussian(streams_of[10], (D,), 0.5, 3.0),
        "ada_weight": gaussian(streams_of[11], (D, 6 * D), D ** -0.5, 0.1875, ((1, 4),)),
        "ada_bias": gaussian(streams_of[12], (6 * D,), 0.5, 3.0, ((0, 4),)),
    }


norm_eps = 1e-06
highest = lax.Precision.HIGHEST

@jax.custom_vjp
def low(v):
    return lax.optimization_barrier(v.astype(jnp.bfloat16)).astype(jnp.float32)

@jax.custom_vjp
def low_back(v):
    return v

def low_keep(v):
    return (low(v), None)

def low_pass(kept, grad):
    return (grad,)

def back_keep(v):
    return (v, None)

def back_low(kept, grad):
    return (low(grad),)
low.defvjp(low_keep, low_pass)
low_back.defvjp(back_keep, back_low)

def layer_norm(values):
    centered = values - lax.optimization_barrier(jnp.mean(values, -1, keepdims=True))
    return centered * lax.rsqrt(lax.optimization_barrier(jnp.mean(centered * centered, -1, keepdims=True)) + norm_eps)

def forward(latents, condition, qkv_weight, qv_bias, proj_weight, proj_bias, fc1_weight, fc1_bias, fc2_weight, fc2_bias, ada_weight, ada_bias):
    group_heads = HEADS // N_MP
    group_width = D // N_MP
    group_hidden = FF // N_MP
    cond_low = low(jax.nn.silu(condition))
    modulation = low_back(jnp.dot(cond_low, ada_weight, precision=highest) + ada_bias)
    modulation = modulation.reshape(-1, 6, D)
    weight_groups = qkv_weight.reshape(D, 3, N_MP, group_width)
    bias_rows = jnp.stack([qv_bias[0], jnp.zeros((D,), jnp.float32), qv_bias[1]])
    bias_groups = bias_rows.reshape(3, N_MP, group_width).transpose(1, 0, 2)[:, None]
    proj_groups = proj_weight.reshape(N_MP, group_heads, HEAD_DIM, D)
    fc1_groups = fc1_weight.reshape(D, N_MP, group_hidden)
    fc2_groups = fc2_weight.reshape(N_MP, group_hidden, D)
    scaling = 1.0 / HEAD_DIM ** 0.5

    def one_latent(pair):
        tokens, mods = pair
        shift_one, scale_one, gate_one = (mods[0], mods[1], mods[2])
        shift_two, scale_two, gate_two = (mods[3], mods[4], mods[5])
        mixed_one = low(layer_norm(tokens) * (1.0 + scale_one) + shift_one)
        copies = low_back(jnp.broadcast_to(mixed_one, (N_MP, SEQ, D)))
        qkv = jnp.einsum('gsd,dcge->gsce', copies, weight_groups, precision=highest)
        qkv = low(low_back(qkv + bias_groups))
        queries = qkv[:, :, 0].reshape(N_MP, SEQ, group_heads, HEAD_DIM)
        key_rows = qkv[:, :, 1].reshape(N_MP, SEQ, group_heads, HEAD_DIM)
        values = qkv[:, :, 2].reshape(N_MP, SEQ, group_heads, HEAD_DIM)
        scores = low_back(jnp.einsum('gqhd,gkhd->ghqk', queries, key_rows, precision=highest) * scaling)
        probs = low(jax.nn.softmax(scores, axis=-1))
        heads_out = low(low_back(jnp.einsum('ghqk,gkhd->gqhd', probs, values, precision=highest)))
        parts = jnp.einsum('gqhd,ghde->gqe', heads_out, proj_groups, precision=highest)
        attn = low_back(lax.optimization_barrier(jnp.sum(low(parts), 0))) + proj_bias
        resid_two = tokens + gate_one * attn
        mixed_two = low(layer_norm(resid_two) * (1.0 + scale_two) + shift_two)
        copies_two = low_back(jnp.broadcast_to(mixed_two, (N_MP, SEQ, D)))
        hidden = jnp.einsum('gsd,dgf->gsf', copies_two, fc1_groups, precision=highest)
        hidden = low_back(hidden + fc1_bias.reshape(N_MP, 1, group_hidden))
        activ = low(jax.nn.gelu(hidden, approximate=True))
        mlp_parts = jnp.einsum('gsf,gfd->gsd', activ, fc2_groups, precision=highest)
        mlp = low_back(lax.optimization_barrier(jnp.sum(low(mlp_parts), 0))) + fc2_bias
        return resid_two + gate_two * mlp
    return lax.map(jax.checkpoint(one_latent), (latents, modulation))

def reference(latents, condition, cotangent, qkv_weight, qv_bias, proj_weight, proj_bias, fc1_weight, fc1_bias, fc2_weight, fc2_bias, ada_weight, ada_bias):
    inputs = (latents, condition, qkv_weight, qv_bias, proj_weight, proj_bias, fc1_weight, fc1_bias, fc2_weight, fc2_bias, ada_weight, ada_bias)
    floats = [item.astype(jnp.float32) for item in inputs]
    output, pullback = jax.vjp(forward, *floats)
    grads = pullback(cotangent.astype(jnp.float32))
    return (output.astype(jnp.bfloat16), grads[0].astype(jnp.bfloat16), grads[1], grads[2], grads[3], grads[4], grads[5], grads[6], grads[7], grads[8], grads[9], grads[10], grads[11])
```

```python
import functools

import jax
import jax.numpy as jnp
from jax import lax
from jax.experimental import pallas as pl
from jax.experimental.pallas import tpu as pltpu
from jax.sharding import PartitionSpec as P

HEAD_DIM = 72
EPS = 1e-06
LOG2E = 1.4426950408889634
GELU_A = 0.7978845608028654
GELU_B = 0.044715
BF = jnp.bfloat16
F32 = jnp.float32
MIB = 2**20


def mm(a, b):
    return jnp.dot(a, b, preferred_element_type=F32)


def nt(a, b):
    return lax.dot_general(a, b, (((1,), (1,)), ((), ())), preferred_element_type=F32)


def tn(a, b):
    return lax.dot_general(a, b, (((0,), (0,)), ((), ())), preferred_element_type=F32)


def norm_stats(values):
    centered = values - jnp.mean(values, -1, keepdims=True)
    inv_std = lax.rsqrt(jnp.mean(centered * centered, -1, keepdims=True) + EPS)
    return centered * inv_std, inv_std


def norm_back(normed, inv_std, grad_normed):
    first = jnp.mean(grad_normed, -1, keepdims=True)
    second = jnp.mean(grad_normed * normed, -1, keepdims=True)
    return inv_std * (grad_normed - first - normed * second)


def attn_fwd_kernel(
    me_ref, lat_ref, mod_ref, w_ref, bias_ref, heads_ref, qkv_ref, lse_ref, h1_ref, h1_all
):
    slot, lat = pl.program_id(0), pl.program_id(1)
    n_heads = qkv_ref.shape[1] // 3
    seq = lat_ref.shape[1]

    @pl.when(slot == 0)
    def _():
        normed, _ = norm_stats(lat_ref[0].astype(F32))
        h1 = (normed * (1.0 + mod_ref[0, 1:2]) + mod_ref[0, 0:1]).astype(BF)
        h1_all[lat] = h1
        h1_ref[0] = h1

    flat = nt(w_ref[0], h1_all[lat]) + bias_ref[0]
    parts = flat.reshape(3 * n_heads, HEAD_DIM, seq)
    scaling = LOG2E / HEAD_DIM**0.5
    outs = []
    lses = []
    for h in range(n_heads):
        q_t = (parts[h] * scaling).astype(BF)
        k_t = parts[n_heads + h]
        v_t = parts[2 * n_heads + h]
        v_ext = jnp.concatenate([v_t, jnp.ones((8, seq), F32)], 0).astype(BF)
        scores = mm(k_t.T.astype(BF), q_t)
        top = jnp.max(scores, 0, keepdims=True)
        probs = jnp.exp2(scores - top).astype(BF)
        out = mm(v_ext, probs)
        total = out[HEAD_DIM : HEAD_DIM + 1]
        outs.append(out[:HEAD_DIM] * (1.0 / total))
        lses.append(top + jnp.log2(total))

        @pl.when(slot == 0)
        def _():
            qkv_ref[0, h] = q_t
            qkv_ref[0, n_heads + h] = k_t.astype(BF)
            qkv_ref[0, 2 * n_heads + h] = v_t.astype(BF)
            lse_ref[0, h : h + 1] = lses[h]

    heads_ref[0, 0] = jnp.concatenate(outs, 0).astype(BF)


def attn_fwd(me, latents, mod, gathered, bias, n_mp):
    lat, seq, dim = latents.shape
    local = dim // n_mp
    n_heads = local // HEAD_DIM
    last = lat - 1
    first = lambda s, l: jnp.where(s == 0, l, last)
    return pl.pallas_call(
        attn_fwd_kernel,
        grid_spec=pltpu.PrefetchScalarGridSpec(
            num_scalar_prefetch=1,
            grid=(n_mp, lat),
            in_specs=[
                pl.BlockSpec((1, seq, dim), lambda s, l, me: (first(s, l), 0, 0)),
                pl.BlockSpec((1, 6, dim), lambda s, l, me: (l, 0, 0)),
                pl.BlockSpec(
                    (1, 3 * local, dim), lambda s, l, me: (lax.rem(me[0] + s, n_mp), 0, 0)
                ),
                pl.BlockSpec((1, 3 * local, 1), lambda s, l, me: (lax.rem(me[0] + s, n_mp), 0, 0)),
            ],
            out_specs=[
                pl.BlockSpec(
                    (1, 1, local, seq), lambda s, l, me: (lax.rem(me[0] + s, n_mp), l, 0, 0)
                ),
                pl.BlockSpec(
                    (1, 3 * n_heads, HEAD_DIM, seq), lambda s, l, me: (first(s, l), 0, 0, 0)
                ),
                pl.BlockSpec((1, n_heads, seq), lambda s, l, me: (first(s, l), 0, 0)),
                pl.BlockSpec((1, seq, dim), lambda s, l, me: (first(s, l), 0, 0)),
            ],
            scratch_shapes=[pltpu.VMEM((lat, seq, dim), BF)],
        ),
        out_shape=[
            jax.ShapeDtypeStruct((n_mp, lat, local, seq), BF),
            jax.ShapeDtypeStruct((lat, 3 * n_heads, HEAD_DIM, seq), BF),
            jax.ShapeDtypeStruct((lat, n_heads, seq), F32),
            jax.ShapeDtypeStruct((lat, seq, dim), BF),
        ],
        compiler_params=pltpu.CompilerParams(vmem_limit_bytes=60 * MIB),
        name="attn_fwd",
    )(me, latents, mod, gathered, bias)


def mlp_kernel(
    me_ref,
    heads_ref,
    lat_ref,
    cot_ref,
    mod_ref,
    wp_ref,
    w1_ref,
    w2_ref,
    bp_ref,
    b1_ref,
    b2_ref,
    out_ref,
    dx1_ref,
    da_ref,
    h2_ref,
    dm_ref,
    z_ref,
    du_ref,
    stats_ref,
    macc,
    dacc,
):
    n_mp, hid, dim = w1_ref.shape
    rows = lat_ref.shape[1]
    gate_one, shift_two = mod_ref[0, 2:3], mod_ref[0, 3:4]
    scale_two, gate_two = mod_ref[0, 4:5], mod_ref[0, 5:6]
    heads = heads_ref[:, 0].reshape(dim, rows)
    attn = tn(heads, wp_ref[...].reshape(dim, dim)) + bp_ref[...]
    x1 = lat_ref[0].astype(F32) + gate_one * attn
    n2, inv2 = norm_stats(x1)
    h2 = (n2 * (1.0 + scale_two) + shift_two).astype(BF)
    h2_ref[0] = h2
    cot = cot_ref[0].astype(F32)
    dm = (gate_two * cot).astype(BF)
    dm_ref[0] = dm

    macc[...] = jnp.zeros_like(macc)
    dacc[...] = jnp.zeros_like(dacc)

    def part(slot, own):
        w1 = w1_ref[slot]
        w2 = w2_ref[slot]
        u = nt(h2_ref[0], w1) + b1_ref[slot]
        dz = nt(dm_ref[0], w2)
        u2 = u * u
        t = jnp.tanh(u * (GELU_A + (GELU_A * GELU_B) * u2))
        half = 0.5 + 0.5 * t
        z = (u * half).astype(BF)
        slope = half + u * (1.0 - t * t) * (0.5 * GELU_A + (1.5 * GELU_A * GELU_B) * u2)
        du = (dz * slope).astype(BF)
        if own:
            z_ref[0] = z
            du_ref[0] = du
        macc[...] += mm(z, w2)
        dacc[...] += mm(du, w1)

    part(me_ref[0], True)

    def body(s, carry):
        part(lax.rem(me_ref[0] + s, n_mp), False)
        return carry

    lax.fori_loop(1, n_mp, body, 0)
    mlp = macc[...] + b2_ref[...]
    out_ref[0] = (x1 + gate_two * mlp).astype(BF)
    dh2 = dacc[...]
    dx1 = cot + norm_back(n2, inv2, dh2 * (1.0 + scale_two))
    dx1_ref[0] = dx1.astype(BF)
    da_ref[0] = (gate_one * dx1).astype(BF)
    total = lambda v: jnp.sum(v, 0, keepdims=True)
    stats = jnp.concatenate(
        [
            total(dx1 * attn),
            total(dh2),
            total(dh2 * n2),
            total(cot * mlp),
            total(cot),
            total(dx1),
            jnp.zeros((2, dim), F32),
        ],
        0,
    )

    @pl.when(pl.program_id(1) == 0)
    def _():
        stats_ref[0] = stats

    @pl.when(pl.program_id(1) > 0)
    def _():
        stats_ref[0] += stats


def mlp_both(me, heads, latents, cotangent, mod, gathered, bp, b1, b2, n_mp, rows):
    lat, seq, dim = latents.shape
    local = dim // n_mp
    hid = b1.shape[2]
    tok = pl.BlockSpec((1, rows, dim), lambda l, t, me: (l, t, 0))
    hidden = pl.BlockSpec((1, rows, hid), lambda l, t, me: (l, t, 0))
    once = lambda shape, at: pl.BlockSpec(
        shape, lambda l, t, me: at, pipeline_mode=pl.Buffered(1)
    )
    return pl.pallas_call(
        mlp_kernel,
        grid_spec=pltpu.PrefetchScalarGridSpec(
            num_scalar_prefetch=1,
            grid=(lat, seq // rows),
            in_specs=[
                pl.BlockSpec((n_mp, 1, local, rows), lambda l, t, me: (0, l, 0, t)),
                tok,
                tok,
                pl.BlockSpec((1, 6, dim), lambda l, t, me: (l, 0, 0)),
                once((n_mp, local, dim), (0, 3, 0)),
                once((n_mp, hid, dim), (0, 1, 0)),
                once((n_mp, hid, dim), (0, 2, 0)),
                once((1, dim), (0, 0)),
                once((n_mp, 1, hid), (0, 0, 0)),
                once((1, dim), (0, 0)),
            ],
            out_specs=[
                tok,
                tok,
                tok,
                tok,
                tok,
                hidden,
                hidden,
                pl.BlockSpec((1, 8, dim), lambda l, t, me: (l, 0, 0)),
            ],
            scratch_shapes=[pltpu.VMEM((rows, dim), F32)] * 2,
        ),
        out_shape=[jax.ShapeDtypeStruct((lat, seq, dim), BF)] * 5
        + [jax.ShapeDtypeStruct((lat, seq, hid), BF)] * 2
        + [jax.ShapeDtypeStruct((lat, 8, dim), F32)],
        compiler_params=pltpu.CompilerParams(vmem_limit_bytes=60 * MIB),
        name="mlp_both",
    )(me, heads, latents, cotangent, mod, gathered, gathered, gathered, bp, b1, b2)


def attn_bwd_kernel(da_ref, heads_ref, qkv_ref, lse_ref, wp_ref, wq_ref, dqkv_ref, dh1_ref, *, rows):
    n_heads = lse_ref.shape[1]
    seq = da_ref.shape[1]
    dheads = nt(wp_ref[...], da_ref[0]).reshape(n_heads, HEAD_DIM, seq)
    heads = heads_ref[0].astype(F32).reshape(n_heads, HEAD_DIM, seq)
    scaling = 1.0 / HEAD_DIM**0.5
    dq_list, dk_list, dv_list = [], [], []
    for h in range(n_heads):
        q_t = qkv_ref[0, h]
        k_t = qkv_ref[0, n_heads + h]
        v_t = qkv_ref[0, 2 * n_heads + h]
        q = q_t.astype(F32).T.astype(BF)
        k = k_t.astype(F32).T.astype(BF)
        v = v_t.astype(F32).T.astype(BF)
        do_t = dheads[h].astype(BF)
        do = dheads[h].T.astype(BF)
        inner = jnp.sum(do_t.astype(F32) * heads[h], 0, keepdims=True)
        dq_parts = []
        for i in range(seq // rows):
            cols = slice(i * rows, (i + 1) * rows)
            probs = jnp.exp2(mm(k, q_t[:, cols]) - lse_ref[0, h : h + 1, cols])
            dprobs = mm(v, do_t[:, cols])
            dscores = (probs * (dprobs - inner[:, cols])).astype(BF)
            dq_parts.append(mm(k_t, dscores))
            dv_new = mm(probs.astype(BF), do[cols])
            dk_new = mm(dscores, q[cols])
            dv = dv_new if i == 0 else dv + dv_new
            dk = dk_new if i == 0 else dk + dk_new
        dq_list.append(jnp.concatenate(dq_parts, 1) * scaling)
        dk_list.append(dk.T * (1.0 / LOG2E))
        dv_list.append(dv.T)
    dqkv = jnp.concatenate(dq_list + dk_list + dv_list, 0).astype(BF)
    dqkv_ref[0] = dqkv
    dh1_ref[0] = tn(dqkv, wq_ref[...]).astype(BF)


def attn_bwd(da, heads_own, qkv, lse, wp, wq, index, rows):
    lat, seq, dim = da.shape
    n_heads = lse.shape[1]
    local = n_heads * HEAD_DIM
    one = lambda shape: pl.BlockSpec((1,) + shape, lambda i: (index,) + (0,) * len(shape))
    whole = lambda shape: pl.BlockSpec(shape, lambda i: (0,) * len(shape))
    out = lambda shape: pl.BlockSpec((1,) + shape, lambda i: (0,) * (len(shape) + 1))
    return pl.pallas_call(
        functools.partial(attn_bwd_kernel, rows=rows),
        grid=(1,),
        in_specs=[
            one((seq, dim)),
            one((local, seq)),
            one((3 * n_heads, HEAD_DIM, seq)),
            one((n_heads, seq)),
            whole((local, dim)),
            whole((3 * local, dim)),
        ],
        out_specs=[out((3 * local, seq)), out((seq, dim))],
        out_shape=[
            jax.ShapeDtypeStruct((1, 3 * local, seq), BF),
            jax.ShapeDtypeStruct((1, seq, dim), BF),
        ],
        compiler_params=pltpu.CompilerParams(vmem_limit_bytes=60 * MIB),
        name="attn_bwd",
    )(da, heads_own, qkv, lse, wp, wq)


def latents_kernel(dh1_ref, dx1_ref, lat_ref, mod_ref, grad_ref, stats_ref):
    n1, inv1 = norm_stats(lat_ref[0].astype(F32))
    dh1 = dh1_ref[0].astype(F32)
    grad = dx1_ref[0].astype(F32) + norm_back(n1, inv1, dh1 * (1.0 + mod_ref[0, 1:2]))
    grad_ref[0] = grad.astype(BF)
    stats = jnp.concatenate(
        [
            jnp.sum(dh1, 0, keepdims=True),
            jnp.sum(dh1 * n1, 0, keepdims=True),
            jnp.zeros((6, dh1.shape[1]), F32),
        ],
        0,
    )

    @pl.when(pl.program_id(1) == 0)
    def _():
        stats_ref[0] = stats

    @pl.when(pl.program_id(1) > 0)
    def _():
        stats_ref[0] += stats


def latents_back(dh1, dx1, latents, mod, rows):
    lat, seq, dim = latents.shape
    tok = pl.BlockSpec((1, rows, dim), lambda l, t: (l, t, 0))
    return pl.pallas_call(
        latents_kernel,
        grid=(lat, seq // rows),
        in_specs=[tok, tok, tok, pl.BlockSpec((1, 6, dim), lambda l, t: (l, 0, 0))],
        out_specs=[tok, pl.BlockSpec((1, 8, dim), lambda l, t: (l, 0, 0))],
        out_shape=[
            jax.ShapeDtypeStruct((lat, seq, dim), BF),
            jax.ShapeDtypeStruct((lat, 8, dim), F32),
        ],
        compiler_params=pltpu.CompilerParams(vmem_limit_bytes=40 * MIB),
        name="latents_back",
    )(dh1, dx1, latents, mod)


def per_device(
    n_dp,
    n_mp,
    latents,
    condition,
    cotangent,
    qkv_weight,
    qv_bias,
    proj_weight,
    proj_bias,
    fc1_weight,
    fc1_bias,
    fc2_weight,
    fc2_bias,
    ada_weight,
    ada_bias,
):
    lat, seq, dim = latents.shape
    local = qkv_weight.shape[2]
    n_heads = local // HEAD_DIM
    hid = fc1_weight.shape[1]
    cols = ada_weight.shape[1]
    mp_at = lax.axis_index("mp")
    dp_at = lax.axis_index("dp")
    me = jnp.full((1,), mp_at, jnp.int32)

    cond_low = jax.nn.silu(condition).astype(BF)
    mod_part = mm(cond_low, ada_weight) + ada_bias.astype(F32)
    bias_row = jnp.concatenate([qv_bias.reshape(-1), fc1_bias]).astype(F32)[None]
    small = lax.all_gather(jnp.concatenate([mod_part, bias_row], 0), "mp", axis=0)
    mod = small[:, :lat].transpose(1, 0, 2).reshape(lat, 6, dim)
    qv_all = small[:, lat, : 2 * local].reshape(n_mp, 2, local)
    b_qkv = jnp.stack([qv_all[:, 0], jnp.zeros((n_mp, local), F32), qv_all[:, 1]], 1).reshape(
        n_mp, 3 * local, 1
    )
    b_fc1 = small[:, lat, 2 * local :].reshape(n_mp, 1, hid)

    wq_own = (
        qkv_weight.reshape(dim, 3, n_heads, HEAD_DIM).transpose(1, 2, 3, 0).reshape(3 * local, dim)
    )
    own = jnp.concatenate([wq_own, proj_weight, fc1_weight.T, fc2_weight], 0)
    share = own.shape[0] // n_dp
    mine = lax.dynamic_slice_in_dim(own, dp_at * share, share, 0)
    gathered = lax.all_gather(mine, ("dp", "mp"), axis=0).reshape(n_dp, n_mp, share, dim)
    gathered = gathered.transpose(1, 0, 2, 3).reshape(n_mp, n_dp * share, dim)

    heads, qkv, lse, h1 = attn_fwd(me, latents, mod, gathered, b_qkv, n_mp)
    block_out, dx1, da, h2, dm, z, du, stats_two = mlp_both(
        me,
        heads,
        latents,
        cotangent,
        mod,
        gathered,
        proj_bias.astype(F32)[None],
        b_fc1,
        fc2_bias.astype(F32)[None],
        n_mp,
        256,
    )
    flat = lambda v: v.reshape(lat * seq, v.shape[-1])
    grad_fc2 = tn(flat(z), flat(dm)).astype(BF)
    grad_fc1 = tn(flat(h2), flat(du)).astype(BF)
    grad_fc1_bias = jnp.sum(flat(du).astype(F32), 0)
    gate_one, gate_two = mod[:, 2], mod[:, 5]
    grad_fc2_bias = jnp.sum(gate_two * stats_two[:, 4], 0)
    grad_proj_bias = jnp.sum(gate_one * stats_two[:, 5], 0)
    grad_fc1, grad_fc2 = lax.psum((grad_fc1, grad_fc2), "dp")

    heads_own = lax.dynamic_index_in_dim(heads, mp_at, 0, keepdims=False)
    dqkv, dh1 = [], []
    for i in range(lat):
        dqkv_i, dh1_i = attn_bwd(da, heads_own, qkv, lse, proj_weight, wq_own, i, min(512, seq))
        dqkv.append(dqkv_i)
        dh1.append(lax.psum(dh1_i, "mp"))
    dqkv = jnp.concatenate(dqkv, 0)
    dh1 = jnp.concatenate(dh1, 0)
    grad_qkv = jnp.einsum("les,lsd->ed", dqkv, h1, preferred_element_type=F32).astype(BF)
    grad_proj = jnp.einsum("les,lsd->ed", heads_own, da, preferred_element_type=F32).astype(BF)
    bias_sums = jnp.sum(dqkv.astype(F32), (0, 2)).reshape(3, local)
    grad_qv_bias = jnp.stack([bias_sums[0], bias_sums[2]])
    grad_qkv, grad_proj = lax.psum((grad_qkv, grad_proj), "dp")
    biases = lax.psum(
        (grad_fc1_bias, grad_fc2_bias, grad_proj_bias, grad_qv_bias), "dp"
    )
    grad_fc1_bias, grad_fc2_bias, grad_proj_bias, grad_qv_bias = biases

    latents_grad, stats_one = latents_back(dh1, dx1, latents, mod, 256)

    dmod = jnp.stack(
        [
            stats_one[:, 0],
            stats_one[:, 1],
            stats_two[:, 0],
            stats_two[:, 1],
            stats_two[:, 2],
            stats_two[:, 3],
        ],
        1,
    )
    dmod = dmod.reshape(lat, 6 * dim).astype(BF)
    dmod_own = lax.dynamic_slice_in_dim(dmod, mp_at * cols, cols, 1)
    every = lax.all_gather(jnp.concatenate([cond_low, dmod_own], 1), "dp", axis=0, tiled=True)
    grad_ada = tn(every[:, :dim], every[:, dim:])
    grad_ada_bias = jnp.sum(every[:, dim:].astype(F32), 0)
    grad_act = lax.psum(nt(dmod_own, ada_weight), "mp")
    condition_grad = jax.vjp(jax.nn.silu, condition)[1](grad_act)[0]

    back = lambda v: v.astype(F32)
    return (
        block_out,
        latents_grad,
        condition_grad,
        back(grad_qkv).reshape(3, local, dim).transpose(2, 0, 1),
        grad_qv_bias,
        back(grad_proj),
        grad_proj_bias,
        back(grad_fc1),
        grad_fc1_bias,
        back(grad_fc2),
        grad_fc2_bias,
        grad_ada,
        grad_ada_bias,
    )


def solution(mesh):
    in_specs = (
        P("dp", None, None),
        P("dp", None),
        P("dp", None, None),
        P(None, None, "mp"),
        P(None, "mp"),
        P("mp", None),
        P(),
        P(None, "mp"),
        P("mp"),
        P("mp", None),
        P(),
        P(None, "mp"),
        P("mp"),
    )
    out_specs = (
        P("dp", None, None),
        P("dp", None, None),
        P("dp", None),
        P(None, None, "mp"),
        P(None, "mp"),
        P("mp", None),
        P(),
        P(None, "mp"),
        P("mp"),
        P("mp", None),
        P(),
        P(None, "mp"),
        P("mp"),
    )
    body = functools.partial(per_device, mesh.shape["dp"], mesh.shape["mp"])
    return jax.shard_map(body, mesh=mesh, in_specs=in_specs, out_specs=out_specs, check_vma=False)
```

```python
import functools

import jax
import jax.numpy as jnp
from jax import lax
from jax.experimental import pallas as pl
from jax.experimental.pallas import tpu as pltpu
from jax.sharding import PartitionSpec as P

HEAD_DIM = 72
EPS = 1e-06
LOG2E = 1.4426950408889634
GELU_A = 0.7978845608028654
GELU_B = 0.044715
BF = jnp.bfloat16
F32 = jnp.float32
MIB = 2**20


def mm(a, b):
    return jnp.dot(a, b, preferred_element_type=F32)


def nt(a, b):
    return lax.dot_general(a, b, (((1,), (1,)), ((), ())), preferred_element_type=F32)


def tn(a, b):
    return lax.dot_general(a, b, (((0,), (0,)), ((), ())), preferred_element_type=F32)


def norm_stats(values):
    centered = values - jnp.mean(values, -1, keepdims=True)
    inv_std = lax.rsqrt(jnp.mean(centered * centered, -1, keepdims=True) + EPS)
    return centered * inv_std, inv_std


def norm_back(normed, inv_std, grad_normed):
    first = jnp.mean(grad_normed, -1, keepdims=True)
    second = jnp.mean(grad_normed * normed, -1, keepdims=True)
    return inv_std * (grad_normed - first - normed * second)


def flip(value, bit):
    step = 1 << bit
    return value + step - 2 * step * (value // step % 2)


def other_part(me, k):
    return (me + k) % 2 + 2 * ((me // 2 + k // 2) % 2)


def line_peers(me, n):
    return jnp.minimum(me, 1) + jnp.minimum(n - 1 - me, 1)


def at_mesh(dp_at, mp_at):
    return {"device_id": (dp_at, mp_at), "device_id_type": pl.DeviceIdType.MESH}


def modulation_kernel(cond_ref, w_ref, bias_ref, row_ref, out_ref, low_ref, send, recv):
    dp_at, me = lax.axis_index("dp"), lax.axis_index("mp")
    n_mp = out_ref.shape[0]
    lat = cond_ref.shape[0]
    barrier = pltpu.get_barrier_semaphore()
    for k in range(1, n_mp):
        pl.semaphore_signal(barrier, inc=1, **at_mesh(dp_at, (me + k) % n_mp))
    cond = cond_ref[...]
    low = (cond * jax.nn.sigmoid(cond)).astype(BF)
    low_ref[...] = low
    part = mm(low, w_ref[...]) + bias_ref[...]
    cols = part.shape[1]
    out_ref[me] = jnp.concatenate([part, row_ref[...], jnp.zeros((8 - lat - 1, cols), F32)], 0)
    pl.semaphore_wait(barrier, n_mp - 1)
    copies = []
    for k in range(1, n_mp):
        copies.append(
            pltpu.make_async_remote_copy(
                out_ref.at[me],
                out_ref.at[me],
                send.at[k - 1],
                recv.at[k - 1],
                **at_mesh(dp_at, (me + k) % n_mp),
            )
        )
        copies[-1].start()
    for k in range(1, n_mp):
        came = out_ref.at[(me + n_mp - k) % n_mp]
        pltpu.make_async_remote_copy(
            came, came, send.at[k - 1], recv.at[k - 1], **at_mesh(dp_at, (me + k) % n_mp)
        ).wait_recv()
    for copy in copies:
        copy.wait_send()


def modulation_all(condition, ada_weight, ada_bias, bias_row, n_mp):
    cols = ada_weight.shape[1]
    vmem = pl.BlockSpec(memory_space=pltpu.VMEM)
    return pl.pallas_call(
        modulation_kernel,
        in_specs=[vmem] * 4,
        out_specs=[vmem, vmem],
        out_shape=[
            jax.ShapeDtypeStruct((n_mp, 8, cols), F32),
            jax.ShapeDtypeStruct(condition.shape, BF),
        ],
        scratch_shapes=[pltpu.SemaphoreType.DMA((n_mp - 1,))] * 2,
        compiler_params=pltpu.CompilerParams(
            collective_id=0, has_side_effects=True, vmem_limit_bytes=40 * MIB
        ),
        name="modulation",
    )(condition, ada_weight, ada_bias, bias_row)


def attend(flat, n_heads, slot, heads_ref, qkv_ref, lse_ref, between):
    seq = flat.shape[1]
    parts = flat.reshape(3 * n_heads, HEAD_DIM, seq)
    scaling = LOG2E / HEAD_DIM**0.5
    outs = []
    for h in range(n_heads):
        q_t = (parts[h] * scaling).astype(BF)
        k_t = parts[n_heads + h]
        v_t = parts[2 * n_heads + h]
        v_ext = jnp.concatenate([v_t, jnp.ones((8, seq), F32)], 0).astype(BF)
        scores = mm(k_t.T.astype(BF), q_t)
        top = jnp.max(scores, 0, keepdims=True)
        probs = jnp.exp2(scores - top).astype(BF)
        out = mm(v_ext, probs)
        total = out[HEAD_DIM : HEAD_DIM + 1]
        outs.append(out[:HEAD_DIM] * (1.0 / total))
        lse = top + jnp.log2(total)

        @pl.when(slot == 0)
        def _():
            qkv_ref[0, h] = q_t
            qkv_ref[0, n_heads + h] = k_t.astype(BF)
            qkv_ref[0, 2 * n_heads + h] = v_t.astype(BF)
            lse_ref[0, h : h + 1] = lse

        between(h + 1)
    heads_ref[0, 0] = jnp.concatenate(outs, 0).astype(BF)


def mixed_one(lat_ref, mod_ref, h1_ref, h1_all, lat):
    normed, _ = norm_stats(lat_ref[0].astype(F32))
    h1 = (normed * (1.0 + mod_ref[0, 1:2]) + mod_ref[0, 0:1]).astype(BF)
    h1_all[lat] = h1
    h1_ref[0] = h1


def attn_fwd_kernel(
    me_ref, lat_ref, mod_ref, w_ref, bias_ref, heads_ref, qkv_ref, lse_ref, h1_ref, h1_all
):
    slot, lat = pl.program_id(0), pl.program_id(1)

    @pl.when(slot == 0)
    def _():
        mixed_one(lat_ref, mod_ref, h1_ref, h1_all, lat)

    flat = nt(w_ref[0], h1_all[lat]) + bias_ref[0]
    attend(flat, qkv_ref.shape[1] // 3, slot, heads_ref, qkv_ref, lse_ref, lambda h: None)


def attn_gather_kernel(
    lat_ref,
    mod_ref,
    bias_ref,
    own_ref,
    heads_ref,
    qkv_ref,
    lse_ref,
    h1_ref,
    all_ref,
    h1_all,
    w_buf,
    local_sem,
    z_own,
    z_on,
    z_got,
    sends,
    recvs,
):
    n_mp = all_ref.shape[0]
    lats = h1_all.shape[0]
    units = 3 * (n_mp - 1)
    slot, lat = pl.program_id(0), pl.program_id(1)
    step = slot * lats + lat
    dp_at, me = lax.axis_index("dp"), lax.axis_index("mp")
    core, x, y = dp_at % 2, dp_at // 2 % 2, dp_at // 4
    rows = own_ref.shape[4]
    cut = rows // 32 * 16 + 16
    near, far = pl.ds(0, cut), pl.ds(cut, rows - cut)
    every = pl.ds(0, rows)
    both = pl.ds(0, 2)
    core_id = at_mesh(flip(dp_at, 0), me)
    x_id = at_mesh(flip(dp_at, 1), me)
    y_id = at_mesh(flip(dp_at, 2), me)
    right_id, left_id = at_mesh(dp_at, me + 1), at_mesh(dp_at, me - 1)

    def piece(s, c, at_y, at_x, at_core, part):
        return all_ref.at[s, c, at_y, at_x, at_core, part]

    def own_copy(c, side, target):
        return pltpu.make_async_remote_copy(
            own_ref.at[c, y, x, core],
            piece(me, c, y, x, core, every),
            z_own.at[side, c],
            z_got.at[c, me],
            **target,
        )

    def pass_on(s, c, target):
        ref = piece(s, c, y, x, core, every)
        return pltpu.make_async_remote_copy(
            ref, ref, z_on.at[c, s], z_got.at[c, s], **target
        )

    def move(kind, c, s, arrived=False):
        flipped = lambda v: 1 - v if arrived else v
        at_y, at_x, at_core, part, target = (
            (pl.ds(y, 1), pl.ds(flipped(x), 1), pl.ds(core, 1), near, x_id),
            (pl.ds(flipped(y), 1), pl.ds(x, 1), pl.ds(core, 1), far, y_id),
            (pl.ds(flipped(y), 1), both, pl.ds(core, 1), near, y_id),
            (both, pl.ds(flipped(x), 1), pl.ds(core, 1), far, x_id),
            (both, both, pl.ds(flipped(core), 1), every, core_id),
        )[kind]
        ref = piece(s, c, at_y, at_x, at_core, part)
        return pltpu.make_async_remote_copy(
            ref, ref, sends.at[kind, c, s], recvs.at[kind, c, s], **target
        )

    def unit(u):
        return u // (n_mp - 1), other_part(me, 1 + u % (n_mp - 1))

    def event(stage, u):
        c, s = unit(u)

        @pl.when((u >= 0) & (u < units))
        def _():
            if stage == 1:
                pass_on(s, c, right_id).wait_recv()

                @pl.when((s < me) & (me < n_mp - 1))
                def _():
                    pass_on(s, c, right_id).start()

                @pl.when((s > me) & (me > 0))
                def _():
                    pass_on(s, c, left_id).start()

                move(0, c, s).start()
                move(1, c, s).start()
            if stage == 2:
                move(0, c, s, True).wait_recv()
                move(1, c, s, True).wait_recv()
                move(2, c, s).start()
                move(3, c, s).start()
            if stage == 3:
                move(2, c, s, True).wait_recv()
                move(3, c, s, True).wait_recv()
                move(4, c, s).start()
            if stage == 4:
                move(4, c, s, True).wait_recv()

    def send_own(c):
        @pl.when(me < n_mp - 1)
        def _():
            own_copy(c, 0, right_id).start()

        @pl.when(me > 0)
        def _():
            own_copy(c, 1, left_id).start()

    @pl.when(step == 0)
    def _():
        barrier = pltpu.get_barrier_semaphore()
        for target in (core_id, x_id, y_id):
            pl.semaphore_signal(barrier, inc=1, **target)

        @pl.when(me < n_mp - 1)
        def _():
            pl.semaphore_signal(barrier, inc=1, **right_id)

        @pl.when(me > 0)
        def _():
            pl.semaphore_signal(barrier, inc=1, **left_id)

        pl.semaphore_wait(barrier, 3 + line_peers(me, n_mp))
        send_own(0)

    for c in (1, 2):

        @pl.when(step == 3 * c - 1)
        def _():
            send_own(c)

    event(4, step - 3)
    event(3, step - 2)

    @pl.when((lat == 0) & (slot == 0))
    def _():
        load = pltpu.make_async_copy(own_ref.at[0], w_buf, local_sem.at[0])
        load.start()
        load.wait()

    @pl.when((lat == 0) & (slot > 0))
    def _():
        load = pltpu.make_async_copy(all_ref.at[other_part(me, slot), 0], w_buf, local_sem.at[0])
        load.start()
        load.wait()

    @pl.when(slot == 0)
    def _():
        mixed_one(lat_ref, mod_ref, h1_ref, h1_all, lat)

    n_heads = qkv_ref.shape[1] // 3
    weights = w_buf[...].reshape(8 * rows, w_buf.shape[-1])[: 3 * n_heads * HEAD_DIM]
    flat = nt(weights, h1_all[lat]) + bias_ref[0]

    def between(h):
        if h == 1:
            event(2, step - 1)
        if h == 3:
            event(1, step)

    attend(flat, n_heads, slot, heads_ref, qkv_ref, lse_ref, between)

    @pl.when(step == n_mp * lats - 1)
    def _():
        for c in range(3):

            @pl.when(me < n_mp - 1)
            def _():
                own_copy(c, 0, right_id).wait_send()

            @pl.when(me > 0)
            def _():
                own_copy(c, 1, left_id).wait_send()

        def drain(u, carry):
            c, s = unit(u)

            @pl.when((s < me) & (me < n_mp - 1))
            def _():
                pass_on(s, c, right_id).wait_send()

            @pl.when((s > me) & (me > 0))
            def _():
                pass_on(s, c, left_id).wait_send()

            for kind in range(5):
                move(kind, c, s).wait_send()
            return carry

        lax.fori_loop(0, units, drain, 0)


def attn_gather(latents, mod, bias, own, n_mp):
    lat, seq, dim = latents.shape
    local = dim // n_mp
    n_heads = local // HEAD_DIM
    rows = own.shape[0] // 24
    own = own.reshape(3, 2, 2, 2, rows, dim)
    last = lat - 1
    first = lambda s, l: s // n_mp * 0 + jnp.where(s == 0, l, last)
    part = lambda s: other_part(lax.axis_index("mp"), s)
    heads, qkv, lse, h1, gathered = pl.pallas_call(
        attn_gather_kernel,
        grid=(n_mp, lat),
        in_specs=[
            pl.BlockSpec((1, seq, dim), lambda s, l: (first(s, l), 0, 0)),
            pl.BlockSpec((1, 6, dim), lambda s, l: (l, 0, 0)),
            pl.BlockSpec((1, 3 * local, 1), lambda s, l: (part(s), 0, 0)),
            pl.BlockSpec(memory_space=pl.ANY),
        ],
        out_specs=[
            pl.BlockSpec((1, 1, local, seq), lambda s, l: (part(s), l, 0, 0)),
            pl.BlockSpec((1, 3 * n_heads, HEAD_DIM, seq), lambda s, l: (first(s, l), 0, 0, 0)),
            pl.BlockSpec((1, n_heads, seq), lambda s, l: (first(s, l), 0, 0)),
            pl.BlockSpec((1, seq, dim), lambda s, l: (first(s, l), 0, 0)),
            pl.BlockSpec(memory_space=pl.ANY),
        ],
        out_shape=[
            jax.ShapeDtypeStruct((n_mp, lat, local, seq), BF),
            jax.ShapeDtypeStruct((lat, 3 * n_heads, HEAD_DIM, seq), BF),
            jax.ShapeDtypeStruct((lat, n_heads, seq), F32),
            jax.ShapeDtypeStruct((lat, seq, dim), BF),
            jax.ShapeDtypeStruct((n_mp, 3, 2, 2, 2, rows, dim), BF),
        ],
        scratch_shapes=[
            pltpu.VMEM((lat, seq, dim), BF),
            pltpu.VMEM((2, 2, 2, rows, dim), BF),
            pltpu.SemaphoreType.DMA((1,)),
            pltpu.SemaphoreType.DMA((2, 3)),
            pltpu.SemaphoreType.DMA((3, n_mp)),
            pltpu.SemaphoreType.DMA((3, n_mp)),
            pltpu.SemaphoreType.DMA((5, 3, n_mp)),
            pltpu.SemaphoreType.DMA((5, 3, n_mp)),
        ],
        compiler_params=pltpu.CompilerParams(
            collective_id=1, has_side_effects=True, vmem_limit_bytes=60 * MIB
        ),
        name="attn_gather",
    )(latents, mod, bias, own)
    return heads, qkv, lse, h1, gathered.reshape(n_mp, 24 * rows, dim)


def attn_fwd(me, latents, mod, gathered, bias, n_mp):
    lat, seq, dim = latents.shape
    local = dim // n_mp
    n_heads = local // HEAD_DIM
    last = lat - 1
    first = lambda s, l: jnp.where(s == 0, l, last)
    return pl.pallas_call(
        attn_fwd_kernel,
        grid_spec=pltpu.PrefetchScalarGridSpec(
            num_scalar_prefetch=1,
            grid=(n_mp, lat),
            in_specs=[
                pl.BlockSpec((1, seq, dim), lambda s, l, me: (first(s, l), 0, 0)),
                pl.BlockSpec((1, 6, dim), lambda s, l, me: (l, 0, 0)),
                pl.BlockSpec(
                    (1, 3 * local, dim), lambda s, l, me: (lax.rem(me[0] + s, n_mp), 0, 0)
                ),
                pl.BlockSpec((1, 3 * local, 1), lambda s, l, me: (lax.rem(me[0] + s, n_mp), 0, 0)),
            ],
            out_specs=[
                pl.BlockSpec(
                    (1, 1, local, seq), lambda s, l, me: (lax.rem(me[0] + s, n_mp), l, 0, 0)
                ),
                pl.BlockSpec(
                    (1, 3 * n_heads, HEAD_DIM, seq), lambda s, l, me: (first(s, l), 0, 0, 0)
                ),
                pl.BlockSpec((1, n_heads, seq), lambda s, l, me: (first(s, l), 0, 0)),
                pl.BlockSpec((1, seq, dim), lambda s, l, me: (first(s, l), 0, 0)),
            ],
            scratch_shapes=[pltpu.VMEM((lat, seq, dim), BF)],
        ),
        out_shape=[
            jax.ShapeDtypeStruct((n_mp, lat, local, seq), BF),
            jax.ShapeDtypeStruct((lat, 3 * n_heads, HEAD_DIM, seq), BF),
            jax.ShapeDtypeStruct((lat, n_heads, seq), F32),
            jax.ShapeDtypeStruct((lat, seq, dim), BF),
        ],
        compiler_params=pltpu.CompilerParams(vmem_limit_bytes=60 * MIB),
        name="attn_fwd",
    )(me, latents, mod, gathered, bias)


class LineSum:
    def __init__(self, own_ref, up, down, sems, out_ref):
        self.own, self.up, self.down, self.sems, self.out = own_ref, up, down, sems, out_ref
        self.count, self.rows = up.shape[0], up.shape[1]
        self.me = lax.axis_index("mp")
        self.n = lax.axis_size("mp")
        dp_at = lax.axis_index("dp")
        self.ends = (at_mesh(dp_at, self.me + 1), at_mesh(dp_at, self.me - 1))
        self.place = (self.me, self.n - 1 - self.me)

    def guarded(self, side, first, action):
        there = self.place[side] > 0 if first else self.place[side] < self.n - 1

        @pl.when(there)
        def _():
            action()

    def barrier(self):
        sem = pltpu.get_barrier_semaphore()
        for side in (0, 1):
            self.guarded(side, False, lambda: pl.semaphore_signal(sem, inc=1, **self.ends[side]))
        pl.semaphore_wait(sem, line_peers(self.me, self.n))

    def copy(self, side, c):
        ref = (self.up, self.down)[side].at[c]
        return pltpu.make_async_remote_copy(
            ref, ref, self.sems.at[2 * side, c], self.sems.at[2 * side + 1, c], **self.ends[side]
        )

    def handle(self, side, c):
        ref = (self.up, self.down)[side]
        own = self.own[0, pl.ds(pl.multiple_of(c * self.rows, self.rows), self.rows)]

        @pl.when(self.place[side] == 0)
        def _():
            ref[c] = own

        @pl.when(self.place[side] > 0)
        def _():
            self.copy(side, c).wait_recv()
            ref[c] = (ref[c].astype(F32) + own.astype(F32)).astype(BF)

        self.guarded(side, False, lambda: self.copy(side, c).start())

    def tick(self, t):
        for side in (0, 1):
            at = t - 2 * self.place[side]

            @pl.when((at >= 0) & (at % 3 < 2) & (at - at // 3 < self.count))
            def _():
                self.handle(side, at - at // 3)

    def finish(self, ticks):
        for side in (0, 1):
            done = jnp.maximum(ticks - 2 * self.place[side], 0)
            done = jnp.minimum(done - done // 3, self.count)

            def late(c, carry):
                self.handle(side, c)
                return carry

            lax.fori_loop(done, self.count, late, 0)

        def add(c, carry):
            rows = pl.ds(pl.multiple_of(c * self.rows, self.rows), self.rows)
            total = self.up[c].astype(F32) + self.down[c].astype(F32)
            self.out[0, rows] = (total - self.own[0, rows].astype(F32)).astype(BF)
            return carry

        lax.fori_loop(0, self.count, add, 0)
        for side in (0, 1):

            def sent(c, carry):
                self.copy(side, c).wait_send()
                return carry

            self.guarded(side, False, lambda: lax.fori_loop(0, self.count, sent, 0))


def mlp_kernel(*refs, summing):
    heads_ref, lat_ref, cot_ref, mod_ref, own_ref, all_ref, bp_ref, b1_ref, b2_ref = refs[:9]
    refs = refs[9:]
    if summing:
        part_ref, refs = refs[0], refs[1:]
    out_ref, dx1_ref, da_ref, h2_ref, dm_ref, z_ref, du_ref, stats_ref = refs[:8]
    refs = refs[8:]
    if summing:
        sum_ref, refs = refs[0], refs[1:]
    macc, dacc, wp, w1, w2, load_sems = refs[:6]
    n_mp, hid, dim = w1.shape
    local = wp.shape[1]
    rows = lat_ref.shape[1]
    me = lax.axis_index("mp")
    step = pl.program_id(0)
    line = LineSum(part_ref, refs[6], refs[7], refs[8], sum_ref) if summing else None

    def load(kind, k):
        at = own_ref if k == 0 else all_ref.at[(me + k) % n_mp]
        first, count, ref = (
            (3 * local, local, wp.at[(me + k) % n_mp]),
            (4 * local, hid, w1.at[k]),
            (4 * local + hid, hid, w2.at[k]),
        )[kind]
        return pltpu.make_async_copy(at.at[pl.ds(first, count)], ref, load_sems.at[kind, k])

    @pl.when(step == 0)
    def _():
        if summing:
            line.barrier()
        for k in range(n_mp):
            load(0, k).start()
        for k in range(n_mp):
            load(1, k).start()
            load(2, k).start()
        for k in range(n_mp):
            load(0, k).wait()

    gate_one, shift_two = mod_ref[0, 2:3], mod_ref[0, 3:4]
    scale_two, gate_two = mod_ref[0, 4:5], mod_ref[0, 5:6]
    heads = heads_ref[:, 0].reshape(dim, rows)
    attn = tn(heads, wp[...].reshape(dim, dim)) + bp_ref[...]
    x1 = lat_ref[0].astype(F32) + gate_one * attn
    n2, inv2 = norm_stats(x1)
    h2 = (n2 * (1.0 + scale_two) + shift_two).astype(BF)
    h2_ref[0] = h2
    cot = cot_ref[0].astype(F32)
    dm = (gate_two * cot).astype(BF)
    dm_ref[0] = dm

    macc[...] = jnp.zeros_like(macc)
    dacc[...] = jnp.zeros_like(dacc)

    def part(k, own):
        if summing:
            line.tick(step * n_mp + k)

        @pl.when(step == 0)
        def _():
            for kind in (1, 2):
                ref = (w1, w2)[kind - 1].at[k]
                pltpu.make_async_copy(ref, ref, load_sems.at[kind, k]).wait()

        u = nt(h2_ref[0], w1[k]) + b1_ref[(me + k) % n_mp]
        dz = nt(dm_ref[0], w2[k])
        u2 = u * u
        t = jnp.tanh(u * (GELU_A + (GELU_A * GELU_B) * u2))
        half = 0.5 + 0.5 * t
        z = (u * half).astype(BF)
        slope = half + u * (1.0 - t * t) * (0.5 * GELU_A + (1.5 * GELU_A * GELU_B) * u2)
        du = (dz * slope).astype(BF)
        if own:
            z_ref[0] = z
            du_ref[0] = du
        macc[...] += mm(z, w2[k])
        dacc[...] += mm(du, w1[k])

    part(0, True)

    def body(k, carry):
        part(k, False)
        return carry

    lax.fori_loop(1, n_mp, body, 0)
    mlp = macc[...] + b2_ref[...]
    out_ref[0] = (x1 + gate_two * mlp).astype(BF)
    dh2 = dacc[...]
    dx1 = cot + norm_back(n2, inv2, dh2 * (1.0 + scale_two))
    dx1_ref[0] = dx1.astype(BF)
    da_ref[0] = (gate_one * dx1).astype(BF)
    total = lambda v: jnp.sum(v, 0, keepdims=True)
    stats = jnp.concatenate(
        [
            total(dx1 * attn),
            total(dh2),
            total(dh2 * n2),
            total(cot * mlp),
            total(cot),
            total(dx1),
            jnp.zeros((2, dim), F32),
        ],
        0,
    )

    @pl.when(step == 0)
    def _():
        stats_ref[0] = stats

    @pl.when(step > 0)
    def _():
        stats_ref[0] += stats

    if summing:

        @pl.when(step == pl.num_programs(0) - 1)
        def _():
            line.finish(pl.num_programs(0) * n_mp)


LINE_CHUNKS = 8


def line_scratch(seq, dim):
    rows = seq // LINE_CHUNKS
    return [
        pltpu.VMEM((LINE_CHUNKS, rows, dim), BF),
        pltpu.VMEM((LINE_CHUNKS, rows, dim), BF),
        pltpu.SemaphoreType.DMA((4, LINE_CHUNKS)),
    ]


def mlp_both(index, heads, latents, cotangent, mod, own, gathered, bp, b1, b2, n_mp, rows, part):
    lat, seq, dim = latents.shape
    local = dim // n_mp
    hid = b1.shape[2]
    tok = pl.BlockSpec((1, rows, dim), lambda t: (index, t, 0))
    new = pl.BlockSpec((1, rows, dim), lambda t: (0, t, 0))
    hidden = pl.BlockSpec((1, rows, hid), lambda t: (0, t, 0))
    once = lambda shape: pl.BlockSpec(
        shape, lambda t: (0,) * len(shape), pipeline_mode=pl.Buffered(1)
    )
    any_spec = pl.BlockSpec(memory_space=pl.ANY)
    summing = part is not None
    extra = [once((1, seq, dim))] if summing else []
    return pl.pallas_call(
        functools.partial(mlp_kernel, summing=summing),
        grid=(seq // rows,),
        in_specs=[
            pl.BlockSpec((n_mp, 1, local, rows), lambda t: (0, index, 0, t)),
            tok,
            tok,
            pl.BlockSpec((1, 6, dim), lambda t: (index, 0, 0)),
            any_spec,
            any_spec,
            once((1, dim)),
            once((n_mp, 1, hid)),
            once((1, dim)),
        ]
        + extra,
        out_specs=[new] * 5
        + [hidden, hidden, pl.BlockSpec((1, 8, dim), lambda t: (0, 0, 0))]
        + extra,
        out_shape=[jax.ShapeDtypeStruct((1, seq, dim), BF)] * 5
        + [jax.ShapeDtypeStruct((1, seq, hid), BF)] * 2
        + [jax.ShapeDtypeStruct((1, 8, dim), F32)]
        + ([jax.ShapeDtypeStruct((1, seq, dim), BF)] if summing else []),
        scratch_shapes=[
            pltpu.VMEM((rows, dim), F32),
            pltpu.VMEM((rows, dim), F32),
            pltpu.VMEM((n_mp, local, dim), BF),
            pltpu.VMEM((n_mp, hid, dim), BF),
            pltpu.VMEM((n_mp, hid, dim), BF),
            pltpu.SemaphoreType.DMA((3, n_mp)),
        ]
        + (line_scratch(seq, dim) if summing else []),
        compiler_params=pltpu.CompilerParams(
            vmem_limit_bytes=63 * MIB,
            **(dict(collective_id=3 + index, has_side_effects=True) if summing else {}),
        ),
        name="mlp_sum" if summing else "mlp_both",
    )(
        heads,
        latents,
        cotangent,
        mod,
        own,
        gathered,
        bp,
        b1,
        b2,
        *([part] if summing else []),
    )


def line_kernel(part_ref, sum_ref, up, down, sems):
    line = LineSum(part_ref, up, down, sems, sum_ref)
    line.barrier()
    line.finish(0)


def line_sum(part):
    _, seq, dim = part.shape
    vmem = pl.BlockSpec(memory_space=pltpu.VMEM)
    return pl.pallas_call(
        line_kernel,
        in_specs=[vmem],
        out_specs=vmem,
        out_shape=jax.ShapeDtypeStruct(part.shape, BF),
        scratch_shapes=line_scratch(seq, dim),
        compiler_params=pltpu.CompilerParams(
            collective_id=2, has_side_effects=True, vmem_limit_bytes=40 * MIB
        ),
        name="line_sum",
    )(part)


def attn_bwd_kernel(da_ref, heads_ref, qkv_ref, lse_ref, wp_ref, wq_ref, dqkv_ref, dh1_ref, *, rows):
    n_heads = lse_ref.shape[1]
    seq = da_ref.shape[1]
    dheads = nt(wp_ref[...], da_ref[0]).reshape(n_heads, HEAD_DIM, seq)
    heads = heads_ref[0].astype(F32).reshape(n_heads, HEAD_DIM, seq)
    scaling = 1.0 / HEAD_DIM**0.5
    dq_list, dk_list, dv_list = [], [], []
    for h in range(n_heads):
        q_t = qkv_ref[0, h]
        k_t = qkv_ref[0, n_heads + h]
        v_t = qkv_ref[0, 2 * n_heads + h]
        q = q_t.astype(F32).T.astype(BF)
        k = k_t.astype(F32).T.astype(BF)
        v = v_t.astype(F32).T.astype(BF)
        do_t = dheads[h].astype(BF)
        do = dheads[h].T.astype(BF)
        inner = jnp.sum(do_t.astype(F32) * heads[h], 0, keepdims=True)
        dq_parts = []
        for i in range(seq // rows):
            cols = slice(i * rows, (i + 1) * rows)
            probs = jnp.exp2(mm(k, q_t[:, cols]) - lse_ref[0, h : h + 1, cols])
            dprobs = mm(v, do_t[:, cols])
            dscores = (probs * (dprobs - inner[:, cols])).astype(BF)
            dq_parts.append(mm(k_t, dscores))
            dv_new = mm(probs.astype(BF), do[cols])
            dk_new = mm(dscores, q[cols])
            dv = dv_new if i == 0 else dv + dv_new
            dk = dk_new if i == 0 else dk + dk_new
        dq_list.append(jnp.concatenate(dq_parts, 1) * scaling)
        dk_list.append(dk.T * (1.0 / LOG2E))
        dv_list.append(dv.T)
    dqkv = jnp.concatenate(dq_list + dk_list + dv_list, 0).astype(BF)
    dqkv_ref[0] = dqkv
    dh1_ref[0] = tn(dqkv, wq_ref[...]).astype(BF)


def attn_bwd(da, heads_own, qkv, lse, wp, wq, index, rows):
    lat, seq, dim = da.shape
    n_heads = lse.shape[1]
    local = n_heads * HEAD_DIM
    one = lambda shape: pl.BlockSpec((1,) + shape, lambda i: (index,) + (0,) * len(shape))
    only = lambda shape: pl.BlockSpec((1,) + shape, lambda i: (0,) * (len(shape) + 1))
    whole = lambda shape: pl.BlockSpec(shape, lambda i: (0,) * len(shape))
    out = lambda shape: pl.BlockSpec((1,) + shape, lambda i: (0,) * (len(shape) + 1))
    return pl.pallas_call(
        functools.partial(attn_bwd_kernel, rows=rows),
        grid=(1,),
        in_specs=[
            only((seq, dim)),
            one((local, seq)),
            one((3 * n_heads, HEAD_DIM, seq)),
            one((n_heads, seq)),
            whole((local, dim)),
            whole((3 * local, dim)),
        ],
        out_specs=[out((3 * local, seq)), out((seq, dim))],
        out_shape=[
            jax.ShapeDtypeStruct((1, 3 * local, seq), BF),
            jax.ShapeDtypeStruct((1, seq, dim), BF),
        ],
        compiler_params=pltpu.CompilerParams(vmem_limit_bytes=60 * MIB),
        name="attn_bwd",
    )(da, heads_own, qkv, lse, wp, wq)


def latents_kernel(dh1_ref, dx1_ref, lat_ref, mod_ref, grad_ref, stats_ref):
    n1, inv1 = norm_stats(lat_ref[0].astype(F32))
    dh1 = dh1_ref[0].astype(F32)
    grad = dx1_ref[0].astype(F32) + norm_back(n1, inv1, dh1 * (1.0 + mod_ref[0, 1:2]))
    grad_ref[0] = grad.astype(BF)
    stats = jnp.concatenate(
        [
            jnp.sum(dh1, 0, keepdims=True),
            jnp.sum(dh1 * n1, 0, keepdims=True),
            jnp.zeros((6, dh1.shape[1]), F32),
        ],
        0,
    )

    @pl.when(pl.program_id(0) == 0)
    def _():
        stats_ref[0] = stats

    @pl.when(pl.program_id(0) > 0)
    def _():
        stats_ref[0] += stats


def latents_back(dh1, dx1, latents, mod, index, rows):
    lat, seq, dim = latents.shape
    tok = pl.BlockSpec((1, rows, dim), lambda t: (index, t, 0))
    new = pl.BlockSpec((1, rows, dim), lambda t: (0, t, 0))
    return pl.pallas_call(
        latents_kernel,
        grid=(seq // rows,),
        in_specs=[new, new, tok, pl.BlockSpec((1, 6, dim), lambda t: (index, 0, 0))],
        out_specs=[new, pl.BlockSpec((1, 8, dim), lambda t: (0, 0, 0))],
        out_shape=[
            jax.ShapeDtypeStruct((1, seq, dim), BF),
            jax.ShapeDtypeStruct((1, 8, dim), F32),
        ],
        compiler_params=pltpu.CompilerParams(vmem_limit_bytes=40 * MIB),
        name="latents_back",
    )(dh1, dx1, latents, mod)


def per_device(
    n_dp,
    n_mp,
    latents,
    condition,
    cotangent,
    qkv_weight,
    qv_bias,
    proj_weight,
    proj_bias,
    fc1_weight,
    fc1_bias,
    fc2_weight,
    fc2_bias,
    ada_weight,
    ada_bias,
):
    lat, seq, dim = latents.shape
    local = qkv_weight.shape[2]
    n_heads = local // HEAD_DIM
    hid = fc1_weight.shape[1]
    cols = ada_weight.shape[1]
    mp_at = lax.axis_index("mp")
    dp_at = lax.axis_index("dp")
    me = jnp.full((1,), mp_at, jnp.int32)

    direct = n_mp == 4 and n_dp == 8
    bias_row = jnp.concatenate([qv_bias.reshape(-1), fc1_bias]).astype(F32)[None]
    ada_row = ada_bias.astype(F32)[None]
    if direct:
        small, cond_low = modulation_all(condition, ada_weight, ada_row, bias_row, n_mp)
    else:
        cond_low = jax.nn.silu(condition).astype(BF)
        mod_part = mm(cond_low, ada_weight) + ada_row
        small = lax.all_gather(jnp.concatenate([mod_part, bias_row], 0), "mp", axis=0)
    mod = small[:, :lat].transpose(1, 0, 2).reshape(lat, 6, dim)
    qv_all = small[:, lat, : 2 * local].reshape(n_mp, 2, local)
    b_qkv = jnp.stack([qv_all[:, 0], jnp.zeros((n_mp, local), F32), qv_all[:, 1]], 1).reshape(
        n_mp, 3 * local, 1
    )
    b_fc1 = small[:, lat, 2 * local :].reshape(n_mp, 1, hid)

    wq_own = (
        qkv_weight.reshape(dim, 3, n_heads, HEAD_DIM).transpose(1, 2, 3, 0).reshape(3 * local, dim)
    )
    own = jnp.concatenate([wq_own, proj_weight, fc1_weight.T, fc2_weight], 0)
    if direct:
        heads, qkv, lse, h1, gathered = attn_gather(latents, mod, b_qkv, own, n_mp)
    else:
        share = own.shape[0] // n_dp
        mine = lax.dynamic_slice_in_dim(own, dp_at * share, share, 0)
        gathered = lax.all_gather(mine, ("dp", "mp"), axis=0).reshape(n_dp, n_mp, share, dim)
        gathered = gathered.transpose(1, 0, 2, 3).reshape(n_mp, n_dp * share, dim)
        heads, qkv, lse, h1 = attn_fwd(me, latents, mod, gathered, b_qkv, n_mp)
    heads_own = lax.dynamic_index_in_dim(heads, mp_at, 0, keepdims=False)
    rows = min(256, seq)
    results, dqkv, dh1 = [], [], []
    for i in range(lat):
        waiting = dqkv and direct
        outs = mlp_both(
            i,
            heads,
            latents,
            cotangent,
            mod,
            own,
            gathered,
            proj_bias.astype(F32)[None],
            b_fc1,
            fc2_bias.astype(F32)[None],
            n_mp,
            rows,
            dh1_i if waiting else None,
        )
        if waiting:
            dh1.append(outs[-1])
        results.append(outs[:8])
        dqkv_i, dh1_i = attn_bwd(
            outs[2], heads_own, qkv, lse, proj_weight, wq_own, i, min(512, seq)
        )
        dqkv.append(dqkv_i)
        if not direct:
            dh1.append(lax.psum(dh1_i, "mp"))
    if direct:
        dh1.append(line_sum(dh1_i))
    dqkv = jnp.concatenate(dqkv, 0)
    block_out, dx1, da, h2, dm, z, du, stats_two = [
        jnp.concatenate(parts, 0) for parts in zip(*results)
    ]
    flat = lambda v: v.reshape(lat * seq, v.shape[-1])
    grad_fc2 = tn(flat(z), flat(dm)).astype(BF)
    grad_fc1 = tn(flat(h2), flat(du)).astype(BF)
    grad_fc1_bias = jnp.sum(flat(du).astype(F32), 0)
    gate_one, gate_two = mod[:, 2], mod[:, 5]
    grad_fc2_bias = jnp.sum(gate_two * stats_two[:, 4], 0)
    grad_proj_bias = jnp.sum(gate_one * stats_two[:, 5], 0)
    grad_fc1, grad_fc2 = lax.psum((grad_fc1, grad_fc2), "dp")
    grad_qkv = jnp.einsum("les,lsd->ed", dqkv, h1, preferred_element_type=F32).astype(BF)
    grad_proj = jnp.einsum("les,lsd->ed", heads_own, da, preferred_element_type=F32).astype(BF)
    bias_sums = jnp.sum(dqkv.astype(F32), (0, 2)).reshape(3, local)
    grad_qv_bias = jnp.stack([bias_sums[0], bias_sums[2]])
    grad_qkv, grad_proj = lax.psum((grad_qkv, grad_proj), "dp")
    biases = lax.psum((grad_fc1_bias, grad_fc2_bias, grad_proj_bias, grad_qv_bias), "dp")
    grad_fc1_bias, grad_fc2_bias, grad_proj_bias, grad_qv_bias = biases

    backs = [
        latents_back(dh1[i], results[i][1], latents, mod, i, rows) for i in range(lat)
    ]
    latents_grad = jnp.concatenate([grad for grad, _ in backs], 0)
    stats_one = jnp.concatenate([stats for _, stats in backs], 0)

    dmod = jnp.stack(
        [
            stats_one[:, 0],
            stats_one[:, 1],
            stats_two[:, 0],
            stats_two[:, 1],
            stats_two[:, 2],
            stats_two[:, 3],
        ],
        1,
    )
    dmod = dmod.reshape(lat, 6 * dim).astype(BF)
    dmod_own = lax.dynamic_slice_in_dim(dmod, mp_at * cols, cols, 1)
    every = lax.all_gather(jnp.concatenate([cond_low, dmod_own], 1), "dp", axis=0, tiled=True)
    grad_ada = tn(every[:, :dim], every[:, dim:])
    grad_ada_bias = jnp.sum(every[:, dim:].astype(F32), 0)
    grad_act = lax.psum(nt(dmod_own, ada_weight), "mp")
    condition_grad = jax.vjp(jax.nn.silu, condition)[1](grad_act)[0]

    back = lambda v: v.astype(F32)
    return (
        block_out,
        latents_grad,
        condition_grad,
        back(grad_qkv).reshape(3, local, dim).transpose(2, 0, 1),
        grad_qv_bias,
        back(grad_proj),
        grad_proj_bias,
        back(grad_fc1),
        grad_fc1_bias,
        back(grad_fc2),
        grad_fc2_bias,
        grad_ada,
        grad_ada_bias,
    )


def solution(mesh):
    in_specs = (
        P("dp", None, None),
        P("dp", None),
        P("dp", None, None),
        P(None, None, "mp"),
        P(None, "mp"),
        P("mp", None),
        P(),
        P(None, "mp"),
        P("mp"),
        P("mp", None),
        P(),
        P(None, "mp"),
        P("mp"),
    )
    out_specs = (
        P("dp", None, None),
        P("dp", None, None),
        P("dp", None),
        P(None, None, "mp"),
        P(None, "mp"),
        P("mp", None),
        P(),
        P(None, "mp"),
        P("mp"),
        P("mp", None),
        P(),
        P(None, "mp"),
        P("mp"),
    )
    body = functools.partial(per_device, mesh.shape["dp"], mesh.shape["mp"])
    return jax.shard_map(body, mesh=mesh, in_specs=in_specs, out_specs=out_specs, check_vma=False)
```

```python
import functools

import jax
import jax.numpy as jnp
from jax import lax
from jax.experimental import pallas as pl
from jax.experimental.pallas import tpu as pltpu
from jax.sharding import PartitionSpec as P

HEAD_DIM = 72
EPS = 1e-06
LOG2E = 1.4426950408889634
GELU_A = 0.7978845608028654
GELU_B = 0.044715
BF = jnp.bfloat16
F32 = jnp.float32
MIB = 2**20


def mm(a, b):
    return jnp.dot(a, b, preferred_element_type=F32)


def nt(a, b):
    return lax.dot_general(a, b, (((1,), (1,)), ((), ())), preferred_element_type=F32)


def tn(a, b):
    return lax.dot_general(a, b, (((0,), (0,)), ((), ())), preferred_element_type=F32)


def norm_stats(values):
    centered = values - jnp.mean(values, -1, keepdims=True)
    inv_std = lax.rsqrt(jnp.mean(centered * centered, -1, keepdims=True) + EPS)
    return centered * inv_std, inv_std


def norm_back(normed, inv_std, grad_normed):
    first = jnp.mean(grad_normed, -1, keepdims=True)
    second = jnp.mean(grad_normed * normed, -1, keepdims=True)
    return inv_std * (grad_normed - first - normed * second)


def flip(value, bit):
    step = 1 << bit
    return value + step - 2 * step * (value // step % 2)


def other_part(me, k):
    return (me + k) % 2 + 2 * ((me // 2 + k // 2) % 2)


def line_peers(me, n):
    return jnp.minimum(me, 1) + jnp.minimum(n - 1 - me, 1)


def at_mesh(dp_at, mp_at):
    return {"device_id": (dp_at, mp_at), "device_id_type": pl.DeviceIdType.MESH}


def modulation_kernel(cond_ref, w_ref, bias_ref, row_ref, out_ref, low_ref, send, recv):
    dp_at, me = lax.axis_index("dp"), lax.axis_index("mp")
    n_mp = out_ref.shape[0]
    lat = cond_ref.shape[0]
    barrier = pltpu.get_barrier_semaphore()
    for k in range(1, n_mp):
        pl.semaphore_signal(barrier, inc=1, **at_mesh(dp_at, (me + k) % n_mp))
    cond = cond_ref[...]
    low = (cond * jax.nn.sigmoid(cond)).astype(BF)
    low_ref[...] = low
    part = mm(low, w_ref[...]) + bias_ref[...]
    cols = part.shape[1]
    out_ref[me] = jnp.concatenate([part, row_ref[...], jnp.zeros((8 - lat - 1, cols), F32)], 0)
    pl.semaphore_wait(barrier, n_mp - 1)
    copies = []
    for k in range(1, n_mp):
        copies.append(
            pltpu.make_async_remote_copy(
                out_ref.at[me],
                out_ref.at[me],
                send.at[k - 1],
                recv.at[k - 1],
                **at_mesh(dp_at, (me + k) % n_mp),
            )
        )
        copies[-1].start()
    for k in range(1, n_mp):
        came = out_ref.at[(me + n_mp - k) % n_mp]
        pltpu.make_async_remote_copy(
            came, came, send.at[k - 1], recv.at[k - 1], **at_mesh(dp_at, (me + k) % n_mp)
        ).wait_recv()
    for copy in copies:
        copy.wait_send()


def modulation_all(condition, ada_weight, ada_bias, bias_row, n_mp):
    cols = ada_weight.shape[1]
    vmem = pl.BlockSpec(memory_space=pltpu.VMEM)
    return pl.pallas_call(
        modulation_kernel,
        in_specs=[vmem] * 4,
        out_specs=[vmem, vmem],
        out_shape=[
            jax.ShapeDtypeStruct((n_mp, 8, cols), F32),
            jax.ShapeDtypeStruct(condition.shape, BF),
        ],
        scratch_shapes=[pltpu.SemaphoreType.DMA((n_mp - 1,))] * 2,
        compiler_params=pltpu.CompilerParams(
            collective_id=0, has_side_effects=True, vmem_limit_bytes=40 * MIB
        ),
        name="modulation",
    )(condition, ada_weight, ada_bias, bias_row)


def attend(flat, n_heads, slot, heads_ref, qkv_ref, lse_ref, between):
    seq = flat.shape[1]
    parts = flat.reshape(3 * n_heads, HEAD_DIM, seq)
    scaling = LOG2E / HEAD_DIM**0.5
    outs = []
    for h in range(n_heads):
        q_t = (parts[h] * scaling).astype(BF)
        k_t = parts[n_heads + h]
        v_t = parts[2 * n_heads + h]
        v_ext = jnp.concatenate([v_t, jnp.ones((8, seq), F32)], 0).astype(BF)
        scores = mm(k_t.T.astype(BF), q_t)
        top = jnp.max(scores, 0, keepdims=True)
        probs = jnp.exp2(scores - top).astype(BF)
        out = mm(v_ext, probs)
        total = out[HEAD_DIM : HEAD_DIM + 1]
        outs.append(out[:HEAD_DIM] * (1.0 / total))
        lse = top + jnp.log2(total)

        @pl.when(slot == 0)
        def _():
            qkv_ref[0, h] = q_t
            qkv_ref[0, n_heads + h] = k_t.astype(BF)
            qkv_ref[0, 2 * n_heads + h] = v_t.astype(BF)
            lse_ref[0, h : h + 1] = lse

        between(h + 1)
    heads_ref[0, 0] = jnp.concatenate(outs, 0).astype(BF)


def mixed_one(lat_ref, mod_ref, h1_ref, h1_all, lat):
    normed, _ = norm_stats(lat_ref[0].astype(F32))
    h1 = (normed * (1.0 + mod_ref[0, 1:2]) + mod_ref[0, 0:1]).astype(BF)
    h1_all[lat] = h1
    h1_ref[0] = h1


def attn_fwd_kernel(
    me_ref, lat_ref, mod_ref, w_ref, bias_ref, heads_ref, qkv_ref, lse_ref, h1_ref, h1_all
):
    slot, lat = pl.program_id(0), pl.program_id(1)

    @pl.when(slot == 0)
    def _():
        mixed_one(lat_ref, mod_ref, h1_ref, h1_all, lat)

    flat = nt(w_ref[0], h1_all[lat]) + bias_ref[0]
    attend(flat, qkv_ref.shape[1] // 3, slot, heads_ref, qkv_ref, lse_ref, lambda h: None)


def attn_gather_kernel(
    lat_ref,
    mod_ref,
    bias_ref,
    wq_ref,
    wp_ref,
    w1_ref,
    w2_ref,
    heads_ref,
    qkv_ref,
    lse_ref,
    h1_ref,
    all_ref,
    h1_all,
    w_buf,
    local_sem,
    z_own,
    z_on,
    z_got,
    sends,
    recvs,
):
    n_mp = all_ref.shape[0]
    lats = h1_all.shape[0]
    units = 3 * (n_mp - 1)
    slot, lat = pl.program_id(0), pl.program_id(1)
    step = slot * lats + lat
    dp_at, me = lax.axis_index("dp"), lax.axis_index("mp")
    core, x, y = dp_at % 2, dp_at // 2 % 2, dp_at // 4
    rows = all_ref.shape[5]
    upper = wq_ref.shape[0] // rows
    cut = rows // 32 * 16 + 16
    near, far = pl.ds(0, cut), pl.ds(cut, rows - cut)
    every = pl.ds(0, rows)
    both = pl.ds(0, 2)
    core_id = at_mesh(flip(dp_at, 0), me)
    x_id = at_mesh(flip(dp_at, 1), me)
    y_id = at_mesh(flip(dp_at, 2), me)
    right_id, left_id = at_mesh(dp_at, me + 1), at_mesh(dp_at, me - 1)

    def piece(s, c, at_y, at_x, at_core, part):
        return all_ref.at[s, c, at_y, at_x, at_core, part]

    def own_copy(c, side, target, source=None):
        ref = piece(me, c, y, x, core, every)
        return pltpu.make_async_remote_copy(
            ref if source is None else source,
            ref,
            z_own.at[side, c],
            z_got.at[c, me],
            **target,
        )

    def pass_on(s, c, target):
        ref = piece(s, c, y, x, core, every)
        return pltpu.make_async_remote_copy(
            ref, ref, z_on.at[c, s], z_got.at[c, s], **target
        )

    def move(kind, c, s, arrived=False):
        flipped = lambda v: 1 - v if arrived else v
        at_y, at_x, at_core, part, target = (
            (pl.ds(y, 1), pl.ds(flipped(x), 1), pl.ds(core, 1), near, x_id),
            (pl.ds(flipped(y), 1), pl.ds(x, 1), pl.ds(core, 1), far, y_id),
            (pl.ds(flipped(y), 1), both, pl.ds(core, 1), near, y_id),
            (both, pl.ds(flipped(x), 1), pl.ds(core, 1), far, x_id),
            (both, both, pl.ds(flipped(core), 1), every, core_id),
        )[kind]
        ref = piece(s, c, at_y, at_x, at_core, part)
        return pltpu.make_async_remote_copy(
            ref, ref, sends.at[kind, c, s], recvs.at[kind, c, s], **target
        )

    def unit(u):
        return u // (n_mp - 1), other_part(me, 1 + u % (n_mp - 1))

    def event(stage, u):
        c, s = unit(u)

        @pl.when((u >= 0) & (u < units))
        def _():
            if stage == 1:
                pass_on(s, c, right_id).wait_recv()

                @pl.when((s < me) & (me < n_mp - 1))
                def _():
                    pass_on(s, c, right_id).start()

                @pl.when((s > me) & (me > 0))
                def _():
                    pass_on(s, c, left_id).start()

                move(0, c, s).start()
                move(1, c, s).start()
            if stage == 2:
                move(0, c, s, True).wait_recv()
                move(1, c, s, True).wait_recv()
                move(2, c, s).start()
                move(3, c, s).start()
            if stage == 3:
                move(2, c, s, True).wait_recv()
                move(3, c, s, True).wait_recv()
                move(4, c, s).start()
            if stage == 4:
                move(4, c, s, True).wait_recv()

    def send_from(c, ref, at):
        source = ref.at[pl.ds(at * rows, rows)]

        @pl.when(me < n_mp - 1)
        def _():
            own_copy(c, 0, right_id, source).start()

        @pl.when(me > 0)
        def _():
            own_copy(c, 1, left_id, source).start()

    def send_own(c):
        if c > 0:
            send_from(c, (w1_ref, w2_ref)[c - 1], dp_at)
        else:
            pl.when(dp_at < upper)(lambda: send_from(0, wq_ref, dp_at))
            pl.when(dp_at >= upper)(lambda: send_from(0, wp_ref, dp_at - upper))

    @pl.when(step == 0)
    def _():
        barrier = pltpu.get_barrier_semaphore()
        for target in (core_id, x_id, y_id):
            pl.semaphore_signal(barrier, inc=1, **target)

        @pl.when(me < n_mp - 1)
        def _():
            pl.semaphore_signal(barrier, inc=1, **right_id)

        @pl.when(me > 0)
        def _():
            pl.semaphore_signal(barrier, inc=1, **left_id)

        pl.semaphore_wait(barrier, 3 + line_peers(me, n_mp))
        send_own(0)

    for c in (1, 2):

        @pl.when(step == 3 * c - 1)
        def _():
            send_own(c)

    event(4, step - 3)
    event(3, step - 2)

    @pl.when((lat == 0) & (slot == 0))
    def _():
        def load(at):
            return pltpu.make_async_copy(
                wq_ref.at[pl.ds(at * rows, rows)],
                w_buf.at[at // 4, at // 2 % 2, at % 2],
                local_sem.at[at],
            )

        for at in range(upper):
            load(at).start()
        for at in range(upper):
            load(at).wait()

    @pl.when((lat == 0) & (slot > 0))
    def _():
        load = pltpu.make_async_copy(all_ref.at[other_part(me, slot), 0], w_buf, local_sem.at[0])
        load.start()
        load.wait()

    @pl.when(slot == 0)
    def _():
        mixed_one(lat_ref, mod_ref, h1_ref, h1_all, lat)

    n_heads = qkv_ref.shape[1] // 3
    weights = w_buf[...].reshape(8 * rows, w_buf.shape[-1])[: 3 * n_heads * HEAD_DIM]
    flat = nt(weights, h1_all[lat]) + bias_ref[0]

    def between(h):
        if h == 1:
            event(2, step - 1)
        if h == 3:
            event(1, step)

    attend(flat, n_heads, slot, heads_ref, qkv_ref, lse_ref, between)

    @pl.when(step == n_mp * lats - 1)
    def _():
        for c in range(3):

            @pl.when(me < n_mp - 1)
            def _():
                own_copy(c, 0, right_id).wait_send()

            @pl.when(me > 0)
            def _():
                own_copy(c, 1, left_id).wait_send()

        def drain(u, carry):
            c, s = unit(u)

            @pl.when((s < me) & (me < n_mp - 1))
            def _():
                pass_on(s, c, right_id).wait_send()

            @pl.when((s > me) & (me > 0))
            def _():
                pass_on(s, c, left_id).wait_send()

            for kind in range(5):
                move(kind, c, s).wait_send()
            return carry

        lax.fori_loop(0, units, drain, 0)


def attn_gather(latents, mod, bias, own, n_mp):
    lat, seq, dim = latents.shape
    local = dim // n_mp
    n_heads = local // HEAD_DIM
    rows = dim // 8
    last = lat - 1
    first = lambda s, l: s // n_mp * 0 + jnp.where(s == 0, l, last)
    part = lambda s: other_part(lax.axis_index("mp"), s)
    heads, qkv, lse, h1, gathered = pl.pallas_call(
        attn_gather_kernel,
        grid=(n_mp, lat),
        in_specs=[
            pl.BlockSpec((1, seq, dim), lambda s, l: (first(s, l), 0, 0)),
            pl.BlockSpec((1, 6, dim), lambda s, l: (l, 0, 0)),
            pl.BlockSpec((1, 3 * local, 1), lambda s, l: (part(s), 0, 0)),
        ]
        + [pl.BlockSpec(memory_space=pl.ANY)] * 4,
        out_specs=[
            pl.BlockSpec((1, 1, local, seq), lambda s, l: (part(s), l, 0, 0)),
            pl.BlockSpec((1, 3 * n_heads, HEAD_DIM, seq), lambda s, l: (first(s, l), 0, 0, 0)),
            pl.BlockSpec((1, n_heads, seq), lambda s, l: (first(s, l), 0, 0)),
            pl.BlockSpec((1, seq, dim), lambda s, l: (first(s, l), 0, 0)),
            pl.BlockSpec(memory_space=pl.ANY),
        ],
        out_shape=[
            jax.ShapeDtypeStruct((n_mp, lat, local, seq), BF),
            jax.ShapeDtypeStruct((lat, 3 * n_heads, HEAD_DIM, seq), BF),
            jax.ShapeDtypeStruct((lat, n_heads, seq), F32),
            jax.ShapeDtypeStruct((lat, seq, dim), BF),
            jax.ShapeDtypeStruct((n_mp, 3, 2, 2, 2, rows, dim), BF),
        ],
        scratch_shapes=[
            pltpu.VMEM((lat, seq, dim), BF),
            pltpu.VMEM((2, 2, 2, rows, dim), BF),
            pltpu.SemaphoreType.DMA((8,)),
            pltpu.SemaphoreType.DMA((2, 3)),
            pltpu.SemaphoreType.DMA((3, n_mp)),
            pltpu.SemaphoreType.DMA((3, n_mp)),
            pltpu.SemaphoreType.DMA((5, 3, n_mp)),
            pltpu.SemaphoreType.DMA((5, 3, n_mp)),
        ],
        compiler_params=pltpu.CompilerParams(
            collective_id=1, has_side_effects=True, vmem_limit_bytes=60 * MIB
        ),
        name="attn_gather",
    )(latents, mod, bias, *own)
    return heads, qkv, lse, h1, gathered.reshape(n_mp, 3, dim, dim)


def attn_fwd(me, latents, mod, gathered, bias, n_mp):
    lat, seq, dim = latents.shape
    local = dim // n_mp
    n_heads = local // HEAD_DIM
    last = lat - 1
    first = lambda s, l: jnp.where(s == 0, l, last)
    return pl.pallas_call(
        attn_fwd_kernel,
        grid_spec=pltpu.PrefetchScalarGridSpec(
            num_scalar_prefetch=1,
            grid=(n_mp, lat),
            in_specs=[
                pl.BlockSpec((1, seq, dim), lambda s, l, me: (first(s, l), 0, 0)),
                pl.BlockSpec((1, 6, dim), lambda s, l, me: (l, 0, 0)),
                pl.BlockSpec(
                    (1, 3 * local, dim), lambda s, l, me: (lax.rem(me[0] + s, n_mp), 0, 0)
                ),
                pl.BlockSpec((1, 3 * local, 1), lambda s, l, me: (lax.rem(me[0] + s, n_mp), 0, 0)),
            ],
            out_specs=[
                pl.BlockSpec(
                    (1, 1, local, seq), lambda s, l, me: (lax.rem(me[0] + s, n_mp), l, 0, 0)
                ),
                pl.BlockSpec(
                    (1, 3 * n_heads, HEAD_DIM, seq), lambda s, l, me: (first(s, l), 0, 0, 0)
                ),
                pl.BlockSpec((1, n_heads, seq), lambda s, l, me: (first(s, l), 0, 0)),
                pl.BlockSpec((1, seq, dim), lambda s, l, me: (first(s, l), 0, 0)),
            ],
            scratch_shapes=[pltpu.VMEM((lat, seq, dim), BF)],
        ),
        out_shape=[
            jax.ShapeDtypeStruct((n_mp, lat, local, seq), BF),
            jax.ShapeDtypeStruct((lat, 3 * n_heads, HEAD_DIM, seq), BF),
            jax.ShapeDtypeStruct((lat, n_heads, seq), F32),
            jax.ShapeDtypeStruct((lat, seq, dim), BF),
        ],
        compiler_params=pltpu.CompilerParams(vmem_limit_bytes=60 * MIB),
        name="attn_fwd",
    )(me, latents, mod, gathered, bias)


class LineSum:
    def __init__(self, own_ref, up, down, sems, out_ref):
        self.own, self.up, self.down, self.sems, self.out = own_ref, up, down, sems, out_ref
        self.count, self.rows = up.shape[0], up.shape[1]
        self.me = lax.axis_index("mp")
        self.n = lax.axis_size("mp")
        dp_at = lax.axis_index("dp")
        self.ends = (at_mesh(dp_at, self.me + 1), at_mesh(dp_at, self.me - 1))
        self.place = (self.me, self.n - 1 - self.me)

    def guarded(self, side, first, action):
        there = self.place[side] > 0 if first else self.place[side] < self.n - 1

        @pl.when(there)
        def _():
            action()

    def greet(self):
        sem = pltpu.get_barrier_semaphore()
        for side in (0, 1):
            self.guarded(side, False, lambda: pl.semaphore_signal(sem, inc=1, **self.ends[side]))

    def barrier(self):
        self.greet()
        pl.semaphore_wait(pltpu.get_barrier_semaphore(), line_peers(self.me, self.n))

    def copy(self, side, c):
        ref = (self.up, self.down)[side].at[c]
        return pltpu.make_async_remote_copy(
            ref, ref, self.sems.at[2 * side, c], self.sems.at[2 * side + 1, c], **self.ends[side]
        )

    def handle(self, side, c):
        ref = (self.up, self.down)[side]
        own = self.own[0, pl.ds(pl.multiple_of(c * self.rows, self.rows), self.rows)]

        @pl.when(self.place[side] == 0)
        def _():
            ref[c] = own

        @pl.when(self.place[side] > 0)
        def _():
            self.copy(side, c).wait_recv()
            ref[c] = (ref[c].astype(F32) + own.astype(F32)).astype(BF)

        self.guarded(side, False, lambda: self.copy(side, c).start())

    def tick(self, t):
        for side in (0, 1):
            at = t - 2 * self.place[side]

            @pl.when((at >= 0) & (at % 3 < 2) & (at - at // 3 < self.count))
            def _():
                self.handle(side, at - at // 3)

    def finish(self, ticks):
        for side in (0, 1):
            done = jnp.maximum(ticks - 2 * self.place[side], 0)
            done = jnp.minimum(done - done // 3, self.count)

            def late(c, carry):
                self.handle(side, c)
                return carry

            lax.fori_loop(done, self.count, late, 0)

        def add(c, carry):
            rows = pl.ds(pl.multiple_of(c * self.rows, self.rows), self.rows)
            total = self.up[c].astype(F32) + self.down[c].astype(F32)
            self.out[0, rows] = (total - self.own[0, rows].astype(F32)).astype(BF)
            return carry

        lax.fori_loop(0, self.count, add, 0)
        for side in (0, 1):

            def sent(c, carry):
                self.copy(side, c).wait_send()
                return carry

            self.guarded(side, False, lambda: lax.fori_loop(0, self.count, sent, 0))


def mlp_kernel(*refs, summing):
    heads_ref, lat_ref, cot_ref, mod_ref, bp_ref, b1_ref, b2_ref = refs[:7]
    own_refs, (wq_all, w1_all, w2_all), refs = refs[7:10], refs[10:13], refs[13:]
    if summing:
        part_ref, refs = refs[0], refs[1:]
    out_ref, dx1_ref, da_ref, h2_ref, dm_ref, z_ref, du_ref, stats_ref = refs[:8]
    refs = refs[8:]
    if summing:
        sum_ref, refs = refs[0], refs[1:]
    macc, dacc, wp, w1, w2, load_sems = refs[:6]
    n_mp, hid, dim = w2.shape
    local = wp.shape[1]
    rows = lat_ref.shape[1]
    me = lax.axis_index("mp")
    step = pl.program_id(0)
    line = LineSum(part_ref, refs[6], refs[7], refs[8], sum_ref) if summing else None

    def load(kind, k):
        slot = (me + k) % n_mp
        source = own_refs[kind]
        if k > 0:
            stack = (wq_all, w1_all, w2_all)[kind]
            source = stack.at[slot, kind] if len(stack.shape) == 4 else stack.at[slot]
        if k > 0 and kind == 0:
            source = source.at[pl.ds(3 * local, local)]
        ref = (wp.at[slot], w1.at[k], w2.at[k])[kind]
        return pltpu.make_async_copy(source, ref, load_sems.at[kind, k])

    @pl.when(step == 0)
    def _():
        if summing:
            line.barrier()
        for k in range(n_mp):
            load(0, k).start()
        for k in range(n_mp):
            load(1, k).start()
            load(2, k).start()
        for k in range(n_mp):
            load(0, k).wait()

    gate_one, shift_two = mod_ref[0, 2:3], mod_ref[0, 3:4]
    scale_two, gate_two = mod_ref[0, 4:5], mod_ref[0, 5:6]
    heads = heads_ref[:, 0].reshape(dim, rows)
    attn = tn(heads, wp[...].reshape(dim, dim)) + bp_ref[...]
    x1 = lat_ref[0].astype(F32) + gate_one * attn
    n2, inv2 = norm_stats(x1)
    h2 = (n2 * (1.0 + scale_two) + shift_two).astype(BF)
    h2_ref[0] = h2
    cot = cot_ref[0].astype(F32)
    dm = (gate_two * cot).astype(BF)
    dm_ref[0] = dm

    macc[...] = jnp.zeros_like(macc)
    dacc[...] = jnp.zeros_like(dacc)

    def part(k, own):
        if summing:
            line.tick(step * n_mp + k)

        @pl.when(step == 0)
        def _():
            for kind in (1, 2):
                ref = (w1, w2)[kind - 1].at[k]
                pltpu.make_async_copy(ref, ref, load_sems.at[kind, k]).wait()

        u = mm(h2_ref[0], w1[k]) + b1_ref[(me + k) % n_mp]
        dz = nt(dm_ref[0], w2[k])
        u2 = u * u
        t = jnp.tanh(u * (GELU_A + (GELU_A * GELU_B) * u2))
        half = 0.5 + 0.5 * t
        z = (u * half).astype(BF)
        slope = half + u * (1.0 - t * t) * (0.5 * GELU_A + (1.5 * GELU_A * GELU_B) * u2)
        du = (dz * slope).astype(BF)
        if own:
            z_ref[0] = z
            du_ref[0] = du
        macc[...] += mm(z, w2[k])
        dacc[...] += nt(du, w1[k])

    part(0, True)

    def body(k, carry):
        part(k, False)
        return carry

    lax.fori_loop(1, n_mp, body, 0)
    mlp = macc[...] + b2_ref[...]
    out_ref[0] = (x1 + gate_two * mlp).astype(BF)
    dh2 = dacc[...]
    dx1 = cot + norm_back(n2, inv2, dh2 * (1.0 + scale_two))
    dx1_ref[0] = dx1.astype(BF)
    da_ref[0] = (gate_one * dx1).astype(BF)
    total = lambda v: jnp.sum(v, 0, keepdims=True)
    stats = jnp.concatenate(
        [
            total(dx1 * attn),
            total(dh2),
            total(dh2 * n2),
            total(cot * mlp),
            total(cot),
            total(dx1),
            jnp.zeros((2, dim), F32),
        ],
        0,
    )

    @pl.when(step == 0)
    def _():
        stats_ref[0] = stats

    @pl.when(step > 0)
    def _():
        stats_ref[0] += stats

    if summing:

        @pl.when(step == pl.num_programs(0) - 1)
        def _():
            line.finish(pl.num_programs(0) * n_mp)


LINE_CHUNKS = 8


def line_scratch(seq, dim):
    rows = seq // LINE_CHUNKS
    return [
        pltpu.VMEM((LINE_CHUNKS, rows, dim), BF),
        pltpu.VMEM((LINE_CHUNKS, rows, dim), BF),
        pltpu.SemaphoreType.DMA((4, LINE_CHUNKS)),
    ]


def mlp_both(index, heads, latents, cotangent, mod, biases, own, gathered, n_mp, rows, part):
    lat, seq, dim = latents.shape
    local = dim // n_mp
    hid = biases[1].shape[2]
    tok = pl.BlockSpec((1, rows, dim), lambda t: (index, t, 0))
    new = pl.BlockSpec((1, rows, dim), lambda t: (0, t, 0))
    hidden = pl.BlockSpec((1, rows, hid), lambda t: (0, t, 0))
    once = lambda shape: pl.BlockSpec(
        shape, lambda t: (0,) * len(shape), pipeline_mode=pl.Buffered(1)
    )
    any_spec = pl.BlockSpec(memory_space=pl.ANY)
    summing = part is not None
    extra = [once((1, seq, dim))] if summing else []
    return pl.pallas_call(
        functools.partial(mlp_kernel, summing=summing),
        grid=(seq // rows,),
        in_specs=[
            pl.BlockSpec((n_mp, 1, local, rows), lambda t: (0, index, 0, t)),
            tok,
            tok,
            pl.BlockSpec((1, 6, dim), lambda t: (index, 0, 0)),
            once((1, dim)),
            once((n_mp, 1, hid)),
            once((1, dim)),
        ]
        + [any_spec] * 6
        + extra,
        out_specs=[new] * 5
        + [hidden, hidden, pl.BlockSpec((1, 8, dim), lambda t: (0, 0, 0))]
        + extra,
        out_shape=[jax.ShapeDtypeStruct((1, seq, dim), BF)] * 5
        + [jax.ShapeDtypeStruct((1, seq, hid), BF)] * 2
        + [jax.ShapeDtypeStruct((1, 8, dim), F32)]
        + ([jax.ShapeDtypeStruct((1, seq, dim), BF)] if summing else []),
        scratch_shapes=[
            pltpu.VMEM((rows, dim), F32),
            pltpu.VMEM((rows, dim), F32),
            pltpu.VMEM((n_mp, local, dim), BF),
            pltpu.VMEM((n_mp, dim, hid), BF),
            pltpu.VMEM((n_mp, hid, dim), BF),
            pltpu.SemaphoreType.DMA((3, n_mp)),
        ]
        + (line_scratch(seq, dim) if summing else []),
        compiler_params=pltpu.CompilerParams(
            vmem_limit_bytes=63 * MIB,
            **(dict(collective_id=4 + index, has_side_effects=True) if summing else {}),
        ),
        name="mlp_sum" if summing else "mlp_both",
    )(
        heads,
        latents,
        cotangent,
        mod,
        *biases,
        *own,
        *gathered,
        *([part] if summing else []),
    )


class CubeSum:
    def __init__(self, terms, full, halves, firsts, seconds, sems):
        self.terms, self.full = terms, full
        self.halves, self.firsts, self.seconds, self.sems = halves, firsts, seconds, sems
        self.units = terms.shape[0]
        dp_at, me = lax.axis_index("dp"), lax.axis_index("mp")
        self.core, x, y = dp_at % 2, dp_at // 2 % 2, dp_at // 4
        self.core_id = at_mesh(flip(dp_at, 0), me)
        x_id, y_id = at_mesh(flip(dp_at, 1), me), at_mesh(flip(dp_at, 2), me)
        self.ids = ((x_id, y_id), (y_id, x_id))
        self.place = ((x, y), (y, x))

    def barrier(self):
        sem = pltpu.get_barrier_semaphore()
        for target in (self.core_id,) + self.ids[0]:
            pl.semaphore_signal(sem, inc=1, **target)

    def send(self, stage, u, q, arrived=False):
        core = self.core
        terms, full = self.terms, self.full
        first, second = self.place[q]
        if stage == 0:
            pair, target = (terms.at[u, 1 - core], self.halves.at[u]), self.core_id
        elif stage == 1:
            pair = (terms.at[u, core, q, 1 - first], self.firsts.at[u, q])
            target = self.ids[q][0]
        elif stage == 2:
            pair = (terms.at[u, core, q, first, 1 - second], self.seconds.at[u, q])
            target = self.ids[q][1]
        elif stage == 3:
            at = 1 - second if arrived else second
            pair = (full.at[u, core, q, first, at],) * 2
            target = self.ids[q][1]
        elif stage == 4:
            at = 1 - first if arrived else first
            pair = (full.at[u, core, q, at],) * 2
            target = self.ids[q][0]
        else:
            at = 1 - core if arrived else core
            pair, target = (full.at[u, at],) * 2, self.core_id
        return pltpu.make_async_remote_copy(
            *pair, self.sems.at[0, stage, q, u], self.sems.at[1, stage, q, u], **target
        )

    def quarters(self, stage):
        return (0,) if stage in (0, 5) else (0, 1)

    def event(self, stage, u):
        terms, core = self.terms, self.core

        @pl.when((u >= 0) & (u < self.units))
        def _():
            if stage > 0:
                for q in self.quarters(stage - 1):
                    self.send(stage - 1, u, q, True).wait_recv()
            if stage == 1:
                total = terms[u, core].astype(F32) + self.halves[u].astype(F32)
                terms[u, core] = total.astype(BF)
            for q in (0, 1):
                first, second = self.place[q]
                if stage == 2:
                    total = terms[u, core, q, first].astype(F32) + self.firsts[u, q].astype(F32)
                    terms[u, core, q, first] = total.astype(BF)
                if stage == 3:
                    total = terms[u, core, q, first, second].astype(F32)
                    total = total + self.seconds[u, q].astype(F32)
                    self.full[u, core, q, first, second] = total.astype(BF)
            if stage < 6:
                for q in self.quarters(stage):
                    self.send(stage, u, q).start()

    def finish(self):
        def sent(u, carry):
            for stage in range(6):
                for q in self.quarters(stage):
                    self.send(stage, u, q).wait_send()
            return carry

        lax.fori_loop(0, self.units, sent, 0)


def tail_kernel(
    part_ref, terms_ref, sum_ref, full_ref, up, down, line_sems, terms, full, *refs
):
    halves, firsts, seconds, cube_sems, local_sem = refs
    line = LineSum(part_ref, up, down, line_sems, sum_ref)
    cube = CubeSum(terms, full, halves, firsts, seconds, cube_sems)
    load = pltpu.make_async_copy(terms_ref, terms, local_sem.at[0])
    load.start()
    cube.barrier()
    line.greet()
    pl.semaphore_wait(pltpu.get_barrier_semaphore(), 3 + line_peers(line.me, line.n))
    load.wait()
    rounds = cube.units + 6

    def advance(t, carry):
        line.tick(2 * t)
        for stage in (6, 5, 4, 3):
            cube.event(stage, t - stage)
        line.tick(2 * t + 1)
        for stage in (2, 1, 0):
            cube.event(stage, t - stage)
        return carry

    lax.fori_loop(0, rounds, advance, 0)
    store = pltpu.make_async_copy(full, full_ref, local_sem.at[0])
    store.start()
    line.finish(2 * rounds)
    cube.finish()
    store.wait()


def tail_sums(part, terms):
    _, seq, dim = part.shape
    units, rows, _ = terms.shape
    rows = rows // 16
    vmem = pl.BlockSpec(memory_space=pltpu.VMEM)
    any_spec = pl.BlockSpec(memory_space=pl.ANY)
    shape = (units, 2, 2, 2, 2, rows, dim)
    total, full = pl.pallas_call(
        tail_kernel,
        in_specs=[vmem, any_spec],
        out_specs=[vmem, any_spec],
        out_shape=[jax.ShapeDtypeStruct(part.shape, BF), jax.ShapeDtypeStruct(shape, BF)],
        scratch_shapes=line_scratch(seq, dim)
        + [
            pltpu.VMEM(shape, BF),
            pltpu.VMEM(shape, BF),
            pltpu.VMEM((units, 2, 2, 2, rows, dim), BF),
            pltpu.VMEM((units, 2, 2, rows, dim), BF),
            pltpu.VMEM((units, 2, rows, dim), BF),
            pltpu.SemaphoreType.DMA((2, 6, 2, units)),
            pltpu.SemaphoreType.DMA((1,)),
        ],
        compiler_params=pltpu.CompilerParams(
            collective_id=2, has_side_effects=True, vmem_limit_bytes=60 * MIB
        ),
        name="tail_sums",
    )(part, terms.reshape(shape))
    return total, full.reshape(units * rows * 16, dim)


def rows_kernel(rows_ref, act_ref, every_ref, total_ref, acts, sems):
    dp_at, me = lax.axis_index("dp"), lax.axis_index("mp")
    n_dp, n_mp = every_ref.shape[0], acts.shape[0]
    barrier = pltpu.get_barrier_semaphore()
    for k in range(1, n_dp):
        pl.semaphore_signal(barrier, inc=1, **at_mesh((dp_at + k) % n_dp, me))
    for k in range(1, n_mp):
        pl.semaphore_signal(barrier, inc=1, **at_mesh(dp_at, (me + k) % n_mp))
    every_ref[dp_at] = rows_ref[...]
    acts[me] = act_ref[...]
    pl.semaphore_wait(barrier, n_dp + n_mp - 2)

    def copy(ref, k, target):
        return pltpu.make_async_remote_copy(ref, ref, sems.at[0, k], sems.at[1, k], **target)

    def act_copy(k, source):
        return copy(acts.at[source % n_mp], k - 1, at_mesh(dp_at, (me + k) % n_mp))

    def row_copy(k, source):
        target = at_mesh((dp_at + k) % n_dp, me)
        return copy(every_ref.at[source % n_dp], n_mp + k - 2, target)

    for k in range(1, n_mp):
        act_copy(k, me).start()
    for k in range(1, n_dp):
        row_copy(k, dp_at).start()
    for k in range(1, n_mp):
        act_copy(k, me + n_mp - k).wait_recv()
    total = acts[0]
    for i in range(1, n_mp):
        total = total + acts[i]
    total_ref[...] = total
    for k in range(1, n_dp):
        row_copy(k, dp_at + n_dp - k).wait_recv()
    for k in range(1, n_mp):
        act_copy(k, me).wait_send()
    for k in range(1, n_dp):
        row_copy(k, dp_at).wait_send()


def rows_exchange(rows, act, n_dp, n_mp):
    vmem = pl.BlockSpec(memory_space=pltpu.VMEM)
    return pl.pallas_call(
        rows_kernel,
        in_specs=[vmem, vmem],
        out_specs=[vmem, vmem],
        out_shape=[
            jax.ShapeDtypeStruct((n_dp,) + rows.shape, rows.dtype),
            jax.ShapeDtypeStruct(act.shape, act.dtype),
        ],
        scratch_shapes=[
            pltpu.VMEM((n_mp,) + act.shape, act.dtype),
            pltpu.SemaphoreType.DMA((2, n_dp + n_mp - 2)),
        ],
        compiler_params=pltpu.CompilerParams(
            collective_id=3, has_side_effects=True, vmem_limit_bytes=40 * MIB
        ),
        name="rows_exchange",
    )(rows, act)


def attn_bwd_kernel(da_ref, heads_ref, qkv_ref, lse_ref, wp_ref, wq_ref, dqkv_ref, dh1_ref, *, rows):
    n_heads = lse_ref.shape[1]
    seq = da_ref.shape[1]
    dheads = nt(wp_ref[...], da_ref[0]).reshape(n_heads, HEAD_DIM, seq)
    heads = heads_ref[0].astype(F32).reshape(n_heads, HEAD_DIM, seq)
    scaling = 1.0 / HEAD_DIM**0.5
    dq_list, dk_list, dv_list = [], [], []
    for h in range(n_heads):
        q_t = qkv_ref[0, h]
        k_t = qkv_ref[0, n_heads + h]
        v_t = qkv_ref[0, 2 * n_heads + h]
        q = q_t.astype(F32).T.astype(BF)
        k = k_t.astype(F32).T.astype(BF)
        v = v_t.astype(F32).T.astype(BF)
        do_t = dheads[h].astype(BF)
        do = dheads[h].T.astype(BF)
        inner = jnp.sum(do_t.astype(F32) * heads[h], 0, keepdims=True)
        dq_parts = []
        for i in range(seq // rows):
            cols = slice(i * rows, (i + 1) * rows)
            probs = jnp.exp2(mm(k, q_t[:, cols]) - lse_ref[0, h : h + 1, cols])
            dprobs = mm(v, do_t[:, cols])
            dscores = (probs * (dprobs - inner[:, cols])).astype(BF)
            dq_parts.append(mm(k_t, dscores))
            dv_new = mm(probs.astype(BF), do[cols])
            dk_new = mm(dscores, q[cols])
            dv = dv_new if i == 0 else dv + dv_new
            dk = dk_new if i == 0 else dk + dk_new
        dq_list.append(jnp.concatenate(dq_parts, 1) * scaling)
        dk_list.append(dk.T * (1.0 / LOG2E))
        dv_list.append(dv.T)
    dqkv = jnp.concatenate(dq_list + dk_list + dv_list, 0).astype(BF)
    dqkv_ref[0] = dqkv
    dh1_ref[0] = tn(dqkv, wq_ref[...]).astype(BF)


def attn_bwd(da, heads_own, qkv, lse, wp, wq, index, rows):
    lat, seq, dim = da.shape
    n_heads = lse.shape[1]
    local = n_heads * HEAD_DIM
    one = lambda shape: pl.BlockSpec((1,) + shape, lambda i: (index,) + (0,) * len(shape))
    only = lambda shape: pl.BlockSpec((1,) + shape, lambda i: (0,) * (len(shape) + 1))
    whole = lambda shape: pl.BlockSpec(shape, lambda i: (0,) * len(shape))
    out = lambda shape: pl.BlockSpec((1,) + shape, lambda i: (0,) * (len(shape) + 1))
    return pl.pallas_call(
        functools.partial(attn_bwd_kernel, rows=rows),
        grid=(1,),
        in_specs=[
            only((seq, dim)),
            one((local, seq)),
            one((3 * n_heads, HEAD_DIM, seq)),
            one((n_heads, seq)),
            whole((local, dim)),
            whole((3 * local, dim)),
        ],
        out_specs=[out((3 * local, seq)), out((seq, dim))],
        out_shape=[
            jax.ShapeDtypeStruct((1, 3 * local, seq), BF),
            jax.ShapeDtypeStruct((1, seq, dim), BF),
        ],
        compiler_params=pltpu.CompilerParams(vmem_limit_bytes=60 * MIB),
        name="attn_bwd",
    )(da, heads_own, qkv, lse, wp, wq)


def latents_kernel(dh1_ref, dx1_ref, lat_ref, mod_ref, grad_ref, stats_ref):
    n1, inv1 = norm_stats(lat_ref[0].astype(F32))
    dh1 = dh1_ref[0].astype(F32)
    grad = dx1_ref[0].astype(F32) + norm_back(n1, inv1, dh1 * (1.0 + mod_ref[0, 1:2]))
    grad_ref[0] = grad.astype(BF)
    stats = jnp.concatenate(
        [
            jnp.sum(dh1, 0, keepdims=True),
            jnp.sum(dh1 * n1, 0, keepdims=True),
            jnp.zeros((6, dh1.shape[1]), F32),
        ],
        0,
    )

    @pl.when(pl.program_id(0) == 0)
    def _():
        stats_ref[0] = stats

    @pl.when(pl.program_id(0) > 0)
    def _():
        stats_ref[0] += stats


def latents_back(dh1, dx1, latents, mod, index, rows):
    lat, seq, dim = latents.shape
    tok = pl.BlockSpec((1, rows, dim), lambda t: (index, t, 0))
    new = pl.BlockSpec((1, rows, dim), lambda t: (0, t, 0))
    return pl.pallas_call(
        latents_kernel,
        grid=(seq // rows,),
        in_specs=[new, new, tok, pl.BlockSpec((1, 6, dim), lambda t: (index, 0, 0))],
        out_specs=[new, pl.BlockSpec((1, 8, dim), lambda t: (0, 0, 0))],
        out_shape=[
            jax.ShapeDtypeStruct((1, seq, dim), BF),
            jax.ShapeDtypeStruct((1, 8, dim), F32),
        ],
        compiler_params=pltpu.CompilerParams(vmem_limit_bytes=40 * MIB),
        name="latents_back",
    )(dh1, dx1, latents, mod)


def per_device(
    n_dp,
    n_mp,
    latents,
    condition,
    cotangent,
    qkv_weight,
    qv_bias,
    proj_weight,
    proj_bias,
    fc1_weight,
    fc1_bias,
    fc2_weight,
    fc2_bias,
    ada_weight,
    ada_bias,
):
    lat, seq, dim = latents.shape
    local = qkv_weight.shape[2]
    n_heads = local // HEAD_DIM
    hid = fc1_weight.shape[1]
    cols = ada_weight.shape[1]
    mp_at = lax.axis_index("mp")
    dp_at = lax.axis_index("dp")
    me = jnp.full((1,), mp_at, jnp.int32)

    direct = n_mp == 4 and n_dp == 8
    bias_row = jnp.concatenate([qv_bias.reshape(-1), fc1_bias]).astype(F32)[None]
    ada_row = ada_bias.astype(F32)[None]
    if direct:
        small, cond_low = modulation_all(condition, ada_weight, ada_row, bias_row, n_mp)
    else:
        cond_low = jax.nn.silu(condition).astype(BF)
        mod_part = mm(cond_low, ada_weight) + ada_row
        small = lax.all_gather(jnp.concatenate([mod_part, bias_row], 0), "mp", axis=0)
    mod = small[:, :lat].transpose(1, 0, 2).reshape(lat, 6, dim)
    qv_all = small[:, lat, : 2 * local].reshape(n_mp, 2, local)
    b_qkv = jnp.stack([qv_all[:, 0], jnp.zeros((n_mp, local), F32), qv_all[:, 1]], 1).reshape(
        n_mp, 3 * local, 1
    )
    b_fc1 = small[:, lat, 2 * local :].reshape(n_mp, 1, hid)

    wq_own = (
        qkv_weight.reshape(dim, 3, n_heads, HEAD_DIM).transpose(1, 2, 3, 0).reshape(3 * local, dim)
    )
    if direct:
        own = (wq_own, proj_weight, fc1_weight, fc2_weight)
        heads, qkv, lse, h1, gathered = attn_gather(latents, mod, b_qkv, own, n_mp)
        gathered = (gathered,) * 3
    else:

        def gather(weight):
            share = weight.shape[0] // n_dp
            mine = lax.dynamic_slice_in_dim(weight, dp_at * share, share, 0)
            whole = lax.all_gather(mine, ("dp", "mp"), axis=0)
            whole = whole.reshape(n_dp, n_mp, share, weight.shape[1]).transpose(1, 0, 2, 3)
            return whole.reshape(n_mp, weight.shape[0], weight.shape[1])

        gathered = (
            gather(jnp.concatenate([wq_own, proj_weight], 0)),
            gather(fc1_weight),
            gather(fc2_weight),
        )
        heads, qkv, lse, h1 = attn_fwd(me, latents, mod, gathered[0], b_qkv, n_mp)
    heads_own = lax.dynamic_index_in_dim(heads, mp_at, 0, keepdims=False)
    rows = min(256, seq)
    results, dqkv, dh1 = [], [], []
    for i in range(lat):
        waiting = dqkv and direct
        outs = mlp_both(
            i,
            heads,
            latents,
            cotangent,
            mod,
            (proj_bias.astype(F32)[None], b_fc1, fc2_bias.astype(F32)[None]),
            (proj_weight, fc1_weight, fc2_weight),
            gathered,
            n_mp,
            rows,
            dh1_i if waiting else None,
        )
        if waiting:
            dh1.append(outs[-1])
        results.append(outs[:8])
        dqkv_i, dh1_i = attn_bwd(
            outs[2], heads_own, qkv, lse, proj_weight, wq_own, i, min(512, seq)
        )
        dqkv.append(dqkv_i)
        if not direct:
            dh1.append(lax.psum(dh1_i, "mp"))
    dqkv = jnp.concatenate(dqkv, 0)
    block_out, dx1, da, h2, dm, z, du, stats_two = [
        jnp.concatenate(parts, 0) for parts in zip(*results)
    ]
    flat = lambda v: v.reshape(lat * seq, v.shape[-1])
    grad_fc2 = tn(flat(z), flat(dm)).astype(BF)
    grad_fc1 = tn(flat(h2), flat(du)).astype(BF)
    grad_fc1_bias = jnp.sum(flat(du).astype(F32), 0)
    gate_one, gate_two = mod[:, 2], mod[:, 5]
    grad_fc2_bias = jnp.sum(gate_two * stats_two[:, 4], 0)
    grad_proj_bias = jnp.sum(gate_one * stats_two[:, 5], 0)
    grad_qkv = jnp.einsum("les,lsd->ed", dqkv, h1, preferred_element_type=F32).astype(BF)
    grad_proj = jnp.einsum("les,lsd->ed", heads_own, da, preferred_element_type=F32).astype(BF)
    bias_sums = jnp.sum(dqkv.astype(F32), (0, 2)).reshape(3, local)
    grad_qv_bias = jnp.stack([bias_sums[0], bias_sums[2]])
    if direct:
        bias_rows = jnp.stack(
            [
                grad_fc1_bias,
                grad_fc2_bias,
                grad_proj_bias,
                jnp.pad(grad_qv_bias.reshape(-1), (0, dim - 2 * local)),
            ]
        ).astype(BF)
        unit = 512
        terms = jnp.concatenate([grad_fc1, grad_fc2, grad_qkv, grad_proj, bias_rows], 0)
        terms = jnp.pad(terms, ((0, -terms.shape[0] % unit), (0, 0))).reshape(-1, unit, dim)
        dh1_i, sums = tail_sums(dh1_i, terms)
        dh1.append(dh1_i)
        grad_fc1, grad_fc2 = sums[:dim], sums[dim : 2 * dim]
        grad_qkv = sums[2 * dim : 2 * dim + 3 * local]
        grad_proj = sums[2 * dim + 3 * local : 3 * dim]
        bias_rows = sums[3 * dim : 3 * dim + 4].astype(F32)
        grad_fc1_bias, grad_fc2_bias, grad_proj_bias = bias_rows[:3]
        grad_qv_bias = bias_rows[3, : 2 * local].reshape(2, local)
    else:
        grad_fc1, grad_fc2 = lax.psum((grad_fc1, grad_fc2), "dp")
        grad_qkv, grad_proj = lax.psum((grad_qkv, grad_proj), "dp")
        biases = lax.psum((grad_fc1_bias, grad_fc2_bias, grad_proj_bias, grad_qv_bias), "dp")
        grad_fc1_bias, grad_fc2_bias, grad_proj_bias, grad_qv_bias = biases

    backs = [
        latents_back(dh1[i], results[i][1], latents, mod, i, rows) for i in range(lat)
    ]
    latents_grad = jnp.concatenate([grad for grad, _ in backs], 0)
    stats_one = jnp.concatenate([stats for _, stats in backs], 0)

    dmod = jnp.stack(
        [
            stats_one[:, 0],
            stats_one[:, 1],
            stats_two[:, 0],
            stats_two[:, 1],
            stats_two[:, 2],
            stats_two[:, 3],
        ],
        1,
    )
    dmod = dmod.reshape(lat, 6 * dim).astype(BF)
    dmod_own = lax.dynamic_slice_in_dim(dmod, mp_at * cols, cols, 1)
    both = jnp.concatenate([cond_low, dmod_own], 1)
    grad_act = nt(dmod_own, ada_weight)
    if direct:
        both = jnp.pad(both, ((0, 16 - lat), (0, 0)))
        grad_act = jnp.pad(grad_act, ((0, 8 - lat), (0, 0)))
        every, grad_act = rows_exchange(both, grad_act, n_dp, n_mp)
        every, grad_act = every.reshape(n_dp * 16, dim + cols), grad_act[:lat]
    else:
        every = lax.all_gather(both, "dp", axis=0, tiled=True)
        grad_act = lax.psum(grad_act, "mp")
    grad_ada = tn(every[:, :dim], every[:, dim:])
    grad_ada_bias = jnp.sum(every[:, dim:].astype(F32), 0)
    condition_grad = jax.vjp(jax.nn.silu, condition)[1](grad_act)[0]

    back = lambda v: v.astype(F32)
    return (
        block_out,
        latents_grad,
        condition_grad,
        back(grad_qkv).reshape(3, local, dim).transpose(2, 0, 1),
        grad_qv_bias,
        back(grad_proj),
        grad_proj_bias,
        back(grad_fc1),
        grad_fc1_bias,
        back(grad_fc2),
        grad_fc2_bias,
        grad_ada,
        grad_ada_bias,
    )


def solution(mesh):
    in_specs = (
        P("dp", None, None),
        P("dp", None),
        P("dp", None, None),
        P(None, None, "mp"),
        P(None, "mp"),
        P("mp", None),
        P(),
        P(None, "mp"),
        P("mp"),
        P("mp", None),
        P(),
        P(None, "mp"),
        P("mp"),
    )
    out_specs = (
        P("dp", None, None),
        P("dp", None, None),
        P("dp", None),
        P(None, None, "mp"),
        P(None, "mp"),
        P("mp", None),
        P(),
        P(None, "mp"),
        P("mp"),
        P("mp", None),
        P(),
        P(None, "mp"),
        P("mp"),
    )
    body = functools.partial(per_device, mesh.shape["dp"], mesh.shape["mp"])
    return jax.shard_map(body, mesh=mesh, in_specs=in_specs, out_specs=out_specs, check_vma=False)
```

```python
import functools

import jax
import jax.numpy as jnp
from jax import lax
from jax.experimental import pallas as pl
from jax.experimental.pallas import tpu as pltpu
from jax.sharding import PartitionSpec as P

HEAD_DIM = 72
EPS = 1e-06
LOG2E = 1.4426950408889634
GELU_A = 0.7978845608028654
GELU_B = 0.044715
BF = jnp.bfloat16
F32 = jnp.float32
MIB = 2**20


def mm(a, b):
    return jnp.dot(a, b, preferred_element_type=F32)


def nt(a, b):
    return lax.dot_general(a, b, (((1,), (1,)), ((), ())), preferred_element_type=F32)


def tn(a, b):
    return lax.dot_general(a, b, (((0,), (0,)), ((), ())), preferred_element_type=F32)


def norm_stats(values):
    centered = values - jnp.mean(values, -1, keepdims=True)
    inv_std = lax.rsqrt(jnp.mean(centered * centered, -1, keepdims=True) + EPS)
    return centered * inv_std, inv_std


def norm_back(normed, inv_std, grad_normed):
    first = jnp.mean(grad_normed, -1, keepdims=True)
    second = jnp.mean(grad_normed * normed, -1, keepdims=True)
    return inv_std * (grad_normed - first - normed * second)


def flip(value, bit):
    step = 1 << bit
    return value + step - 2 * step * (value // step % 2)


def near_part(me, k):
    side = me // 2
    end = jnp.minimum(me, 3 - me)
    at = k + end * (1 - 2 * k) * ((3 - k) // 2)
    return at + side * (3 - 2 * at)


def line_peers(me, n):
    return jnp.minimum(me, 1) + jnp.minimum(n - 1 - me, 1)


def at_mesh(dp_at, mp_at):
    return {"device_id": (dp_at, mp_at), "device_id_type": pl.DeviceIdType.MESH}


def modulation_kernel(cond_ref, w_ref, bias_ref, row_ref, out_ref, low_ref, send, recv):
    dp_at, me = lax.axis_index("dp"), lax.axis_index("mp")
    n_mp = out_ref.shape[0]
    lat = cond_ref.shape[0]
    barrier = pltpu.get_barrier_semaphore()
    for k in range(1, n_mp):
        pl.semaphore_signal(barrier, inc=1, **at_mesh(dp_at, (me + k) % n_mp))
    cond = cond_ref[...]
    low = (cond * jax.nn.sigmoid(cond)).astype(BF)
    low_ref[...] = low
    part = mm(low, w_ref[...]) + bias_ref[...]
    cols = part.shape[1]
    out_ref[me] = jnp.concatenate([part, row_ref[...], jnp.zeros((8 - lat - 1, cols), F32)], 0)
    pl.semaphore_wait(barrier, n_mp - 1)
    copies = []
    for k in range(1, n_mp):
        copies.append(
            pltpu.make_async_remote_copy(
                out_ref.at[me],
                out_ref.at[me],
                send.at[k - 1],
                recv.at[k - 1],
                **at_mesh(dp_at, (me + k) % n_mp),
            )
        )
        copies[-1].start()
    for k in range(1, n_mp):
        came = out_ref.at[(me + n_mp - k) % n_mp]
        pltpu.make_async_remote_copy(
            came, came, send.at[k - 1], recv.at[k - 1], **at_mesh(dp_at, (me + k) % n_mp)
        ).wait_recv()
    for copy in copies:
        copy.wait_send()


def modulation_all(condition, ada_weight, ada_bias, bias_row, n_mp):
    cols = ada_weight.shape[1]
    vmem = pl.BlockSpec(memory_space=pltpu.VMEM)
    return pl.pallas_call(
        modulation_kernel,
        in_specs=[vmem] * 4,
        out_specs=[vmem, vmem],
        out_shape=[
            jax.ShapeDtypeStruct((n_mp, 8, cols), F32),
            jax.ShapeDtypeStruct(condition.shape, BF),
        ],
        scratch_shapes=[pltpu.SemaphoreType.DMA((n_mp - 1,))] * 2,
        compiler_params=pltpu.CompilerParams(
            collective_id=0, has_side_effects=True, vmem_limit_bytes=40 * MIB
        ),
        name="modulation",
    )(condition, ada_weight, ada_bias, bias_row)


def attend(flat, n_heads, slot, heads_ref, qkv_ref, lse_ref, between):
    seq = flat.shape[1]
    parts = flat.reshape(3 * n_heads, HEAD_DIM, seq)
    scaling = LOG2E / HEAD_DIM**0.5
    outs = []
    for h in range(n_heads):
        q_t = (parts[h] * scaling).astype(BF)
        k_t = parts[n_heads + h]
        v_t = parts[2 * n_heads + h]
        v_ext = jnp.concatenate([v_t, jnp.ones((8, seq), F32)], 0).astype(BF)
        scores = mm(k_t.T.astype(BF), q_t)
        top = jnp.max(scores, 0, keepdims=True)
        probs = jnp.exp2(scores - top).astype(BF)
        out = mm(v_ext, probs)
        total = out[HEAD_DIM : HEAD_DIM + 1]
        outs.append(out[:HEAD_DIM] * (1.0 / total))
        lse = top + jnp.log2(total)

        @pl.when(slot == 0)
        def _():
            qkv_ref[0, h] = q_t
            qkv_ref[0, n_heads + h] = k_t.astype(BF)
            qkv_ref[0, 2 * n_heads + h] = v_t.astype(BF)
            lse_ref[0, h : h + 1] = lse

        between(h + 1)
    heads_ref[0, 0] = jnp.concatenate(outs, 0).astype(BF)


def mixed_one(lat_ref, mod_ref, h1_ref, h1_all, lat):
    normed, _ = norm_stats(lat_ref[0].astype(F32))
    h1 = (normed * (1.0 + mod_ref[0, 1:2]) + mod_ref[0, 0:1]).astype(BF)
    h1_all[lat] = h1
    h1_ref[0] = h1


def attn_fwd_kernel(
    me_ref, lat_ref, mod_ref, w_ref, bias_ref, heads_ref, qkv_ref, lse_ref, h1_ref, h1_all
):
    slot, lat = pl.program_id(0), pl.program_id(1)

    @pl.when(slot == 0)
    def _():
        mixed_one(lat_ref, mod_ref, h1_ref, h1_all, lat)

    flat = nt(w_ref[0], h1_all[lat]) + bias_ref[0]
    attend(flat, qkv_ref.shape[1] // 3, slot, heads_ref, qkv_ref, lse_ref, lambda h: None)


def attn_gather_kernel(
    lat_ref,
    mod_ref,
    bias_ref,
    wq_ref,
    wp_ref,
    w1_ref,
    w2_ref,
    heads_ref,
    qkv_ref,
    lse_ref,
    h1_ref,
    all_ref,
    h1_all,
    w_buf,
    local_sem,
    z_own,
    z_on,
    z_got,
    sends,
    recvs,
):
    n_mp = all_ref.shape[0]
    lats = h1_all.shape[0]
    units, pace = 3 * (n_mp - 1), 4
    slot, lat = pl.program_id(0), pl.program_id(1)
    step = slot * lats + lat
    dp_at, me = lax.axis_index("dp"), lax.axis_index("mp")
    core, x, y = dp_at % 2, dp_at // 2 % 2, dp_at // 4
    rows = all_ref.shape[5]
    upper = wq_ref.shape[0] // rows
    cut = rows // 32 * 16 + 16
    near, far = pl.ds(0, cut), pl.ds(cut, rows - cut)
    every = pl.ds(0, rows)
    both = pl.ds(0, 2)
    core_id = at_mesh(flip(dp_at, 0), me)
    x_id = at_mesh(flip(dp_at, 1), me)
    y_id = at_mesh(flip(dp_at, 2), me)
    right_id, left_id = at_mesh(dp_at, me + 1), at_mesh(dp_at, me - 1)

    def piece(s, c, at_y, at_x, at_core, part):
        return all_ref.at[s, c, at_y, at_x, at_core, part]

    def own_copy(c, side, target, source=None):
        ref = piece(me, c, y, x, core, every)
        return pltpu.make_async_remote_copy(
            ref if source is None else source,
            ref,
            z_own.at[side, c],
            z_got.at[c, me],
            **target,
        )

    def pass_on(s, c, target):
        ref = piece(s, c, y, x, core, every)
        return pltpu.make_async_remote_copy(
            ref, ref, z_on.at[c, s], z_got.at[c, s], **target
        )

    def move(kind, c, s, arrived=False):
        flipped = lambda v: 1 - v if arrived else v
        at_y, at_x, at_core, part, target = (
            (pl.ds(y, 1), pl.ds(flipped(x), 1), pl.ds(core, 1), near, x_id),
            (pl.ds(flipped(y), 1), pl.ds(x, 1), pl.ds(core, 1), far, y_id),
            (pl.ds(flipped(y), 1), both, pl.ds(core, 1), near, y_id),
            (both, pl.ds(flipped(x), 1), pl.ds(core, 1), far, x_id),
            (both, both, pl.ds(flipped(core), 1), every, core_id),
        )[kind]
        ref = piece(s, c, at_y, at_x, at_core, part)
        return pltpu.make_async_remote_copy(
            ref, ref, sends.at[kind, c, s], recvs.at[kind, c, s], **target
        )

    def unit(u):
        return u // (n_mp - 1), near_part(me, 1 + u % (n_mp - 1))

    def event(stage, u):
        c, s = unit(u)

        @pl.when((u >= 0) & (u < units))
        def _():
            if stage == 0:

                @pl.when((me > 0) & (me < n_mp - 1))
                def _():
                    pass_on(s, c, right_id).wait_recv()
                    pl.when(s < me)(lambda: pass_on(s, c, right_id).start())
                    pl.when(s > me)(lambda: pass_on(s, c, left_id).start())

            if stage == 1:

                @pl.when((me == 0) | (me == n_mp - 1))
                def _():
                    pass_on(s, c, right_id).wait_recv()

                move(0, c, s).start()
                move(1, c, s).start()
            if stage == 2:
                move(0, c, s, True).wait_recv()
                move(1, c, s, True).wait_recv()
                move(2, c, s).start()
                move(3, c, s).start()
            if stage == 3:
                move(2, c, s, True).wait_recv()
                move(3, c, s, True).wait_recv()
                move(4, c, s).start()
            if stage == 4:
                move(4, c, s, True).wait_recv()

    def send_from(c, ref, at):
        source = ref.at[pl.ds(at * rows, rows)]

        @pl.when(me < n_mp - 1)
        def _():
            own_copy(c, 0, right_id, source).start()

        @pl.when(me > 0)
        def _():
            own_copy(c, 1, left_id, source).start()

    def send_own(c):
        if c > 0:
            send_from(c, (w1_ref, w2_ref)[c - 1], dp_at)
        else:
            pl.when(dp_at < upper)(lambda: send_from(0, wq_ref, dp_at))
            pl.when(dp_at >= upper)(lambda: send_from(0, wp_ref, dp_at - upper))

    @pl.when(step == 0)
    def _():
        barrier = pltpu.get_barrier_semaphore()
        for target in (core_id, x_id, y_id):
            pl.semaphore_signal(barrier, inc=1, **target)

        @pl.when(me < n_mp - 1)
        def _():
            pl.semaphore_signal(barrier, inc=1, **right_id)

        @pl.when(me > 0)
        def _():
            pl.semaphore_signal(barrier, inc=1, **left_id)

        pl.semaphore_wait(barrier, 3 + line_peers(me, n_mp))
        send_own(0)

    def next_weights(k):
        return pltpu.make_async_copy(all_ref.at[near_part(me, k), 0], w_buf, local_sem.at[0])

    def tick(t):
        def due(at, every):
            return jnp.where((t - at) % every == 0, (t - at) // every, -1)

        for k, at in ((0, 3), (1, 4), (2, 7)):
            nth = due(at, 3 * pace)
            event(0, jnp.where(nth < 0, -1, nth * 3 + k))
        for stage, at in ((1, 3), (3, 8), (2, 5), (4, 11)):
            event(stage, due(at, pace))
        for c in (1, 2):
            pl.when(t == 3 * pace * c - 3)(lambda: send_own(c))

    @pl.when((lat == 0) & (slot == 0))
    def _():
        def load(at):
            return pltpu.make_async_copy(
                wq_ref.at[pl.ds(at * rows, rows)],
                w_buf.at[at // 4, at // 2 % 2, at % 2],
                local_sem.at[at],
            )

        for at in range(upper):
            load(at).start()
        for at in range(upper):
            load(at).wait()

    @pl.when((lat == 0) & (slot > 0))
    def _():
        next_weights(slot).wait()

    @pl.when(slot == 0)
    def _():
        mixed_one(lat_ref, mod_ref, h1_ref, h1_all, lat)

    n_heads = qkv_ref.shape[1] // 3
    weights = w_buf[...].reshape(8 * rows, w_buf.shape[-1])[: 3 * n_heads * HEAD_DIM]
    flat = nt(weights, h1_all[lat]) + bias_ref[0]

    def between(h):
        tick(step * n_heads + h - 1)

        @pl.when((lat == lats - 1) & (slot < n_mp - 1) & (h == n_heads))
        def _():
            next_weights(slot + 1).start()

    attend(flat, n_heads, slot, heads_ref, qkv_ref, lse_ref, between)

    @pl.when(step == n_mp * lats - 1)
    def _():
        def rest(t, carry):
            tick(t)
            return carry

        lax.fori_loop(n_mp * lats * n_heads, pace * units + 11, rest, 0)
        for c in range(3):

            @pl.when(me < n_mp - 1)
            def _():
                own_copy(c, 0, right_id).wait_send()

            @pl.when(me > 0)
            def _():
                own_copy(c, 1, left_id).wait_send()

        def drain(u, carry):
            c, s = unit(u)

            @pl.when((me > 0) & (me < n_mp - 1))
            def _():
                pass_on(s, c, right_id).wait_send()

            for kind in range(5):
                move(kind, c, s).wait_send()
            return carry

        lax.fori_loop(0, units, drain, 0)


def attn_gather(latents, mod, bias, own, n_mp):
    lat, seq, dim = latents.shape
    local = dim // n_mp
    n_heads = local // HEAD_DIM
    rows = dim // 8
    last = lat - 1
    first = lambda s, l: s // n_mp * 0 + jnp.where(s == 0, l, last)
    part = lambda s: near_part(lax.axis_index("mp"), s)
    heads, qkv, lse, h1, gathered = pl.pallas_call(
        attn_gather_kernel,
        grid=(n_mp, lat),
        in_specs=[
            pl.BlockSpec((1, seq, dim), lambda s, l: (first(s, l), 0, 0)),
            pl.BlockSpec((1, 6, dim), lambda s, l: (l, 0, 0)),
            pl.BlockSpec((1, 3 * local, 1), lambda s, l: (part(s), 0, 0)),
        ]
        + [pl.BlockSpec(memory_space=pl.ANY)] * 4,
        out_specs=[
            pl.BlockSpec((1, 1, local, seq), lambda s, l: (part(s), l, 0, 0)),
            pl.BlockSpec((1, 3 * n_heads, HEAD_DIM, seq), lambda s, l: (first(s, l), 0, 0, 0)),
            pl.BlockSpec((1, n_heads, seq), lambda s, l: (first(s, l), 0, 0)),
            pl.BlockSpec((1, seq, dim), lambda s, l: (first(s, l), 0, 0)),
            pl.BlockSpec(memory_space=pl.ANY),
        ],
        out_shape=[
            jax.ShapeDtypeStruct((n_mp, lat, local, seq), BF),
            jax.ShapeDtypeStruct((lat, 3 * n_heads, HEAD_DIM, seq), BF),
            jax.ShapeDtypeStruct((lat, n_heads, seq), F32),
            jax.ShapeDtypeStruct((lat, seq, dim), BF),
            jax.ShapeDtypeStruct((n_mp, 3, 2, 2, 2, rows, dim), BF),
        ],
        scratch_shapes=[
            pltpu.VMEM((lat, seq, dim), BF),
            pltpu.VMEM((2, 2, 2, rows, dim), BF),
            pltpu.SemaphoreType.DMA((8,)),
            pltpu.SemaphoreType.DMA((2, 3)),
            pltpu.SemaphoreType.DMA((3, n_mp)),
            pltpu.SemaphoreType.DMA((3, n_mp)),
            pltpu.SemaphoreType.DMA((5, 3, n_mp)),
            pltpu.SemaphoreType.DMA((5, 3, n_mp)),
        ],
        compiler_params=pltpu.CompilerParams(
            collective_id=1, has_side_effects=True, vmem_limit_bytes=60 * MIB
        ),
        name="attn_gather",
    )(latents, mod, bias, *own)
    return heads, qkv, lse, h1, gathered.reshape(n_mp, 3, dim, dim)


def attn_fwd(me, latents, mod, gathered, bias, n_mp):
    lat, seq, dim = latents.shape
    local = dim // n_mp
    n_heads = local // HEAD_DIM
    last = lat - 1
    first = lambda s, l: jnp.where(s == 0, l, last)
    return pl.pallas_call(
        attn_fwd_kernel,
        grid_spec=pltpu.PrefetchScalarGridSpec(
            num_scalar_prefetch=1,
            grid=(n_mp, lat),
            in_specs=[
                pl.BlockSpec((1, seq, dim), lambda s, l, me: (first(s, l), 0, 0)),
                pl.BlockSpec((1, 6, dim), lambda s, l, me: (l, 0, 0)),
                pl.BlockSpec(
                    (1, 3 * local, dim), lambda s, l, me: (lax.rem(me[0] + s, n_mp), 0, 0)
                ),
                pl.BlockSpec((1, 3 * local, 1), lambda s, l, me: (lax.rem(me[0] + s, n_mp), 0, 0)),
            ],
            out_specs=[
                pl.BlockSpec(
                    (1, 1, local, seq), lambda s, l, me: (lax.rem(me[0] + s, n_mp), l, 0, 0)
                ),
                pl.BlockSpec(
                    (1, 3 * n_heads, HEAD_DIM, seq), lambda s, l, me: (first(s, l), 0, 0, 0)
                ),
                pl.BlockSpec((1, n_heads, seq), lambda s, l, me: (first(s, l), 0, 0)),
                pl.BlockSpec((1, seq, dim), lambda s, l, me: (first(s, l), 0, 0)),
            ],
            scratch_shapes=[pltpu.VMEM((lat, seq, dim), BF)],
        ),
        out_shape=[
            jax.ShapeDtypeStruct((n_mp, lat, local, seq), BF),
            jax.ShapeDtypeStruct((lat, 3 * n_heads, HEAD_DIM, seq), BF),
            jax.ShapeDtypeStruct((lat, n_heads, seq), F32),
            jax.ShapeDtypeStruct((lat, seq, dim), BF),
        ],
        compiler_params=pltpu.CompilerParams(vmem_limit_bytes=60 * MIB),
        name="attn_fwd",
    )(me, latents, mod, gathered, bias)


class LineSum:
    def __init__(self, own_ref, up, down, sems, out_ref):
        self.own, self.up, self.down, self.sems, self.out = own_ref, up, down, sems, out_ref
        self.count, self.rows = up.shape[0], up.shape[1]
        self.me = lax.axis_index("mp")
        self.n = lax.axis_size("mp")
        dp_at = lax.axis_index("dp")
        self.ends = (at_mesh(dp_at, self.me + 1), at_mesh(dp_at, self.me - 1))
        self.place = (self.me, self.n - 1 - self.me)

    def guarded(self, side, first, action):
        there = self.place[side] > 0 if first else self.place[side] < self.n - 1

        @pl.when(there)
        def _():
            action()

    def greet(self):
        sem = pltpu.get_barrier_semaphore()
        for side in (0, 1):
            self.guarded(side, False, lambda: pl.semaphore_signal(sem, inc=1, **self.ends[side]))

    def barrier(self):
        self.greet()
        pl.semaphore_wait(pltpu.get_barrier_semaphore(), line_peers(self.me, self.n))

    def copy(self, side, c):
        ref = (self.up, self.down)[side].at[c]
        return pltpu.make_async_remote_copy(
            ref, ref, self.sems.at[2 * side, c], self.sems.at[2 * side + 1, c], **self.ends[side]
        )

    def handle(self, side, c):
        ref = (self.up, self.down)[side]
        own = self.own[0, pl.ds(pl.multiple_of(c * self.rows, self.rows), self.rows)]

        @pl.when(self.place[side] == 0)
        def _():
            ref[c] = own

        @pl.when(self.place[side] > 0)
        def _():
            self.copy(side, c).wait_recv()
            ref[c] = (ref[c].astype(F32) + own.astype(F32)).astype(BF)

        self.guarded(side, False, lambda: self.copy(side, c).start())

    def tick(self, t):
        for side in (0, 1):
            at = t - 2 * self.place[side]

            @pl.when((at >= 0) & (at % 3 < 2) & (at - at // 3 < self.count))
            def _():
                self.handle(side, at - at // 3)

    def finish(self, ticks):
        for side in (0, 1):
            done = jnp.maximum(ticks - 2 * self.place[side], 0)
            done = jnp.minimum(done - done // 3, self.count)

            def late(c, carry):
                self.handle(side, c)
                return carry

            lax.fori_loop(done, self.count, late, 0)

        def add(c, carry):
            rows = pl.ds(pl.multiple_of(c * self.rows, self.rows), self.rows)
            total = self.up[c].astype(F32) + self.down[c].astype(F32)
            self.out[0, rows] = (total - self.own[0, rows].astype(F32)).astype(BF)
            return carry

        lax.fori_loop(0, self.count, add, 0)
        for side in (0, 1):

            def sent(c, carry):
                self.copy(side, c).wait_send()
                return carry

            self.guarded(side, False, lambda: lax.fori_loop(0, self.count, sent, 0))


def mlp_kernel(*refs, summing):
    heads_ref, lat_ref, cot_ref, mod_ref, bp_ref, b1_ref, b2_ref = refs[:7]
    own_refs, (wq_all, w1_all, w2_all), refs = refs[7:10], refs[10:13], refs[13:]
    if summing:
        part_ref, refs = refs[0], refs[1:]
    out_ref, dx1_ref, da_ref, h2_ref, dm_ref, z_ref, du_ref, stats_ref, dusum_ref = refs[:9]
    refs = refs[9:]
    if summing:
        sum_ref, refs = refs[0], refs[1:]
    macc, dacc, wp, w1, w2, load_sems = refs[:6]
    n_mp, hid, dim = w2.shape
    local = wp.shape[1]
    rows = lat_ref.shape[1]
    me = lax.axis_index("mp")
    step = pl.program_id(0)
    line = LineSum(part_ref, refs[6], refs[7], refs[8], sum_ref) if summing else None

    def load(kind, k):
        slot = (me + k) % n_mp
        source = own_refs[kind]
        if k > 0:
            stack = (wq_all, w1_all, w2_all)[kind]
            source = stack.at[slot, kind] if len(stack.shape) == 4 else stack.at[slot]
        if k > 0 and kind == 0:
            source = source.at[pl.ds(3 * local, local)]
        ref = (wp.at[slot], w1.at[k], w2.at[k])[kind]
        return pltpu.make_async_copy(source, ref, load_sems.at[kind, k])

    @pl.when(step == 0)
    def _():
        if summing:
            line.barrier()
        for k in range(n_mp):
            load(0, k).start()
        for k in range(n_mp):
            load(1, k).start()
            load(2, k).start()
        for k in range(n_mp):
            load(0, k).wait()

    gate_one, shift_two = mod_ref[0, 2:3], mod_ref[0, 3:4]
    scale_two, gate_two = mod_ref[0, 4:5], mod_ref[0, 5:6]
    heads = heads_ref[:, 0].reshape(dim, rows)
    attn = tn(heads, wp[...].reshape(dim, dim)) + bp_ref[...]
    x1 = lat_ref[0].astype(F32) + gate_one * attn
    n2, inv2 = norm_stats(x1)
    h2 = (n2 * (1.0 + scale_two) + shift_two).astype(BF)
    h2_ref[0] = h2
    cot = cot_ref[0].astype(F32)
    dm = (gate_two * cot).astype(BF)
    dm_ref[0] = dm

    macc[...] = jnp.zeros_like(macc)
    dacc[...] = jnp.zeros_like(dacc)

    def part(k, own):
        if summing:
            line.tick(step * n_mp + k)

        @pl.when(step == 0)
        def _():
            for kind in (1, 2):
                ref = (w1, w2)[kind - 1].at[k]
                pltpu.make_async_copy(ref, ref, load_sems.at[kind, k]).wait()

        u = mm(h2_ref[0], w1[k]) + b1_ref[(me + k) % n_mp]
        dz = nt(dm_ref[0], w2[k])
        u2 = u * u
        t = jnp.tanh(u * (GELU_A + (GELU_A * GELU_B) * u2))
        half = 0.5 + 0.5 * t
        z = (u * half).astype(BF)
        slope = half + u * (1.0 - t * t) * (0.5 * GELU_A + (1.5 * GELU_A * GELU_B) * u2)
        du = dz * slope
        if own:
            before = jnp.where(step == 0, 0.0, dusum_ref[0])
            dusum_ref[0] = before + jnp.sum(du, 0, keepdims=True)
        du = du.astype(BF)
        if own:
            z_ref[0] = z
            du_ref[0] = du
        macc[...] += mm(z, w2[k])
        dacc[...] += nt(du, w1[k])

    part(0, True)

    def body(k, carry):
        part(k, False)
        return carry

    lax.fori_loop(1, n_mp, body, 0)
    mlp = macc[...] + b2_ref[...]
    out_ref[0] = (x1 + gate_two * mlp).astype(BF)
    dh2 = dacc[...]
    dx1 = cot + norm_back(n2, inv2, dh2 * (1.0 + scale_two))
    dx1_ref[0] = dx1.astype(BF)
    da_ref[0] = (gate_one * dx1).astype(BF)
    total = lambda v: jnp.sum(v, 0, keepdims=True)
    stats = jnp.concatenate(
        [
            total(dx1 * attn),
            total(dh2),
            total(dh2 * n2),
            total(cot * mlp),
            total(cot),
            total(dx1),
            jnp.zeros((2, dim), F32),
        ],
        0,
    )

    @pl.when(step == 0)
    def _():
        stats_ref[0] = stats

    @pl.when(step > 0)
    def _():
        stats_ref[0] += stats

    if summing:

        @pl.when(step == pl.num_programs(0) - 1)
        def _():
            line.finish(pl.num_programs(0) * n_mp)


LINE_CHUNKS = 8


def line_scratch(seq, dim):
    rows = seq // LINE_CHUNKS
    return [
        pltpu.VMEM((LINE_CHUNKS, rows, dim), BF),
        pltpu.VMEM((LINE_CHUNKS, rows, dim), BF),
        pltpu.SemaphoreType.DMA((4, LINE_CHUNKS)),
    ]


def mlp_both(index, heads, latents, cotangent, mod, biases, own, gathered, n_mp, rows, part):
    lat, seq, dim = latents.shape
    local = dim // n_mp
    hid = biases[1].shape[2]
    tok = pl.BlockSpec((1, rows, dim), lambda t: (index, t, 0))
    new = pl.BlockSpec((1, rows, dim), lambda t: (0, t, 0))
    hidden = pl.BlockSpec((1, rows, hid), lambda t: (0, t, 0))
    once = lambda shape: pl.BlockSpec(
        shape, lambda t: (0,) * len(shape), pipeline_mode=pl.Buffered(1)
    )
    any_spec = pl.BlockSpec(memory_space=pl.ANY)
    summing = part is not None
    extra = [once((1, seq, dim))] if summing else []
    return pl.pallas_call(
        functools.partial(mlp_kernel, summing=summing),
        grid=(seq // rows,),
        in_specs=[
            pl.BlockSpec((n_mp, 1, local, rows), lambda t: (0, index, 0, t)),
            tok,
            tok,
            pl.BlockSpec((1, 6, dim), lambda t: (index, 0, 0)),
            once((1, dim)),
            once((n_mp, 1, hid)),
            once((1, dim)),
        ]
        + [any_spec] * 6
        + extra,
        out_specs=[new] * 5
        + [
            hidden,
            hidden,
            pl.BlockSpec((1, 8, dim), lambda t: (0, 0, 0)),
            pl.BlockSpec((1, 1, hid), lambda t: (0, 0, 0)),
        ]
        + extra,
        out_shape=[jax.ShapeDtypeStruct((1, seq, dim), BF)] * 5
        + [jax.ShapeDtypeStruct((1, seq, hid), BF)] * 2
        + [jax.ShapeDtypeStruct((1, 8, dim), F32), jax.ShapeDtypeStruct((1, 1, hid), F32)]
        + ([jax.ShapeDtypeStruct((1, seq, dim), BF)] if summing else []),
        scratch_shapes=[
            pltpu.VMEM((rows, dim), F32),
            pltpu.VMEM((rows, dim), F32),
            pltpu.VMEM((n_mp, local, dim), BF),
            pltpu.VMEM((n_mp, dim, hid), BF),
            pltpu.VMEM((n_mp, hid, dim), BF),
            pltpu.SemaphoreType.DMA((3, n_mp)),
        ]
        + (line_scratch(seq, dim) if summing else []),
        compiler_params=pltpu.CompilerParams(
            vmem_limit_bytes=63 * MIB,
            **(dict(collective_id=4 + index, has_side_effects=True) if summing else {}),
        ),
        name="mlp_sum" if summing else "mlp_both",
    )(
        heads,
        latents,
        cotangent,
        mod,
        *biases,
        *own,
        *gathered,
        *([part] if summing else []),
    )


class CubeSum:
    def __init__(self, terms, full, halves, firsts, seconds, sems):
        self.terms, self.full = terms, full
        self.halves, self.firsts, self.seconds, self.sems = halves, firsts, seconds, sems
        self.units = halves.shape[0]
        dp_at, me = lax.axis_index("dp"), lax.axis_index("mp")
        self.core, x, y = dp_at % 2, dp_at // 2 % 2, dp_at // 4
        self.core_id = at_mesh(flip(dp_at, 0), me)
        x_id, y_id = at_mesh(flip(dp_at, 1), me), at_mesh(flip(dp_at, 2), me)
        self.ids = ((x_id, y_id), (y_id, x_id))
        self.place = ((x, y), (y, x))

    def barrier(self):
        sem = pltpu.get_barrier_semaphore()
        for target in (self.core_id,) + self.ids[0]:
            pl.semaphore_signal(sem, inc=1, **target)

    def blocks(self, u, core, q=None, first=None, second=None):
        at, count = 16 * u + 8 * core, 8
        if q is not None:
            at, count = at + 4 * q, 4
        if first is not None:
            at, count = at + 2 * first, 2
        if second is not None:
            at, count = at + second, 1
        return pl.ds(at, count)

    def send(self, stage, u, q, arrived=False):
        core, blocks = self.core, self.blocks
        first, second = self.place[q]
        other = lambda v: 1 - v if arrived else v
        if stage == 0:
            pair = (self.terms.at[blocks(u, 1 - core)], self.halves.at[u])
        elif stage == 1:
            pair = (self.terms.at[blocks(u, core, q, 1 - first)], self.firsts.at[u, q])
        elif stage == 2:
            pair = (self.terms.at[blocks(u, core, q, first, 1 - second)], self.seconds.at[u, q])
        elif stage == 3:
            pair = (self.full.at[blocks(u, core, q, first, other(second))],) * 2
        elif stage == 4:
            pair = (self.full.at[blocks(u, core, q, other(first))],) * 2
        else:
            pair = (self.full.at[blocks(u, other(core))],) * 2
        near, far = self.ids[q]
        target = (self.core_id, near, far, far, near, self.core_id)[stage]
        return pltpu.make_async_remote_copy(
            *pair, self.sems.at[0, stage, q, u], self.sems.at[1, stage, q, u], **target
        )

    def quarters(self, stage):
        return (0,) if stage in (0, 5) else (0, 1)

    def event(self, stage, u):
        terms, core, blocks = self.terms, self.core, self.blocks

        @pl.when((u >= 0) & (u < self.units))
        def _():
            if stage > 0:
                for q in self.quarters(stage - 1):
                    self.send(stage - 1, u, q, True).wait_recv()
            if stage == 1:
                at = blocks(u, core)
                terms[at] = (terms[at].astype(F32) + self.halves[u].astype(F32)).astype(BF)
            for q in (0, 1):
                first, second = self.place[q]
                if stage == 2:
                    at = blocks(u, core, q, first)
                    terms[at] = (terms[at].astype(F32) + self.firsts[u, q].astype(F32)).astype(BF)
                if stage == 3:
                    at = blocks(u, core, q, first, second)
                    total = terms[at].astype(F32) + self.seconds[u, q].astype(F32)
                    self.full[at] = total.astype(BF)
            if stage < 6:
                for q in self.quarters(stage):
                    self.send(stage, u, q).start()

    def finish(self):
        def sent(u, carry):
            for stage in range(6):
                for q in self.quarters(stage):
                    self.send(stage, u, q).wait_send()
            return carry

        lax.fori_loop(0, self.units, sent, 0)


BLOCK = 32


class WeightGrads:
    def __init__(self, operands, terms, right, left_cols, left_rows, right_sems, left_sems):
        self.operands, self.terms, self.right = operands, terms, right
        self.left_cols, self.left_rows = left_cols, left_rows
        self.right_sems, self.left_sems = right_sems, left_sems
        self.lats = right.shape[1]
        dim = right.shape[3]
        qkv_blocks = operands[2][0][0].shape[0] // BLOCK
        half = (qkv_blocks + 1) // 2 * BLOCK
        third = dim // 3
        self.pieces = [(job, i * third, third) for job in (0, 1) for i in range(3)]
        self.pieces += [(2, 0, half), (2, half, qkv_blocks * BLOCK - half)]
        self.pieces += [(3, 0, operands[3][0][0].shape[0])]

    def right_copies(self, job):
        slot = job % 2
        return [
            pltpu.make_async_copy(
                self.operands[job][1][i], self.right.at[slot, i], self.right_sems.at[slot, i]
            )
            for i in range(self.lats)
        ]

    def left_copies(self, at):
        job, first, count = self.pieces[at]
        copies = []
        for i in range(self.lats):
            source = self.operands[job][0][i]
            if job < 2:
                source = source.at[:, pl.ds(first, count)]
                ref = self.left_cols.at[at % 2, i]
            else:
                source = source.at[pl.ds(first, count)]
                ref = self.left_rows.at[at % 2, i, pl.ds(0, count)]
            copies.append(pltpu.make_async_copy(source, ref, self.left_sems.at[at % 2, i]))
        return copies

    def begin(self):
        for copy in self.right_copies(0) + self.left_copies(0):
            copy.start()

    def compute(self, at):
        job, _, count = self.pieces[at]
        opens = at == 0 or self.pieces[at - 1][0] != job
        if at + 1 < len(self.pieces):
            for copy in self.left_copies(at + 1):
                copy.start()
        if opens:
            if job + 1 < len(self.operands):
                for copy in self.right_copies(job + 1):
                    copy.start()
            for copy in self.right_copies(job):
                copy.wait()
        for copy in self.left_copies(at):
            copy.wait()
        slot, dim = job % 2, self.right.shape[3]
        if job < 2:
            left = self.left_cols[at % 2].reshape(-1, count)
            total = tn(left, self.right[slot].reshape(-1, dim))
        else:
            total = mm(self.left_rows[at % 2, 0, :count], self.right[slot, 0])
            for i in range(1, self.lats):
                total = total + mm(self.left_rows[at % 2, i, :count], self.right[slot, i])
        done = sum(rows for _, _, rows in self.pieces[:at]) // BLOCK
        self.terms[pl.ds(done, count // BLOCK)] = total.reshape(-1, BLOCK, dim).astype(BF)


def tail_kernel(*refs, lats):
    part_ref, bias_ref, heads_ref, h1_ref = refs[:4]
    lists = [refs[4 + i * lats : 4 + (i + 1) * lats] for i in range(6)]
    h2s, dus, zs, dms, dqkvs, das = [[ref.at[0] for ref in group] for group in lists]
    sum_ref, full_ref = refs[4 + 6 * lats : 6 + 6 * lats]
    refs = refs[6 + 6 * lats :]
    up, down, line_sems, terms, full, halves, firsts, seconds, cube_sems = refs[:9]
    right, left_cols, left_rows, right_sems, left_sems, local_sem = refs[9:]
    line = LineSum(part_ref, up, down, line_sems, sum_ref)
    cube = CubeSum(terms, full, halves, firsts, seconds, cube_sems)
    heads = [heads_ref.at[line.me, i] for i in range(lats)]
    h1s = [h1_ref.at[i] for i in range(lats)]
    grads = WeightGrads(
        ((h2s, dus), (zs, dms), (dqkvs, h1s), (heads, das)),
        terms,
        right,
        left_cols,
        left_rows,
        right_sems,
        left_sems,
    )
    grads.begin()
    cube.barrier()
    line.greet()
    pl.semaphore_wait(pltpu.get_barrier_semaphore(), 3 + line_peers(line.me, line.n))
    spare = bias_ref.shape[0]
    terms[pl.ds(terms.shape[0] - spare, spare)] = bias_ref[...]
    line.tick(0)
    unit_rows = 16 * BLOCK
    ready = 0
    for t in range(cube.units):
        line.tick(2 * t + 1)
        while ready < len(grads.pieces) and (
            sum(rows for _, _, rows in grads.pieces[:ready]) < (t + 1) * unit_rows
        ):
            grads.compute(ready)
            ready += 1
        line.tick(2 * t + 2)
        for stage in range(min(t, 6), -1, -1):
            cube.event(stage, t - stage)

    def advance(t, carry):
        line.tick(2 * t + 1)
        for stage in range(6, 0, -1):
            cube.event(stage, t - stage)
        line.tick(2 * t + 2)
        return carry

    lax.fori_loop(cube.units, cube.units + 6, advance, 0)
    store = pltpu.make_async_copy(full, full_ref, local_sem.at[0])
    store.start()
    line.finish(2 * (cube.units + 6) + 1)
    cube.finish()
    store.wait()


def tail_sums(part, biases, heads, h1, lists):
    n_mp, lats, local, seq = heads.shape
    dim = h1.shape[2]
    rows = 2 * dim + 4 * local
    units = -(-(rows + BLOCK) // (16 * BLOCK))
    spare = units * 16 - rows // BLOCK
    biases = jnp.pad(biases, ((0, spare * BLOCK - biases.shape[0]), (0, 0)))
    vmem = pl.BlockSpec(memory_space=pltpu.VMEM)
    any_spec = pl.BlockSpec(memory_space=pl.ANY)
    shape = (units * 16, BLOCK, dim)
    flat = [array for group in lists for array in group]
    total, full = pl.pallas_call(
        functools.partial(tail_kernel, lats=lats),
        in_specs=[vmem, vmem] + [any_spec] * (2 + len(flat)),
        out_specs=[vmem, any_spec],
        out_shape=[jax.ShapeDtypeStruct(part.shape, BF), jax.ShapeDtypeStruct(shape, BF)],
        scratch_shapes=line_scratch(seq, dim)
        + [
            pltpu.VMEM(shape, BF),
            pltpu.VMEM(shape, BF),
            pltpu.VMEM((units, 8, BLOCK, dim), BF),
            pltpu.VMEM((units, 2, 2, BLOCK, dim), BF),
            pltpu.VMEM((units, 2, 1, BLOCK, dim), BF),
            pltpu.SemaphoreType.DMA((2, 6, 2, units)),
            pltpu.VMEM((2, lats, seq, dim), BF),
            pltpu.VMEM((2, lats, seq, dim // 3), BF),
            pltpu.VMEM((2, lats, (3 * local // BLOCK + 1) // 2 * BLOCK, seq), BF),
            pltpu.SemaphoreType.DMA((2, lats)),
            pltpu.SemaphoreType.DMA((2, lats)),
            pltpu.SemaphoreType.DMA((1,)),
        ],
        compiler_params=pltpu.CompilerParams(
            collective_id=2, has_side_effects=True, vmem_limit_bytes=63 * MIB
        ),
        name="tail_sums",
    )(part, biases.reshape(spare, BLOCK, dim), heads, h1, *flat)
    return total, full.reshape(units * 16 * BLOCK, dim)


def rows_kernel(rows_ref, act_ref, every_ref, total_ref, acts, sems):
    dp_at, me = lax.axis_index("dp"), lax.axis_index("mp")
    n_dp, n_mp = every_ref.shape[0], acts.shape[0]
    barrier = pltpu.get_barrier_semaphore()
    for k in range(1, n_dp):
        pl.semaphore_signal(barrier, inc=1, **at_mesh((dp_at + k) % n_dp, me))
    for k in range(1, n_mp):
        pl.semaphore_signal(barrier, inc=1, **at_mesh(dp_at, (me + k) % n_mp))
    every_ref[dp_at] = rows_ref[...]
    acts[me] = act_ref[...]
    pl.semaphore_wait(barrier, n_dp + n_mp - 2)

    def copy(ref, k, target):
        return pltpu.make_async_remote_copy(ref, ref, sems.at[0, k], sems.at[1, k], **target)

    def act_copy(k, source):
        return copy(acts.at[source % n_mp], k - 1, at_mesh(dp_at, (me + k) % n_mp))

    def row_copy(k, source):
        target = at_mesh((dp_at + k) % n_dp, me)
        return copy(every_ref.at[source % n_dp], n_mp + k - 2, target)

    for k in range(1, n_mp):
        act_copy(k, me).start()
    for k in range(1, n_dp):
        row_copy(k, dp_at).start()
    for k in range(1, n_mp):
        act_copy(k, me + n_mp - k).wait_recv()
    total = acts[0]
    for i in range(1, n_mp):
        total = total + acts[i]
    total_ref[...] = total
    for k in range(1, n_dp):
        row_copy(k, dp_at + n_dp - k).wait_recv()
    for k in range(1, n_mp):
        act_copy(k, me).wait_send()
    for k in range(1, n_dp):
        row_copy(k, dp_at).wait_send()


def rows_exchange(rows, act, n_dp, n_mp):
    vmem = pl.BlockSpec(memory_space=pltpu.VMEM)
    return pl.pallas_call(
        rows_kernel,
        in_specs=[vmem, vmem],
        out_specs=[vmem, vmem],
        out_shape=[
            jax.ShapeDtypeStruct((n_dp,) + rows.shape, rows.dtype),
            jax.ShapeDtypeStruct(act.shape, act.dtype),
        ],
        scratch_shapes=[
            pltpu.VMEM((n_mp,) + act.shape, act.dtype),
            pltpu.SemaphoreType.DMA((2, n_dp + n_mp - 2)),
        ],
        compiler_params=pltpu.CompilerParams(
            collective_id=3, has_side_effects=True, vmem_limit_bytes=40 * MIB
        ),
        name="rows_exchange",
    )(rows, act)


def attn_bwd_kernel(da_ref, heads_ref, qkv_ref, lse_ref, wp_ref, wq_ref, dqkv_ref, dh1_ref, bias_ref, *, rows):
    n_heads = lse_ref.shape[1]
    seq = da_ref.shape[1]
    dheads = nt(wp_ref[...], da_ref[0]).reshape(n_heads, HEAD_DIM, seq)
    heads = heads_ref[0].astype(F32).reshape(n_heads, HEAD_DIM, seq)
    scaling = 1.0 / HEAD_DIM**0.5
    dq_list, dk_list, dv_list = [], [], []
    for h in range(n_heads):
        q_t = qkv_ref[0, h]
        k_t = qkv_ref[0, n_heads + h]
        v_t = qkv_ref[0, 2 * n_heads + h]
        q = q_t.astype(F32).T.astype(BF)
        k = k_t.astype(F32).T.astype(BF)
        v = v_t.astype(F32).T.astype(BF)
        do_t = dheads[h].astype(BF)
        do = dheads[h].T.astype(BF)
        inner = jnp.sum(do_t.astype(F32) * heads[h], 0, keepdims=True)
        dq_parts = []
        for i in range(seq // rows):
            cols = slice(i * rows, (i + 1) * rows)
            probs = jnp.exp2(mm(k, q_t[:, cols]) - lse_ref[0, h : h + 1, cols])
            dprobs = mm(v, do_t[:, cols])
            dscores = (probs * (dprobs - inner[:, cols])).astype(BF)
            dq_parts.append(mm(k_t, dscores))
            dv_new = mm(probs.astype(BF), do[cols])
            dk_new = mm(dscores, q[cols])
            dv = dv_new if i == 0 else dv + dv_new
            dk = dk_new if i == 0 else dk + dk_new
        dq_list.append(jnp.concatenate(dq_parts, 1) * scaling)
        dk_list.append(dk.T * (1.0 / LOG2E))
        dv_list.append(dv.T)
    dqkv = jnp.concatenate(dq_list + dk_list + dv_list, 0)
    bias_ref[0] = jnp.sum(dqkv, 1, keepdims=True)
    dqkv = dqkv.astype(BF)
    dqkv_ref[0] = dqkv
    dh1_ref[0] = tn(dqkv, wq_ref[...]).astype(BF)


def attn_bwd(da, heads_own, qkv, lse, wp, wq, index, rows):
    lat, seq, dim = da.shape
    n_heads = lse.shape[1]
    local = n_heads * HEAD_DIM
    one = lambda shape: pl.BlockSpec((1,) + shape, lambda i: (index,) + (0,) * len(shape))
    only = lambda shape: pl.BlockSpec((1,) + shape, lambda i: (0,) * (len(shape) + 1))
    whole = lambda shape: pl.BlockSpec(shape, lambda i: (0,) * len(shape))
    out = lambda shape: pl.BlockSpec((1,) + shape, lambda i: (0,) * (len(shape) + 1))
    return pl.pallas_call(
        functools.partial(attn_bwd_kernel, rows=rows),
        grid=(1,),
        in_specs=[
            only((seq, dim)),
            one((local, seq)),
            one((3 * n_heads, HEAD_DIM, seq)),
            one((n_heads, seq)),
            whole((local, dim)),
            whole((3 * local, dim)),
        ],
        out_specs=[out((3 * local, seq)), out((seq, dim)), out((3 * local, 1))],
        out_shape=[
            jax.ShapeDtypeStruct((1, 3 * local, seq), BF),
            jax.ShapeDtypeStruct((1, seq, dim), BF),
            jax.ShapeDtypeStruct((1, 3 * local, 1), F32),
        ],
        compiler_params=pltpu.CompilerParams(vmem_limit_bytes=60 * MIB),
        name="attn_bwd",
    )(da, heads_own, qkv, lse, wp, wq)


def latents_kernel(dh1_ref, dx1_ref, lat_ref, mod_ref, grad_ref, stats_ref):
    n1, inv1 = norm_stats(lat_ref[0].astype(F32))
    dh1 = dh1_ref[0].astype(F32)
    grad = dx1_ref[0].astype(F32) + norm_back(n1, inv1, dh1 * (1.0 + mod_ref[0, 1:2]))
    grad_ref[0] = grad.astype(BF)
    stats = jnp.concatenate(
        [
            jnp.sum(dh1, 0, keepdims=True),
            jnp.sum(dh1 * n1, 0, keepdims=True),
            jnp.zeros((6, dh1.shape[1]), F32),
        ],
        0,
    )

    @pl.when(pl.program_id(0) == 0)
    def _():
        stats_ref[0] = stats

    @pl.when(pl.program_id(0) > 0)
    def _():
        stats_ref[0] += stats


def latents_back(dh1, dx1, latents, mod, index, rows):
    lat, seq, dim = latents.shape
    tok = pl.BlockSpec((1, rows, dim), lambda t: (index, t, 0))
    new = pl.BlockSpec((1, rows, dim), lambda t: (0, t, 0))
    return pl.pallas_call(
        latents_kernel,
        grid=(seq // rows,),
        in_specs=[new, new, tok, pl.BlockSpec((1, 6, dim), lambda t: (index, 0, 0))],
        out_specs=[new, pl.BlockSpec((1, 8, dim), lambda t: (0, 0, 0))],
        out_shape=[
            jax.ShapeDtypeStruct((1, seq, dim), BF),
            jax.ShapeDtypeStruct((1, 8, dim), F32),
        ],
        compiler_params=pltpu.CompilerParams(vmem_limit_bytes=40 * MIB),
        name="latents_back",
    )(dh1, dx1, latents, mod)


def per_device(
    n_dp,
    n_mp,
    latents,
    condition,
    cotangent,
    qkv_weight,
    qv_bias,
    proj_weight,
    proj_bias,
    fc1_weight,
    fc1_bias,
    fc2_weight,
    fc2_bias,
    ada_weight,
    ada_bias,
):
    lat, seq, dim = latents.shape
    local = qkv_weight.shape[2]
    n_heads = local // HEAD_DIM
    hid = fc1_weight.shape[1]
    cols = ada_weight.shape[1]
    mp_at = lax.axis_index("mp")
    dp_at = lax.axis_index("dp")
    me = jnp.full((1,), mp_at, jnp.int32)

    direct = n_mp == 4 and n_dp == 8
    bias_row = jnp.concatenate([qv_bias.reshape(-1), fc1_bias]).astype(F32)[None]
    ada_row = ada_bias.astype(F32)[None]
    if direct:
        small, cond_low = modulation_all(condition, ada_weight, ada_row, bias_row, n_mp)
    else:
        cond_low = jax.nn.silu(condition).astype(BF)
        mod_part = mm(cond_low, ada_weight) + ada_row
        small = lax.all_gather(jnp.concatenate([mod_part, bias_row], 0), "mp", axis=0)
    mod = small[:, :lat].transpose(1, 0, 2).reshape(lat, 6, dim)
    qv_all = small[:, lat, : 2 * local].reshape(n_mp, 2, local)
    b_qkv = jnp.stack([qv_all[:, 0], jnp.zeros((n_mp, local), F32), qv_all[:, 1]], 1).reshape(
        n_mp, 3 * local, 1
    )
    b_fc1 = small[:, lat, 2 * local :].reshape(n_mp, 1, hid)

    wq_own = (
        qkv_weight.reshape(dim, 3, n_heads, HEAD_DIM).transpose(1, 2, 3, 0).reshape(3 * local, dim)
    )
    if direct:
        own = (wq_own, proj_weight, fc1_weight, fc2_weight)
        heads, qkv, lse, h1, gathered = attn_gather(latents, mod, b_qkv, own, n_mp)
        gathered = (gathered,) * 3
    else:

        def gather(weight):
            share = weight.shape[0] // n_dp
            mine = lax.dynamic_slice_in_dim(weight, dp_at * share, share, 0)
            whole = lax.all_gather(mine, ("dp", "mp"), axis=0)
            whole = whole.reshape(n_dp, n_mp, share, weight.shape[1]).transpose(1, 0, 2, 3)
            return whole.reshape(n_mp, weight.shape[0], weight.shape[1])

        gathered = (
            gather(jnp.concatenate([wq_own, proj_weight], 0)),
            gather(fc1_weight),
            gather(fc2_weight),
        )
        heads, qkv, lse, h1 = attn_fwd(me, latents, mod, gathered[0], b_qkv, n_mp)
    heads_own = lax.dynamic_index_in_dim(heads, mp_at, 0, keepdims=False)
    rows = min(256, seq)
    results, dqkv, dh1, bias_sums = [], [], [], []
    for i in range(lat):
        waiting = dqkv and direct
        outs = mlp_both(
            i,
            heads,
            latents,
            cotangent,
            mod,
            (proj_bias.astype(F32)[None], b_fc1, fc2_bias.astype(F32)[None]),
            (proj_weight, fc1_weight, fc2_weight),
            gathered,
            n_mp,
            rows,
            dh1_i if waiting else None,
        )
        if waiting:
            dh1.append(outs[-1])
        results.append(outs[:9])
        dqkv_i, dh1_i, sums_i = attn_bwd(
            outs[2], heads_own, qkv, lse, proj_weight, wq_own, i, min(512, seq)
        )
        dqkv.append(dqkv_i)
        bias_sums.append(sums_i)
        if not direct:
            dh1.append(lax.psum(dh1_i, "mp"))
    outs_by_kind = list(zip(*results))
    h2, dm, z, du = outs_by_kind[3:7]
    da = outs_by_kind[2]
    block_out = jnp.concatenate(outs_by_kind[0], 0)
    stats_two = jnp.concatenate(outs_by_kind[7], 0)
    grad_fc1_bias = sum(outs_by_kind[8])[0, 0]
    gate_one, gate_two = mod[:, 2], mod[:, 5]
    grad_fc2_bias = jnp.sum(gate_two * stats_two[:, 4], 0)
    grad_proj_bias = jnp.sum(gate_one * stats_two[:, 5], 0)
    bias_sums = sum(bias_sums).reshape(3, local)
    grad_qv_bias = jnp.stack([bias_sums[0], bias_sums[2]])
    if direct:
        bias_rows = jnp.stack(
            [
                grad_fc1_bias,
                grad_fc2_bias,
                grad_proj_bias,
                jnp.pad(grad_qv_bias.reshape(-1), (0, dim - 2 * local)),
            ]
        ).astype(BF)
        dh1_i, sums = tail_sums(dh1_i, bias_rows, heads, h1, (h2, du, z, dm, dqkv, da))
        dh1.append(dh1_i)
        grad_fc1, grad_fc2 = sums[:dim], sums[dim : 2 * dim]
        grad_qkv = sums[2 * dim : 2 * dim + 3 * local]
        grad_proj = sums[2 * dim + 3 * local : 3 * dim]
        bias_rows = sums[3 * dim : 3 * dim + 4].astype(F32)
        grad_fc1_bias, grad_fc2_bias, grad_proj_bias = bias_rows[:3]
        grad_qv_bias = bias_rows[3, : 2 * local].reshape(2, local)
    else:
        flat = lambda parts: jnp.concatenate(parts, 0).reshape(lat * seq, -1)
        grad_fc2 = tn(flat(z), flat(dm))
        grad_fc1 = tn(flat(h2), flat(du))
        grad_qkv = sum(mm(dqkv[i][0], h1[i]) for i in range(lat))
        grad_proj = sum(mm(heads_own[i], da[i][0]) for i in range(lat))
        grads = [grad.astype(BF) for grad in (grad_fc1, grad_fc2, grad_qkv, grad_proj)]
        grad_fc1, grad_fc2, grad_qkv, grad_proj = lax.psum(grads, "dp")
        biases = lax.psum((grad_fc1_bias, grad_fc2_bias, grad_proj_bias, grad_qv_bias), "dp")
        grad_fc1_bias, grad_fc2_bias, grad_proj_bias, grad_qv_bias = biases

    backs = [
        latents_back(dh1[i], results[i][1], latents, mod, i, rows) for i in range(lat)
    ]
    latents_grad = jnp.concatenate([grad for grad, _ in backs], 0)
    stats_one = jnp.concatenate([stats for _, stats in backs], 0)

    dmod = jnp.stack(
        [
            stats_one[:, 0],
            stats_one[:, 1],
            stats_two[:, 0],
            stats_two[:, 1],
            stats_two[:, 2],
            stats_two[:, 3],
        ],
        1,
    )
    dmod = dmod.reshape(lat, 6 * dim).astype(BF)
    dmod_own = lax.dynamic_slice_in_dim(dmod, mp_at * cols, cols, 1)
    both = jnp.concatenate([cond_low, dmod_own], 1)
    grad_act = nt(dmod_own, ada_weight)
    if direct:
        both = jnp.pad(both, ((0, 16 - lat), (0, 0)))
        grad_act = jnp.pad(grad_act, ((0, 8 - lat), (0, 0)))
        every, grad_act = rows_exchange(both, grad_act, n_dp, n_mp)
        every, grad_act = every.reshape(n_dp * 16, dim + cols), grad_act[:lat]
    else:
        every = lax.all_gather(both, "dp", axis=0, tiled=True)
        grad_act = lax.psum(grad_act, "mp")
    grad_ada = tn(every[:, :dim], every[:, dim:])
    grad_ada_bias = jnp.sum(every[:, dim:].astype(F32), 0)
    condition_grad = jax.vjp(jax.nn.silu, condition)[1](grad_act)[0]

    back = lambda v: v.astype(F32)
    return (
        block_out,
        latents_grad,
        condition_grad,
        back(grad_qkv).reshape(3, local, dim).transpose(2, 0, 1),
        grad_qv_bias,
        back(grad_proj),
        grad_proj_bias,
        back(grad_fc1),
        grad_fc1_bias,
        back(grad_fc2),
        grad_fc2_bias,
        grad_ada,
        grad_ada_bias,
    )


def solution(mesh):
    in_specs = (
        P("dp", None, None),
        P("dp", None),
        P("dp", None, None),
        P(None, None, "mp"),
        P(None, "mp"),
        P("mp", None),
        P(),
        P(None, "mp"),
        P("mp"),
        P("mp", None),
        P(),
        P(None, "mp"),
        P("mp"),
    )
    out_specs = (
        P("dp", None, None),
        P("dp", None, None),
        P("dp", None),
        P(None, None, "mp"),
        P(None, "mp"),
        P("mp", None),
        P(),
        P(None, "mp"),
        P("mp"),
        P("mp", None),
        P(),
        P(None, "mp"),
        P("mp"),
    )
    body = functools.partial(per_device, mesh.shape["dp"], mesh.shape["mp"])
    return jax.shard_map(body, mesh=mesh, in_specs=in_specs, out_specs=out_specs, check_vma=False)
```

```python
import functools

import jax
import jax.numpy as jnp
from jax import lax
from jax.experimental import pallas as pl
from jax.experimental.pallas import tpu as pltpu
from jax.sharding import PartitionSpec as P

HEAD_DIM = 72
EPS = 1e-06
LOG2E = 1.4426950408889634
GELU_A = 0.7978845608028654
GELU_B = 0.044715
BF = jnp.bfloat16
F32 = jnp.float32
MIB = 2**20


def mm(a, b):
    return jnp.dot(a, b, preferred_element_type=F32)


def nt(a, b):
    return lax.dot_general(a, b, (((1,), (1,)), ((), ())), preferred_element_type=F32)


def tn(a, b):
    return lax.dot_general(a, b, (((0,), (0,)), ((), ())), preferred_element_type=F32)


def norm_stats(values):
    centered = values - jnp.mean(values, -1, keepdims=True)
    inv_std = lax.rsqrt(jnp.mean(centered * centered, -1, keepdims=True) + EPS)
    return centered * inv_std, inv_std


def norm_back(normed, inv_std, grad_normed):
    first = jnp.mean(grad_normed, -1, keepdims=True)
    second = jnp.mean(grad_normed * normed, -1, keepdims=True)
    return inv_std * (grad_normed - first - normed * second)


def flip(value, bit):
    step = 1 << bit
    return value + step - 2 * step * (value // step % 2)


def near_part(me, k):
    side = me // 2
    end = jnp.minimum(me, 3 - me)
    at = k + end * (1 - 2 * k) * ((3 - k) // 2)
    return at + side * (3 - 2 * at)


def line_peers(me, n):
    return jnp.minimum(me, 1) + jnp.minimum(n - 1 - me, 1)


def at_mesh(dp_at, mp_at):
    return {"device_id": (dp_at, mp_at), "device_id_type": pl.DeviceIdType.MESH}


def modulation_kernel(cond_ref, w_ref, bias_ref, row_ref, out_ref, low_ref, send, recv):
    dp_at, me = lax.axis_index("dp"), lax.axis_index("mp")
    n_mp = out_ref.shape[0]
    lat = cond_ref.shape[0]
    barrier = pltpu.get_barrier_semaphore()
    for k in range(1, n_mp):
        pl.semaphore_signal(barrier, inc=1, **at_mesh(dp_at, (me + k) % n_mp))
    cond = cond_ref[...]
    low = (cond * jax.nn.sigmoid(cond)).astype(BF)
    low_ref[...] = low
    part = nt(low, w_ref[...]) + bias_ref[...]
    cols = part.shape[1]
    out_ref[me] = jnp.concatenate([part, row_ref[...], jnp.zeros((8 - lat - 1, cols), F32)], 0)
    pl.semaphore_wait(barrier, n_mp - 1)
    copies = []
    for k in range(1, n_mp):
        copies.append(
            pltpu.make_async_remote_copy(
                out_ref.at[me],
                out_ref.at[me],
                send.at[k - 1],
                recv.at[k - 1],
                **at_mesh(dp_at, (me + k) % n_mp),
            )
        )
        copies[-1].start()
    for k in range(1, n_mp):
        came = out_ref.at[(me + n_mp - k) % n_mp]
        pltpu.make_async_remote_copy(
            came, came, send.at[k - 1], recv.at[k - 1], **at_mesh(dp_at, (me + k) % n_mp)
        ).wait_recv()
    for copy in copies:
        copy.wait_send()


def modulation_all(condition, ada_rows, ada_bias, bias_row, n_mp):
    cols = ada_rows.shape[0]
    vmem = pl.BlockSpec(memory_space=pltpu.VMEM)
    return pl.pallas_call(
        modulation_kernel,
        in_specs=[vmem] * 4,
        out_specs=[vmem, vmem],
        out_shape=[
            jax.ShapeDtypeStruct((n_mp, 8, cols), F32),
            jax.ShapeDtypeStruct(condition.shape, BF),
        ],
        scratch_shapes=[pltpu.SemaphoreType.DMA((n_mp - 1,))] * 2,
        compiler_params=pltpu.CompilerParams(
            collective_id=0, has_side_effects=True, vmem_limit_bytes=40 * MIB
        ),
        name="modulation",
    )(condition, ada_rows, ada_bias, bias_row)


def attend(flat, n_heads, slot, heads_ref, qkv_ref, lse_ref, between):
    seq = flat.shape[1]
    parts = flat.reshape(3 * n_heads, HEAD_DIM, seq)
    scaling = LOG2E / HEAD_DIM**0.5
    outs = []
    for h in range(n_heads):
        q_t = (parts[h] * scaling).astype(BF)
        k_t = parts[n_heads + h]
        v_t = parts[2 * n_heads + h]
        v_ext = jnp.concatenate([v_t, jnp.ones((8, seq), F32)], 0).astype(BF)
        scores = mm(k_t.T.astype(BF), q_t)
        top = jnp.max(scores, 0, keepdims=True)
        probs = jnp.exp2(scores - top).astype(BF)
        out = mm(v_ext, probs)
        total = out[HEAD_DIM : HEAD_DIM + 1]
        outs.append(out[:HEAD_DIM] * (1.0 / total))
        lse = top + jnp.log2(total)

        @pl.when(slot == 0)
        def _():
            qkv_ref[0, h] = q_t
            qkv_ref[0, n_heads + h] = k_t.astype(BF)
            qkv_ref[0, 2 * n_heads + h] = v_t.astype(BF)
            lse_ref[0, h : h + 1] = lse

        between(h + 1)
    heads_ref[0, 0] = jnp.concatenate(outs, 0).astype(BF)


def as_column(row):
    return jnp.broadcast_to(row, (8, row.shape[1])).T[:, :1]


def mixed_one(lat_ref, mod_ref, h1_ref, h1_all, lat):
    normed, _ = norm_stats(lat_ref[0].astype(F32))
    h1 = (normed * (1.0 + mod_ref[0, 1:2]) + mod_ref[0, 0:1]).astype(BF)
    h1_all[lat] = h1
    h1_ref[0] = h1


def attn_fwd_kernel(
    me_ref, lat_ref, mod_ref, w_ref, bias_ref, heads_ref, qkv_ref, lse_ref, h1_ref, h1_all
):
    slot, lat = pl.program_id(0), pl.program_id(1)

    @pl.when(slot == 0)
    def _():
        mixed_one(lat_ref, mod_ref, h1_ref, h1_all, lat)

    flat = nt(w_ref[0], h1_all[lat]) + as_column(bias_ref[0])
    attend(flat, qkv_ref.shape[1] // 3, slot, heads_ref, qkv_ref, lse_ref, lambda h: None)


def attn_gather_kernel(
    lat_ref,
    mod_ref,
    bias_ref,
    wq_ref,
    wp_ref,
    w1_ref,
    w2_ref,
    heads_ref,
    qkv_ref,
    lse_ref,
    h1_ref,
    all_ref,
    h1_all,
    w_buf,
    local_sem,
    z_own,
    z_on,
    z_got,
    sends,
    recvs,
):
    n_mp = all_ref.shape[0]
    lats = h1_all.shape[0]
    units, pace = 3 * (n_mp - 1), 4
    slot, lat = pl.program_id(0), pl.program_id(1)
    step = slot * lats + lat
    dp_at, me = lax.axis_index("dp"), lax.axis_index("mp")
    core, x, y = dp_at % 2, dp_at // 2 % 2, dp_at // 4
    rows = all_ref.shape[5]
    upper = wq_ref.shape[0] // rows
    cut = rows // 32 * 16 + 16
    near, far = pl.ds(0, cut), pl.ds(cut, rows - cut)
    every = pl.ds(0, rows)
    both = pl.ds(0, 2)
    core_id = at_mesh(flip(dp_at, 0), me)
    x_id = at_mesh(flip(dp_at, 1), me)
    y_id = at_mesh(flip(dp_at, 2), me)
    right_id, left_id = at_mesh(dp_at, me + 1), at_mesh(dp_at, me - 1)

    def piece(s, c, at_y, at_x, at_core, part):
        return all_ref.at[s, c, at_y, at_x, at_core, part]

    def own_copy(c, side, target, source=None):
        ref = piece(me, c, y, x, core, every)
        return pltpu.make_async_remote_copy(
            ref if source is None else source,
            ref,
            z_own.at[side, c],
            z_got.at[c, me],
            **target,
        )

    def pass_on(s, c, target):
        ref = piece(s, c, y, x, core, every)
        return pltpu.make_async_remote_copy(
            ref, ref, z_on.at[c, s], z_got.at[c, s], **target
        )

    def move(kind, c, s, arrived=False):
        flipped = lambda v: 1 - v if arrived else v
        at_y, at_x, at_core, part, target = (
            (pl.ds(y, 1), pl.ds(flipped(x), 1), pl.ds(core, 1), near, x_id),
            (pl.ds(flipped(y), 1), pl.ds(x, 1), pl.ds(core, 1), far, y_id),
            (pl.ds(flipped(y), 1), both, pl.ds(core, 1), near, y_id),
            (both, pl.ds(flipped(x), 1), pl.ds(core, 1), far, x_id),
            (both, both, pl.ds(flipped(core), 1), every, core_id),
        )[kind]
        ref = piece(s, c, at_y, at_x, at_core, part)
        return pltpu.make_async_remote_copy(
            ref, ref, sends.at[kind, c, s], recvs.at[kind, c, s], **target
        )

    def unit(u):
        return u // (n_mp - 1), near_part(me, 1 + u % (n_mp - 1))

    def event(stage, u):
        c, s = unit(u)

        @pl.when((u >= 0) & (u < units))
        def _():
            if stage == 0:

                @pl.when((me > 0) & (me < n_mp - 1))
                def _():
                    pass_on(s, c, right_id).wait_recv()
                    pl.when(s < me)(lambda: pass_on(s, c, right_id).start())
                    pl.when(s > me)(lambda: pass_on(s, c, left_id).start())

            if stage == 1:

                @pl.when((me == 0) | (me == n_mp - 1))
                def _():
                    pass_on(s, c, right_id).wait_recv()

                move(0, c, s).start()
                move(1, c, s).start()
            if stage == 2:
                move(0, c, s, True).wait_recv()
                move(1, c, s, True).wait_recv()
                move(2, c, s).start()
                move(3, c, s).start()
            if stage == 3:
                move(2, c, s, True).wait_recv()
                move(3, c, s, True).wait_recv()
                move(4, c, s).start()
            if stage == 4:
                move(4, c, s, True).wait_recv()

    def send_from(c, ref, at):
        source = ref.at[pl.ds(at * rows, rows)]

        @pl.when(me < n_mp - 1)
        def _():
            own_copy(c, 0, right_id, source).start()

        @pl.when(me > 0)
        def _():
            own_copy(c, 1, left_id, source).start()

    def send_own(c):
        if c > 0:
            send_from(c, (w1_ref, w2_ref)[c - 1], dp_at)
        else:
            pl.when(dp_at < upper)(lambda: send_from(0, wq_ref, dp_at))
            pl.when(dp_at >= upper)(lambda: send_from(0, wp_ref, dp_at - upper))

    @pl.when(step == 0)
    def _():
        barrier = pltpu.get_barrier_semaphore()
        for target in (core_id, x_id, y_id):
            pl.semaphore_signal(barrier, inc=1, **target)

        @pl.when(me < n_mp - 1)
        def _():
            pl.semaphore_signal(barrier, inc=1, **right_id)

        @pl.when(me > 0)
        def _():
            pl.semaphore_signal(barrier, inc=1, **left_id)

        pl.semaphore_wait(barrier, 3 + line_peers(me, n_mp))
        send_own(0)

    def next_weights(k):
        return pltpu.make_async_copy(all_ref.at[near_part(me, k), 0], w_buf, local_sem.at[0])

    def tick(t):
        def due(at, every):
            return jnp.where((t - at) % every == 0, (t - at) // every, -1)

        for k, at in ((0, 3), (1, 4), (2, 7)):
            nth = due(at, 3 * pace)
            event(0, jnp.where(nth < 0, -1, nth * 3 + k))
        for stage, at in ((1, 3), (3, 8), (2, 5), (4, 11)):
            event(stage, due(at, pace))
        for c in (1, 2):
            pl.when(t == 3 * pace * c - 3)(lambda: send_own(c))

    @pl.when((lat == 0) & (slot == 0))
    def _():
        def load(at):
            return pltpu.make_async_copy(
                wq_ref.at[pl.ds(at * rows, rows)],
                w_buf.at[at // 4, at // 2 % 2, at % 2],
                local_sem.at[at],
            )

        for at in range(upper):
            load(at).start()
        for at in range(upper):
            load(at).wait()

    @pl.when((lat == 0) & (slot > 0))
    def _():
        next_weights(slot).wait()

    @pl.when(slot == 0)
    def _():
        mixed_one(lat_ref, mod_ref, h1_ref, h1_all, lat)

    n_heads = qkv_ref.shape[1] // 3
    weights = w_buf[...].reshape(8 * rows, w_buf.shape[-1])[: 3 * n_heads * HEAD_DIM]
    flat = nt(weights, h1_all[lat]) + as_column(bias_ref[0])

    def between(h):
        tick(step * n_heads + h - 1)

        @pl.when((lat == lats - 1) & (slot < n_mp - 1) & (h == n_heads))
        def _():
            next_weights(slot + 1).start()

    attend(flat, n_heads, slot, heads_ref, qkv_ref, lse_ref, between)

    @pl.when(step == n_mp * lats - 1)
    def _():
        def rest(t, carry):
            tick(t)
            return carry

        lax.fori_loop(n_mp * lats * n_heads, pace * units + 11, rest, 0)
        for c in range(3):

            @pl.when(me < n_mp - 1)
            def _():
                own_copy(c, 0, right_id).wait_send()

            @pl.when(me > 0)
            def _():
                own_copy(c, 1, left_id).wait_send()

        def drain(u, carry):
            c, s = unit(u)

            @pl.when((me > 0) & (me < n_mp - 1))
            def _():
                pass_on(s, c, right_id).wait_send()

            for kind in range(5):
                move(kind, c, s).wait_send()
            return carry

        lax.fori_loop(0, units, drain, 0)


def attn_gather(latents, mod, bias, own, n_mp):
    lat, seq, dim = latents.shape
    local = dim // n_mp
    n_heads = local // HEAD_DIM
    rows = dim // 8
    last = lat - 1
    first = lambda s, l: s // n_mp * 0 + jnp.where(s == 0, l, last)
    part = lambda s: near_part(lax.axis_index("mp"), s)
    heads, qkv, lse, h1, gathered = pl.pallas_call(
        attn_gather_kernel,
        grid=(n_mp, lat),
        in_specs=[
            pl.BlockSpec((1, seq, dim), lambda s, l: (first(s, l), 0, 0)),
            pl.BlockSpec((1, 6, dim), lambda s, l: (l, 0, 0)),
            pl.BlockSpec((1, 1, 3 * local), lambda s, l: (part(s), 0, 0)),
        ]
        + [pl.BlockSpec(memory_space=pl.ANY)] * 4,
        out_specs=[
            pl.BlockSpec((1, 1, local, seq), lambda s, l: (part(s), l, 0, 0)),
            pl.BlockSpec((1, 3 * n_heads, HEAD_DIM, seq), lambda s, l: (first(s, l), 0, 0, 0)),
            pl.BlockSpec((1, n_heads, seq), lambda s, l: (first(s, l), 0, 0)),
            pl.BlockSpec((1, seq, dim), lambda s, l: (first(s, l), 0, 0)),
            pl.BlockSpec(memory_space=pl.ANY),
        ],
        out_shape=[
            jax.ShapeDtypeStruct((n_mp, lat, local, seq), BF),
            jax.ShapeDtypeStruct((lat, 3 * n_heads, HEAD_DIM, seq), BF),
            jax.ShapeDtypeStruct((lat, n_heads, seq), F32),
            jax.ShapeDtypeStruct((lat, seq, dim), BF),
            jax.ShapeDtypeStruct((n_mp, 3, 2, 2, 2, rows, dim), BF),
        ],
        scratch_shapes=[
            pltpu.VMEM((lat, seq, dim), BF),
            pltpu.VMEM((2, 2, 2, rows, dim), BF),
            pltpu.SemaphoreType.DMA((8,)),
            pltpu.SemaphoreType.DMA((2, 3)),
            pltpu.SemaphoreType.DMA((3, n_mp)),
            pltpu.SemaphoreType.DMA((3, n_mp)),
            pltpu.SemaphoreType.DMA((5, 3, n_mp)),
            pltpu.SemaphoreType.DMA((5, 3, n_mp)),
        ],
        compiler_params=pltpu.CompilerParams(
            collective_id=1, has_side_effects=True, vmem_limit_bytes=60 * MIB
        ),
        name="attn_gather",
    )(latents, mod, bias, *own)
    return heads, qkv, lse, h1, gathered.reshape(n_mp, 3, dim, dim)


def attn_fwd(me, latents, mod, gathered, bias, n_mp):
    lat, seq, dim = latents.shape
    local = dim // n_mp
    n_heads = local // HEAD_DIM
    last = lat - 1
    first = lambda s, l: jnp.where(s == 0, l, last)
    return pl.pallas_call(
        attn_fwd_kernel,
        grid_spec=pltpu.PrefetchScalarGridSpec(
            num_scalar_prefetch=1,
            grid=(n_mp, lat),
            in_specs=[
                pl.BlockSpec((1, seq, dim), lambda s, l, me: (first(s, l), 0, 0)),
                pl.BlockSpec((1, 6, dim), lambda s, l, me: (l, 0, 0)),
                pl.BlockSpec(
                    (1, 3 * local, dim), lambda s, l, me: (lax.rem(me[0] + s, n_mp), 0, 0)
                ),
                pl.BlockSpec((1, 1, 3 * local), lambda s, l, me: (lax.rem(me[0] + s, n_mp), 0, 0)),
            ],
            out_specs=[
                pl.BlockSpec(
                    (1, 1, local, seq), lambda s, l, me: (lax.rem(me[0] + s, n_mp), l, 0, 0)
                ),
                pl.BlockSpec(
                    (1, 3 * n_heads, HEAD_DIM, seq), lambda s, l, me: (first(s, l), 0, 0, 0)
                ),
                pl.BlockSpec((1, n_heads, seq), lambda s, l, me: (first(s, l), 0, 0)),
                pl.BlockSpec((1, seq, dim), lambda s, l, me: (first(s, l), 0, 0)),
            ],
            scratch_shapes=[pltpu.VMEM((lat, seq, dim), BF)],
        ),
        out_shape=[
            jax.ShapeDtypeStruct((n_mp, lat, local, seq), BF),
            jax.ShapeDtypeStruct((lat, 3 * n_heads, HEAD_DIM, seq), BF),
            jax.ShapeDtypeStruct((lat, n_heads, seq), F32),
            jax.ShapeDtypeStruct((lat, seq, dim), BF),
        ],
        compiler_params=pltpu.CompilerParams(vmem_limit_bytes=60 * MIB),
        name="attn_fwd",
    )(me, latents, mod, gathered, bias)


class LineSum:
    def __init__(self, own_ref, up, down, sems, out_ref):
        self.own, self.up, self.down, self.sems, self.out = own_ref, up, down, sems, out_ref
        self.count, self.rows = up.shape[0], up.shape[1]
        self.me = lax.axis_index("mp")
        self.n = lax.axis_size("mp")
        dp_at = lax.axis_index("dp")
        self.ends = (at_mesh(dp_at, self.me + 1), at_mesh(dp_at, self.me - 1))
        self.place = (self.me, self.n - 1 - self.me)

    def guarded(self, side, first, action):
        there = self.place[side] > 0 if first else self.place[side] < self.n - 1

        @pl.when(there)
        def _():
            action()

    def greet(self):
        sem = pltpu.get_barrier_semaphore()
        for side in (0, 1):
            self.guarded(side, False, lambda: pl.semaphore_signal(sem, inc=1, **self.ends[side]))

    def barrier(self):
        self.greet()
        pl.semaphore_wait(pltpu.get_barrier_semaphore(), line_peers(self.me, self.n))

    def copy(self, side, c):
        ref = (self.up, self.down)[side].at[c]
        return pltpu.make_async_remote_copy(
            ref, ref, self.sems.at[2 * side, c], self.sems.at[2 * side + 1, c], **self.ends[side]
        )

    def handle(self, side, c):
        ref = (self.up, self.down)[side]
        own = self.own[0, pl.ds(pl.multiple_of(c * self.rows, self.rows), self.rows)]

        @pl.when(self.place[side] == 0)
        def _():
            ref[c] = own

        @pl.when(self.place[side] > 0)
        def _():
            self.copy(side, c).wait_recv()
            ref[c] = (ref[c].astype(F32) + own.astype(F32)).astype(BF)

        self.guarded(side, False, lambda: self.copy(side, c).start())

    def tick(self, t):
        for side in (0, 1):
            at = t - 2 * self.place[side]

            @pl.when((at >= 0) & (at % 3 < 2) & (at - at // 3 < self.count))
            def _():
                self.handle(side, at - at // 3)

    def finish(self, ticks):
        for side in (0, 1):
            done = jnp.maximum(ticks - 2 * self.place[side], 0)
            done = jnp.minimum(done - done // 3, self.count)

            def late(c, carry):
                self.handle(side, c)
                return carry

            lax.fori_loop(done, self.count, late, 0)

        def add(c, carry):
            rows = pl.ds(pl.multiple_of(c * self.rows, self.rows), self.rows)
            total = self.up[c].astype(F32) + self.down[c].astype(F32)
            self.out[0, rows] = (total - self.own[0, rows].astype(F32)).astype(BF)
            return carry

        lax.fori_loop(0, self.count, add, 0)
        for side in (0, 1):

            def sent(c, carry):
                self.copy(side, c).wait_send()
                return carry

            self.guarded(side, False, lambda: lax.fori_loop(0, self.count, sent, 0))


def mlp_kernel(*refs, summing):
    heads_ref, lat_ref, cot_ref, mod_ref, bp_ref, b1_ref, b2_ref = refs[:7]
    own_refs, (wq_all, w1_all, w2_all), refs = refs[7:10], refs[10:13], refs[13:]
    if summing:
        part_ref, refs = refs[0], refs[1:]
    out_ref, dx1_ref, da_ref, h2_ref, dm_ref, z_ref, du_ref, stats_ref, dusum_ref = refs[:9]
    refs = refs[9:]
    if summing:
        sum_ref, refs = refs[0], refs[1:]
    macc, dacc, wp, w1, w2, load_sems = refs[:6]
    n_mp, hid, dim = w2.shape
    local = wp.shape[1]
    rows = lat_ref.shape[1]
    me = lax.axis_index("mp")
    step = pl.program_id(0)
    line = LineSum(part_ref, refs[6], refs[7], refs[8], sum_ref) if summing else None

    def load(kind, k):
        slot = (me + k) % n_mp
        source = own_refs[kind]
        if k > 0:
            stack = (wq_all, w1_all, w2_all)[kind]
            source = stack.at[slot, kind] if len(stack.shape) == 4 else stack.at[slot]
        if k > 0 and kind == 0:
            source = source.at[pl.ds(3 * local, local)]
        ref = (wp.at[slot], w1.at[k], w2.at[k])[kind]
        return pltpu.make_async_copy(source, ref, load_sems.at[kind, k])

    @pl.when(step == 0)
    def _():
        if summing:
            line.barrier()
        for k in range(n_mp):
            load(0, k).start()
        for k in range(n_mp):
            load(1, k).start()
            load(2, k).start()
        for k in range(n_mp):
            load(0, k).wait()

    gate_one, shift_two = mod_ref[0, 2:3], mod_ref[0, 3:4]
    scale_two, gate_two = mod_ref[0, 4:5], mod_ref[0, 5:6]
    heads = heads_ref[:, 0].reshape(dim, rows)
    attn = tn(heads, wp[...].reshape(dim, dim)) + bp_ref[...]
    x1 = lat_ref[0].astype(F32) + gate_one * attn
    n2, inv2 = norm_stats(x1)
    h2 = (n2 * (1.0 + scale_two) + shift_two).astype(BF)
    h2_ref[0] = h2
    cot = cot_ref[0].astype(F32)
    dm = (gate_two * cot).astype(BF)
    dm_ref[0] = dm

    macc[...] = jnp.zeros_like(macc)
    dacc[...] = jnp.zeros_like(dacc)

    def part(k, own):
        if summing:
            line.tick(step * n_mp + k)

        @pl.when(step == 0)
        def _():
            for kind in (1, 2):
                ref = (w1, w2)[kind - 1].at[k]
                pltpu.make_async_copy(ref, ref, load_sems.at[kind, k]).wait()

        u = mm(h2_ref[0], w1[k]) + b1_ref[(me + k) % n_mp]
        dz = nt(dm_ref[0], w2[k])
        u2 = u * u
        t = jnp.tanh(u * (GELU_A + (GELU_A * GELU_B) * u2))
        half = 0.5 + 0.5 * t
        z = (u * half).astype(BF)
        slope = half + u * (1.0 - t * t) * (0.5 * GELU_A + (1.5 * GELU_A * GELU_B) * u2)
        du = dz * slope
        if own:
            before = jnp.where(step == 0, 0.0, dusum_ref[0])
            dusum_ref[0] = before + jnp.sum(du, 0, keepdims=True)
        du = du.astype(BF)
        if own:
            z_ref[0] = z
            du_ref[0] = du
        macc[...] += mm(z, w2[k])
        dacc[...] += nt(du, w1[k])

    part(0, True)

    for k in range(1, n_mp):
        part(k, False)
    mlp = macc[...] + b2_ref[...]
    out_ref[0] = (x1 + gate_two * mlp).astype(BF)
    dh2 = dacc[...]
    dx1 = cot + norm_back(n2, inv2, dh2 * (1.0 + scale_two))
    dx1_ref[0] = dx1.astype(BF)
    da_ref[0] = (gate_one * dx1).astype(BF)
    total = lambda v: jnp.sum(v, 0, keepdims=True)
    stats = jnp.concatenate(
        [
            total(dx1 * attn),
            total(dh2),
            total(dh2 * n2),
            total(cot * mlp),
            total(cot),
            total(dx1),
            jnp.zeros((2, dim), F32),
        ],
        0,
    )

    @pl.when(step == 0)
    def _():
        stats_ref[0] = stats

    @pl.when(step > 0)
    def _():
        stats_ref[0] += stats

    if summing:

        @pl.when(step == pl.num_programs(0) - 1)
        def _():
            line.finish(pl.num_programs(0) * n_mp)


LINE_CHUNKS = 8


def line_scratch(seq, dim):
    rows = seq // LINE_CHUNKS
    return [
        pltpu.VMEM((LINE_CHUNKS, rows, dim), BF),
        pltpu.VMEM((LINE_CHUNKS, rows, dim), BF),
        pltpu.SemaphoreType.DMA((4, LINE_CHUNKS)),
    ]


def mlp_both(index, heads, latents, cotangent, mod, biases, own, gathered, n_mp, rows, part):
    lat, seq, dim = latents.shape
    local = dim // n_mp
    hid = biases[1].shape[2]
    tok = pl.BlockSpec((1, rows, dim), lambda t: (index, t, 0))
    new = pl.BlockSpec((1, rows, dim), lambda t: (0, t, 0))
    hidden = pl.BlockSpec((1, rows, hid), lambda t: (0, t, 0))
    once = lambda shape: pl.BlockSpec(
        shape, lambda t: (0,) * len(shape), pipeline_mode=pl.Buffered(1)
    )
    any_spec = pl.BlockSpec(memory_space=pl.ANY)
    summing = part is not None
    extra = [once((1, seq, dim))] if summing else []
    return pl.pallas_call(
        functools.partial(mlp_kernel, summing=summing),
        grid=(seq // rows,),
        in_specs=[
            pl.BlockSpec((n_mp, 1, local, rows), lambda t: (0, index, 0, t)),
            tok,
            tok,
            pl.BlockSpec((1, 6, dim), lambda t: (index, 0, 0)),
            once((1, dim)),
            once((n_mp, 1, hid)),
            once((1, dim)),
        ]
        + [any_spec] * 6
        + extra,
        out_specs=[new] * 5
        + [
            hidden,
            hidden,
            pl.BlockSpec((1, 8, dim), lambda t: (0, 0, 0)),
            pl.BlockSpec((1, 1, hid), lambda t: (0, 0, 0)),
        ]
        + extra,
        out_shape=[jax.ShapeDtypeStruct((1, seq, dim), BF)] * 5
        + [jax.ShapeDtypeStruct((1, seq, hid), BF)] * 2
        + [jax.ShapeDtypeStruct((1, 8, dim), F32), jax.ShapeDtypeStruct((1, 1, hid), F32)]
        + ([jax.ShapeDtypeStruct((1, seq, dim), BF)] if summing else []),
        scratch_shapes=[
            pltpu.VMEM((rows, dim), F32),
            pltpu.VMEM((rows, dim), F32),
            pltpu.VMEM((n_mp, local, dim), BF),
            pltpu.VMEM((n_mp, dim, hid), BF),
            pltpu.VMEM((n_mp, hid, dim), BF),
            pltpu.SemaphoreType.DMA((3, n_mp)),
        ]
        + (line_scratch(seq, dim) if summing else []),
        compiler_params=pltpu.CompilerParams(
            vmem_limit_bytes=63 * MIB,
            **(dict(collective_id=4 + index, has_side_effects=True) if summing else {}),
        ),
        name="mlp_sum" if summing else "mlp_both",
    )(
        heads,
        latents,
        cotangent,
        mod,
        *biases,
        *own,
        *gathered,
        *([part] if summing else []),
    )


class CubeSum:
    def __init__(self, terms, full, halves, firsts, seconds, sems):
        self.terms, self.full = terms, full
        self.halves, self.firsts, self.seconds, self.sems = halves, firsts, seconds, sems
        self.units = halves.shape[0]
        dp_at, me = lax.axis_index("dp"), lax.axis_index("mp")
        self.core, x, y = dp_at % 2, dp_at // 2 % 2, dp_at // 4
        self.core_id = at_mesh(flip(dp_at, 0), me)
        x_id, y_id = at_mesh(flip(dp_at, 1), me), at_mesh(flip(dp_at, 2), me)
        self.ids = ((x_id, y_id), (y_id, x_id))
        self.place = ((x, y), (y, x))

    def barrier(self):
        sem = pltpu.get_barrier_semaphore()
        for target in (self.core_id,) + self.ids[0]:
            pl.semaphore_signal(sem, inc=1, **target)

    def blocks(self, u, core, q=None, first=None, second=None):
        at, count = 16 * u + 8 * core, 8
        if q is not None:
            at, count = at + 4 * q, 4
        if first is not None:
            at, count = at + 2 * first, 2
        if second is not None:
            at, count = at + second, 1
        return pl.ds(at, count)

    def send(self, stage, u, q, arrived=False):
        core, blocks = self.core, self.blocks
        first, second = self.place[q]
        other = lambda v: 1 - v if arrived else v
        if stage == 0:
            pair = (self.terms.at[blocks(u, 1 - core)], self.halves.at[u])
        elif stage == 1:
            pair = (self.terms.at[blocks(u, core, q, 1 - first)], self.firsts.at[u, q])
        elif stage == 2:
            pair = (self.terms.at[blocks(u, core, q, first, 1 - second)], self.seconds.at[u, q])
        elif stage == 3:
            pair = (self.full.at[blocks(u, core, q, first, other(second))],) * 2
        elif stage == 4:
            pair = (self.full.at[blocks(u, core, q, other(first))],) * 2
        else:
            pair = (self.full.at[blocks(u, other(core))],) * 2
        near, far = self.ids[q]
        target = (self.core_id, near, far, far, near, self.core_id)[stage]
        return pltpu.make_async_remote_copy(
            *pair, self.sems.at[0, stage, q, u], self.sems.at[1, stage, q, u], **target
        )

    def quarters(self, stage):
        return (0,) if stage in (0, 5) else (0, 1)

    def event(self, stage, u):
        terms, core, blocks = self.terms, self.core, self.blocks

        @pl.when((u >= 0) & (u < self.units))
        def _():
            if stage > 0:
                for q in self.quarters(stage - 1):
                    self.send(stage - 1, u, q, True).wait_recv()
            if stage == 1:
                at = blocks(u, core)
                terms[at] = (terms[at].astype(F32) + self.halves[u].astype(F32)).astype(BF)
            for q in (0, 1):
                first, second = self.place[q]
                if stage == 2:
                    at = blocks(u, core, q, first)
                    terms[at] = (terms[at].astype(F32) + self.firsts[u, q].astype(F32)).astype(BF)
                if stage == 3:
                    at = blocks(u, core, q, first, second)
                    total = terms[at].astype(F32) + self.seconds[u, q].astype(F32)
                    self.full[at] = total.astype(BF)
            if stage < 6:
                for q in self.quarters(stage):
                    self.send(stage, u, q).start()

    def finish(self):
        def sent(u, carry):
            for stage in range(6):
                for q in self.quarters(stage):
                    self.send(stage, u, q).wait_send()
            return carry

        lax.fori_loop(0, self.units, sent, 0)


BLOCK = 32


class WeightGrads:
    def __init__(self, operands, terms, right, left_cols, left_rows, right_sems, left_sems):
        self.operands, self.terms, self.right = operands, terms, right
        self.left_cols, self.left_rows = left_cols, left_rows
        self.right_sems, self.left_sems = right_sems, left_sems
        self.lats = right.shape[1]
        dim = right.shape[3]
        qkv_blocks = operands[2][0][0].shape[0] // BLOCK
        half = (qkv_blocks + 1) // 2 * BLOCK
        third = dim // 3
        self.pieces = [(job, i * third, third) for job in (0, 1) for i in range(3)]
        self.pieces += [(2, 0, half), (2, half, qkv_blocks * BLOCK - half)]
        self.pieces += [(3, 0, operands[3][0][0].shape[0])]

    def right_copies(self, job):
        slot = job % 2
        return [
            pltpu.make_async_copy(
                self.operands[job][1][i], self.right.at[slot, i], self.right_sems.at[slot, i]
            )
            for i in range(self.lats)
        ]

    def left_copies(self, at):
        job, first, count = self.pieces[at]
        copies = []
        for i in range(self.lats):
            source = self.operands[job][0][i]
            if job < 2:
                source = source.at[:, pl.ds(first, count)]
                ref = self.left_cols.at[at % 2, i]
            else:
                source = source.at[pl.ds(first, count)]
                ref = self.left_rows.at[at % 2, i, pl.ds(0, count)]
            copies.append(pltpu.make_async_copy(source, ref, self.left_sems.at[at % 2, i]))
        return copies

    def begin(self):
        for copy in self.right_copies(0) + self.left_copies(0):
            copy.start()

    def compute(self, at):
        job, _, count = self.pieces[at]
        opens = at == 0 or self.pieces[at - 1][0] != job
        if at + 1 < len(self.pieces):
            for copy in self.left_copies(at + 1):
                copy.start()
        if opens:
            if job + 1 < len(self.operands):
                for copy in self.right_copies(job + 1):
                    copy.start()
            for copy in self.right_copies(job):
                copy.wait()
        for copy in self.left_copies(at):
            copy.wait()
        slot, dim = job % 2, self.right.shape[3]
        if job < 2:
            left = self.left_cols[at % 2].reshape(-1, count)
            total = tn(left, self.right[slot].reshape(-1, dim))
        else:
            total = mm(self.left_rows[at % 2, 0, :count], self.right[slot, 0])
            for i in range(1, self.lats):
                total = total + mm(self.left_rows[at % 2, i, :count], self.right[slot, i])
        done = sum(rows for _, _, rows in self.pieces[:at]) // BLOCK
        self.terms[pl.ds(done, count // BLOCK)] = total.reshape(-1, BLOCK, dim).astype(BF)


def tail_kernel(*refs, lats):
    part_ref, bias_ref, heads_ref, h1_ref = refs[:4]
    lists = [refs[4 + i * lats : 4 + (i + 1) * lats] for i in range(6)]
    h2s, dus, zs, dms, dqkvs, das = [[ref.at[0] for ref in group] for group in lists]
    sum_ref, full_ref = refs[4 + 6 * lats : 6 + 6 * lats]
    refs = refs[6 + 6 * lats :]
    up, down, line_sems, terms, full, halves, firsts, seconds, cube_sems = refs[:9]
    right, left_cols, left_rows, right_sems, left_sems, local_sem = refs[9:]
    line = LineSum(part_ref, up, down, line_sems, sum_ref)
    cube = CubeSum(terms, full, halves, firsts, seconds, cube_sems)
    heads = [heads_ref.at[line.me, i] for i in range(lats)]
    h1s = [h1_ref.at[i] for i in range(lats)]
    grads = WeightGrads(
        ((h2s, dus), (zs, dms), (dqkvs, h1s), (heads, das)),
        terms,
        right,
        left_cols,
        left_rows,
        right_sems,
        left_sems,
    )
    grads.begin()
    cube.barrier()
    line.greet()
    pl.semaphore_wait(pltpu.get_barrier_semaphore(), 3 + line_peers(line.me, line.n))
    spare = bias_ref.shape[0]
    terms[pl.ds(terms.shape[0] - spare, spare)] = bias_ref[...]
    line.tick(0)
    unit_rows = 16 * BLOCK
    ready = 0
    for t in range(cube.units):
        line.tick(2 * t + 1)
        while ready < len(grads.pieces) and (
            sum(rows for _, _, rows in grads.pieces[:ready]) < (t + 1) * unit_rows
        ):
            grads.compute(ready)
            ready += 1
        line.tick(2 * t + 2)
        for stage in range(min(t, 6), -1, -1):
            cube.event(stage, t - stage)

    def advance(t, carry):
        line.tick(2 * t + 1)
        for stage in range(6, 0, -1):
            cube.event(stage, t - stage)
        line.tick(2 * t + 2)
        return carry

    lax.fori_loop(cube.units, cube.units + 6, advance, 0)
    store = pltpu.make_async_copy(full, full_ref, local_sem.at[0])
    store.start()
    line.finish(2 * (cube.units + 6) + 1)
    cube.finish()
    store.wait()


def tail_sums(part, biases, heads, h1, lists):
    n_mp, lats, local, seq = heads.shape
    dim = h1.shape[2]
    rows = 2 * dim + 4 * local
    units = -(-(rows + BLOCK) // (16 * BLOCK))
    spare = units * 16 - rows // BLOCK
    biases = jnp.pad(biases, ((0, spare * BLOCK - biases.shape[0]), (0, 0)))
    vmem = pl.BlockSpec(memory_space=pltpu.VMEM)
    any_spec = pl.BlockSpec(memory_space=pl.ANY)
    shape = (units * 16, BLOCK, dim)
    flat = [array for group in lists for array in group]
    total, full = pl.pallas_call(
        functools.partial(tail_kernel, lats=lats),
        in_specs=[vmem, vmem] + [any_spec] * (2 + len(flat)),
        out_specs=[vmem, any_spec],
        out_shape=[jax.ShapeDtypeStruct(part.shape, BF), jax.ShapeDtypeStruct(shape, BF)],
        scratch_shapes=line_scratch(seq, dim)
        + [
            pltpu.VMEM(shape, BF),
            pltpu.VMEM(shape, BF),
            pltpu.VMEM((units, 8, BLOCK, dim), BF),
            pltpu.VMEM((units, 2, 2, BLOCK, dim), BF),
            pltpu.VMEM((units, 2, 1, BLOCK, dim), BF),
            pltpu.SemaphoreType.DMA((2, 6, 2, units)),
            pltpu.VMEM((2, lats, seq, dim), BF),
            pltpu.VMEM((2, lats, seq, dim // 3), BF),
            pltpu.VMEM((2, lats, (3 * local // BLOCK + 1) // 2 * BLOCK, seq), BF),
            pltpu.SemaphoreType.DMA((2, lats)),
            pltpu.SemaphoreType.DMA((2, lats)),
            pltpu.SemaphoreType.DMA((1,)),
        ],
        compiler_params=pltpu.CompilerParams(
            collective_id=2, has_side_effects=True, vmem_limit_bytes=63 * MIB
        ),
        name="tail_sums",
    )(part, biases.reshape(spare, BLOCK, dim), heads, h1, *flat)
    return total, full.reshape(units * 16 * BLOCK, dim)


def rows_kernel(rows_ref, act_ref, every_ref, total_ref, acts, sems):
    dp_at, me = lax.axis_index("dp"), lax.axis_index("mp")
    n_dp, n_mp = every_ref.shape[0], acts.shape[0]
    barrier = pltpu.get_barrier_semaphore()
    for k in range(1, n_dp):
        pl.semaphore_signal(barrier, inc=1, **at_mesh((dp_at + k) % n_dp, me))
    for k in range(1, n_mp):
        pl.semaphore_signal(barrier, inc=1, **at_mesh(dp_at, (me + k) % n_mp))
    every_ref[dp_at] = rows_ref[...]
    acts[me] = act_ref[...]
    pl.semaphore_wait(barrier, n_dp + n_mp - 2)

    def copy(ref, k, target):
        return pltpu.make_async_remote_copy(ref, ref, sems.at[0, k], sems.at[1, k], **target)

    def act_copy(k, source):
        return copy(acts.at[source % n_mp], k - 1, at_mesh(dp_at, (me + k) % n_mp))

    def row_copy(k, source):
        target = at_mesh((dp_at + k) % n_dp, me)
        return copy(every_ref.at[source % n_dp], n_mp + k - 2, target)

    for k in range(1, n_mp):
        act_copy(k, me).start()
    for k in range(1, n_dp):
        row_copy(k, dp_at).start()
    for k in range(1, n_mp):
        act_copy(k, me + n_mp - k).wait_recv()
    total = acts[0]
    for i in range(1, n_mp):
        total = total + acts[i]
    total_ref[...] = total
    for k in range(1, n_dp):
        row_copy(k, dp_at + n_dp - k).wait_recv()
    for k in range(1, n_mp):
        act_copy(k, me).wait_send()
    for k in range(1, n_dp):
        row_copy(k, dp_at).wait_send()


def rows_exchange(rows, act, n_dp, n_mp):
    vmem = pl.BlockSpec(memory_space=pltpu.VMEM)
    return pl.pallas_call(
        rows_kernel,
        in_specs=[vmem, vmem],
        out_specs=[vmem, vmem],
        out_shape=[
            jax.ShapeDtypeStruct((n_dp,) + rows.shape, rows.dtype),
            jax.ShapeDtypeStruct(act.shape, act.dtype),
        ],
        scratch_shapes=[
            pltpu.VMEM((n_mp,) + act.shape, act.dtype),
            pltpu.SemaphoreType.DMA((2, n_dp + n_mp - 2)),
        ],
        compiler_params=pltpu.CompilerParams(
            collective_id=3, has_side_effects=True, vmem_limit_bytes=40 * MIB
        ),
        name="rows_exchange",
    )(rows, act)


def attn_bwd_kernel(da_ref, heads_ref, qkv_ref, lse_ref, wp_ref, wq_ref, dqkv_ref, dh1_ref, bias_ref, *, rows):
    n_heads = lse_ref.shape[1]
    seq = da_ref.shape[1]
    dheads = nt(wp_ref[...], da_ref[0]).reshape(n_heads, HEAD_DIM, seq)
    heads = heads_ref[0, 0].astype(F32).reshape(n_heads, HEAD_DIM, seq)
    scaling = 1.0 / HEAD_DIM**0.5
    dq_list, dk_list, dv_list = [], [], []
    for h in range(n_heads):
        q_t = qkv_ref[0, h]
        k_t = qkv_ref[0, n_heads + h]
        v_t = qkv_ref[0, 2 * n_heads + h]
        q = q_t.astype(F32).T.astype(BF)
        k = k_t.astype(F32).T.astype(BF)
        v = v_t.astype(F32).T.astype(BF)
        do_t = dheads[h].astype(BF)
        do = dheads[h].T.astype(BF)
        inner = jnp.sum(do_t.astype(F32) * heads[h], 0, keepdims=True)
        dq_parts = []
        for i in range(seq // rows):
            cols = slice(i * rows, (i + 1) * rows)
            probs = jnp.exp2(mm(k, q_t[:, cols]) - lse_ref[0, h : h + 1, cols])
            dprobs = mm(v, do_t[:, cols])
            dscores = (probs * (dprobs - inner[:, cols])).astype(BF)
            dq_parts.append(mm(k_t, dscores))
            dv_new = mm(probs.astype(BF), do[cols])
            dk_new = mm(dscores, q[cols])
            dv = dv_new if i == 0 else dv + dv_new
            dk = dk_new if i == 0 else dk + dk_new
        dq_list.append(jnp.concatenate(dq_parts, 1) * scaling)
        dk_list.append(dk.T * (1.0 / LOG2E))
        dv_list.append(dv.T)
    dqkv = jnp.concatenate(dq_list + dk_list + dv_list, 0)
    bias_ref[0] = jnp.sum(dqkv, 1, keepdims=True)
    dqkv = dqkv.astype(BF)
    dqkv_ref[0] = dqkv
    dh1_ref[0] = tn(dqkv, wq_ref[...]).astype(BF)


def attn_bwd(da, heads, qkv, lse, wp, wq, index, rows):
    lat, seq, dim = da.shape
    n_heads = lse.shape[1]
    local = n_heads * HEAD_DIM
    one = lambda shape: pl.BlockSpec((1,) + shape, lambda i: (index,) + (0,) * len(shape))
    only = lambda shape: pl.BlockSpec((1,) + shape, lambda i: (0,) * (len(shape) + 1))
    whole = lambda shape: pl.BlockSpec(shape, lambda i: (0,) * len(shape))
    out = lambda shape: pl.BlockSpec((1,) + shape, lambda i: (0,) * (len(shape) + 1))
    return pl.pallas_call(
        functools.partial(attn_bwd_kernel, rows=rows),
        grid=(1,),
        in_specs=[
            only((seq, dim)),
            pl.BlockSpec((1, 1, local, seq), lambda i: (lax.axis_index("mp"), index, 0, 0)),
            one((3 * n_heads, HEAD_DIM, seq)),
            one((n_heads, seq)),
            whole((local, dim)),
            whole((3 * local, dim)),
        ],
        out_specs=[out((3 * local, seq)), out((seq, dim)), out((3 * local, 1))],
        out_shape=[
            jax.ShapeDtypeStruct((1, 3 * local, seq), BF),
            jax.ShapeDtypeStruct((1, seq, dim), BF),
            jax.ShapeDtypeStruct((1, 3 * local, 1), F32),
        ],
        compiler_params=pltpu.CompilerParams(vmem_limit_bytes=60 * MIB),
        name="attn_bwd",
    )(da, heads, qkv, lse, wp, wq)


def latents_kernel(dh1_ref, dx1_ref, lat_ref, mod_ref, *refs):
    grad_ref, stats_ref = refs[-2:]
    n1, inv1 = norm_stats(lat_ref[0].astype(F32))
    dh1 = dh1_ref[0].astype(F32)
    grad = dx1_ref[0].astype(F32) + norm_back(n1, inv1, dh1 * (1.0 + mod_ref[0, 1:2]))
    grad_ref[0] = grad.astype(BF)
    stats = jnp.concatenate(
        [
            jnp.sum(dh1, 0, keepdims=True),
            jnp.sum(dh1 * n1, 0, keepdims=True),
            jnp.zeros((6, dh1.shape[1]), F32),
        ],
        0,
    )

    @pl.when(pl.program_id(0) == 0)
    def _():
        stats_ref[0] = stats

    @pl.when(pl.program_id(0) > 0)
    def _():
        stats_ref[0] += stats


def latents_back(dh1, dx1, latents, mod, index, rows, before):
    lat, seq, dim = latents.shape
    tok = pl.BlockSpec((1, rows, dim), lambda t: (index, t, 0))
    new = pl.BlockSpec((1, rows, dim), lambda t: (0, t, 0))
    return pl.pallas_call(
        latents_kernel,
        grid=(seq // rows,),
        in_specs=[new, new, tok, pl.BlockSpec((1, 6, dim), lambda t: (index, 0, 0))]
        + [pl.BlockSpec(memory_space=pl.ANY)] * len(before),
        out_specs=[tok, pl.BlockSpec((1, 8, dim), lambda t: (0, 0, 0))],
        out_shape=[
            jax.ShapeDtypeStruct((lat, seq, dim), BF),
            jax.ShapeDtypeStruct((1, 8, dim), F32),
        ],
        input_output_aliases={4: 0} if before else {},
        compiler_params=pltpu.CompilerParams(vmem_limit_bytes=63 * MIB),
        name="latents_back",
    )(dh1, dx1, latents, mod, *before)


def per_device(
    n_dp,
    n_mp,
    latents,
    condition,
    cotangent,
    qkv_weight,
    qv_bias,
    proj_weight,
    proj_bias,
    fc1_weight,
    fc1_bias,
    fc2_weight,
    fc2_bias,
    ada_weight,
    ada_bias,
):
    lat, seq, dim = latents.shape
    local = qkv_weight.shape[2]
    n_heads = local // HEAD_DIM
    hid = fc1_weight.shape[1]
    cols = ada_weight.shape[1]
    mp_at = lax.axis_index("mp")
    dp_at = lax.axis_index("dp")
    me = jnp.full((1,), mp_at, jnp.int32)

    direct = n_mp == 4 and n_dp == 8
    bias_row = jnp.concatenate([qv_bias.reshape(-1), fc1_bias]).astype(F32)[None]
    ada_row = ada_bias.astype(F32)[None]
    if direct:
        small, cond_low = modulation_all(condition, ada_weight.T, ada_row, bias_row, n_mp)
    else:
        cond_low = jax.nn.silu(condition).astype(BF)
        mod_part = mm(cond_low, ada_weight) + ada_row
        small = lax.all_gather(jnp.concatenate([mod_part, bias_row], 0), "mp", axis=0)
    mod = small[:, :lat].transpose(1, 0, 2).reshape(lat, 6, dim)
    qv_all = small[:, lat, : 2 * local].reshape(n_mp, 2, local)
    b_qkv = jnp.stack([qv_all[:, 0], jnp.zeros((n_mp, local), F32), qv_all[:, 1]], 1).reshape(
        n_mp, 1, 3 * local
    )
    b_fc1 = small[:, lat, 2 * local :].reshape(n_mp, 1, hid)

    wq_own = (
        qkv_weight.reshape(dim, 3, n_heads, HEAD_DIM).transpose(1, 2, 3, 0).reshape(3 * local, dim)
    )
    if direct:
        own = (wq_own, proj_weight, fc1_weight, fc2_weight)
        heads, qkv, lse, h1, gathered = attn_gather(latents, mod, b_qkv, own, n_mp)
        gathered = (gathered,) * 3
    else:

        def gather(weight):
            share = weight.shape[0] // n_dp
            mine = lax.dynamic_slice_in_dim(weight, dp_at * share, share, 0)
            whole = lax.all_gather(mine, ("dp", "mp"), axis=0)
            whole = whole.reshape(n_dp, n_mp, share, weight.shape[1]).transpose(1, 0, 2, 3)
            return whole.reshape(n_mp, weight.shape[0], weight.shape[1])

        gathered = (
            gather(jnp.concatenate([wq_own, proj_weight], 0)),
            gather(fc1_weight),
            gather(fc2_weight),
        )
        heads, qkv, lse, h1 = attn_fwd(me, latents, mod, gathered[0], b_qkv, n_mp)
    rows = min(256, seq)
    results, dqkv, dh1, bias_sums = [], [], [], []
    for i in range(lat):
        waiting = dqkv and direct
        outs = mlp_both(
            i,
            heads,
            latents,
            cotangent,
            mod,
            (proj_bias.astype(F32)[None], b_fc1, fc2_bias.astype(F32)[None]),
            (proj_weight, fc1_weight, fc2_weight),
            gathered,
            n_mp,
            rows,
            dh1_i if waiting else None,
        )
        if waiting:
            dh1.append(outs[-1])
        results.append(outs[:9])
        dqkv_i, dh1_i, sums_i = attn_bwd(
            outs[2], heads, qkv, lse, proj_weight, wq_own, i, min(512, seq)
        )
        dqkv.append(dqkv_i)
        bias_sums.append(sums_i)
        if not direct:
            dh1.append(lax.psum(dh1_i, "mp"))
    outs_by_kind = list(zip(*results))
    h2, dm, z, du = outs_by_kind[3:7]
    da = outs_by_kind[2]
    block_out = jnp.concatenate(outs_by_kind[0], 0)
    stats_two = jnp.concatenate(outs_by_kind[7], 0)
    grad_fc1_bias = sum(outs_by_kind[8])[0, 0]
    gate_one, gate_two = mod[:, 2], mod[:, 5]
    grad_fc2_bias = jnp.sum(gate_two * stats_two[:, 4], 0)
    grad_proj_bias = jnp.sum(gate_one * stats_two[:, 5], 0)
    bias_sums = sum(bias_sums).reshape(3, local)
    grad_qv_bias = jnp.stack([bias_sums[0], bias_sums[2]])
    if direct:
        bias_rows = jnp.stack(
            [
                grad_fc1_bias,
                grad_fc2_bias,
                grad_proj_bias,
                jnp.pad(grad_qv_bias.reshape(-1), (0, dim - 2 * local)),
            ]
        ).astype(BF)
        dh1_i, sums = tail_sums(dh1_i, bias_rows, heads, h1, (h2, du, z, dm, dqkv, da))
        dh1.append(dh1_i)
        grad_fc1, grad_fc2 = sums[:dim], sums[dim : 2 * dim]
        grad_qkv = sums[2 * dim : 2 * dim + 3 * local]
        grad_proj = sums[2 * dim + 3 * local : 3 * dim]
        bias_rows = sums[3 * dim : 3 * dim + 4].astype(F32)
        grad_fc1_bias, grad_fc2_bias, grad_proj_bias = bias_rows[:3]
        grad_qv_bias = bias_rows[3, : 2 * local].reshape(2, local)
    else:
        flat = lambda parts: jnp.concatenate(parts, 0).reshape(lat * seq, -1)
        grad_fc2 = tn(flat(z), flat(dm))
        grad_fc1 = tn(flat(h2), flat(du))
        grad_qkv = sum(mm(dqkv[i][0], h1[i]) for i in range(lat))
        heads_own = lax.dynamic_index_in_dim(heads, mp_at, 0, keepdims=False)
        grad_proj = sum(mm(heads_own[i], da[i][0]) for i in range(lat))
        grads = [grad.astype(BF) for grad in (grad_fc1, grad_fc2, grad_qkv, grad_proj)]
        grad_fc1, grad_fc2, grad_qkv, grad_proj = lax.psum(grads, "dp")
        biases = lax.psum((grad_fc1_bias, grad_fc2_bias, grad_proj_bias, grad_qv_bias), "dp")
        grad_fc1_bias, grad_fc2_bias, grad_proj_bias, grad_qv_bias = biases

    before, stats_one = [], []
    for i in range(lat):
        latents_grad, stats = latents_back(dh1[i], results[i][1], latents, mod, i, rows, before)
        before = [latents_grad]
        stats_one.append(stats)
    stats_one = jnp.concatenate(stats_one, 0)

    dmod = jnp.stack(
        [
            stats_one[:, 0],
            stats_one[:, 1],
            stats_two[:, 0],
            stats_two[:, 1],
            stats_two[:, 2],
            stats_two[:, 3],
        ],
        1,
    )
    dmod = dmod.reshape(lat, 6 * dim).astype(BF)
    dmod_own = lax.dynamic_slice_in_dim(dmod, mp_at * cols, cols, 1)
    both = jnp.concatenate([cond_low, dmod_own], 1)
    grad_act = nt(dmod_own, ada_weight)
    if direct:
        both = jnp.pad(both, ((0, 16 - lat), (0, 0)))
        grad_act = jnp.pad(grad_act, ((0, 8 - lat), (0, 0)))
        every, grad_act = rows_exchange(both, grad_act, n_dp, n_mp)
        every, grad_act = every.reshape(n_dp * 16, dim + cols), grad_act[:lat]
    else:
        every = lax.all_gather(both, "dp", axis=0, tiled=True)
        grad_act = lax.psum(grad_act, "mp")
    grad_ada = tn(every[:, :dim], every[:, dim:])
    grad_ada_bias = jnp.sum(every[:, dim:].astype(F32), 0)
    condition_grad = jax.vjp(jax.nn.silu, condition)[1](grad_act)[0]

    back = lambda v: v.astype(F32)
    return (
        block_out,
        latents_grad,
        condition_grad,
        back(grad_qkv).reshape(3, local, dim).transpose(2, 0, 1),
        grad_qv_bias,
        back(grad_proj),
        grad_proj_bias,
        back(grad_fc1),
        grad_fc1_bias,
        back(grad_fc2),
        grad_fc2_bias,
        grad_ada,
        grad_ada_bias,
    )


def solution(mesh):
    in_specs = (
        P("dp", None, None),
        P("dp", None),
        P("dp", None, None),
        P(None, None, "mp"),
        P(None, "mp"),
        P("mp", None),
        P(),
        P(None, "mp"),
        P("mp"),
        P("mp", None),
        P(),
        P(None, "mp"),
        P("mp"),
    )
    out_specs = (
        P("dp", None, None),
        P("dp", None, None),
        P("dp", None),
        P(None, None, "mp"),
        P(None, "mp"),
        P("mp", None),
        P(),
        P(None, "mp"),
        P("mp"),
        P("mp", None),
        P(),
        P(None, "mp"),
        P("mp"),
    )
    body = functools.partial(per_device, mesh.shape["dp"], mesh.shape["mp"])
    return jax.shard_map(body, mesh=mesh, in_specs=in_specs, out_specs=out_specs, check_vma=False)
```

```python
import functools

import jax
import jax.numpy as jnp
from jax import lax
from jax.experimental import pallas as pl
from jax.experimental.pallas import tpu as pltpu
from jax.sharding import PartitionSpec as P

HEAD_DIM = 72
EPS = 1e-06
LOG2E = 1.4426950408889634
GELU_A = 0.7978845608028654
GELU_B = 0.044715
BF = jnp.bfloat16
F32 = jnp.float32
MIB = 2**20


def mm(a, b):
    return jnp.dot(a, b, preferred_element_type=F32)


def nt(a, b):
    return lax.dot_general(a, b, (((1,), (1,)), ((), ())), preferred_element_type=F32)


def tn(a, b):
    return lax.dot_general(a, b, (((0,), (0,)), ((), ())), preferred_element_type=F32)


def norm_stats(values):
    centered = values - jnp.mean(values, -1, keepdims=True)
    inv_std = lax.rsqrt(jnp.mean(centered * centered, -1, keepdims=True) + EPS)
    return centered * inv_std, inv_std


def norm_back(normed, inv_std, grad_normed):
    first = jnp.mean(grad_normed, -1, keepdims=True)
    second = jnp.mean(grad_normed * normed, -1, keepdims=True)
    return inv_std * (grad_normed - first - normed * second)


def flip(value, bit):
    step = 1 << bit
    return value + step - 2 * step * (value // step % 2)


def near_part(me, k):
    side = me // 2
    end = jnp.minimum(me, 3 - me)
    at = k + end * (1 - 2 * k) * ((3 - k) // 2)
    return at + side * (3 - 2 * at)


def line_peers(me, n):
    return jnp.minimum(me, 1) + jnp.minimum(n - 1 - me, 1)


def at_mesh(dp_at, mp_at):
    return {"device_id": (dp_at, mp_at), "device_id_type": pl.DeviceIdType.MESH}


def modulation_start(dp_at, me, n_mp, small, sems):
    def copy(k, arrived=False):
        at = small.at[(me + n_mp - k) % n_mp if arrived else me]
        target = at_mesh(dp_at, (me + k) % n_mp)
        return pltpu.make_async_remote_copy(at, at, sems.at[0, k - 1], sems.at[1, k - 1], **target)

    return copy


def attend(flat, n_heads, slot, heads_ref, qkv_ref, lse_ref, between):
    seq = flat.shape[1]
    parts = flat.reshape(3 * n_heads, HEAD_DIM, seq)
    scaling = LOG2E / HEAD_DIM**0.5
    outs = []
    for h in range(n_heads):
        q_t = (parts[h] * scaling).astype(BF)
        k_t = parts[n_heads + h]
        v_t = parts[2 * n_heads + h]
        v_ext = jnp.concatenate([v_t, jnp.ones((8, seq), F32)], 0).astype(BF)
        scores = mm(k_t.T.astype(BF), q_t)
        top = jnp.max(scores, 0, keepdims=True)
        probs = jnp.exp2(scores - top).astype(BF)
        out = mm(v_ext, probs)
        total = out[HEAD_DIM : HEAD_DIM + 1]
        outs.append(out[:HEAD_DIM] * (1.0 / total))
        lse = top + jnp.log2(total)

        @pl.when(slot == 0)
        def _():
            qkv_ref[0, h] = q_t
            qkv_ref[0, n_heads + h] = k_t.astype(BF)
            qkv_ref[0, 2 * n_heads + h] = v_t.astype(BF)
            lse_ref[0, h : h + 1] = lse

        between(h + 1)
    heads_ref[0, 0] = jnp.concatenate(outs, 0).astype(BF)


def as_column(row):
    return jnp.broadcast_to(row, (8, row.shape[1])).T[:, :1]


def mixed_one(lat_ref, shift, scale, h1_ref, h1_all, lat):
    normed, _ = norm_stats(lat_ref[0].astype(F32))
    h1 = (normed * (1.0 + scale) + shift).astype(BF)
    h1_all[lat] = h1
    h1_ref[0] = h1


def attn_fwd_kernel(
    me_ref, lat_ref, mod_ref, w_ref, bias_ref, heads_ref, qkv_ref, lse_ref, h1_ref, h1_all
):
    slot, lat = pl.program_id(0), pl.program_id(1)

    @pl.when(slot == 0)
    def _():
        mixed_one(lat_ref, mod_ref[0, 0:1], mod_ref[0, 1:2], h1_ref, h1_all, lat)

    flat = nt(w_ref[0], h1_all[lat]) + as_column(bias_ref[0])
    attend(flat, qkv_ref.shape[1] // 3, slot, heads_ref, qkv_ref, lse_ref, lambda h: None)


def attn_gather_kernel(
    lat_ref,
    cond_ref,
    rows_ref,
    ada_ref,
    wq_ref,
    wp_ref,
    w1_ref,
    w2_ref,
    heads_ref,
    qkv_ref,
    lse_ref,
    h1_ref,
    small_ref,
    low_ref,
    all_ref,
    h1_all,
    w_buf,
    ada_buf,
    small,
    local_sem,
    z_own,
    z_on,
    z_got,
    sends,
    recvs,
    small_sems,
):
    n_mp = all_ref.shape[0]
    lats = h1_all.shape[0]
    units, pace = 3 * (n_mp - 1), 4
    slot, lat = pl.program_id(0), pl.program_id(1)
    step = slot * lats + lat
    dp_at, me = lax.axis_index("dp"), lax.axis_index("mp")
    core, x, y = dp_at % 2, dp_at // 2 % 2, dp_at // 4
    rows = all_ref.shape[5]
    upper = wq_ref.shape[0] // rows
    cut = rows // 32 * 16 + 16
    near, far = pl.ds(0, cut), pl.ds(cut, rows - cut)
    every = pl.ds(0, rows)
    both = pl.ds(0, 2)
    core_id = at_mesh(flip(dp_at, 0), me)
    x_id = at_mesh(flip(dp_at, 1), me)
    y_id = at_mesh(flip(dp_at, 2), me)
    right_id, left_id = at_mesh(dp_at, me + 1), at_mesh(dp_at, me - 1)

    def piece(s, c, at_y, at_x, at_core, part):
        return all_ref.at[s, c, at_y, at_x, at_core, part]

    def own_copy(c, side, target, source=None):
        ref = piece(me, c, y, x, core, every)
        return pltpu.make_async_remote_copy(
            ref if source is None else source,
            ref,
            z_own.at[side, c],
            z_got.at[c, me],
            **target,
        )

    def pass_on(s, c, target):
        ref = piece(s, c, y, x, core, every)
        return pltpu.make_async_remote_copy(
            ref, ref, z_on.at[c, s], z_got.at[c, s], **target
        )

    def move(kind, c, s, arrived=False):
        flipped = lambda v: 1 - v if arrived else v
        at_y, at_x, at_core, part, target = (
            (pl.ds(y, 1), pl.ds(flipped(x), 1), pl.ds(core, 1), near, x_id),
            (pl.ds(flipped(y), 1), pl.ds(x, 1), pl.ds(core, 1), far, y_id),
            (pl.ds(flipped(y), 1), both, pl.ds(core, 1), near, y_id),
            (both, pl.ds(flipped(x), 1), pl.ds(core, 1), far, x_id),
            (both, both, pl.ds(flipped(core), 1), every, core_id),
        )[kind]
        ref = piece(s, c, at_y, at_x, at_core, part)
        return pltpu.make_async_remote_copy(
            ref, ref, sends.at[kind, c, s], recvs.at[kind, c, s], **target
        )

    def unit(u):
        return u // (n_mp - 1), near_part(me, 1 + u % (n_mp - 1))

    def event(stage, u):
        c, s = unit(u)

        @pl.when((u >= 0) & (u < units))
        def _():
            if stage == 0:

                @pl.when((me > 0) & (me < n_mp - 1))
                def _():
                    pass_on(s, c, right_id).wait_recv()
                    pl.when(s < me)(lambda: pass_on(s, c, right_id).start())
                    pl.when(s > me)(lambda: pass_on(s, c, left_id).start())

            if stage == 1:

                @pl.when((me == 0) | (me == n_mp - 1))
                def _():
                    pass_on(s, c, right_id).wait_recv()

                move(0, c, s).start()
                move(1, c, s).start()
            if stage == 2:
                move(0, c, s, True).wait_recv()
                move(1, c, s, True).wait_recv()
                move(2, c, s).start()
                move(3, c, s).start()
            if stage == 3:
                move(2, c, s, True).wait_recv()
                move(3, c, s, True).wait_recv()
                move(4, c, s).start()
            if stage == 4:
                move(4, c, s, True).wait_recv()

    def send_from(c, ref, at):
        source = ref.at[pl.ds(at * rows, rows)]

        @pl.when(me < n_mp - 1)
        def _():
            own_copy(c, 0, right_id, source).start()

        @pl.when(me > 0)
        def _():
            own_copy(c, 1, left_id, source).start()

    def send_own(c):
        if c > 0:
            send_from(c, (w1_ref, w2_ref)[c - 1], dp_at)
        else:
            pl.when(dp_at < upper)(lambda: send_from(0, wq_ref, dp_at))
            pl.when(dp_at >= upper)(lambda: send_from(0, wp_ref, dp_at - upper))

    small_copy = modulation_start(dp_at, me, n_mp, small, small_sems)
    ada_load = lambda: pltpu.make_async_copy(ada_ref, ada_buf, local_sem.at[8])

    @pl.when(step == 0)
    def _():
        barrier = pltpu.get_barrier_semaphore()
        for target in (core_id, x_id, y_id):
            pl.semaphore_signal(barrier, inc=1, **target)

        @pl.when(me < n_mp - 1)
        def _():
            pl.semaphore_signal(barrier, inc=1, **right_id)

        @pl.when(me > 0)
        def _():
            pl.semaphore_signal(barrier, inc=1, **left_id)

        for k in range(1, n_mp):
            pl.semaphore_signal(barrier, inc=1, **at_mesh(dp_at, (me + k) % n_mp))
        ada_load().start()
        pl.semaphore_wait(barrier, 3 + line_peers(me, n_mp) + n_mp - 1)
        send_own(0)
        cond = cond_ref[...]
        low = (cond * jax.nn.sigmoid(cond)).astype(BF)
        low_ref[...] = low
        ada_load().wait()
        part = nt(low, ada_buf[...]) + rows_ref[0:1]
        pad = jnp.zeros((8 - lats - 1, part.shape[1]), F32)
        small[me] = jnp.concatenate([part, rows_ref[1:2], pad], 0)
        for k in range(1, n_mp):
            small_copy(k).start()
        for k in range(1, n_mp):
            small_copy(k, True).wait_recv()
        small_ref[...] = small[...]

    def next_weights(k):
        return pltpu.make_async_copy(all_ref.at[near_part(me, k), 0], w_buf, local_sem.at[0])

    def tick(t):
        def due(at, every):
            return jnp.where((t - at) % every == 0, (t - at) // every, -1)

        for k, at in ((0, 3), (1, 4), (2, 7)):
            nth = due(at, 3 * pace)
            event(0, jnp.where(nth < 0, -1, nth * 3 + k))
        for stage, at in ((1, 3), (3, 8), (2, 5), (4, 11)):
            event(stage, due(at, pace))
        for c in (1, 2):
            pl.when(t == 3 * pace * c - 3)(lambda: send_own(c))

    @pl.when((lat == 0) & (slot == 0))
    def _():
        def load(at):
            return pltpu.make_async_copy(
                wq_ref.at[pl.ds(at * rows, rows)],
                w_buf.at[at // 4, at // 2 % 2, at % 2],
                local_sem.at[at],
            )

        for at in range(upper):
            load(at).start()
        for at in range(upper):
            load(at).wait()

    @pl.when((lat == 0) & (slot > 0))
    def _():
        next_weights(slot).wait()

    n_heads = qkv_ref.shape[1] // 3
    local = n_heads * HEAD_DIM

    @pl.when(slot == 0)
    def _():
        dim, cols = h1_all.shape[2], small.shape[2]
        shift = small[0, pl.ds(lat, 1), :dim]
        scale = jnp.concatenate(
            [small[0, pl.ds(lat, 1), dim:], small[1, pl.ds(lat, 1), : 2 * dim - cols]], 1
        )
        mixed_one(lat_ref, shift, scale, h1_ref, h1_all, lat)

    weights = w_buf[...].reshape(8 * rows, w_buf.shape[-1])[: 3 * local]
    biases = as_column(small[near_part(me, slot), lats : lats + 1, : 2 * local])
    bias = jnp.concatenate([biases[:local], jnp.zeros((local, 1), F32), biases[local:]], 0)
    flat = nt(weights, h1_all[lat]) + bias

    def between(h):
        tick(step * n_heads + h - 1)

        @pl.when((lat == lats - 1) & (slot < n_mp - 1) & (h == n_heads))
        def _():
            next_weights(slot + 1).start()

    attend(flat, n_heads, slot, heads_ref, qkv_ref, lse_ref, between)

    @pl.when(step == n_mp * lats - 1)
    def _():
        def rest(t, carry):
            tick(t)
            return carry

        lax.fori_loop(n_mp * lats * n_heads, pace * units + 11, rest, 0)
        for k in range(1, n_mp):
            small_copy(k).wait_send()
        for c in range(3):

            @pl.when(me < n_mp - 1)
            def _():
                own_copy(c, 0, right_id).wait_send()

            @pl.when(me > 0)
            def _():
                own_copy(c, 1, left_id).wait_send()

        def drain(u, carry):
            c, s = unit(u)

            @pl.when((me > 0) & (me < n_mp - 1))
            def _():
                pass_on(s, c, right_id).wait_send()

            for kind in range(5):
                move(kind, c, s).wait_send()
            return carry

        lax.fori_loop(0, units, drain, 0)


def attn_gather(latents, condition, small_rows, ada_rows, own, n_mp):
    lat, seq, dim = latents.shape
    local = dim // n_mp
    n_heads = local // HEAD_DIM
    rows = dim // 8
    cols = ada_rows.shape[0]
    last = lat - 1
    first = lambda s, l: jnp.where(s == 0, l, last)
    part = lambda s: near_part(lax.axis_index("mp"), s)
    whole = lambda shape: pl.BlockSpec(shape, lambda s, l: (0,) * len(shape))
    any_spec = pl.BlockSpec(memory_space=pl.ANY)
    heads, qkv, lse, h1, small, cond_low, gathered = pl.pallas_call(
        attn_gather_kernel,
        grid=(n_mp, lat),
        in_specs=[
            pl.BlockSpec((1, seq, dim), lambda s, l: (first(s, l), 0, 0)),
            whole(condition.shape),
            whole(small_rows.shape),
        ]
        + [any_spec] * 5,
        out_specs=[
            pl.BlockSpec((1, 1, local, seq), lambda s, l: (part(s), l, 0, 0)),
            pl.BlockSpec((1, 3 * n_heads, HEAD_DIM, seq), lambda s, l: (first(s, l), 0, 0, 0)),
            pl.BlockSpec((1, n_heads, seq), lambda s, l: (first(s, l), 0, 0)),
            pl.BlockSpec((1, seq, dim), lambda s, l: (first(s, l), 0, 0)),
            whole((n_mp, 8, cols)),
            whole(condition.shape),
            any_spec,
        ],
        out_shape=[
            jax.ShapeDtypeStruct((n_mp, lat, local, seq), BF),
            jax.ShapeDtypeStruct((lat, 3 * n_heads, HEAD_DIM, seq), BF),
            jax.ShapeDtypeStruct((lat, n_heads, seq), F32),
            jax.ShapeDtypeStruct((lat, seq, dim), BF),
            jax.ShapeDtypeStruct((n_mp, 8, cols), F32),
            jax.ShapeDtypeStruct(condition.shape, BF),
            jax.ShapeDtypeStruct((n_mp, 3, 2, 2, 2, rows, dim), BF),
        ],
        scratch_shapes=[
            pltpu.VMEM((lat, seq, dim), BF),
            pltpu.VMEM((2, 2, 2, rows, dim), BF),
            pltpu.VMEM(ada_rows.shape, BF),
            pltpu.VMEM((n_mp, 8, cols), F32),
            pltpu.SemaphoreType.DMA((9,)),
            pltpu.SemaphoreType.DMA((2, 3)),
            pltpu.SemaphoreType.DMA((3, n_mp)),
            pltpu.SemaphoreType.DMA((3, n_mp)),
            pltpu.SemaphoreType.DMA((5, 3, n_mp)),
            pltpu.SemaphoreType.DMA((5, 3, n_mp)),
            pltpu.SemaphoreType.DMA((2, n_mp - 1)),
        ],
        compiler_params=pltpu.CompilerParams(
            collective_id=1, has_side_effects=True, vmem_limit_bytes=62 * MIB
        ),
        name="attn_gather",
    )(latents, condition, small_rows, ada_rows, *own)
    return heads, qkv, lse, h1, small, cond_low, gathered.reshape(n_mp, 3, dim, dim)


def attn_fwd(me, latents, mod, gathered, bias, n_mp):
    lat, seq, dim = latents.shape
    local = dim // n_mp
    n_heads = local // HEAD_DIM
    last = lat - 1
    first = lambda s, l: jnp.where(s == 0, l, last)
    return pl.pallas_call(
        attn_fwd_kernel,
        grid_spec=pltpu.PrefetchScalarGridSpec(
            num_scalar_prefetch=1,
            grid=(n_mp, lat),
            in_specs=[
                pl.BlockSpec((1, seq, dim), lambda s, l, me: (first(s, l), 0, 0)),
                pl.BlockSpec((1, 6, dim), lambda s, l, me: (l, 0, 0)),
                pl.BlockSpec(
                    (1, 3 * local, dim), lambda s, l, me: (lax.rem(me[0] + s, n_mp), 0, 0)
                ),
                pl.BlockSpec((1, 1, 3 * local), lambda s, l, me: (lax.rem(me[0] + s, n_mp), 0, 0)),
            ],
            out_specs=[
                pl.BlockSpec(
                    (1, 1, local, seq), lambda s, l, me: (lax.rem(me[0] + s, n_mp), l, 0, 0)
                ),
                pl.BlockSpec(
                    (1, 3 * n_heads, HEAD_DIM, seq), lambda s, l, me: (first(s, l), 0, 0, 0)
                ),
                pl.BlockSpec((1, n_heads, seq), lambda s, l, me: (first(s, l), 0, 0)),
                pl.BlockSpec((1, seq, dim), lambda s, l, me: (first(s, l), 0, 0)),
            ],
            scratch_shapes=[pltpu.VMEM((lat, seq, dim), BF)],
        ),
        out_shape=[
            jax.ShapeDtypeStruct((n_mp, lat, local, seq), BF),
            jax.ShapeDtypeStruct((lat, 3 * n_heads, HEAD_DIM, seq), BF),
            jax.ShapeDtypeStruct((lat, n_heads, seq), F32),
            jax.ShapeDtypeStruct((lat, seq, dim), BF),
        ],
        compiler_params=pltpu.CompilerParams(vmem_limit_bytes=60 * MIB),
        name="attn_fwd",
    )(me, latents, mod, gathered, bias)


class LineSum:
    def __init__(self, own_ref, up, down, sems, out_ref, lag=2):
        self.lag = lag
        self.own, self.up, self.down, self.sems, self.out = own_ref, up, down, sems, out_ref
        self.count, self.rows = up.shape[0], up.shape[1]
        self.me = lax.axis_index("mp")
        self.n = lax.axis_size("mp")
        dp_at = lax.axis_index("dp")
        self.ends = (at_mesh(dp_at, self.me + 1), at_mesh(dp_at, self.me - 1))
        self.place = (self.me, self.n - 1 - self.me)

    def guarded(self, side, first, action):
        there = self.place[side] > 0 if first else self.place[side] < self.n - 1

        @pl.when(there)
        def _():
            action()

    def greet(self):
        sem = pltpu.get_barrier_semaphore()
        for side in (0, 1):
            self.guarded(side, False, lambda: pl.semaphore_signal(sem, inc=1, **self.ends[side]))

    def barrier(self):
        self.greet()
        pl.semaphore_wait(pltpu.get_barrier_semaphore(), line_peers(self.me, self.n))

    def copy(self, side, c):
        ref = (self.up, self.down)[side].at[c]
        return pltpu.make_async_remote_copy(
            ref, ref, self.sems.at[2 * side, c], self.sems.at[2 * side + 1, c], **self.ends[side]
        )

    def handle(self, side, c):
        ref = (self.up, self.down)[side]
        own = self.own[0, pl.ds(pl.multiple_of(c * self.rows, self.rows), self.rows)]

        @pl.when(self.place[side] == 0)
        def _():
            ref[c] = own

        @pl.when(self.place[side] > 0)
        def _():
            self.copy(side, c).wait_recv()
            ref[c] = (ref[c].astype(F32) + own.astype(F32)).astype(BF)

        self.guarded(side, False, lambda: self.copy(side, c).start())

    def tick(self, t):
        for side in (0, 1):
            at = t - self.lag * self.place[side]

            @pl.when((at >= 0) & (at % 3 < 2) & (at - at // 3 < self.count))
            def _():
                self.handle(side, at - at // 3)

    def finish(self, ticks):
        for side in (0, 1):
            done = jnp.maximum(ticks - self.lag * self.place[side], 0)
            done = jnp.minimum(done - done // 3, self.count)

            def late(c, carry):
                self.handle(side, c)
                return carry

            lax.fori_loop(done, self.count, late, 0)

        def add(c, carry):
            rows = pl.ds(pl.multiple_of(c * self.rows, self.rows), self.rows)
            total = self.up[c].astype(F32) + self.down[c].astype(F32)
            self.out[0, rows] = (total - self.own[0, rows].astype(F32)).astype(BF)
            return carry

        lax.fori_loop(0, self.count, add, 0)
        for side in (0, 1):

            def sent(c, carry):
                self.copy(side, c).wait_send()
                return carry

            self.guarded(side, False, lambda: lax.fori_loop(0, self.count, sent, 0))


def mlp_kernel(*refs, summing):
    heads_ref, lat_ref, cot_ref, mod_ref, bp_ref, b1_ref, b2_ref = refs[:7]
    own_refs, (wq_all, w1_all, w2_all), refs = refs[7:10], refs[10:13], refs[13:]
    if summing:
        part_ref, refs = refs[0], refs[1:]
    out_ref, dx1_ref, da_ref, h2_ref, dm_ref, z_ref, du_ref, stats_ref, dusum_ref = refs[:9]
    refs = refs[9:]
    if summing:
        sum_ref, refs = refs[0], refs[1:]
    macc, dacc, wp, w1, w2, load_sems = refs[:6]
    n_mp, hid, dim = w2.shape
    local = wp.shape[1]
    rows = lat_ref.shape[1]
    me = lax.axis_index("mp")
    step = pl.program_id(0)
    line = LineSum(part_ref, refs[6], refs[7], refs[8], sum_ref) if summing else None

    def load(kind, k):
        slot = (me + k) % n_mp
        source = own_refs[kind]
        if k > 0:
            stack = (wq_all, w1_all, w2_all)[kind]
            source = stack.at[slot, kind] if len(stack.shape) == 4 else stack.at[slot]
        if k > 0 and kind == 0:
            source = source.at[pl.ds(3 * local, local)]
        ref = (wp.at[slot], w1.at[k], w2.at[k])[kind]
        return pltpu.make_async_copy(source, ref, load_sems.at[kind, k])

    @pl.when(step == 0)
    def _():
        if summing:
            line.barrier()
        for k in range(n_mp):
            load(0, k).start()
        for k in range(n_mp):
            load(1, k).start()
            load(2, k).start()
        for k in range(n_mp):
            load(0, k).wait()

    gate_one, shift_two = mod_ref[0, 2:3], mod_ref[0, 3:4]
    scale_two, gate_two = mod_ref[0, 4:5], mod_ref[0, 5:6]
    heads = heads_ref[:, 0].reshape(dim, rows)
    attn = tn(heads, wp[...].reshape(dim, dim)) + bp_ref[...]
    x1 = lat_ref[0].astype(F32) + gate_one * attn
    n2, inv2 = norm_stats(x1)
    h2 = (n2 * (1.0 + scale_two) + shift_two).astype(BF)
    h2_ref[0] = h2
    cot = cot_ref[0].astype(F32)
    dm = (gate_two * cot).astype(BF)
    dm_ref[0] = dm

    macc[...] = jnp.zeros_like(macc)
    dacc[...] = jnp.zeros_like(dacc)

    def part(k, own):
        if summing:
            line.tick(step * n_mp + k)

        @pl.when(step == 0)
        def _():
            for kind in (1, 2):
                ref = (w1, w2)[kind - 1].at[k]
                pltpu.make_async_copy(ref, ref, load_sems.at[kind, k]).wait()

        u = mm(h2_ref[0], w1[k]) + b1_ref[(me + k) % n_mp]
        dz = nt(dm_ref[0], w2[k])
        u2 = u * u
        t = jnp.tanh(u * (GELU_A + (GELU_A * GELU_B) * u2))
        half = 0.5 + 0.5 * t
        z = (u * half).astype(BF)
        slope = half + u * (1.0 - t * t) * (0.5 * GELU_A + (1.5 * GELU_A * GELU_B) * u2)
        du = dz * slope
        if own:
            before = jnp.where(step == 0, 0.0, dusum_ref[0])
            dusum_ref[0] = before + jnp.sum(du, 0, keepdims=True)
        du = du.astype(BF)
        if own:
            z_ref[0] = z
            du_ref[0] = du
        macc[...] += mm(z, w2[k])
        dacc[...] += nt(du, w1[k])

    part(0, True)

    for k in range(1, n_mp):
        part(k, False)
    mlp = macc[...] + b2_ref[...]
    out_ref[0] = (x1 + gate_two * mlp).astype(BF)
    dh2 = dacc[...]
    dx1 = cot + norm_back(n2, inv2, dh2 * (1.0 + scale_two))
    dx1_ref[0] = dx1.astype(BF)
    da_ref[0] = (gate_one * dx1).astype(BF)
    total = lambda v: jnp.sum(v, 0, keepdims=True)
    stats = jnp.concatenate(
        [
            total(dx1 * attn),
            total(dh2),
            total(dh2 * n2),
            total(cot * mlp),
            total(cot),
            total(dx1),
            jnp.zeros((2, dim), F32),
        ],
        0,
    )

    @pl.when(step == 0)
    def _():
        stats_ref[0] = stats

    @pl.when(step > 0)
    def _():
        stats_ref[0] += stats

    if summing:

        @pl.when(step == pl.num_programs(0) - 1)
        def _():
            line.finish(pl.num_programs(0) * n_mp)


LINE_CHUNKS = 8


def line_scratch(seq, dim):
    rows = seq // LINE_CHUNKS
    return [
        pltpu.VMEM((LINE_CHUNKS, rows, dim), BF),
        pltpu.VMEM((LINE_CHUNKS, rows, dim), BF),
        pltpu.SemaphoreType.DMA((4, LINE_CHUNKS)),
    ]


def mlp_both(index, heads, latents, cotangent, mod, biases, own, gathered, n_mp, rows, part):
    lat, seq, dim = latents.shape
    local = dim // n_mp
    hid = biases[1].shape[2]
    tok = pl.BlockSpec((1, rows, dim), lambda t: (index, t, 0))
    new = pl.BlockSpec((1, rows, dim), lambda t: (0, t, 0))
    hidden = pl.BlockSpec((1, rows, hid), lambda t: (0, t, 0))
    once = lambda shape: pl.BlockSpec(
        shape, lambda t: (0,) * len(shape), pipeline_mode=pl.Buffered(1)
    )
    any_spec = pl.BlockSpec(memory_space=pl.ANY)
    summing = part is not None
    extra = [once((1, seq, dim))] if summing else []
    return pl.pallas_call(
        functools.partial(mlp_kernel, summing=summing),
        grid=(seq // rows,),
        in_specs=[
            pl.BlockSpec((n_mp, 1, local, rows), lambda t: (0, index, 0, t)),
            tok,
            tok,
            pl.BlockSpec((1, 6, dim), lambda t: (index, 0, 0)),
            once((1, dim)),
            once((n_mp, 1, hid)),
            once((1, dim)),
        ]
        + [any_spec] * 6
        + extra,
        out_specs=[new] * 5
        + [
            hidden,
            hidden,
            pl.BlockSpec((1, 8, dim), lambda t: (0, 0, 0)),
            pl.BlockSpec((1, 1, hid), lambda t: (0, 0, 0)),
        ]
        + extra,
        out_shape=[jax.ShapeDtypeStruct((1, seq, dim), BF)] * 5
        + [jax.ShapeDtypeStruct((1, seq, hid), BF)] * 2
        + [jax.ShapeDtypeStruct((1, 8, dim), F32), jax.ShapeDtypeStruct((1, 1, hid), F32)]
        + ([jax.ShapeDtypeStruct((1, seq, dim), BF)] if summing else []),
        scratch_shapes=[
            pltpu.VMEM((rows, dim), F32),
            pltpu.VMEM((rows, dim), F32),
            pltpu.VMEM((n_mp, local, dim), BF),
            pltpu.VMEM((n_mp, dim, hid), BF),
            pltpu.VMEM((n_mp, hid, dim), BF),
            pltpu.SemaphoreType.DMA((3, n_mp)),
        ]
        + (line_scratch(seq, dim) if summing else []),
        compiler_params=pltpu.CompilerParams(
            vmem_limit_bytes=63 * MIB,
            **(dict(collective_id=4 + index, has_side_effects=True) if summing else {}),
        ),
        name="mlp_sum" if summing else "mlp_both",
    )(
        heads,
        latents,
        cotangent,
        mod,
        *biases,
        *own,
        *gathered,
        *([part] if summing else []),
    )


class CubeSum:
    def __init__(self, terms, full, halves, firsts, seconds, sems):
        self.terms, self.full = terms, full
        self.halves, self.firsts, self.seconds, self.sems = halves, firsts, seconds, sems
        self.units = halves.shape[0]
        dp_at, me = lax.axis_index("dp"), lax.axis_index("mp")
        self.core, x, y = dp_at % 2, dp_at // 2 % 2, dp_at // 4
        self.core_id = at_mesh(flip(dp_at, 0), me)
        x_id, y_id = at_mesh(flip(dp_at, 1), me), at_mesh(flip(dp_at, 2), me)
        self.ids = ((x_id, y_id), (y_id, x_id))
        self.place = ((x, y), (y, x))

    def barrier(self):
        sem = pltpu.get_barrier_semaphore()
        for target in (self.core_id,) + self.ids[0]:
            pl.semaphore_signal(sem, inc=1, **target)

    def blocks(self, u, core, q=None, first=None, second=None):
        at, count = 16 * u + 8 * core, 8
        if q is not None:
            at, count = at + 4 * q, 4
        if first is not None:
            at, count = at + 2 * first, 2
        if second is not None:
            at, count = at + second, 1
        return pl.ds(at, count)

    def send(self, stage, u, q, arrived=False):
        core, blocks = self.core, self.blocks
        first, second = self.place[q]
        other = lambda v: 1 - v if arrived else v
        if stage == 0:
            pair = (self.terms.at[blocks(u, 1 - core)], self.halves.at[u])
        elif stage == 1:
            pair = (self.terms.at[blocks(u, core, q, 1 - first)], self.firsts.at[u, q])
        elif stage == 2:
            pair = (self.terms.at[blocks(u, core, q, first, 1 - second)], self.seconds.at[u, q])
        elif stage == 3:
            pair = (self.full.at[blocks(u, core, q, first, other(second))],) * 2
        elif stage == 4:
            pair = (self.full.at[blocks(u, core, q, other(first))],) * 2
        else:
            pair = (self.full.at[blocks(u, other(core))],) * 2
        near, far = self.ids[q]
        target = (self.core_id, near, far, far, near, self.core_id)[stage]
        return pltpu.make_async_remote_copy(
            *pair, self.sems.at[0, stage, q, u], self.sems.at[1, stage, q, u], **target
        )

    def quarters(self, stage):
        return (0,) if stage in (0, 5) else (0, 1)

    def event(self, stage, u):
        terms, core, blocks = self.terms, self.core, self.blocks

        @pl.when((u >= 0) & (u < self.units))
        def _():
            if stage > 0:
                for q in self.quarters(stage - 1):
                    self.send(stage - 1, u, q, True).wait_recv()
            if stage == 1:
                at = blocks(u, core)
                terms[at] = (terms[at].astype(F32) + self.halves[u].astype(F32)).astype(BF)
            for q in (0, 1):
                first, second = self.place[q]
                if stage == 2:
                    at = blocks(u, core, q, first)
                    terms[at] = (terms[at].astype(F32) + self.firsts[u, q].astype(F32)).astype(BF)
                if stage == 3:
                    at = blocks(u, core, q, first, second)
                    total = terms[at].astype(F32) + self.seconds[u, q].astype(F32)
                    self.full[at] = total.astype(BF)
            if stage < 6:
                for q in self.quarters(stage):
                    self.send(stage, u, q).start()

    def finish(self):
        def sent(u, carry):
            for stage in range(6):
                for q in self.quarters(stage):
                    self.send(stage, u, q).wait_send()
            return carry

        lax.fori_loop(0, self.units, sent, 0)


BLOCK = 32


class WeightGrads:
    def __init__(self, operands, terms, right, left_cols, left_rows, right_sems, left_sems):
        self.operands, self.terms, self.right = operands, terms, right
        self.left_cols, self.left_rows = left_cols, left_rows
        self.right_sems, self.left_sems = right_sems, left_sems
        self.lats = right.shape[1]
        dim = right.shape[3]
        qkv_blocks = operands[2][0][0].shape[0] // BLOCK
        half = (qkv_blocks + 1) // 2 * BLOCK
        third = dim // 3
        self.pieces = [(job, i * third, third) for job in (0, 1) for i in range(3)]
        self.pieces += [(2, 0, half), (2, half, qkv_blocks * BLOCK - half)]
        self.pieces += [(3, 0, operands[3][0][0].shape[0])]

    def right_copies(self, job):
        slot = job % 2
        return [
            pltpu.make_async_copy(
                self.operands[job][1][i], self.right.at[slot, i], self.right_sems.at[slot, i]
            )
            for i in range(self.lats)
        ]

    def left_copies(self, at):
        job, first, count = self.pieces[at]
        copies = []
        for i in range(self.lats):
            source = self.operands[job][0][i]
            if job < 2:
                source = source.at[:, pl.ds(first, count)]
                ref = self.left_cols.at[at % 2, i]
            else:
                source = source.at[pl.ds(first, count)]
                ref = self.left_rows.at[at % 2, i, pl.ds(0, count)]
            copies.append(pltpu.make_async_copy(source, ref, self.left_sems.at[at % 2, i]))
        return copies

    def begin(self):
        for copy in self.right_copies(0) + self.left_copies(0):
            copy.start()

    def compute(self, at):
        job, _, count = self.pieces[at]
        opens = at == 0 or self.pieces[at - 1][0] != job
        if at + 1 < len(self.pieces):
            for copy in self.left_copies(at + 1):
                copy.start()
        if opens:
            if job + 1 < len(self.operands):
                for copy in self.right_copies(job + 1):
                    copy.start()
            for copy in self.right_copies(job):
                copy.wait()
        for copy in self.left_copies(at):
            copy.wait()
        slot, dim = job % 2, self.right.shape[3]
        if job < 2:
            left = self.left_cols[at % 2].reshape(-1, count)
            total = tn(left, self.right[slot].reshape(-1, dim))
        else:
            total = mm(self.left_rows[at % 2, 0, :count], self.right[slot, 0])
            for i in range(1, self.lats):
                total = total + mm(self.left_rows[at % 2, i, :count], self.right[slot, i])
        done = sum(rows for _, _, rows in self.pieces[:at]) // BLOCK
        self.terms[pl.ds(done, count // BLOCK)] = total.reshape(-1, BLOCK, dim).astype(BF)


def tail_kernel(*refs, lats):
    part_ref, bias_ref, heads_ref, h1_ref = refs[:4]
    lists = [refs[4 + i * lats : 4 + (i + 1) * lats] for i in range(6)]
    h2s, dus, zs, dms, dqkvs, das = [[ref.at[0] for ref in group] for group in lists]
    sum_ref, full_ref = refs[4 + 6 * lats : 6 + 6 * lats]
    refs = refs[6 + 6 * lats :]
    up, down, line_sems, terms, full, halves, firsts, seconds, cube_sems = refs[:9]
    right, left_cols, left_rows, right_sems, left_sems, local_sem = refs[9:]
    line = LineSum(part_ref, up, down, line_sems, sum_ref, 3)
    cube = CubeSum(terms, full, halves, firsts, seconds, cube_sems)
    heads = [heads_ref.at[line.me, i] for i in range(lats)]
    h1s = [h1_ref.at[i] for i in range(lats)]
    grads = WeightGrads(
        ((h2s, dus), (zs, dms), (dqkvs, h1s), (heads, das)),
        terms,
        right,
        left_cols,
        left_rows,
        right_sems,
        left_sems,
    )
    grads.begin()
    cube.barrier()
    line.greet()
    pl.semaphore_wait(pltpu.get_barrier_semaphore(), 3 + line_peers(line.me, line.n))
    spare = bias_ref.shape[0]
    terms[pl.ds(terms.shape[0] - spare, spare)] = bias_ref[...]
    line.tick(0)
    unit_rows = 16 * BLOCK
    ready = 0
    for t in range(cube.units):
        line.tick(2 * t + 1)
        while ready < len(grads.pieces) and (
            sum(rows for _, _, rows in grads.pieces[:ready]) < (t + 1) * unit_rows
        ):
            grads.compute(ready)
            ready += 1
        line.tick(2 * t + 2)
        for stage in range(min(t, 6), -1, -1):
            cube.event(stage, t - stage)

    def advance(t, carry):
        line.tick(2 * t + 1)
        for stage in range(6, 0, -1):
            cube.event(stage, t - stage)
        line.tick(2 * t + 2)
        return carry

    lax.fori_loop(cube.units, cube.units + 6, advance, 0)
    store = pltpu.make_async_copy(full, full_ref, local_sem.at[0])
    store.start()
    line.finish(2 * (cube.units + 6) + 1)
    cube.finish()
    store.wait()


def tail_sums(part, biases, heads, h1, lists):
    n_mp, lats, local, seq = heads.shape
    dim = h1.shape[2]
    rows = 2 * dim + 4 * local
    units = -(-(rows + BLOCK) // (16 * BLOCK))
    spare = units * 16 - rows // BLOCK
    biases = jnp.pad(biases, ((0, spare * BLOCK - biases.shape[0]), (0, 0)))
    vmem = pl.BlockSpec(memory_space=pltpu.VMEM)
    any_spec = pl.BlockSpec(memory_space=pl.ANY)
    shape = (units * 16, BLOCK, dim)
    flat = [array for group in lists for array in group]
    total, full = pl.pallas_call(
        functools.partial(tail_kernel, lats=lats),
        in_specs=[vmem, vmem] + [any_spec] * (2 + len(flat)),
        out_specs=[vmem, any_spec],
        out_shape=[jax.ShapeDtypeStruct(part.shape, BF), jax.ShapeDtypeStruct(shape, BF)],
        scratch_shapes=line_scratch(seq, dim)
        + [
            pltpu.VMEM(shape, BF),
            pltpu.VMEM(shape, BF),
            pltpu.VMEM((units, 8, BLOCK, dim), BF),
            pltpu.VMEM((units, 2, 2, BLOCK, dim), BF),
            pltpu.VMEM((units, 2, 1, BLOCK, dim), BF),
            pltpu.SemaphoreType.DMA((2, 6, 2, units)),
            pltpu.VMEM((2, lats, seq, dim), BF),
            pltpu.VMEM((2, lats, seq, dim // 3), BF),
            pltpu.VMEM((2, lats, (3 * local // BLOCK + 1) // 2 * BLOCK, seq), BF),
            pltpu.SemaphoreType.DMA((2, lats)),
            pltpu.SemaphoreType.DMA((2, lats)),
            pltpu.SemaphoreType.DMA((1,)),
        ],
        compiler_params=pltpu.CompilerParams(
            collective_id=2, has_side_effects=True, vmem_limit_bytes=63 * MIB
        ),
        name="tail_sums",
    )(part, biases.reshape(spare, BLOCK, dim), heads, h1, *flat)
    return total, full.reshape(units * 16 * BLOCK, dim)


def rows_kernel(rows_ref, act_ref, every_ref, total_ref, acts, sems):
    dp_at, me = lax.axis_index("dp"), lax.axis_index("mp")
    n_dp, n_mp = every_ref.shape[0], acts.shape[0]
    barrier = pltpu.get_barrier_semaphore()
    for k in range(1, n_dp):
        pl.semaphore_signal(barrier, inc=1, **at_mesh((dp_at + k) % n_dp, me))
    for k in range(1, n_mp):
        pl.semaphore_signal(barrier, inc=1, **at_mesh(dp_at, (me + k) % n_mp))
    every_ref[dp_at] = rows_ref[...]
    acts[me] = act_ref[...]
    pl.semaphore_wait(barrier, n_dp + n_mp - 2)

    def copy(ref, k, target):
        return pltpu.make_async_remote_copy(ref, ref, sems.at[0, k], sems.at[1, k], **target)

    def act_copy(k, source):
        return copy(acts.at[source % n_mp], k - 1, at_mesh(dp_at, (me + k) % n_mp))

    def row_copy(k, source):
        target = at_mesh((dp_at + k) % n_dp, me)
        return copy(every_ref.at[source % n_dp], n_mp + k - 2, target)

    for k in range(1, n_mp):
        act_copy(k, me).start()
    for k in range(1, n_dp):
        row_copy(k, dp_at).start()
    for k in range(1, n_mp):
        act_copy(k, me + n_mp - k).wait_recv()
    total = acts[0]
    for i in range(1, n_mp):
        total = total + acts[i]
    total_ref[...] = total
    for k in range(1, n_dp):
        row_copy(k, dp_at + n_dp - k).wait_recv()
    for k in range(1, n_mp):
        act_copy(k, me).wait_send()
    for k in range(1, n_dp):
        row_copy(k, dp_at).wait_send()


def rows_exchange(rows, act, n_dp, n_mp):
    vmem = pl.BlockSpec(memory_space=pltpu.VMEM)
    return pl.pallas_call(
        rows_kernel,
        in_specs=[vmem, vmem],
        out_specs=[vmem, vmem],
        out_shape=[
            jax.ShapeDtypeStruct((n_dp,) + rows.shape, rows.dtype),
            jax.ShapeDtypeStruct(act.shape, act.dtype),
        ],
        scratch_shapes=[
            pltpu.VMEM((n_mp,) + act.shape, act.dtype),
            pltpu.SemaphoreType.DMA((2, n_dp + n_mp - 2)),
        ],
        compiler_params=pltpu.CompilerParams(
            collective_id=3, has_side_effects=True, vmem_limit_bytes=40 * MIB
        ),
        name="rows_exchange",
    )(rows, act)


def attn_bwd_kernel(da_ref, heads_ref, qkv_ref, lse_ref, wp_ref, wq_ref, dqkv_ref, dh1_ref, bias_ref, *, rows):
    n_heads = lse_ref.shape[1]
    seq = da_ref.shape[1]
    dheads = nt(wp_ref[...], da_ref[0]).reshape(n_heads, HEAD_DIM, seq)
    heads = heads_ref[0, 0].astype(F32).reshape(n_heads, HEAD_DIM, seq)
    scaling = 1.0 / HEAD_DIM**0.5
    dq_list, dk_list, dv_list = [], [], []
    for h in range(n_heads):
        q_t = qkv_ref[0, h]
        k_t = qkv_ref[0, n_heads + h]
        v_t = qkv_ref[0, 2 * n_heads + h]
        q = q_t.astype(F32).T.astype(BF)
        k = k_t.astype(F32).T.astype(BF)
        v = v_t.astype(F32).T.astype(BF)
        do_t = dheads[h].astype(BF)
        do = dheads[h].T.astype(BF)
        inner = jnp.sum(do_t.astype(F32) * heads[h], 0, keepdims=True)
        dq_parts = []
        for i in range(seq // rows):
            cols = slice(i * rows, (i + 1) * rows)
            probs = jnp.exp2(mm(k, q_t[:, cols]) - lse_ref[0, h : h + 1, cols])
            dprobs = mm(v, do_t[:, cols])
            dscores = (probs * (dprobs - inner[:, cols])).astype(BF)
            dq_parts.append(mm(k_t, dscores))
            dv_new = mm(probs.astype(BF), do[cols])
            dk_new = mm(dscores, q[cols])
            dv = dv_new if i == 0 else dv + dv_new
            dk = dk_new if i == 0 else dk + dk_new
        dq_list.append(jnp.concatenate(dq_parts, 1) * scaling)
        dk_list.append(dk.T * (1.0 / LOG2E))
        dv_list.append(dv.T)
    dqkv = jnp.concatenate(dq_list + dk_list + dv_list, 0)
    bias_ref[0] = jnp.sum(dqkv, 1, keepdims=True)
    dqkv = dqkv.astype(BF)
    dqkv_ref[0] = dqkv
    dh1_ref[0] = tn(dqkv, wq_ref[...]).astype(BF)


def attn_bwd(da, heads, qkv, lse, wp, wq, index, rows):
    lat, seq, dim = da.shape
    n_heads = lse.shape[1]
    local = n_heads * HEAD_DIM
    one = lambda shape: pl.BlockSpec((1,) + shape, lambda i: (index,) + (0,) * len(shape))
    only = lambda shape: pl.BlockSpec((1,) + shape, lambda i: (0,) * (len(shape) + 1))
    whole = lambda shape: pl.BlockSpec(shape, lambda i: (0,) * len(shape))
    out = lambda shape: pl.BlockSpec((1,) + shape, lambda i: (0,) * (len(shape) + 1))
    return pl.pallas_call(
        functools.partial(attn_bwd_kernel, rows=rows),
        grid=(1,),
        in_specs=[
            only((seq, dim)),
            pl.BlockSpec((1, 1, local, seq), lambda i: (lax.axis_index("mp"), index, 0, 0)),
            one((3 * n_heads, HEAD_DIM, seq)),
            one((n_heads, seq)),
            whole((local, dim)),
            whole((3 * local, dim)),
        ],
        out_specs=[out((3 * local, seq)), out((seq, dim)), out((3 * local, 1))],
        out_shape=[
            jax.ShapeDtypeStruct((1, 3 * local, seq), BF),
            jax.ShapeDtypeStruct((1, seq, dim), BF),
            jax.ShapeDtypeStruct((1, 3 * local, 1), F32),
        ],
        compiler_params=pltpu.CompilerParams(vmem_limit_bytes=60 * MIB),
        name="attn_bwd",
    )(da, heads, qkv, lse, wp, wq)


def latents_kernel(*refs, lats):
    lat_ref, mod_ref = refs[:2]
    dh1_refs, dx1_refs, out_refs = [refs[2 + i * lats : 2 + (i + 1) * lats] for i in range(3)]
    grad_ref, stats_ref, out_ref = refs[2 + 3 * lats :]
    lat, step = pl.program_id(0), pl.program_id(1)
    n1, inv1 = norm_stats(lat_ref[0].astype(F32))
    for i in range(lats):

        @pl.when(lat == i)
        def _():
            dh1 = dh1_refs[i][0].astype(F32)
            back = norm_back(n1, inv1, dh1 * (1.0 + mod_ref[0, 1:2]))
            grad_ref[0] = (dx1_refs[i][0].astype(F32) + back).astype(BF)
            out_ref[0] = out_refs[i][0]
            pad = jnp.zeros((6, dh1.shape[1]), F32)
            sums = [jnp.sum(dh1, 0, keepdims=True), jnp.sum(dh1 * n1, 0, keepdims=True), pad]
            stats_ref[0] = jnp.where(step == 0, 0.0, stats_ref[0]) + jnp.concatenate(sums, 0)


def latents_back(dh1, dx1, outs, latents, mod, rows):
    lat, seq, dim = latents.shape
    steps = seq // rows
    tok = pl.BlockSpec((1, rows, dim), lambda l, t: (l, t, 0))
    at = lambda i: (lambda l, t: (0, jnp.where(l < i, 0, jnp.where(l == i, t, steps - 1)), 0))
    each = [pl.BlockSpec((1, rows, dim), at(i)) for i in range(lat)]
    return pl.pallas_call(
        functools.partial(latents_kernel, lats=lat),
        grid=(lat, steps),
        in_specs=[tok, pl.BlockSpec((1, 6, dim), lambda l, t: (l, 0, 0))] + each * 3,
        out_specs=[tok, pl.BlockSpec((1, 8, dim), lambda l, t: (l, 0, 0)), tok],
        out_shape=[
            jax.ShapeDtypeStruct((lat, seq, dim), BF),
            jax.ShapeDtypeStruct((lat, 8, dim), F32),
            jax.ShapeDtypeStruct((lat, seq, dim), BF),
        ],
        compiler_params=pltpu.CompilerParams(vmem_limit_bytes=63 * MIB),
        name="latents_back",
    )(latents, mod, *dh1, *dx1, *outs)


def per_device(
    n_dp,
    n_mp,
    latents,
    condition,
    cotangent,
    qkv_weight,
    qv_bias,
    proj_weight,
    proj_bias,
    fc1_weight,
    fc1_bias,
    fc2_weight,
    fc2_bias,
    ada_weight,
    ada_bias,
):
    lat, seq, dim = latents.shape
    local = qkv_weight.shape[2]
    n_heads = local // HEAD_DIM
    hid = fc1_weight.shape[1]
    cols = ada_weight.shape[1]
    mp_at = lax.axis_index("mp")
    dp_at = lax.axis_index("dp")
    me = jnp.full((1,), mp_at, jnp.int32)

    direct = n_mp == 4 and n_dp == 8
    bias_row = jnp.concatenate([qv_bias.reshape(-1), fc1_bias]).astype(F32)[None]
    ada_row = ada_bias.astype(F32)[None]
    wq_own = (
        qkv_weight.reshape(dim, 3, n_heads, HEAD_DIM).transpose(1, 2, 3, 0).reshape(3 * local, dim)
    )
    if direct:
        own = (wq_own, proj_weight, fc1_weight, fc2_weight)
        small_rows = jnp.concatenate([ada_row, bias_row], 0)
        heads, qkv, lse, h1, small, cond_low, gathered = attn_gather(
            latents, condition, small_rows, ada_weight.T, own, n_mp
        )
        gathered = (gathered,) * 3
    else:
        cond_low = jax.nn.silu(condition).astype(BF)
        mod_part = mm(cond_low, ada_weight) + ada_row
        small = lax.all_gather(jnp.concatenate([mod_part, bias_row], 0), "mp", axis=0)
    mod = small[:, :lat].transpose(1, 0, 2).reshape(lat, 6, dim)
    b_fc1 = small[:, lat, 2 * local :].reshape(n_mp, 1, hid)
    if not direct:
        qv_all = small[:, lat, : 2 * local].reshape(n_mp, 2, local)
        b_qkv = jnp.stack([qv_all[:, 0], jnp.zeros((n_mp, local), F32), qv_all[:, 1]], 1)
        b_qkv = b_qkv.reshape(n_mp, 1, 3 * local)

        def gather(weight):
            share = weight.shape[0] // n_dp
            mine = lax.dynamic_slice_in_dim(weight, dp_at * share, share, 0)
            whole = lax.all_gather(mine, ("dp", "mp"), axis=0)
            whole = whole.reshape(n_dp, n_mp, share, weight.shape[1]).transpose(1, 0, 2, 3)
            return whole.reshape(n_mp, weight.shape[0], weight.shape[1])

        gathered = (
            gather(jnp.concatenate([wq_own, proj_weight], 0)),
            gather(fc1_weight),
            gather(fc2_weight),
        )
        heads, qkv, lse, h1 = attn_fwd(me, latents, mod, gathered[0], b_qkv, n_mp)
    rows = min(256, seq)
    results, dqkv, dh1, bias_sums = [], [], [], []
    for i in range(lat):
        waiting = dqkv and direct
        outs = mlp_both(
            i,
            heads,
            latents,
            cotangent,
            mod,
            (proj_bias.astype(F32)[None], b_fc1, fc2_bias.astype(F32)[None]),
            (proj_weight, fc1_weight, fc2_weight),
            gathered,
            n_mp,
            rows,
            dh1_i if waiting else None,
        )
        if waiting:
            dh1.append(outs[-1])
        results.append(outs[:9])
        dqkv_i, dh1_i, sums_i = attn_bwd(
            outs[2], heads, qkv, lse, proj_weight, wq_own, i, min(512, seq)
        )
        dqkv.append(dqkv_i)
        bias_sums.append(sums_i)
        if not direct:
            dh1.append(lax.psum(dh1_i, "mp"))
    outs_by_kind = list(zip(*results))
    h2, dm, z, du = outs_by_kind[3:7]
    da = outs_by_kind[2]
    stats_two = jnp.concatenate(outs_by_kind[7], 0)
    grad_fc1_bias = sum(outs_by_kind[8])[0, 0]
    gate_one, gate_two = mod[:, 2], mod[:, 5]
    grad_fc2_bias = jnp.sum(gate_two * stats_two[:, 4], 0)
    grad_proj_bias = jnp.sum(gate_one * stats_two[:, 5], 0)
    bias_sums = sum(bias_sums).reshape(3, local)
    grad_qv_bias = jnp.stack([bias_sums[0], bias_sums[2]])
    if direct:
        bias_rows = jnp.stack(
            [
                grad_fc1_bias,
                grad_fc2_bias,
                grad_proj_bias,
                jnp.pad(grad_qv_bias.reshape(-1), (0, dim - 2 * local)),
            ]
        ).astype(BF)
        dh1_i, sums = tail_sums(dh1_i, bias_rows, heads, h1, (h2, du, z, dm, dqkv, da))
        dh1.append(dh1_i)
        grad_fc1, grad_fc2 = sums[:dim], sums[dim : 2 * dim]
        grad_qkv = sums[2 * dim : 2 * dim + 3 * local]
        grad_proj = sums[2 * dim + 3 * local : 3 * dim]
        bias_rows = sums[3 * dim : 3 * dim + 4].astype(F32)
        grad_fc1_bias, grad_fc2_bias, grad_proj_bias = bias_rows[:3]
        grad_qv_bias = bias_rows[3, : 2 * local].reshape(2, local)
    else:
        flat = lambda parts: jnp.concatenate(parts, 0).reshape(lat * seq, -1)
        grad_fc2 = tn(flat(z), flat(dm))
        grad_fc1 = tn(flat(h2), flat(du))
        grad_qkv = sum(mm(dqkv[i][0], h1[i]) for i in range(lat))
        heads_own = lax.dynamic_index_in_dim(heads, mp_at, 0, keepdims=False)
        grad_proj = sum(mm(heads_own[i], da[i][0]) for i in range(lat))
        grads = [grad.astype(BF) for grad in (grad_fc1, grad_fc2, grad_qkv, grad_proj)]
        grad_fc1, grad_fc2, grad_qkv, grad_proj = lax.psum(grads, "dp")
        biases = lax.psum((grad_fc1_bias, grad_fc2_bias, grad_proj_bias, grad_qv_bias), "dp")
        grad_fc1_bias, grad_fc2_bias, grad_proj_bias, grad_qv_bias = biases

    latents_grad, stats_one, block_out = latents_back(
        dh1, outs_by_kind[1], outs_by_kind[0], latents, mod, rows
    )

    dmod = jnp.stack(
        [
            stats_one[:, 0],
            stats_one[:, 1],
            stats_two[:, 0],
            stats_two[:, 1],
            stats_two[:, 2],
            stats_two[:, 3],
        ],
        1,
    )
    dmod = dmod.reshape(lat, 6 * dim).astype(BF)
    dmod_own = lax.dynamic_slice_in_dim(dmod, mp_at * cols, cols, 1)
    both = jnp.concatenate([cond_low, dmod_own], 1)
    grad_act = nt(dmod_own, ada_weight)
    if direct:
        both = jnp.pad(both, ((0, 16 - lat), (0, 0)))
        grad_act = jnp.pad(grad_act, ((0, 8 - lat), (0, 0)))
        every, grad_act = rows_exchange(both, grad_act, n_dp, n_mp)
        every, grad_act = every.reshape(n_dp * 16, dim + cols), grad_act[:lat]
    else:
        every = lax.all_gather(both, "dp", axis=0, tiled=True)
        grad_act = lax.psum(grad_act, "mp")
    grad_ada = tn(every[:, :dim], every[:, dim:])
    grad_ada_bias = jnp.sum(every[:, dim:].astype(F32), 0)
    condition_grad = jax.vjp(jax.nn.silu, condition)[1](grad_act)[0]

    back = lambda v: v.astype(F32)
    return (
        block_out,
        latents_grad,
        condition_grad,
        back(grad_qkv).reshape(3, local, dim).transpose(2, 0, 1),
        grad_qv_bias,
        back(grad_proj),
        grad_proj_bias,
        back(grad_fc1),
        grad_fc1_bias,
        back(grad_fc2),
        grad_fc2_bias,
        grad_ada,
        grad_ada_bias,
    )


def solution(mesh):
    in_specs = (
        P("dp", None, None),
        P("dp", None),
        P("dp", None, None),
        P(None, None, "mp"),
        P(None, "mp"),
        P("mp", None),
        P(),
        P(None, "mp"),
        P("mp"),
        P("mp", None),
        P(),
        P(None, "mp"),
        P("mp"),
    )
    out_specs = (
        P("dp", None, None),
        P("dp", None, None),
        P("dp", None),
        P(None, None, "mp"),
        P(None, "mp"),
        P("mp", None),
        P(),
        P(None, "mp"),
        P("mp"),
        P("mp", None),
        P(),
        P(None, "mp"),
        P("mp"),
    )
    body = functools.partial(per_device, mesh.shape["dp"], mesh.shape["mp"])
    return jax.shard_map(body, mesh=mesh, in_specs=in_specs, out_specs=out_specs, check_vma=False)
```

```python
import functools

import jax
import jax.numpy as jnp
from jax import lax
from jax.experimental import pallas as pl
from jax.experimental.pallas import tpu as pltpu
from jax.sharding import PartitionSpec as P

HEAD_DIM = 72
EPS = 1e-06
LOG2E = 1.4426950408889634
GELU_A = 0.7978845608028654
GELU_B = 0.044715
BF = jnp.bfloat16
F32 = jnp.float32
MIB = 2**20


def mm(a, b):
    return jnp.dot(a, b, preferred_element_type=F32)


def nt(a, b):
    return lax.dot_general(a, b, (((1,), (1,)), ((), ())), preferred_element_type=F32)


def tn(a, b):
    return lax.dot_general(a, b, (((0,), (0,)), ((), ())), preferred_element_type=F32)


def norm_stats(values):
    centered = values - jnp.mean(values, -1, keepdims=True)
    inv_std = lax.rsqrt(jnp.mean(centered * centered, -1, keepdims=True) + EPS)
    return centered * inv_std, inv_std


def norm_back(normed, inv_std, grad_normed):
    first = jnp.mean(grad_normed, -1, keepdims=True)
    second = jnp.mean(grad_normed * normed, -1, keepdims=True)
    return inv_std * (grad_normed - first - normed * second)


def flip(value, bit):
    step = 1 << bit
    return value + step - 2 * step * (value // step % 2)


def near_part(me, k):
    side = me // 2
    end = jnp.minimum(me, 3 - me)
    at = k + end * (1 - 2 * k) * ((3 - k) // 2)
    return at + side * (3 - 2 * at)


def line_peers(me, n):
    return jnp.minimum(me, 1) + jnp.minimum(n - 1 - me, 1)


def at_mesh(dp_at, mp_at):
    return {"device_id": (dp_at, mp_at), "device_id_type": pl.DeviceIdType.MESH}


def modulation_start(dp_at, me, n_mp, small, sems):
    def copy(k, arrived=False):
        at = small.at[(me + n_mp - k) % n_mp if arrived else me]
        target = at_mesh(dp_at, (me + k) % n_mp)
        return pltpu.make_async_remote_copy(at, at, sems.at[0, k - 1], sems.at[1, k - 1], **target)

    return copy


def attend(flat, n_heads, slot, heads_ref, qkv_ref, lse_ref, between):
    seq = flat.shape[1]
    parts = flat.reshape(3 * n_heads, HEAD_DIM, seq)
    scaling = LOG2E / HEAD_DIM**0.5
    outs = []
    for h in range(n_heads):
        q_t = (parts[h] * scaling).astype(BF)
        k_t = parts[n_heads + h]
        v_t = parts[2 * n_heads + h]
        v_ext = jnp.concatenate([v_t, jnp.ones((8, seq), F32)], 0).astype(BF)
        scores = mm(k_t.T.astype(BF), q_t)
        top = jnp.max(scores, 0, keepdims=True)
        probs = jnp.exp2(scores - top).astype(BF)
        out = mm(v_ext, probs)
        total = out[HEAD_DIM : HEAD_DIM + 1]
        outs.append(out[:HEAD_DIM] * (1.0 / total))
        lse = top + jnp.log2(total)

        @pl.when(slot == 0)
        def _():
            qkv_ref[0, h] = q_t
            qkv_ref[0, n_heads + h] = k_t.astype(BF)
            qkv_ref[0, 2 * n_heads + h] = v_t.astype(BF)
            lse_ref[0, h : h + 1] = lse

        between(h + 1)
    heads_ref[0, 0] = jnp.concatenate(outs, 0).astype(BF)


def as_column(row):
    return jnp.broadcast_to(row, (8, row.shape[1])).T[:, :1]


def mixed_one(lat_ref, shift, scale, h1_ref, h1_all, lat):
    normed, _ = norm_stats(lat_ref[0].astype(F32))
    h1 = (normed * (1.0 + scale) + shift).astype(BF)
    h1_all[lat] = h1
    h1_ref[0] = h1


def attn_fwd_kernel(
    me_ref, lat_ref, mod_ref, w_ref, bias_ref, heads_ref, qkv_ref, lse_ref, h1_ref, h1_all
):
    slot, lat = pl.program_id(0), pl.program_id(1)

    @pl.when(slot == 0)
    def _():
        mixed_one(lat_ref, mod_ref[0, 0:1], mod_ref[0, 1:2], h1_ref, h1_all, lat)

    flat = nt(w_ref[0], h1_all[lat]) + as_column(bias_ref[0])
    attend(flat, qkv_ref.shape[1] // 3, slot, heads_ref, qkv_ref, lse_ref, lambda h: None)


def attn_gather_kernel(
    lat_ref,
    cond_ref,
    rows_ref,
    ada_ref,
    wq_ref,
    wp_ref,
    w1_ref,
    w2_ref,
    heads_ref,
    qkv_ref,
    lse_ref,
    h1_ref,
    small_ref,
    low_ref,
    all_ref,
    h1_all,
    w_buf,
    ada_buf,
    small,
    local_sem,
    z_own,
    z_on,
    z_got,
    sends,
    recvs,
    small_sems,
):
    n_mp = all_ref.shape[0]
    lats = h1_all.shape[0]
    units, pace = 3 * (n_mp - 1), 5
    slot, lat = pl.program_id(0), pl.program_id(1)
    step = slot * lats + lat
    dp_at, me = lax.axis_index("dp"), lax.axis_index("mp")
    core, x, y = dp_at % 2, dp_at // 2 % 2, dp_at // 4
    rows = all_ref.shape[5]
    upper = wq_ref.shape[0] // rows
    cut = rows // 32 * 16 + 16
    near, far = pl.ds(0, cut), pl.ds(cut, rows - cut)
    every = pl.ds(0, rows)
    both = pl.ds(0, 2)
    core_id = at_mesh(flip(dp_at, 0), me)
    x_id = at_mesh(flip(dp_at, 1), me)
    y_id = at_mesh(flip(dp_at, 2), me)
    right_id, left_id = at_mesh(dp_at, me + 1), at_mesh(dp_at, me - 1)

    def piece(s, c, at_y, at_x, at_core, part):
        return all_ref.at[s, c, at_y, at_x, at_core, part]

    def own_copy(c, side, target, source=None):
        ref = piece(me, c, y, x, core, every)
        return pltpu.make_async_remote_copy(
            ref if source is None else source,
            ref,
            z_own.at[side, c],
            z_got.at[c, me],
            **target,
        )

    def pass_on(s, c, target):
        ref = piece(s, c, y, x, core, every)
        return pltpu.make_async_remote_copy(
            ref, ref, z_on.at[c, s], z_got.at[c, s], **target
        )

    def move(kind, c, s, arrived=False):
        flipped = lambda v: 1 - v if arrived else v
        at_y, at_x, at_core, part, target = (
            (pl.ds(y, 1), pl.ds(flipped(x), 1), pl.ds(core, 1), near, x_id),
            (pl.ds(flipped(y), 1), pl.ds(x, 1), pl.ds(core, 1), far, y_id),
            (pl.ds(flipped(y), 1), both, pl.ds(core, 1), near, y_id),
            (both, pl.ds(flipped(x), 1), pl.ds(core, 1), far, x_id),
            (both, both, pl.ds(flipped(core), 1), every, core_id),
        )[kind]
        ref = piece(s, c, at_y, at_x, at_core, part)
        return pltpu.make_async_remote_copy(
            ref, ref, sends.at[kind, c, s], recvs.at[kind, c, s], **target
        )

    def unit(u):
        return u // (n_mp - 1), near_part(me, 1 + u % (n_mp - 1))

    def event(stage, u):
        c, s = unit(u)

        @pl.when((u >= 0) & (u < units))
        def _():
            if stage == 0:

                @pl.when((me > 0) & (me < n_mp - 1))
                def _():
                    pass_on(s, c, right_id).wait_recv()
                    pl.when(s < me)(lambda: pass_on(s, c, right_id).start())
                    pl.when(s > me)(lambda: pass_on(s, c, left_id).start())

            if stage == 1:

                @pl.when((me == 0) | (me == n_mp - 1))
                def _():
                    pass_on(s, c, right_id).wait_recv()

                move(0, c, s).start()
                move(1, c, s).start()
            if stage == 2:
                move(0, c, s, True).wait_recv()
                move(1, c, s, True).wait_recv()
                move(2, c, s).start()
                move(3, c, s).start()
            if stage == 3:
                move(2, c, s, True).wait_recv()
                move(3, c, s, True).wait_recv()
                move(4, c, s).start()
            if stage == 4:
                move(4, c, s, True).wait_recv()

    def send_from(c, ref, at):
        source = ref.at[pl.ds(at * rows, rows)]

        @pl.when(me < n_mp - 1)
        def _():
            own_copy(c, 0, right_id, source).start()

        @pl.when(me > 0)
        def _():
            own_copy(c, 1, left_id, source).start()

    def send_own(c):
        if c > 0:
            send_from(c, (w1_ref, w2_ref)[c - 1], dp_at)
        else:
            pl.when(dp_at < upper)(lambda: send_from(0, wq_ref, dp_at))
            pl.when(dp_at >= upper)(lambda: send_from(0, wp_ref, dp_at - upper))

    small_copy = modulation_start(dp_at, me, n_mp, small, small_sems)
    ada_load = lambda: pltpu.make_async_copy(ada_ref, ada_buf, local_sem.at[8])

    @pl.when(step == 0)
    def _():
        barrier = pltpu.get_barrier_semaphore()
        for target in (core_id, x_id, y_id):
            pl.semaphore_signal(barrier, inc=1, **target)

        @pl.when(me < n_mp - 1)
        def _():
            pl.semaphore_signal(barrier, inc=1, **right_id)

        @pl.when(me > 0)
        def _():
            pl.semaphore_signal(barrier, inc=1, **left_id)

        for k in range(1, n_mp):
            pl.semaphore_signal(barrier, inc=1, **at_mesh(dp_at, (me + k) % n_mp))
        ada_load().start()
        pl.semaphore_wait(barrier, 3 + line_peers(me, n_mp) + n_mp - 1)
        send_own(0)
        cond = cond_ref[...]
        low = (cond * jax.nn.sigmoid(cond)).astype(BF)
        low_ref[...] = low
        ada_load().wait()
        part = nt(low, ada_buf[...]) + rows_ref[0:1]
        pad = jnp.zeros((8 - lats - 1, part.shape[1]), F32)
        small[me] = jnp.concatenate([part, rows_ref[1:2], pad], 0)
        for k in range(1, n_mp):
            small_copy(k).start()
        for k in range(1, n_mp):
            small_copy(k, True).wait_recv()
        small_ref[...] = small[...]

    def next_weights(k):
        return pltpu.make_async_copy(all_ref.at[near_part(me, k), 0], w_buf, local_sem.at[0])

    def tick(t):
        def due(at, every):
            return jnp.where((t - at) % every == 0, (t - at) // every, -1)

        for k, at in ((0, 0), (1, 0), (2, 4)):
            nth = due(at, 3 * pace)
            event(0, jnp.where(nth < 0, -1, nth * 3 + k))
        for stage, at in ((3, 8), (2, 3), (1, 0), (4, 11)):
            event(stage, due(at, pace))
        for c in (1, 2):
            pl.when(t == 3 * pace * c - 6)(lambda: send_own(c))

    @pl.when((lat == 0) & (slot == 0))
    def _():
        def load(at):
            return pltpu.make_async_copy(
                wq_ref.at[pl.ds(at * rows, rows)],
                w_buf.at[at // 4, at // 2 % 2, at % 2],
                local_sem.at[at],
            )

        for at in range(upper):
            load(at).start()
        for at in range(upper):
            load(at).wait()

    @pl.when((lat == 0) & (slot > 0))
    def _():
        next_weights(slot).wait()

    n_heads = qkv_ref.shape[1] // 3
    local = n_heads * HEAD_DIM

    @pl.when(slot == 0)
    def _():
        dim, cols = h1_all.shape[2], small.shape[2]
        shift = small[0, pl.ds(lat, 1), :dim]
        scale = jnp.concatenate(
            [small[0, pl.ds(lat, 1), dim:], small[1, pl.ds(lat, 1), : 2 * dim - cols]], 1
        )
        mixed_one(lat_ref, shift, scale, h1_ref, h1_all, lat)

    weights = w_buf[...].reshape(8 * rows, w_buf.shape[-1])[: 3 * local]
    biases = as_column(small[near_part(me, slot), lats : lats + 1, : 2 * local])
    bias = jnp.concatenate([biases[:local], jnp.zeros((local, 1), F32), biases[local:]], 0)
    flat = nt(weights, h1_all[lat]) + bias

    def between(h):
        tick(step * n_heads + h - 1)

        @pl.when((lat == lats - 1) & (slot < n_mp - 1) & (h == n_heads))
        def _():
            next_weights(slot + 1).start()

    attend(flat, n_heads, slot, heads_ref, qkv_ref, lse_ref, between)

    @pl.when(step == n_mp * lats - 1)
    def _():
        def rest(t, carry):
            tick(t)
            return carry

        lax.fori_loop(n_mp * lats * n_heads, pace * units + 11, rest, 0)
        for k in range(1, n_mp):
            small_copy(k).wait_send()
        for c in range(3):

            @pl.when(me < n_mp - 1)
            def _():
                own_copy(c, 0, right_id).wait_send()

            @pl.when(me > 0)
            def _():
                own_copy(c, 1, left_id).wait_send()

        def drain(u, carry):
            c, s = unit(u)

            @pl.when((me > 0) & (me < n_mp - 1))
            def _():
                pass_on(s, c, right_id).wait_send()

            for kind in range(5):
                move(kind, c, s).wait_send()
            return carry

        lax.fori_loop(0, units, drain, 0)


def attn_gather(latents, condition, small_rows, ada_rows, own, n_mp):
    lat, seq, dim = latents.shape
    local = dim // n_mp
    n_heads = local // HEAD_DIM
    rows = dim // 8
    cols = ada_rows.shape[0]
    last = lat - 1
    first = lambda s, l: jnp.where(s == 0, l, last)
    part = lambda s: near_part(lax.axis_index("mp"), s)
    whole = lambda shape: pl.BlockSpec(shape, lambda s, l: (0,) * len(shape))
    any_spec = pl.BlockSpec(memory_space=pl.ANY)
    heads, qkv, lse, h1, small, cond_low, gathered = pl.pallas_call(
        attn_gather_kernel,
        grid=(n_mp, lat),
        in_specs=[
            pl.BlockSpec((1, seq, dim), lambda s, l: (first(s, l), 0, 0)),
            whole(condition.shape),
            whole(small_rows.shape),
        ]
        + [any_spec] * 5,
        out_specs=[
            pl.BlockSpec((1, 1, local, seq), lambda s, l: (part(s), l, 0, 0)),
            pl.BlockSpec((1, 3 * n_heads, HEAD_DIM, seq), lambda s, l: (first(s, l), 0, 0, 0)),
            pl.BlockSpec((1, n_heads, seq), lambda s, l: (first(s, l), 0, 0)),
            pl.BlockSpec((1, seq, dim), lambda s, l: (first(s, l), 0, 0)),
            whole((n_mp, 8, cols)),
            whole(condition.shape),
            any_spec,
        ],
        out_shape=[
            jax.ShapeDtypeStruct((n_mp, lat, local, seq), BF),
            jax.ShapeDtypeStruct((lat, 3 * n_heads, HEAD_DIM, seq), BF),
            jax.ShapeDtypeStruct((lat, n_heads, seq), F32),
            jax.ShapeDtypeStruct((lat, seq, dim), BF),
            jax.ShapeDtypeStruct((n_mp, 8, cols), F32),
            jax.ShapeDtypeStruct(condition.shape, BF),
            jax.ShapeDtypeStruct((n_mp, 3, 2, 2, 2, rows, dim), BF),
        ],
        scratch_shapes=[
            pltpu.VMEM((lat, seq, dim), BF),
            pltpu.VMEM((2, 2, 2, rows, dim), BF),
            pltpu.VMEM(ada_rows.shape, BF),
            pltpu.VMEM((n_mp, 8, cols), F32),
            pltpu.SemaphoreType.DMA((9,)),
            pltpu.SemaphoreType.DMA((2, 3)),
            pltpu.SemaphoreType.DMA((3, n_mp)),
            pltpu.SemaphoreType.DMA((3, n_mp)),
            pltpu.SemaphoreType.DMA((5, 3, n_mp)),
            pltpu.SemaphoreType.DMA((5, 3, n_mp)),
            pltpu.SemaphoreType.DMA((2, n_mp - 1)),
        ],
        compiler_params=pltpu.CompilerParams(
            collective_id=1, has_side_effects=True, vmem_limit_bytes=62 * MIB
        ),
        name="attn_gather",
    )(latents, condition, small_rows, ada_rows, *own)
    return heads, qkv, lse, h1, small, cond_low, gathered.reshape(n_mp, 3, dim, dim)


def attn_fwd(me, latents, mod, gathered, bias, n_mp):
    lat, seq, dim = latents.shape
    local = dim // n_mp
    n_heads = local // HEAD_DIM
    last = lat - 1
    first = lambda s, l: jnp.where(s == 0, l, last)
    return pl.pallas_call(
        attn_fwd_kernel,
        grid_spec=pltpu.PrefetchScalarGridSpec(
            num_scalar_prefetch=1,
            grid=(n_mp, lat),
            in_specs=[
                pl.BlockSpec((1, seq, dim), lambda s, l, me: (first(s, l), 0, 0)),
                pl.BlockSpec((1, 6, dim), lambda s, l, me: (l, 0, 0)),
                pl.BlockSpec(
                    (1, 3 * local, dim), lambda s, l, me: (lax.rem(me[0] + s, n_mp), 0, 0)
                ),
                pl.BlockSpec((1, 1, 3 * local), lambda s, l, me: (lax.rem(me[0] + s, n_mp), 0, 0)),
            ],
            out_specs=[
                pl.BlockSpec(
                    (1, 1, local, seq), lambda s, l, me: (lax.rem(me[0] + s, n_mp), l, 0, 0)
                ),
                pl.BlockSpec(
                    (1, 3 * n_heads, HEAD_DIM, seq), lambda s, l, me: (first(s, l), 0, 0, 0)
                ),
                pl.BlockSpec((1, n_heads, seq), lambda s, l, me: (first(s, l), 0, 0)),
                pl.BlockSpec((1, seq, dim), lambda s, l, me: (first(s, l), 0, 0)),
            ],
            scratch_shapes=[pltpu.VMEM((lat, seq, dim), BF)],
        ),
        out_shape=[
            jax.ShapeDtypeStruct((n_mp, lat, local, seq), BF),
            jax.ShapeDtypeStruct((lat, 3 * n_heads, HEAD_DIM, seq), BF),
            jax.ShapeDtypeStruct((lat, n_heads, seq), F32),
            jax.ShapeDtypeStruct((lat, seq, dim), BF),
        ],
        compiler_params=pltpu.CompilerParams(vmem_limit_bytes=60 * MIB),
        name="attn_fwd",
    )(me, latents, mod, gathered, bias)


class LineSum:
    def __init__(self, own_ref, up, down, sems, out_ref, lag=2):
        self.lag = lag
        self.own, self.up, self.down, self.sems, self.out = own_ref, up, down, sems, out_ref
        self.count, self.rows = up.shape[0], up.shape[1]
        self.me = lax.axis_index("mp")
        self.n = lax.axis_size("mp")
        dp_at = lax.axis_index("dp")
        self.ends = (at_mesh(dp_at, self.me + 1), at_mesh(dp_at, self.me - 1))
        self.place = (self.me, self.n - 1 - self.me)

    def guarded(self, side, first, action):
        there = self.place[side] > 0 if first else self.place[side] < self.n - 1

        @pl.when(there)
        def _():
            action()

    def greet(self):
        sem = pltpu.get_barrier_semaphore()
        for side in (0, 1):
            self.guarded(side, False, lambda: pl.semaphore_signal(sem, inc=1, **self.ends[side]))

    def barrier(self):
        self.greet()
        pl.semaphore_wait(pltpu.get_barrier_semaphore(), line_peers(self.me, self.n))

    def copy(self, side, c):
        ref = (self.up, self.down)[side].at[c]
        return pltpu.make_async_remote_copy(
            ref, ref, self.sems.at[2 * side, c], self.sems.at[2 * side + 1, c], **self.ends[side]
        )

    def handle(self, side, c):
        ref = (self.up, self.down)[side]
        own = self.own[0, pl.ds(pl.multiple_of(c * self.rows, self.rows), self.rows)]

        @pl.when(self.place[side] == 0)
        def _():
            ref[c] = own

        @pl.when(self.place[side] > 0)
        def _():
            self.copy(side, c).wait_recv()
            ref[c] = (ref[c].astype(F32) + own.astype(F32)).astype(BF)

        self.guarded(side, False, lambda: self.copy(side, c).start())

    def tick(self, t):
        for side in (0, 1):
            at = t - self.lag * self.place[side]

            @pl.when((at >= 0) & (at % 3 < 2) & (at - at // 3 < self.count))
            def _():
                self.handle(side, at - at // 3)

    def finish(self, ticks):
        for side in (0, 1):
            done = jnp.maximum(ticks - self.lag * self.place[side], 0)
            done = jnp.minimum(done - done // 3, self.count)

            def late(c, carry):
                self.handle(side, c)
                return carry

            lax.fori_loop(done, self.count, late, 0)

        def add(c, carry):
            rows = pl.ds(pl.multiple_of(c * self.rows, self.rows), self.rows)
            total = self.up[c].astype(F32) + self.down[c].astype(F32)
            self.out[0, rows] = (total - self.own[0, rows].astype(F32)).astype(BF)
            return carry

        lax.fori_loop(0, self.count, add, 0)
        for side in (0, 1):

            def sent(c, carry):
                self.copy(side, c).wait_send()
                return carry

            self.guarded(side, False, lambda: lax.fori_loop(0, self.count, sent, 0))


def mlp_kernel(*refs, summing):
    heads_ref, lat_ref, cot_ref, mod_ref, bp_ref, b1_ref, b2_ref = refs[:7]
    own_refs, (wq_all, w1_all, w2_all), refs = refs[7:10], refs[10:13], refs[13:]
    if summing:
        part_ref, refs = refs[0], refs[1:]
    out_ref, dx1_ref, da_ref, h2_ref, dm_ref, z_ref, du_ref, stats_ref, dusum_ref = refs[:9]
    refs = refs[9:]
    if summing:
        sum_ref, refs = refs[0], refs[1:]
    macc, dacc, wp, w1, w2, load_sems = refs[:6]
    n_mp, hid, dim = w2.shape
    local = wp.shape[1]
    rows = lat_ref.shape[1]
    me = lax.axis_index("mp")
    step = pl.program_id(0)
    line = LineSum(part_ref, refs[6], refs[7], refs[8], sum_ref) if summing else None

    def load(kind, k):
        slot = (me + k) % n_mp
        source = own_refs[kind]
        if k > 0:
            stack = (wq_all, w1_all, w2_all)[kind]
            source = stack.at[slot, kind] if len(stack.shape) == 4 else stack.at[slot]
        if k > 0 and kind == 0:
            source = source.at[pl.ds(3 * local, local)]
        ref = (wp.at[slot], w1.at[k], w2.at[k])[kind]
        return pltpu.make_async_copy(source, ref, load_sems.at[kind, k])

    @pl.when(step == 0)
    def _():
        if summing:
            line.barrier()
        for k in range(n_mp):
            load(0, k).start()
        for k in range(n_mp):
            load(1, k).start()
            load(2, k).start()
        for k in range(n_mp):
            load(0, k).wait()

    gate_one, shift_two = mod_ref[0, 2:3], mod_ref[0, 3:4]
    scale_two, gate_two = mod_ref[0, 4:5], mod_ref[0, 5:6]
    heads = heads_ref[:, 0].reshape(dim, rows)
    attn = tn(heads, wp[...].reshape(dim, dim)) + bp_ref[...]
    x1 = lat_ref[0].astype(F32) + gate_one * attn
    n2, inv2 = norm_stats(x1)
    h2 = (n2 * (1.0 + scale_two) + shift_two).astype(BF)
    h2_ref[0] = h2
    cot = cot_ref[0].astype(F32)
    dm = (gate_two * cot).astype(BF)
    dm_ref[0] = dm

    macc[...] = jnp.zeros_like(macc)
    dacc[...] = jnp.zeros_like(dacc)

    def part(k, own):
        if summing:
            line.tick(step * n_mp + k)

        @pl.when(step == 0)
        def _():
            for kind in (1, 2):
                ref = (w1, w2)[kind - 1].at[k]
                pltpu.make_async_copy(ref, ref, load_sems.at[kind, k]).wait()

        u = mm(h2_ref[0], w1[k]) + b1_ref[(me + k) % n_mp]
        dz = nt(dm_ref[0], w2[k])
        u2 = u * u
        t = jnp.tanh(u * (GELU_A + (GELU_A * GELU_B) * u2))
        half = 0.5 + 0.5 * t
        z = (u * half).astype(BF)
        slope = half + u * (1.0 - t * t) * (0.5 * GELU_A + (1.5 * GELU_A * GELU_B) * u2)
        du = dz * slope
        if own:
            before = jnp.where(step == 0, 0.0, dusum_ref[0])
            dusum_ref[0] = before + jnp.sum(du, 0, keepdims=True)
        du = du.astype(BF)
        if own:
            z_ref[0] = z
            du_ref[0] = du
        macc[...] += mm(z, w2[k])
        dacc[...] += nt(du, w1[k])

    part(0, True)

    for k in range(1, n_mp):
        part(k, False)
    mlp = macc[...] + b2_ref[...]
    out_ref[0] = (x1 + gate_two * mlp).astype(BF)
    dh2 = dacc[...]
    dx1 = cot + norm_back(n2, inv2, dh2 * (1.0 + scale_two))
    dx1_ref[0] = dx1.astype(BF)
    da_ref[0] = (gate_one * dx1).astype(BF)
    total = lambda v: jnp.sum(v, 0, keepdims=True)
    stats = jnp.concatenate(
        [
            total(dx1 * attn),
            total(dh2),
            total(dh2 * n2),
            total(cot * mlp),
            total(cot),
            total(dx1),
            jnp.zeros((2, dim), F32),
        ],
        0,
    )

    @pl.when(step == 0)
    def _():
        stats_ref[0] = stats

    @pl.when(step > 0)
    def _():
        stats_ref[0] += stats

    if summing:

        @pl.when(step == pl.num_programs(0) - 1)
        def _():
            line.finish(pl.num_programs(0) * n_mp)


LINE_CHUNKS = 8


def line_scratch(seq, dim):
    rows = seq // LINE_CHUNKS
    return [
        pltpu.VMEM((LINE_CHUNKS, rows, dim), BF),
        pltpu.VMEM((LINE_CHUNKS, rows, dim), BF),
        pltpu.SemaphoreType.DMA((4, LINE_CHUNKS)),
    ]


def mlp_both(index, heads, latents, cotangent, mod, biases, own, gathered, n_mp, rows, part):
    lat, seq, dim = latents.shape
    local = dim // n_mp
    hid = biases[1].shape[2]
    tok = pl.BlockSpec((1, rows, dim), lambda t: (index, t, 0))
    new = pl.BlockSpec((1, rows, dim), lambda t: (0, t, 0))
    hidden = pl.BlockSpec((1, rows, hid), lambda t: (0, t, 0))
    once = lambda shape: pl.BlockSpec(
        shape, lambda t: (0,) * len(shape), pipeline_mode=pl.Buffered(1)
    )
    any_spec = pl.BlockSpec(memory_space=pl.ANY)
    summing = part is not None
    extra = [once((1, seq, dim))] if summing else []
    return pl.pallas_call(
        functools.partial(mlp_kernel, summing=summing),
        grid=(seq // rows,),
        in_specs=[
            pl.BlockSpec((n_mp, 1, local, rows), lambda t: (0, index, 0, t)),
            tok,
            tok,
            pl.BlockSpec((1, 6, dim), lambda t: (index, 0, 0)),
            once((1, dim)),
            once((n_mp, 1, hid)),
            once((1, dim)),
        ]
        + [any_spec] * 6
        + extra,
        out_specs=[new] * 5
        + [
            hidden,
            hidden,
            pl.BlockSpec((1, 8, dim), lambda t: (0, 0, 0)),
            pl.BlockSpec((1, 1, hid), lambda t: (0, 0, 0)),
        ]
        + extra,
        out_shape=[jax.ShapeDtypeStruct((1, seq, dim), BF)] * 5
        + [jax.ShapeDtypeStruct((1, seq, hid), BF)] * 2
        + [jax.ShapeDtypeStruct((1, 8, dim), F32), jax.ShapeDtypeStruct((1, 1, hid), F32)]
        + ([jax.ShapeDtypeStruct((1, seq, dim), BF)] if summing else []),
        scratch_shapes=[
            pltpu.VMEM((rows, dim), F32),
            pltpu.VMEM((rows, dim), F32),
            pltpu.VMEM((n_mp, local, dim), BF),
            pltpu.VMEM((n_mp, dim, hid), BF),
            pltpu.VMEM((n_mp, hid, dim), BF),
            pltpu.SemaphoreType.DMA((3, n_mp)),
        ]
        + (line_scratch(seq, dim) if summing else []),
        compiler_params=pltpu.CompilerParams(
            vmem_limit_bytes=63 * MIB,
            **(dict(collective_id=4 + index, has_side_effects=True) if summing else {}),
        ),
        name="mlp_sum" if summing else "mlp_both",
    )(
        heads,
        latents,
        cotangent,
        mod,
        *biases,
        *own,
        *gathered,
        *([part] if summing else []),
    )


class CubeSum:
    def __init__(self, terms, full, halves, firsts, seconds, sems):
        self.terms, self.full = terms, full
        self.halves, self.firsts, self.seconds, self.sems = halves, firsts, seconds, sems
        self.units = halves.shape[0]
        dp_at, me = lax.axis_index("dp"), lax.axis_index("mp")
        self.core, x, y = dp_at % 2, dp_at // 2 % 2, dp_at // 4
        self.core_id = at_mesh(flip(dp_at, 0), me)
        x_id, y_id = at_mesh(flip(dp_at, 1), me), at_mesh(flip(dp_at, 2), me)
        self.ids = ((x_id, y_id), (y_id, x_id))
        self.place = ((x, y), (y, x))

    def barrier(self):
        sem = pltpu.get_barrier_semaphore()
        for target in (self.core_id,) + self.ids[0]:
            pl.semaphore_signal(sem, inc=1, **target)

    def blocks(self, u, core, q=None, first=None, second=None):
        at, count = 16 * u + 8 * core, 8
        if q is not None:
            at, count = at + 4 * q, 4
        if first is not None:
            at, count = at + 2 * first, 2
        if second is not None:
            at, count = at + second, 1
        return pl.ds(at, count)

    def send(self, stage, u, q, arrived=False):
        core, blocks = self.core, self.blocks
        first, second = self.place[q]
        other = lambda v: 1 - v if arrived else v
        if stage == 0:
            pair = (self.terms.at[blocks(u, 1 - core)], self.halves.at[u])
        elif stage == 1:
            pair = (self.terms.at[blocks(u, core, q, 1 - first)], self.firsts.at[u, q])
        elif stage == 2:
            pair = (self.terms.at[blocks(u, core, q, first, 1 - second)], self.seconds.at[u, q])
        elif stage == 3:
            pair = (self.full.at[blocks(u, core, q, first, other(second))],) * 2
        elif stage == 4:
            pair = (self.full.at[blocks(u, core, q, other(first))],) * 2
        else:
            pair = (self.full.at[blocks(u, other(core))],) * 2
        near, far = self.ids[q]
        target = (self.core_id, near, far, far, near, self.core_id)[stage]
        return pltpu.make_async_remote_copy(
            *pair, self.sems.at[0, stage, q, u], self.sems.at[1, stage, q, u], **target
        )

    def quarters(self, stage):
        return (0,) if stage in (0, 5) else (0, 1)

    def event(self, stage, u):
        terms, core, blocks = self.terms, self.core, self.blocks

        @pl.when((u >= 0) & (u < self.units))
        def _():
            if stage > 0:
                for q in self.quarters(stage - 1):
                    self.send(stage - 1, u, q, True).wait_recv()
            if stage == 1:
                at = blocks(u, core)
                terms[at] = (terms[at].astype(F32) + self.halves[u].astype(F32)).astype(BF)
            for q in (0, 1):
                first, second = self.place[q]
                if stage == 2:
                    at = blocks(u, core, q, first)
                    terms[at] = (terms[at].astype(F32) + self.firsts[u, q].astype(F32)).astype(BF)
                if stage == 3:
                    at = blocks(u, core, q, first, second)
                    total = terms[at].astype(F32) + self.seconds[u, q].astype(F32)
                    self.full[at] = total.astype(BF)
            if stage < 6:
                for q in self.quarters(stage):
                    self.send(stage, u, q).start()

    def finish(self):
        def sent(u, carry):
            for stage in range(6):
                for q in self.quarters(stage):
                    self.send(stage, u, q).wait_send()
            return carry

        lax.fori_loop(0, self.units, sent, 0)


BLOCK = 32


class WeightGrads:
    def __init__(self, operands, terms, right, left_cols, left_rows, right_sems, left_sems):
        self.operands, self.terms, self.right = operands, terms, right
        self.left_cols, self.left_rows = left_cols, left_rows
        self.right_sems, self.left_sems = right_sems, left_sems
        self.lats = right.shape[1]
        dim = right.shape[3]
        qkv_blocks = operands[2][0][0].shape[0] // BLOCK
        half = (qkv_blocks + 1) // 2 * BLOCK
        third = dim // 3
        self.pieces = [(job, i * third, third) for job in (0, 1) for i in range(3)]
        self.pieces += [(2, 0, half), (2, half, qkv_blocks * BLOCK - half)]
        self.pieces += [(3, 0, operands[3][0][0].shape[0])]

    def right_copies(self, job):
        slot = job % 2
        return [
            pltpu.make_async_copy(
                self.operands[job][1][i], self.right.at[slot, i], self.right_sems.at[slot, i]
            )
            for i in range(self.lats)
        ]

    def left_copies(self, at):
        job, first, count = self.pieces[at]
        copies = []
        for i in range(self.lats):
            source = self.operands[job][0][i]
            if job < 2:
                source = source.at[:, pl.ds(first, count)]
                ref = self.left_cols.at[at % 2, i]
            else:
                source = source.at[pl.ds(first, count)]
                ref = self.left_rows.at[at % 2, i, pl.ds(0, count)]
            copies.append(pltpu.make_async_copy(source, ref, self.left_sems.at[at % 2, i]))
        return copies

    def begin(self):
        for copy in self.right_copies(0) + self.left_copies(0):
            copy.start()

    def compute(self, at):
        job, _, count = self.pieces[at]
        opens = at == 0 or self.pieces[at - 1][0] != job
        if at + 1 < len(self.pieces):
            for copy in self.left_copies(at + 1):
                copy.start()
        if opens:
            if job + 1 < len(self.operands):
                for copy in self.right_copies(job + 1):
                    copy.start()
            for copy in self.right_copies(job):
                copy.wait()
        for copy in self.left_copies(at):
            copy.wait()
        slot, dim = job % 2, self.right.shape[3]
        if job < 2:
            left = self.left_cols[at % 2].reshape(-1, count)
            total = tn(left, self.right[slot].reshape(-1, dim))
        else:
            total = mm(self.left_rows[at % 2, 0, :count], self.right[slot, 0])
            for i in range(1, self.lats):
                total = total + mm(self.left_rows[at % 2, i, :count], self.right[slot, i])
        done = sum(rows for _, _, rows in self.pieces[:at]) // BLOCK
        self.terms[pl.ds(done, count // BLOCK)] = total.reshape(-1, BLOCK, dim).astype(BF)


def tail_kernel(*refs, lats):
    part_ref, bias_ref, heads_ref, h1_ref = refs[:4]
    lists = [refs[4 + i * lats : 4 + (i + 1) * lats] for i in range(6)]
    h2s, dus, zs, dms, dqkvs, das = [[ref.at[0] for ref in group] for group in lists]
    sum_ref, *total_refs = refs[4 + 6 * lats : 10 + 6 * lats]
    refs = refs[10 + 6 * lats :]
    up, down, line_sems, terms, full, halves, firsts, seconds, cube_sems = refs[:9]
    right, left_cols, left_rows, right_sems, left_sems, local_sem = refs[9:]
    line = LineSum(part_ref, up, down, line_sems, sum_ref, 3)
    cube = CubeSum(terms, full, halves, firsts, seconds, cube_sems)
    heads = [heads_ref.at[line.me, i] for i in range(lats)]
    h1s = [h1_ref.at[i] for i in range(lats)]
    grads = WeightGrads(
        ((h2s, dus), (zs, dms), (dqkvs, h1s), (heads, das)),
        terms,
        right,
        left_cols,
        left_rows,
        right_sems,
        left_sems,
    )
    grads.begin()
    cube.barrier()
    line.greet()
    pl.semaphore_wait(pltpu.get_barrier_semaphore(), 3 + line_peers(line.me, line.n))
    spare = bias_ref.shape[0]
    terms[pl.ds(terms.shape[0] - spare, spare)] = bias_ref[...]
    line.tick(0)
    unit_rows = 16 * BLOCK
    ready = 0
    for t in range(cube.units):
        line.tick(2 * t + 1)
        while ready < len(grads.pieces) and (
            sum(rows for _, _, rows in grads.pieces[:ready]) < (t + 1) * unit_rows
        ):
            grads.compute(ready)
            ready += 1
        line.tick(2 * t + 2)
        for stage in range(min(t, 6), -1, -1):
            cube.event(stage, t - stage)

    def advance(t, carry):
        line.tick(2 * t + 1)
        for stage in range(6, 0, -1):
            cube.event(stage, t - stage)
        line.tick(2 * t + 2)
        return carry

    lax.fori_loop(cube.units, cube.units + 6, advance, 0)
    stores = []
    first = 0
    for i, ref in enumerate(total_refs):
        source = full.at[pl.ds(first, ref.shape[0])]
        stores.append(pltpu.make_async_copy(source, ref, local_sem.at[i]))
        stores[-1].start()
        first += ref.shape[0]
    line.finish(2 * (cube.units + 6) + 1)
    cube.finish()
    for store in stores:
        store.wait()


def tail_sums(part, biases, heads, h1, lists):
    n_mp, lats, local, seq = heads.shape
    dim = h1.shape[2]
    rows = 2 * dim + 4 * local
    units = -(-(rows + BLOCK) // (16 * BLOCK))
    spare = units * 16 - rows // BLOCK
    biases = jnp.pad(biases, ((0, spare * BLOCK - biases.shape[0]), (0, 0)))
    vmem = pl.BlockSpec(memory_space=pltpu.VMEM)
    any_spec = pl.BlockSpec(memory_space=pl.ANY)
    shape = (units * 16, BLOCK, dim)
    flat = [array for group in lists for array in group]
    counts = [dim // BLOCK, dim // BLOCK, 3 * local // BLOCK, local // BLOCK, spare]
    total, *grads = pl.pallas_call(
        functools.partial(tail_kernel, lats=lats),
        in_specs=[vmem, vmem] + [any_spec] * (2 + len(flat)),
        out_specs=[vmem] + [any_spec] * len(counts),
        out_shape=[jax.ShapeDtypeStruct(part.shape, BF)]
        + [jax.ShapeDtypeStruct((count, BLOCK, dim), BF) for count in counts],
        scratch_shapes=line_scratch(seq, dim)
        + [
            pltpu.VMEM(shape, BF),
            pltpu.VMEM(shape, BF),
            pltpu.VMEM((units, 8, BLOCK, dim), BF),
            pltpu.VMEM((units, 2, 2, BLOCK, dim), BF),
            pltpu.VMEM((units, 2, 1, BLOCK, dim), BF),
            pltpu.SemaphoreType.DMA((2, 6, 2, units)),
            pltpu.VMEM((2, lats, seq, dim), BF),
            pltpu.VMEM((2, lats, seq, dim // 3), BF),
            pltpu.VMEM((2, lats, (3 * local // BLOCK + 1) // 2 * BLOCK, seq), BF),
            pltpu.SemaphoreType.DMA((2, lats)),
            pltpu.SemaphoreType.DMA((2, lats)),
            pltpu.SemaphoreType.DMA((len(counts),)),
        ],
        compiler_params=pltpu.CompilerParams(
            collective_id=2, has_side_effects=True, vmem_limit_bytes=63 * MIB
        ),
        name="tail_sums",
    )(part, biases.reshape(spare, BLOCK, dim), heads, h1, *flat)
    return total, [grad.reshape(-1, dim) for grad in grads]


def rows_kernel(rows_ref, act_ref, every_ref, total_ref, acts, sems):
    dp_at, me = lax.axis_index("dp"), lax.axis_index("mp")
    n_dp, n_mp = every_ref.shape[0], acts.shape[0]
    barrier = pltpu.get_barrier_semaphore()
    for k in range(1, n_dp):
        pl.semaphore_signal(barrier, inc=1, **at_mesh((dp_at + k) % n_dp, me))
    for k in range(1, n_mp):
        pl.semaphore_signal(barrier, inc=1, **at_mesh(dp_at, (me + k) % n_mp))
    every_ref[dp_at] = rows_ref[...]
    acts[me] = act_ref[...]
    pl.semaphore_wait(barrier, n_dp + n_mp - 2)

    def copy(ref, k, target):
        return pltpu.make_async_remote_copy(ref, ref, sems.at[0, k], sems.at[1, k], **target)

    def act_copy(k, source):
        return copy(acts.at[source % n_mp], k - 1, at_mesh(dp_at, (me + k) % n_mp))

    def row_copy(k, source):
        target = at_mesh((dp_at + k) % n_dp, me)
        return copy(every_ref.at[source % n_dp], n_mp + k - 2, target)

    for k in range(1, n_mp):
        act_copy(k, me).start()
    for k in range(1, n_dp):
        row_copy(k, dp_at).start()
    for k in range(1, n_mp):
        act_copy(k, me + n_mp - k).wait_recv()
    total = acts[0]
    for i in range(1, n_mp):
        total = total + acts[i]
    total_ref[...] = total
    for k in range(1, n_dp):
        row_copy(k, dp_at + n_dp - k).wait_recv()
    for k in range(1, n_mp):
        act_copy(k, me).wait_send()
    for k in range(1, n_dp):
        row_copy(k, dp_at).wait_send()


def rows_exchange(rows, act, n_dp, n_mp):
    vmem = pl.BlockSpec(memory_space=pltpu.VMEM)
    return pl.pallas_call(
        rows_kernel,
        in_specs=[vmem, vmem],
        out_specs=[vmem, vmem],
        out_shape=[
            jax.ShapeDtypeStruct((n_dp,) + rows.shape, rows.dtype),
            jax.ShapeDtypeStruct(act.shape, act.dtype),
        ],
        scratch_shapes=[
            pltpu.VMEM((n_mp,) + act.shape, act.dtype),
            pltpu.SemaphoreType.DMA((2, n_dp + n_mp - 2)),
        ],
        compiler_params=pltpu.CompilerParams(
            collective_id=3, has_side_effects=True, vmem_limit_bytes=40 * MIB
        ),
        name="rows_exchange",
    )(rows, act)


def attn_bwd_kernel(da_ref, heads_ref, qkv_ref, lse_ref, wp_ref, wq_ref, dqkv_ref, dh1_ref, bias_ref, *, rows):
    n_heads = lse_ref.shape[1]
    seq = da_ref.shape[1]
    dheads = nt(wp_ref[...], da_ref[0]).reshape(n_heads, HEAD_DIM, seq)
    heads = heads_ref[0, 0].astype(F32).reshape(n_heads, HEAD_DIM, seq)
    scaling = 1.0 / HEAD_DIM**0.5
    dq_list, dk_list, dv_list = [], [], []
    for h in range(n_heads):
        q_t = qkv_ref[0, h]
        k_t = qkv_ref[0, n_heads + h]
        v_t = qkv_ref[0, 2 * n_heads + h]
        q = q_t.astype(F32).T.astype(BF)
        k = k_t.astype(F32).T.astype(BF)
        v = v_t.astype(F32).T.astype(BF)
        do_t = dheads[h].astype(BF)
        do = dheads[h].T.astype(BF)
        inner = jnp.sum(do_t.astype(F32) * heads[h], 0, keepdims=True)
        dq_parts = []
        for i in range(seq // rows):
            cols = slice(i * rows, (i + 1) * rows)
            probs = jnp.exp2(mm(k, q_t[:, cols]) - lse_ref[0, h : h + 1, cols])
            dprobs = mm(v, do_t[:, cols])
            dscores = (probs * (dprobs - inner[:, cols])).astype(BF)
            dq_parts.append(mm(k_t, dscores))
            dv_new = mm(probs.astype(BF), do[cols])
            dk_new = mm(dscores, q[cols])
            dv = dv_new if i == 0 else dv + dv_new
            dk = dk_new if i == 0 else dk + dk_new
        dq_list.append(jnp.concatenate(dq_parts, 1) * scaling)
        dk_list.append(dk.T * (1.0 / LOG2E))
        dv_list.append(dv.T)
    dqkv = jnp.concatenate(dq_list + dk_list + dv_list, 0)
    bias_ref[0] = jnp.sum(dqkv, 1, keepdims=True)
    dqkv = dqkv.astype(BF)
    dqkv_ref[0] = dqkv
    dh1_ref[0] = tn(dqkv, wq_ref[...]).astype(BF)


def attn_bwd(da, heads, qkv, lse, wp, wq, index, rows):
    lat, seq, dim = da.shape
    n_heads = lse.shape[1]
    local = n_heads * HEAD_DIM
    one = lambda shape: pl.BlockSpec((1,) + shape, lambda i: (index,) + (0,) * len(shape))
    only = lambda shape: pl.BlockSpec((1,) + shape, lambda i: (0,) * (len(shape) + 1))
    whole = lambda shape: pl.BlockSpec(shape, lambda i: (0,) * len(shape))
    out = lambda shape: pl.BlockSpec((1,) + shape, lambda i: (0,) * (len(shape) + 1))
    return pl.pallas_call(
        functools.partial(attn_bwd_kernel, rows=rows),
        grid=(1,),
        in_specs=[
            only((seq, dim)),
            pl.BlockSpec((1, 1, local, seq), lambda i: (lax.axis_index("mp"), index, 0, 0)),
            one((3 * n_heads, HEAD_DIM, seq)),
            one((n_heads, seq)),
            whole((local, dim)),
            whole((3 * local, dim)),
        ],
        out_specs=[out((3 * local, seq)), out((seq, dim)), out((3 * local, 1))],
        out_shape=[
            jax.ShapeDtypeStruct((1, 3 * local, seq), BF),
            jax.ShapeDtypeStruct((1, seq, dim), BF),
            jax.ShapeDtypeStruct((1, 3 * local, 1), F32),
        ],
        compiler_params=pltpu.CompilerParams(vmem_limit_bytes=60 * MIB),
        name="attn_bwd",
    )(da, heads, qkv, lse, wp, wq)


def latents_kernel(*refs, lats):
    lat_ref, mod_ref = refs[:2]
    dh1_refs, dx1_refs, out_refs = [refs[2 + i * lats : 2 + (i + 1) * lats] for i in range(3)]
    grad_ref, stats_ref, out_ref = refs[2 + 3 * lats :]
    lat, step = pl.program_id(0), pl.program_id(1)
    n1, inv1 = norm_stats(lat_ref[0].astype(F32))
    for i in range(lats):

        @pl.when(lat == i)
        def _():
            dh1 = dh1_refs[i][0].astype(F32)
            back = norm_back(n1, inv1, dh1 * (1.0 + mod_ref[0, 1:2]))
            grad_ref[0] = (dx1_refs[i][0].astype(F32) + back).astype(BF)
            out_ref[0] = out_refs[i][0]
            pad = jnp.zeros((6, dh1.shape[1]), F32)
            sums = [jnp.sum(dh1, 0, keepdims=True), jnp.sum(dh1 * n1, 0, keepdims=True), pad]
            stats_ref[0] = jnp.where(step == 0, 0.0, stats_ref[0]) + jnp.concatenate(sums, 0)


def latents_back(dh1, dx1, outs, latents, mod, rows):
    lat, seq, dim = latents.shape
    steps = seq // rows
    tok = pl.BlockSpec((1, rows, dim), lambda l, t: (l, t, 0))
    at = lambda i: (lambda l, t: (0, jnp.where(l < i, 0, jnp.where(l == i, t, steps - 1)), 0))
    each = [pl.BlockSpec((1, rows, dim), at(i)) for i in range(lat)]
    return pl.pallas_call(
        functools.partial(latents_kernel, lats=lat),
        grid=(lat, steps),
        in_specs=[tok, pl.BlockSpec((1, 6, dim), lambda l, t: (l, 0, 0))] + each * 3,
        out_specs=[tok, pl.BlockSpec((1, 8, dim), lambda l, t: (l, 0, 0)), tok],
        out_shape=[
            jax.ShapeDtypeStruct((lat, seq, dim), BF),
            jax.ShapeDtypeStruct((lat, 8, dim), F32),
            jax.ShapeDtypeStruct((lat, seq, dim), BF),
        ],
        compiler_params=pltpu.CompilerParams(vmem_limit_bytes=63 * MIB),
        name="latents_back",
    )(latents, mod, *dh1, *dx1, *outs)


def per_device(
    n_dp,
    n_mp,
    latents,
    condition,
    cotangent,
    qkv_weight,
    qv_bias,
    proj_weight,
    proj_bias,
    fc1_weight,
    fc1_bias,
    fc2_weight,
    fc2_bias,
    ada_weight,
    ada_bias,
):
    lat, seq, dim = latents.shape
    local = qkv_weight.shape[2]
    n_heads = local // HEAD_DIM
    hid = fc1_weight.shape[1]
    cols = ada_weight.shape[1]
    mp_at = lax.axis_index("mp")
    dp_at = lax.axis_index("dp")
    me = jnp.full((1,), mp_at, jnp.int32)

    direct = n_mp == 4 and n_dp == 8
    bias_row = jnp.concatenate([qv_bias.reshape(-1), fc1_bias]).astype(F32)[None]
    ada_row = ada_bias.astype(F32)[None]
    wq_own = (
        qkv_weight.reshape(dim, 3, n_heads, HEAD_DIM).transpose(1, 2, 3, 0).reshape(3 * local, dim)
    )
    if direct:
        own = (wq_own, proj_weight, fc1_weight, fc2_weight)
        small_rows = jnp.concatenate([ada_row, bias_row], 0)
        heads, qkv, lse, h1, small, cond_low, gathered = attn_gather(
            latents, condition, small_rows, ada_weight.T, own, n_mp
        )
        gathered = (gathered,) * 3
    else:
        cond_low = jax.nn.silu(condition).astype(BF)
        mod_part = mm(cond_low, ada_weight) + ada_row
        small = lax.all_gather(jnp.concatenate([mod_part, bias_row], 0), "mp", axis=0)
    mod = small[:, :lat].transpose(1, 0, 2).reshape(lat, 6, dim)
    b_fc1 = small[:, lat, 2 * local :].reshape(n_mp, 1, hid)
    if not direct:
        qv_all = small[:, lat, : 2 * local].reshape(n_mp, 2, local)
        b_qkv = jnp.stack([qv_all[:, 0], jnp.zeros((n_mp, local), F32), qv_all[:, 1]], 1)
        b_qkv = b_qkv.reshape(n_mp, 1, 3 * local)

        def gather(weight):
            share = weight.shape[0] // n_dp
            mine = lax.dynamic_slice_in_dim(weight, dp_at * share, share, 0)
            whole = lax.all_gather(mine, ("dp", "mp"), axis=0)
            whole = whole.reshape(n_dp, n_mp, share, weight.shape[1]).transpose(1, 0, 2, 3)
            return whole.reshape(n_mp, weight.shape[0], weight.shape[1])

        gathered = (
            gather(jnp.concatenate([wq_own, proj_weight], 0)),
            gather(fc1_weight),
            gather(fc2_weight),
        )
        heads, qkv, lse, h1 = attn_fwd(me, latents, mod, gathered[0], b_qkv, n_mp)
    rows = min(256, seq)
    results, dqkv, dh1, bias_sums = [], [], [], []
    for i in range(lat):
        waiting = dqkv and direct
        outs = mlp_both(
            i,
            heads,
            latents,
            cotangent,
            mod,
            (proj_bias.astype(F32)[None], b_fc1, fc2_bias.astype(F32)[None]),
            (proj_weight, fc1_weight, fc2_weight),
            gathered,
            n_mp,
            rows,
            dh1_i if waiting else None,
        )
        if waiting:
            dh1.append(outs[-1])
        results.append(outs[:9])
        dqkv_i, dh1_i, sums_i = attn_bwd(
            outs[2], heads, qkv, lse, proj_weight, wq_own, i, min(512, seq)
        )
        dqkv.append(dqkv_i)
        bias_sums.append(sums_i)
        if not direct:
            dh1.append(lax.psum(dh1_i, "mp"))
    outs_by_kind = list(zip(*results))
    h2, dm, z, du = outs_by_kind[3:7]
    da = outs_by_kind[2]
    stats_two = jnp.concatenate(outs_by_kind[7], 0)
    grad_fc1_bias = sum(outs_by_kind[8])[0, 0]
    gate_one, gate_two = mod[:, 2], mod[:, 5]
    grad_fc2_bias = jnp.sum(gate_two * stats_two[:, 4], 0)
    grad_proj_bias = jnp.sum(gate_one * stats_two[:, 5], 0)
    bias_sums = sum(bias_sums).reshape(3, local)
    grad_qv_bias = jnp.stack([bias_sums[0], bias_sums[2]])
    if direct:
        bias_rows = jnp.stack(
            [
                grad_fc1_bias,
                grad_fc2_bias,
                grad_proj_bias,
                jnp.pad(grad_qv_bias.reshape(-1), (0, dim - 2 * local)),
            ]
        ).astype(BF)
        dh1_i, sums = tail_sums(dh1_i, bias_rows, heads, h1, (h2, du, z, dm, dqkv, da))
        dh1.append(dh1_i)
        grad_fc1, grad_fc2, grad_qkv, grad_proj, bias_rows = sums
        bias_rows = bias_rows[:4].astype(F32)
        grad_fc1_bias, grad_fc2_bias, grad_proj_bias = bias_rows[:3]
        grad_qv_bias = bias_rows[3, : 2 * local].reshape(2, local)
    else:
        flat = lambda parts: jnp.concatenate(parts, 0).reshape(lat * seq, -1)
        grad_fc2 = tn(flat(z), flat(dm))
        grad_fc1 = tn(flat(h2), flat(du))
        grad_qkv = sum(mm(dqkv[i][0], h1[i]) for i in range(lat))
        heads_own = lax.dynamic_index_in_dim(heads, mp_at, 0, keepdims=False)
        grad_proj = sum(mm(heads_own[i], da[i][0]) for i in range(lat))
        grads = [grad.astype(BF) for grad in (grad_fc1, grad_fc2, grad_qkv, grad_proj)]
        grad_fc1, grad_fc2, grad_qkv, grad_proj = lax.psum(grads, "dp")
        biases = lax.psum((grad_fc1_bias, grad_fc2_bias, grad_proj_bias, grad_qv_bias), "dp")
        grad_fc1_bias, grad_fc2_bias, grad_proj_bias, grad_qv_bias = biases

    latents_grad, stats_one, block_out = latents_back(
        dh1, outs_by_kind[1], outs_by_kind[0], latents, mod, rows
    )

    dmod = jnp.stack(
        [
            stats_one[:, 0],
            stats_one[:, 1],
            stats_two[:, 0],
            stats_two[:, 1],
            stats_two[:, 2],
            stats_two[:, 3],
        ],
        1,
    )
    dmod = dmod.reshape(lat, 6 * dim).astype(BF)
    dmod_own = lax.dynamic_slice_in_dim(dmod, mp_at * cols, cols, 1)
    both = jnp.concatenate([cond_low, dmod_own], 1)
    grad_act = nt(dmod_own, ada_weight)
    if direct:
        both = jnp.pad(both, ((0, 16 - lat), (0, 0)))
        grad_act = jnp.pad(grad_act, ((0, 8 - lat), (0, 0)))
        every, grad_act = rows_exchange(both, grad_act, n_dp, n_mp)
        every, grad_act = every.reshape(n_dp * 16, dim + cols), grad_act[:lat]
    else:
        every = lax.all_gather(both, "dp", axis=0, tiled=True)
        grad_act = lax.psum(grad_act, "mp")
    grad_ada = tn(every[:, :dim], every[:, dim:])
    grad_ada_bias = jnp.sum(every[:, dim:].astype(F32), 0)
    condition_grad = jax.vjp(jax.nn.silu, condition)[1](grad_act)[0]

    back = lambda v: v.astype(F32)
    return (
        block_out,
        latents_grad,
        condition_grad,
        back(grad_qkv).reshape(3, local, dim).transpose(2, 0, 1),
        grad_qv_bias,
        back(grad_proj),
        grad_proj_bias,
        back(grad_fc1),
        grad_fc1_bias,
        back(grad_fc2),
        grad_fc2_bias,
        grad_ada,
        grad_ada_bias,
    )


def solution(mesh):
    in_specs = (
        P("dp", None, None),
        P("dp", None),
        P("dp", None, None),
        P(None, None, "mp"),
        P(None, "mp"),
        P("mp", None),
        P(),
        P(None, "mp"),
        P("mp"),
        P("mp", None),
        P(),
        P(None, "mp"),
        P("mp"),
    )
    out_specs = (
        P("dp", None, None),
        P("dp", None, None),
        P("dp", None),
        P(None, None, "mp"),
        P(None, "mp"),
        P("mp", None),
        P(),
        P(None, "mp"),
        P("mp"),
        P("mp", None),
        P(),
        P(None, "mp"),
        P("mp"),
    )
    body = functools.partial(per_device, mesh.shape["dp"], mesh.shape["mp"])
    return jax.shard_map(body, mesh=mesh, in_specs=in_specs, out_specs=out_specs, check_vma=False)
```

```python
import functools

import jax
import jax.numpy as jnp
from jax import lax
from jax.experimental import pallas as pl
from jax.experimental.pallas import tpu as pltpu
from jax.sharding import PartitionSpec as P

HEAD_DIM = 72
EPS = 1e-06
LOG2E = 1.4426950408889634
GELU_A = 0.7978845608028654
GELU_B = 0.044715
BF = jnp.bfloat16
F32 = jnp.float32
MIB = 2**20


def mm(a, b):
    return jnp.dot(a, b, preferred_element_type=F32)


def nt(a, b):
    return lax.dot_general(a, b, (((1,), (1,)), ((), ())), preferred_element_type=F32)


def tn(a, b):
    return lax.dot_general(a, b, (((0,), (0,)), ((), ())), preferred_element_type=F32)


def norm_stats(values):
    centered = values - jnp.mean(values, -1, keepdims=True)
    inv_std = lax.rsqrt(jnp.mean(centered * centered, -1, keepdims=True) + EPS)
    return centered * inv_std, inv_std


def norm_back(normed, inv_std, grad_normed):
    first = jnp.mean(grad_normed, -1, keepdims=True)
    second = jnp.mean(grad_normed * normed, -1, keepdims=True)
    return inv_std * (grad_normed - first - normed * second)


def flip(value, bit):
    step = 1 << bit
    return value + step - 2 * step * (value // step % 2)


def near_part(me, k):
    side = me // 2
    end = jnp.minimum(me, 3 - me)
    at = k + end * (1 - 2 * k) * ((3 - k) // 2)
    return at + side * (3 - 2 * at)


def line_peers(me, n):
    return jnp.minimum(me, 1) + jnp.minimum(n - 1 - me, 1)


def at_mesh(dp_at, mp_at):
    return {"device_id": (dp_at, mp_at), "device_id_type": pl.DeviceIdType.MESH}


def modulation_start(dp_at, me, n_mp, small, sems):
    def copy(k, arrived=False):
        at = small.at[(me + n_mp - k) % n_mp if arrived else me]
        target = at_mesh(dp_at, (me + k) % n_mp)
        return pltpu.make_async_remote_copy(at, at, sems.at[0, k - 1], sems.at[1, k - 1], **target)

    return copy


def attend(flat, n_heads, slot, heads_ref, qkv_ref, lse_ref, between):
    seq = flat.shape[1]
    parts = flat.reshape(3 * n_heads, HEAD_DIM, seq)
    scaling = LOG2E / HEAD_DIM**0.5
    outs = []
    for h in range(n_heads):
        q_t = (parts[h] * scaling).astype(BF)
        k_t = parts[n_heads + h]
        v_t = parts[2 * n_heads + h]
        v_ext = jnp.concatenate([v_t, jnp.ones((8, seq), F32)], 0).astype(BF)
        scores = mm(k_t.T.astype(BF), q_t)
        top = jnp.max(scores, 0, keepdims=True)
        probs = jnp.exp2(scores - top).astype(BF)
        out = mm(v_ext, probs)
        total = out[HEAD_DIM : HEAD_DIM + 1]
        outs.append(out[:HEAD_DIM] * (1.0 / total))
        lse = top + jnp.log2(total)

        @pl.when(slot == 0)
        def _():
            qkv_ref[0, h] = q_t
            qkv_ref[0, n_heads + h] = k_t.astype(BF)
            qkv_ref[0, 2 * n_heads + h] = v_t.astype(BF)
            lse_ref[0, h : h + 1] = lse

        between(h + 1)
    heads_ref[0, 0] = jnp.concatenate(outs, 0).astype(BF)


def as_column(row):
    return jnp.broadcast_to(row, (8, row.shape[1])).T[:, :1]


def mixed_one(lat_ref, shift, scale, h1_ref, h1_all, lat):
    normed, _ = norm_stats(lat_ref[0].astype(F32))
    h1 = (normed * (1.0 + scale) + shift).astype(BF)
    h1_all[lat] = h1
    h1_ref[0] = h1


def attn_fwd_kernel(
    me_ref, lat_ref, mod_ref, w_ref, bias_ref, heads_ref, qkv_ref, lse_ref, h1_ref, h1_all
):
    slot, lat = pl.program_id(0), pl.program_id(1)

    @pl.when(slot == 0)
    def _():
        mixed_one(lat_ref, mod_ref[0, 0:1], mod_ref[0, 1:2], h1_ref, h1_all, lat)

    flat = nt(w_ref[0], h1_all[lat]) + as_column(bias_ref[0])
    attend(flat, qkv_ref.shape[1] // 3, slot, heads_ref, qkv_ref, lse_ref, lambda h: None)


def attn_gather_kernel(
    lat_ref,
    cond_ref,
    rows_ref,
    ada_ref,
    wq_ref,
    wp_ref,
    w1_ref,
    w2_ref,
    heads_ref,
    qkv_ref,
    lse_ref,
    h1_ref,
    mod_ref,
    b1_ref,
    low_ref,
    all_ref,
    h1_all,
    w_buf,
    ada_buf,
    small,
    local_sem,
    z_own,
    z_on,
    z_got,
    sends,
    recvs,
    small_sems,
):
    n_mp = all_ref.shape[0]
    lats = h1_all.shape[0]
    units, pace = 3 * (n_mp - 1), 5
    slot, lat = pl.program_id(0), pl.program_id(1)
    step = slot * lats + lat
    dp_at, me = lax.axis_index("dp"), lax.axis_index("mp")
    core, x, y = dp_at % 2, dp_at // 2 % 2, dp_at // 4
    rows = all_ref.shape[5]
    upper = wq_ref.shape[0] // rows
    cut = rows // 32 * 16 + 16
    near, far = pl.ds(0, cut), pl.ds(cut, rows - cut)
    every = pl.ds(0, rows)
    both = pl.ds(0, 2)
    core_id = at_mesh(flip(dp_at, 0), me)
    x_id = at_mesh(flip(dp_at, 1), me)
    y_id = at_mesh(flip(dp_at, 2), me)
    right_id, left_id = at_mesh(dp_at, me + 1), at_mesh(dp_at, me - 1)

    def piece(s, c, at_y, at_x, at_core, part):
        return all_ref.at[s, c, at_y, at_x, at_core, part]

    def own_copy(c, side, target, source=None):
        ref = piece(me, c, y, x, core, every)
        return pltpu.make_async_remote_copy(
            ref if source is None else source,
            ref,
            z_own.at[side, c],
            z_got.at[c, me],
            **target,
        )

    def pass_on(s, c, target):
        ref = piece(s, c, y, x, core, every)
        return pltpu.make_async_remote_copy(
            ref, ref, z_on.at[c, s], z_got.at[c, s], **target
        )

    def move(kind, c, s, arrived=False):
        flipped = lambda v: 1 - v if arrived else v
        at_y, at_x, at_core, part, target = (
            (pl.ds(y, 1), pl.ds(flipped(x), 1), pl.ds(core, 1), near, x_id),
            (pl.ds(flipped(y), 1), pl.ds(x, 1), pl.ds(core, 1), far, y_id),
            (pl.ds(flipped(y), 1), both, pl.ds(core, 1), near, y_id),
            (both, pl.ds(flipped(x), 1), pl.ds(core, 1), far, x_id),
            (both, both, pl.ds(flipped(core), 1), every, core_id),
        )[kind]
        ref = piece(s, c, at_y, at_x, at_core, part)
        return pltpu.make_async_remote_copy(
            ref, ref, sends.at[kind, c, s], recvs.at[kind, c, s], **target
        )

    def unit(u):
        return u // (n_mp - 1), near_part(me, 1 + u % (n_mp - 1))

    def event(stage, u):
        c, s = unit(u)

        @pl.when((u >= 0) & (u < units))
        def _():
            if stage == 0:

                @pl.when((me > 0) & (me < n_mp - 1))
                def _():
                    pass_on(s, c, right_id).wait_recv()
                    pl.when(s < me)(lambda: pass_on(s, c, right_id).start())
                    pl.when(s > me)(lambda: pass_on(s, c, left_id).start())

            if stage == 1:

                @pl.when((me == 0) | (me == n_mp - 1))
                def _():
                    pass_on(s, c, right_id).wait_recv()

                move(0, c, s).start()
                move(1, c, s).start()
            if stage == 2:
                move(0, c, s, True).wait_recv()
                move(1, c, s, True).wait_recv()
                move(2, c, s).start()
                move(3, c, s).start()
            if stage == 3:
                move(2, c, s, True).wait_recv()
                move(3, c, s, True).wait_recv()
                move(4, c, s).start()
            if stage == 4:
                move(4, c, s, True).wait_recv()

    def send_from(c, ref, at):
        source = ref.at[pl.ds(at * rows, rows)]

        @pl.when(me < n_mp - 1)
        def _():
            own_copy(c, 0, right_id, source).start()

        @pl.when(me > 0)
        def _():
            own_copy(c, 1, left_id, source).start()

    def send_own(c):
        if c > 0:
            send_from(c, (w1_ref, w2_ref)[c - 1], dp_at)
        else:
            pl.when(dp_at < upper)(lambda: send_from(0, wq_ref, dp_at))
            pl.when(dp_at >= upper)(lambda: send_from(0, wp_ref, dp_at - upper))

    small_copy = modulation_start(dp_at, me, n_mp, small, small_sems)
    ada_load = lambda: pltpu.make_async_copy(ada_ref, ada_buf, local_sem.at[8])

    @pl.when(step == 0)
    def _():
        barrier = pltpu.get_barrier_semaphore()
        for target in (core_id, x_id, y_id):
            pl.semaphore_signal(barrier, inc=1, **target)

        @pl.when(me < n_mp - 1)
        def _():
            pl.semaphore_signal(barrier, inc=1, **right_id)

        @pl.when(me > 0)
        def _():
            pl.semaphore_signal(barrier, inc=1, **left_id)

        for k in range(1, n_mp):
            pl.semaphore_signal(barrier, inc=1, **at_mesh(dp_at, (me + k) % n_mp))
        ada_load().start()
        pl.semaphore_wait(barrier, 3 + line_peers(me, n_mp) + n_mp - 1)
        send_own(0)
        cond = cond_ref[...]
        low = (cond * jax.nn.sigmoid(cond)).astype(BF)
        low_ref[...] = low
        ada_load().wait()
        part = nt(low, ada_buf[...]) + rows_ref[0:1]
        pad = jnp.zeros((8 - lats - 1, part.shape[1]), F32)
        small[me] = jnp.concatenate([part, rows_ref[1:2], pad], 0)
        for k in range(1, n_mp):
            small_copy(k).start()
        for k in range(1, n_mp):
            small_copy(k, True).wait_recv()
        dim, cols = h1_all.shape[2], small.shape[2]
        for j in range(6):
            at, off = j * dim // cols, j * dim % cols
            kept = small[at, :lats, :][:, off : off + dim]
            if kept.shape[1] < dim:
                more = small[at + 1, :lats, : dim - kept.shape[1]]
                kept = jnp.concatenate([kept, more], 1)
            for i in range(lats):
                mod_ref[i, j : j + 1] = kept[i : i + 1]
        for at in range(n_mp):
            b1_ref[at] = small[at, lats : lats + 1, :][:, cols - b1_ref.shape[2] :]

    def next_weights(k):
        return pltpu.make_async_copy(all_ref.at[near_part(me, k), 0], w_buf, local_sem.at[0])

    def tick(t):
        def due(at, every):
            return jnp.where((t - at) % every == 0, (t - at) // every, -1)

        for k, at in ((0, 0), (1, 0), (2, 4)):
            nth = due(at, 3 * pace)
            event(0, jnp.where(nth < 0, -1, nth * 3 + k))
        for stage, at in ((3, 8), (2, 3), (1, 0), (4, 11)):
            event(stage, due(at, pace))
        for c in (1, 2):
            pl.when(t == 3 * pace * c - 6)(lambda: send_own(c))

    @pl.when((lat == 0) & (slot == 0))
    def _():
        def load(at):
            return pltpu.make_async_copy(
                wq_ref.at[pl.ds(at * rows, rows)],
                w_buf.at[at // 4, at // 2 % 2, at % 2],
                local_sem.at[at],
            )

        for at in range(upper):
            load(at).start()
        for at in range(upper):
            load(at).wait()

    @pl.when((lat == 0) & (slot > 0))
    def _():
        next_weights(slot).wait()

    n_heads = qkv_ref.shape[1] // 3
    local = n_heads * HEAD_DIM

    @pl.when(slot == 0)
    def _():
        dim, cols = h1_all.shape[2], small.shape[2]
        shift = small[0, pl.ds(lat, 1), :dim]
        scale = jnp.concatenate(
            [small[0, pl.ds(lat, 1), dim:], small[1, pl.ds(lat, 1), : 2 * dim - cols]], 1
        )
        mixed_one(lat_ref, shift, scale, h1_ref, h1_all, lat)

    weights = w_buf[...].reshape(8 * rows, w_buf.shape[-1])[: 3 * local]
    biases = as_column(small[near_part(me, slot), lats : lats + 1, : 2 * local])
    bias = jnp.concatenate([biases[:local], jnp.zeros((local, 1), F32), biases[local:]], 0)
    flat = nt(weights, h1_all[lat]) + bias

    def between(h):
        tick(step * n_heads + h - 1)

        @pl.when((lat == lats - 1) & (slot < n_mp - 1) & (h == n_heads))
        def _():
            next_weights(slot + 1).start()

    attend(flat, n_heads, slot, heads_ref, qkv_ref, lse_ref, between)

    @pl.when(step == n_mp * lats - 1)
    def _():
        def rest(t, carry):
            tick(t)
            return carry

        lax.fori_loop(n_mp * lats * n_heads, pace * units + 11, rest, 0)
        for k in range(1, n_mp):
            small_copy(k).wait_send()
        for c in range(3):

            @pl.when(me < n_mp - 1)
            def _():
                own_copy(c, 0, right_id).wait_send()

            @pl.when(me > 0)
            def _():
                own_copy(c, 1, left_id).wait_send()

        def drain(u, carry):
            c, s = unit(u)

            @pl.when((me > 0) & (me < n_mp - 1))
            def _():
                pass_on(s, c, right_id).wait_send()

            for kind in range(5):
                move(kind, c, s).wait_send()
            return carry

        lax.fori_loop(0, units, drain, 0)


def attn_gather(latents, condition, small_rows, ada_rows, own, n_mp):
    lat, seq, dim = latents.shape
    local = dim // n_mp
    n_heads = local // HEAD_DIM
    rows = dim // 8
    cols = ada_rows.shape[0]
    last = lat - 1
    first = lambda s, l: jnp.where(s == 0, l, last)
    part = lambda s: near_part(lax.axis_index("mp"), s)
    whole = lambda shape: pl.BlockSpec(shape, lambda s, l: (0,) * len(shape))
    any_spec = pl.BlockSpec(memory_space=pl.ANY)
    heads, qkv, lse, h1, mod, b_fc1, cond_low, gathered = pl.pallas_call(
        attn_gather_kernel,
        grid=(n_mp, lat),
        in_specs=[
            pl.BlockSpec((1, seq, dim), lambda s, l: (first(s, l), 0, 0)),
            whole(condition.shape),
            whole(small_rows.shape),
        ]
        + [any_spec] * 5,
        out_specs=[
            pl.BlockSpec((1, 1, local, seq), lambda s, l: (part(s), l, 0, 0)),
            pl.BlockSpec((1, 3 * n_heads, HEAD_DIM, seq), lambda s, l: (first(s, l), 0, 0, 0)),
            pl.BlockSpec((1, n_heads, seq), lambda s, l: (first(s, l), 0, 0)),
            pl.BlockSpec((1, seq, dim), lambda s, l: (first(s, l), 0, 0)),
            whole((lat, 6, dim)),
            whole((n_mp, 1, own[2].shape[1])),
            whole(condition.shape),
            any_spec,
        ],
        out_shape=[
            jax.ShapeDtypeStruct((n_mp, lat, local, seq), BF),
            jax.ShapeDtypeStruct((lat, 3 * n_heads, HEAD_DIM, seq), BF),
            jax.ShapeDtypeStruct((lat, n_heads, seq), F32),
            jax.ShapeDtypeStruct((lat, seq, dim), BF),
            jax.ShapeDtypeStruct((lat, 6, dim), F32),
            jax.ShapeDtypeStruct((n_mp, 1, own[2].shape[1]), F32),
            jax.ShapeDtypeStruct(condition.shape, BF),
            jax.ShapeDtypeStruct((n_mp, 3, 2, 2, 2, rows, dim), BF),
        ],
        scratch_shapes=[
            pltpu.VMEM((lat, seq, dim), BF),
            pltpu.VMEM((2, 2, 2, rows, dim), BF),
            pltpu.VMEM(ada_rows.shape, BF),
            pltpu.VMEM((n_mp, 8, cols), F32),
            pltpu.SemaphoreType.DMA((9,)),
            pltpu.SemaphoreType.DMA((2, 3)),
            pltpu.SemaphoreType.DMA((3, n_mp)),
            pltpu.SemaphoreType.DMA((3, n_mp)),
            pltpu.SemaphoreType.DMA((5, 3, n_mp)),
            pltpu.SemaphoreType.DMA((5, 3, n_mp)),
            pltpu.SemaphoreType.DMA((2, n_mp - 1)),
        ],
        compiler_params=pltpu.CompilerParams(
            collective_id=1, has_side_effects=True, vmem_limit_bytes=62 * MIB
        ),
        name="attn_gather",
    )(latents, condition, small_rows, ada_rows, *own)
    return heads, qkv, lse, h1, mod, b_fc1, cond_low, gathered.reshape(n_mp, 3, dim, dim)


def attn_fwd(me, latents, mod, gathered, bias, n_mp):
    lat, seq, dim = latents.shape
    local = dim // n_mp
    n_heads = local // HEAD_DIM
    last = lat - 1
    first = lambda s, l: jnp.where(s == 0, l, last)
    return pl.pallas_call(
        attn_fwd_kernel,
        grid_spec=pltpu.PrefetchScalarGridSpec(
            num_scalar_prefetch=1,
            grid=(n_mp, lat),
            in_specs=[
                pl.BlockSpec((1, seq, dim), lambda s, l, me: (first(s, l), 0, 0)),
                pl.BlockSpec((1, 6, dim), lambda s, l, me: (l, 0, 0)),
                pl.BlockSpec(
                    (1, 3 * local, dim), lambda s, l, me: (lax.rem(me[0] + s, n_mp), 0, 0)
                ),
                pl.BlockSpec((1, 1, 3 * local), lambda s, l, me: (lax.rem(me[0] + s, n_mp), 0, 0)),
            ],
            out_specs=[
                pl.BlockSpec(
                    (1, 1, local, seq), lambda s, l, me: (lax.rem(me[0] + s, n_mp), l, 0, 0)
                ),
                pl.BlockSpec(
                    (1, 3 * n_heads, HEAD_DIM, seq), lambda s, l, me: (first(s, l), 0, 0, 0)
                ),
                pl.BlockSpec((1, n_heads, seq), lambda s, l, me: (first(s, l), 0, 0)),
                pl.BlockSpec((1, seq, dim), lambda s, l, me: (first(s, l), 0, 0)),
            ],
            scratch_shapes=[pltpu.VMEM((lat, seq, dim), BF)],
        ),
        out_shape=[
            jax.ShapeDtypeStruct((n_mp, lat, local, seq), BF),
            jax.ShapeDtypeStruct((lat, 3 * n_heads, HEAD_DIM, seq), BF),
            jax.ShapeDtypeStruct((lat, n_heads, seq), F32),
            jax.ShapeDtypeStruct((lat, seq, dim), BF),
        ],
        compiler_params=pltpu.CompilerParams(vmem_limit_bytes=60 * MIB),
        name="attn_fwd",
    )(me, latents, mod, gathered, bias)


class LineSum:
    def __init__(self, own_ref, up, down, sems, out_ref, lag=2):
        self.lag = lag
        self.own, self.up, self.down, self.sems, self.out = own_ref, up, down, sems, out_ref
        self.count, self.rows = up.shape[0], up.shape[1]
        self.me = lax.axis_index("mp")
        self.n = lax.axis_size("mp")
        dp_at = lax.axis_index("dp")
        self.ends = (at_mesh(dp_at, self.me + 1), at_mesh(dp_at, self.me - 1))
        self.place = (self.me, self.n - 1 - self.me)

    def guarded(self, side, first, action):
        there = self.place[side] > 0 if first else self.place[side] < self.n - 1

        @pl.when(there)
        def _():
            action()

    def greet(self):
        sem = pltpu.get_barrier_semaphore()
        for side in (0, 1):
            self.guarded(side, False, lambda: pl.semaphore_signal(sem, inc=1, **self.ends[side]))

    def barrier(self):
        self.greet()
        pl.semaphore_wait(pltpu.get_barrier_semaphore(), line_peers(self.me, self.n))

    def copy(self, side, c):
        ref = (self.up, self.down)[side].at[c]
        return pltpu.make_async_remote_copy(
            ref, ref, self.sems.at[2 * side, c], self.sems.at[2 * side + 1, c], **self.ends[side]
        )

    def handle(self, side, c):
        ref = (self.up, self.down)[side]
        own = self.own[0, pl.ds(pl.multiple_of(c * self.rows, self.rows), self.rows)]

        @pl.when(self.place[side] == 0)
        def _():
            ref[c] = own

        @pl.when(self.place[side] > 0)
        def _():
            self.copy(side, c).wait_recv()
            ref[c] = (ref[c].astype(F32) + own.astype(F32)).astype(BF)

        self.guarded(side, False, lambda: self.copy(side, c).start())

    def tick(self, t):
        for side in (0, 1):
            at = t - self.lag * self.place[side]

            @pl.when((at >= 0) & (at % 3 < 2) & (at - at // 3 < self.count))
            def _():
                self.handle(side, at - at // 3)

    def finish(self, ticks):
        for side in (0, 1):
            done = jnp.maximum(ticks - self.lag * self.place[side], 0)
            done = jnp.minimum(done - done // 3, self.count)

            def late(c, carry):
                self.handle(side, c)
                return carry

            lax.fori_loop(done, self.count, late, 0)

        def add(c, carry):
            rows = pl.ds(pl.multiple_of(c * self.rows, self.rows), self.rows)
            total = self.up[c].astype(F32) + self.down[c].astype(F32)
            self.out[0, rows] = (total - self.own[0, rows].astype(F32)).astype(BF)
            return carry

        lax.fori_loop(0, self.count, add, 0)
        for side in (0, 1):

            def sent(c, carry):
                self.copy(side, c).wait_send()
                return carry

            self.guarded(side, False, lambda: lax.fori_loop(0, self.count, sent, 0))


def mlp_kernel(*refs, summing):
    heads_ref, lat_ref, cot_ref, mod_ref, bp_ref, b1_ref, b2_ref = refs[:7]
    own_refs, (wq_all, w1_all, w2_all), refs = refs[7:10], refs[10:13], refs[13:]
    if summing:
        part_ref, refs = refs[0], refs[1:]
    out_ref, dx1_ref, da_ref, h2_ref, dm_ref, z_ref, du_ref, stats_ref, dusum_ref = refs[:9]
    refs = refs[9:]
    if summing:
        sum_ref, refs = refs[0], refs[1:]
    macc, dacc, wp, w1, w2, load_sems = refs[:6]
    n_mp, hid, dim = w2.shape
    local = wp.shape[1]
    rows = lat_ref.shape[1]
    me = lax.axis_index("mp")
    step = pl.program_id(0)
    line = LineSum(part_ref, refs[6], refs[7], refs[8], sum_ref) if summing else None

    def load(kind, k):
        slot = (me + k) % n_mp
        source = own_refs[kind]
        if k > 0:
            stack = (wq_all, w1_all, w2_all)[kind]
            source = stack.at[slot, kind] if len(stack.shape) == 4 else stack.at[slot]
        if k > 0 and kind == 0:
            source = source.at[pl.ds(3 * local, local)]
        ref = (wp.at[slot], w1.at[k], w2.at[k])[kind]
        return pltpu.make_async_copy(source, ref, load_sems.at[kind, k])

    @pl.when(step == 0)
    def _():
        if summing:
            line.barrier()
        for k in range(n_mp):
            load(0, k).start()
        for k in range(n_mp):
            load(1, k).start()
            load(2, k).start()
        for k in range(n_mp):
            load(0, k).wait()

    gate_one, shift_two = mod_ref[0, 2:3], mod_ref[0, 3:4]
    scale_two, gate_two = mod_ref[0, 4:5], mod_ref[0, 5:6]
    heads = heads_ref[:, 0].reshape(dim, rows)
    attn = tn(heads, wp[...].reshape(dim, dim)) + bp_ref[...]
    x1 = lat_ref[0].astype(F32) + gate_one * attn
    n2, inv2 = norm_stats(x1)
    h2 = (n2 * (1.0 + scale_two) + shift_two).astype(BF)
    h2_ref[0] = h2
    cot = cot_ref[0].astype(F32)
    dm = (gate_two * cot).astype(BF)
    dm_ref[0] = dm

    macc[...] = jnp.zeros_like(macc)
    dacc[...] = jnp.zeros_like(dacc)

    def part(k, own):
        if summing:
            line.tick(step * n_mp + k)

        @pl.when(step == 0)
        def _():
            for kind in (1, 2):
                ref = (w1, w2)[kind - 1].at[k]
                pltpu.make_async_copy(ref, ref, load_sems.at[kind, k]).wait()

        u = mm(h2_ref[0], w1[k]) + b1_ref[(me + k) % n_mp]
        dz = nt(dm_ref[0], w2[k])
        u2 = u * u
        t = jnp.tanh(u * (GELU_A + (GELU_A * GELU_B) * u2))
        half = 0.5 + 0.5 * t
        z = (u * half).astype(BF)
        slope = half + u * (1.0 - t * t) * (0.5 * GELU_A + (1.5 * GELU_A * GELU_B) * u2)
        du = dz * slope
        if own:
            before = jnp.where(step == 0, 0.0, dusum_ref[0])
            dusum_ref[0] = before + jnp.sum(du, 0, keepdims=True)
        du = du.astype(BF)
        if own:
            z_ref[0] = z
            du_ref[0] = du
        macc[...] += mm(z, w2[k])
        dacc[...] += nt(du, w1[k])

    part(0, True)

    for k in range(1, n_mp):
        part(k, False)
    mlp = macc[...] + b2_ref[...]
    out_ref[0] = (x1 + gate_two * mlp).astype(BF)
    dh2 = dacc[...]
    dx1 = cot + norm_back(n2, inv2, dh2 * (1.0 + scale_two))
    dx1_ref[0] = dx1.astype(BF)
    da_ref[0] = (gate_one * dx1).astype(BF)
    total = lambda v: jnp.sum(v, 0, keepdims=True)
    stats = jnp.concatenate(
        [
            total(dx1 * attn),
            total(dh2),
            total(dh2 * n2),
            total(cot * mlp),
            total(cot),
            total(dx1),
            jnp.zeros((2, dim), F32),
        ],
        0,
    )

    @pl.when(step == 0)
    def _():
        stats_ref[0] = stats

    @pl.when(step > 0)
    def _():
        stats_ref[0] += stats

    if summing:

        @pl.when(step == pl.num_programs(0) - 1)
        def _():
            line.finish(pl.num_programs(0) * n_mp)


LINE_CHUNKS = 8


def line_scratch(seq, dim):
    rows = seq // LINE_CHUNKS
    return [
        pltpu.VMEM((LINE_CHUNKS, rows, dim), BF),
        pltpu.VMEM((LINE_CHUNKS, rows, dim), BF),
        pltpu.SemaphoreType.DMA((4, LINE_CHUNKS)),
    ]


def mlp_both(index, heads, latents, cotangent, mod, biases, own, gathered, n_mp, rows, part):
    lat, seq, dim = latents.shape
    local = dim // n_mp
    hid = biases[1].shape[2]
    tok = pl.BlockSpec((1, rows, dim), lambda t: (index, t, 0))
    new = pl.BlockSpec((1, rows, dim), lambda t: (0, t, 0))
    hidden = pl.BlockSpec((1, rows, hid), lambda t: (0, t, 0))
    once = lambda shape: pl.BlockSpec(
        shape, lambda t: (0,) * len(shape), pipeline_mode=pl.Buffered(1)
    )
    any_spec = pl.BlockSpec(memory_space=pl.ANY)
    summing = part is not None
    extra = [once((1, seq, dim))] if summing else []
    return pl.pallas_call(
        functools.partial(mlp_kernel, summing=summing),
        grid=(seq // rows,),
        in_specs=[
            pl.BlockSpec((n_mp, 1, local, rows), lambda t: (0, index, 0, t)),
            tok,
            tok,
            pl.BlockSpec((1, 6, dim), lambda t: (index, 0, 0)),
            once((1, dim)),
            once((n_mp, 1, hid)),
            once((1, dim)),
        ]
        + [any_spec] * 6
        + extra,
        out_specs=[new] * 5
        + [
            hidden,
            hidden,
            pl.BlockSpec((1, 8, dim), lambda t: (0, 0, 0)),
            pl.BlockSpec((1, 1, hid), lambda t: (0, 0, 0)),
        ]
        + extra,
        out_shape=[jax.ShapeDtypeStruct((1, seq, dim), BF)] * 5
        + [jax.ShapeDtypeStruct((1, seq, hid), BF)] * 2
        + [jax.ShapeDtypeStruct((1, 8, dim), F32), jax.ShapeDtypeStruct((1, 1, hid), F32)]
        + ([jax.ShapeDtypeStruct((1, seq, dim), BF)] if summing else []),
        scratch_shapes=[
            pltpu.VMEM((rows, dim), F32),
            pltpu.VMEM((rows, dim), F32),
            pltpu.VMEM((n_mp, local, dim), BF),
            pltpu.VMEM((n_mp, dim, hid), BF),
            pltpu.VMEM((n_mp, hid, dim), BF),
            pltpu.SemaphoreType.DMA((3, n_mp)),
        ]
        + (line_scratch(seq, dim) if summing else []),
        compiler_params=pltpu.CompilerParams(
            vmem_limit_bytes=63 * MIB,
            **(dict(collective_id=4 + index, has_side_effects=True) if summing else {}),
        ),
        name="mlp_sum" if summing else "mlp_both",
    )(
        heads,
        latents,
        cotangent,
        mod,
        *biases,
        *own,
        *gathered,
        *([part] if summing else []),
    )


class CubeSum:
    def __init__(self, terms, full, halves, firsts, seconds, sems):
        self.terms, self.full = terms, full
        self.halves, self.firsts, self.seconds, self.sems = halves, firsts, seconds, sems
        self.units = halves.shape[0]
        dp_at, me = lax.axis_index("dp"), lax.axis_index("mp")
        self.core, x, y = dp_at % 2, dp_at // 2 % 2, dp_at // 4
        self.core_id = at_mesh(flip(dp_at, 0), me)
        x_id, y_id = at_mesh(flip(dp_at, 1), me), at_mesh(flip(dp_at, 2), me)
        self.ids = ((x_id, y_id), (y_id, x_id))
        self.place = ((x, y), (y, x))

    def barrier(self):
        sem = pltpu.get_barrier_semaphore()
        for target in (self.core_id,) + self.ids[0]:
            pl.semaphore_signal(sem, inc=1, **target)

    def blocks(self, u, core, q=None, first=None, second=None):
        at, count = 16 * u + 8 * core, 8
        if q is not None:
            at, count = at + 4 * q, 4
        if first is not None:
            at, count = at + 2 * first, 2
        if second is not None:
            at, count = at + second, 1
        return pl.ds(at, count)

    def send(self, stage, u, q, arrived=False):
        core, blocks = self.core, self.blocks
        first, second = self.place[q]
        other = lambda v: 1 - v if arrived else v
        if stage == 0:
            pair = (self.terms.at[blocks(u, 1 - core)], self.halves.at[u])
        elif stage == 1:
            pair = (self.terms.at[blocks(u, core, q, 1 - first)], self.firsts.at[u, q])
        elif stage == 2:
            pair = (self.terms.at[blocks(u, core, q, first, 1 - second)], self.seconds.at[u, q])
        elif stage == 3:
            pair = (self.full.at[blocks(u, core, q, first, other(second))],) * 2
        elif stage == 4:
            pair = (self.full.at[blocks(u, core, q, other(first))],) * 2
        else:
            pair = (self.full.at[blocks(u, other(core))],) * 2
        near, far = self.ids[q]
        target = (self.core_id, near, far, far, near, self.core_id)[stage]
        return pltpu.make_async_remote_copy(
            *pair, self.sems.at[0, stage, q, u], self.sems.at[1, stage, q, u], **target
        )

    def quarters(self, stage):
        return (0,) if stage in (0, 5) else (0, 1)

    def event(self, stage, u):
        terms, core, blocks = self.terms, self.core, self.blocks

        @pl.when((u >= 0) & (u < self.units))
        def _():
            if stage > 0:
                for q in self.quarters(stage - 1):
                    self.send(stage - 1, u, q, True).wait_recv()
            if stage == 1:
                at = blocks(u, core)
                terms[at] = (terms[at].astype(F32) + self.halves[u].astype(F32)).astype(BF)
            for q in (0, 1):
                first, second = self.place[q]
                if stage == 2:
                    at = blocks(u, core, q, first)
                    terms[at] = (terms[at].astype(F32) + self.firsts[u, q].astype(F32)).astype(BF)
                if stage == 3:
                    at = blocks(u, core, q, first, second)
                    total = terms[at].astype(F32) + self.seconds[u, q].astype(F32)
                    self.full[at] = total.astype(BF)
            if stage < 6:
                for q in self.quarters(stage):
                    self.send(stage, u, q).start()

    def finish(self):
        def sent(u, carry):
            for stage in range(6):
                for q in self.quarters(stage):
                    self.send(stage, u, q).wait_send()
            return carry

        lax.fori_loop(0, self.units, sent, 0)


BLOCK = 32


class WeightGrads:
    def __init__(self, operands, terms, right, left_cols, left_rows, right_sems, left_sems):
        self.operands, self.terms, self.right = operands, terms, right
        self.left_cols, self.left_rows = left_cols, left_rows
        self.right_sems, self.left_sems = right_sems, left_sems
        self.lats = right.shape[1]
        dim = right.shape[3]
        qkv_blocks = operands[2][0][0].shape[0] // BLOCK
        half = (qkv_blocks + 1) // 2 * BLOCK
        third = dim // 3
        self.pieces = [(job, i * third, third) for job in (0, 1) for i in range(3)]
        self.pieces += [(2, 0, half), (2, half, qkv_blocks * BLOCK - half)]
        self.pieces += [(3, 0, operands[3][0][0].shape[0])]

    def right_copies(self, job):
        slot = job % 2
        return [
            pltpu.make_async_copy(
                self.operands[job][1][i], self.right.at[slot, i], self.right_sems.at[slot, i]
            )
            for i in range(self.lats)
        ]

    def left_copies(self, at):
        job, first, count = self.pieces[at]
        copies = []
        for i in range(self.lats):
            source = self.operands[job][0][i]
            if job < 2:
                source = source.at[:, pl.ds(first, count)]
                ref = self.left_cols.at[at % 2, i]
            else:
                source = source.at[pl.ds(first, count)]
                ref = self.left_rows.at[at % 2, i, pl.ds(0, count)]
            copies.append(pltpu.make_async_copy(source, ref, self.left_sems.at[at % 2, i]))
        return copies

    def begin(self):
        for copy in self.right_copies(0) + self.left_copies(0):
            copy.start()

    def compute(self, at):
        job, _, count = self.pieces[at]
        opens = at == 0 or self.pieces[at - 1][0] != job
        if at + 1 < len(self.pieces):
            for copy in self.left_copies(at + 1):
                copy.start()
        if opens:
            if job + 1 < len(self.operands):
                for copy in self.right_copies(job + 1):
                    copy.start()
            for copy in self.right_copies(job):
                copy.wait()
        for copy in self.left_copies(at):
            copy.wait()
        slot, dim = job % 2, self.right.shape[3]
        if job < 2:
            left = self.left_cols[at % 2].reshape(-1, count)
            total = tn(left, self.right[slot].reshape(-1, dim))
        else:
            total = mm(self.left_rows[at % 2, 0, :count], self.right[slot, 0])
            for i in range(1, self.lats):
                total = total + mm(self.left_rows[at % 2, i, :count], self.right[slot, i])
        done = sum(rows for _, _, rows in self.pieces[:at]) // BLOCK
        self.terms[pl.ds(done, count // BLOCK)] = total.reshape(-1, BLOCK, dim).astype(BF)


def tail_kernel(*refs, lats):
    part_ref, bias_ref, heads_ref, h1_ref = refs[:4]
    lists = [refs[4 + i * lats : 4 + (i + 1) * lats] for i in range(6)]
    h2s, dus, zs, dms, dqkvs, das = [[ref.at[0] for ref in group] for group in lists]
    sum_ref, *total_refs = refs[4 + 6 * lats : 10 + 6 * lats]
    refs = refs[10 + 6 * lats :]
    up, down, line_sems, terms, full, halves, firsts, seconds, cube_sems = refs[:9]
    right, left_cols, left_rows, right_sems, left_sems, local_sem = refs[9:]
    line = LineSum(part_ref, up, down, line_sems, sum_ref, 3)
    cube = CubeSum(terms, full, halves, firsts, seconds, cube_sems)
    heads = [heads_ref.at[line.me, i] for i in range(lats)]
    h1s = [h1_ref.at[i] for i in range(lats)]
    grads = WeightGrads(
        ((h2s, dus), (zs, dms), (dqkvs, h1s), (heads, das)),
        terms,
        right,
        left_cols,
        left_rows,
        right_sems,
        left_sems,
    )
    grads.begin()
    cube.barrier()
    line.greet()
    pl.semaphore_wait(pltpu.get_barrier_semaphore(), 3 + line_peers(line.me, line.n))
    spare = bias_ref.shape[0]
    terms[pl.ds(terms.shape[0] - spare, spare)] = bias_ref[...]
    line.tick(0)
    unit_rows = 16 * BLOCK
    ready = 0
    for t in range(cube.units):
        line.tick(2 * t + 1)
        while ready < len(grads.pieces) and (
            sum(rows for _, _, rows in grads.pieces[:ready]) < (t + 1) * unit_rows
        ):
            grads.compute(ready)
            ready += 1
        line.tick(2 * t + 2)
        for stage in range(min(t, 6), -1, -1):
            cube.event(stage, t - stage)

    def advance(t, carry):
        line.tick(2 * t + 1)
        for stage in range(6, 0, -1):
            cube.event(stage, t - stage)
        line.tick(2 * t + 2)
        return carry

    lax.fori_loop(cube.units, cube.units + 6, advance, 0)
    stores = []
    first = 0
    for i, ref in enumerate(total_refs):
        source = full.at[pl.ds(first, ref.shape[0])]
        stores.append(pltpu.make_async_copy(source, ref, local_sem.at[i]))
        stores[-1].start()
        first += ref.shape[0]
    line.finish(2 * (cube.units + 6) + 1)
    cube.finish()
    for store in stores:
        store.wait()


def tail_sums(part, biases, heads, h1, lists):
    n_mp, lats, local, seq = heads.shape
    dim = h1.shape[2]
    rows = 2 * dim + 4 * local
    units = -(-(rows + BLOCK) // (16 * BLOCK))
    spare = units * 16 - rows // BLOCK
    biases = jnp.pad(biases, ((0, spare * BLOCK - biases.shape[0]), (0, 0)))
    vmem = pl.BlockSpec(memory_space=pltpu.VMEM)
    any_spec = pl.BlockSpec(memory_space=pl.ANY)
    shape = (units * 16, BLOCK, dim)
    flat = [array for group in lists for array in group]
    counts = [dim // BLOCK, dim // BLOCK, 3 * local // BLOCK, local // BLOCK, spare]
    total, *grads = pl.pallas_call(
        functools.partial(tail_kernel, lats=lats),
        in_specs=[vmem, vmem] + [any_spec] * (2 + len(flat)),
        out_specs=[vmem] + [any_spec] * len(counts),
        out_shape=[jax.ShapeDtypeStruct(part.shape, BF)]
        + [jax.ShapeDtypeStruct((count, BLOCK, dim), BF) for count in counts],
        scratch_shapes=line_scratch(seq, dim)
        + [
            pltpu.VMEM(shape, BF),
            pltpu.VMEM(shape, BF),
            pltpu.VMEM((units, 8, BLOCK, dim), BF),
            pltpu.VMEM((units, 2, 2, BLOCK, dim), BF),
            pltpu.VMEM((units, 2, 1, BLOCK, dim), BF),
            pltpu.SemaphoreType.DMA((2, 6, 2, units)),
            pltpu.VMEM((2, lats, seq, dim), BF),
            pltpu.VMEM((2, lats, seq, dim // 3), BF),
            pltpu.VMEM((2, lats, (3 * local // BLOCK + 1) // 2 * BLOCK, seq), BF),
            pltpu.SemaphoreType.DMA((2, lats)),
            pltpu.SemaphoreType.DMA((2, lats)),
            pltpu.SemaphoreType.DMA((len(counts),)),
        ],
        compiler_params=pltpu.CompilerParams(
            collective_id=2, has_side_effects=True, vmem_limit_bytes=63 * MIB
        ),
        name="tail_sums",
    )(part, biases.reshape(spare, BLOCK, dim), heads, h1, *flat)
    return total, [grad.reshape(-1, dim) for grad in grads]


def rows_kernel(rows_ref, act_ref, every_ref, total_ref, acts, sems):
    dp_at, me = lax.axis_index("dp"), lax.axis_index("mp")
    n_dp, n_mp = every_ref.shape[0], acts.shape[0]
    barrier = pltpu.get_barrier_semaphore()
    for k in range(1, n_dp):
        pl.semaphore_signal(barrier, inc=1, **at_mesh((dp_at + k) % n_dp, me))
    for k in range(1, n_mp):
        pl.semaphore_signal(barrier, inc=1, **at_mesh(dp_at, (me + k) % n_mp))
    every_ref[dp_at] = rows_ref[...]
    acts[me] = act_ref[...]
    pl.semaphore_wait(barrier, n_dp + n_mp - 2)

    def copy(ref, k, target):
        return pltpu.make_async_remote_copy(ref, ref, sems.at[0, k], sems.at[1, k], **target)

    def act_copy(k, source):
        return copy(acts.at[source % n_mp], k - 1, at_mesh(dp_at, (me + k) % n_mp))

    def row_copy(k, source):
        target = at_mesh((dp_at + k) % n_dp, me)
        return copy(every_ref.at[source % n_dp], n_mp + k - 2, target)

    for k in range(1, n_mp):
        act_copy(k, me).start()
    for k in range(1, n_dp):
        row_copy(k, dp_at).start()
    for k in range(1, n_mp):
        act_copy(k, me + n_mp - k).wait_recv()
    total = acts[0]
    for i in range(1, n_mp):
        total = total + acts[i]
    total_ref[...] = total
    for k in range(1, n_dp):
        row_copy(k, dp_at + n_dp - k).wait_recv()
    for k in range(1, n_mp):
        act_copy(k, me).wait_send()
    for k in range(1, n_dp):
        row_copy(k, dp_at).wait_send()


def rows_exchange(rows, act, n_dp, n_mp):
    vmem = pl.BlockSpec(memory_space=pltpu.VMEM)
    return pl.pallas_call(
        rows_kernel,
        in_specs=[vmem, vmem],
        out_specs=[vmem, vmem],
        out_shape=[
            jax.ShapeDtypeStruct((n_dp,) + rows.shape, rows.dtype),
            jax.ShapeDtypeStruct(act.shape, act.dtype),
        ],
        scratch_shapes=[
            pltpu.VMEM((n_mp,) + act.shape, act.dtype),
            pltpu.SemaphoreType.DMA((2, n_dp + n_mp - 2)),
        ],
        compiler_params=pltpu.CompilerParams(
            collective_id=3, has_side_effects=True, vmem_limit_bytes=40 * MIB
        ),
        name="rows_exchange",
    )(rows, act)


def attn_bwd_kernel(da_ref, heads_ref, qkv_ref, lse_ref, wp_ref, wq_ref, dqkv_ref, dh1_ref, bias_ref, *, rows):
    n_heads = lse_ref.shape[1]
    seq = da_ref.shape[1]
    dheads = nt(wp_ref[...], da_ref[0]).reshape(n_heads, HEAD_DIM, seq)
    heads = heads_ref[0, 0].astype(F32).reshape(n_heads, HEAD_DIM, seq)
    scaling = 1.0 / HEAD_DIM**0.5
    dq_list, dk_list, dv_list = [], [], []
    for h in range(n_heads):
        q_t = qkv_ref[0, h]
        k_t = qkv_ref[0, n_heads + h]
        v_t = qkv_ref[0, 2 * n_heads + h]
        q = q_t.astype(F32).T.astype(BF)
        k = k_t.astype(F32).T.astype(BF)
        v = v_t.astype(F32).T.astype(BF)
        do_t = dheads[h].astype(BF)
        do = dheads[h].T.astype(BF)
        inner = jnp.sum(do_t.astype(F32) * heads[h], 0, keepdims=True)
        dq_parts = []
        for i in range(seq // rows):
            cols = slice(i * rows, (i + 1) * rows)
            probs = jnp.exp2(mm(k, q_t[:, cols]) - lse_ref[0, h : h + 1, cols])
            dprobs = mm(v, do_t[:, cols])
            dscores = (probs * (dprobs - inner[:, cols])).astype(BF)
            dq_parts.append(mm(k_t, dscores))
            dv_new = mm(probs.astype(BF), do[cols])
            dk_new = mm(dscores, q[cols])
            dv = dv_new if i == 0 else dv + dv_new
            dk = dk_new if i == 0 else dk + dk_new
        dq_list.append(jnp.concatenate(dq_parts, 1) * scaling)
        dk_list.append(dk.T * (1.0 / LOG2E))
        dv_list.append(dv.T)
    dqkv = jnp.concatenate(dq_list + dk_list + dv_list, 0)
    bias_ref[0] = jnp.sum(dqkv, 1, keepdims=True)
    dqkv = dqkv.astype(BF)
    dqkv_ref[0] = dqkv
    dh1_ref[0] = tn(dqkv, wq_ref[...]).astype(BF)


def attn_bwd(da, heads, qkv, lse, wp, wq, index, rows):
    lat, seq, dim = da.shape
    n_heads = lse.shape[1]
    local = n_heads * HEAD_DIM
    one = lambda shape: pl.BlockSpec((1,) + shape, lambda i: (index,) + (0,) * len(shape))
    only = lambda shape: pl.BlockSpec((1,) + shape, lambda i: (0,) * (len(shape) + 1))
    whole = lambda shape: pl.BlockSpec(shape, lambda i: (0,) * len(shape))
    out = lambda shape: pl.BlockSpec((1,) + shape, lambda i: (0,) * (len(shape) + 1))
    return pl.pallas_call(
        functools.partial(attn_bwd_kernel, rows=rows),
        grid=(1,),
        in_specs=[
            only((seq, dim)),
            pl.BlockSpec((1, 1, local, seq), lambda i: (lax.axis_index("mp"), index, 0, 0)),
            one((3 * n_heads, HEAD_DIM, seq)),
            one((n_heads, seq)),
            whole((local, dim)),
            whole((3 * local, dim)),
        ],
        out_specs=[out((3 * local, seq)), out((seq, dim)), out((3 * local, 1))],
        out_shape=[
            jax.ShapeDtypeStruct((1, 3 * local, seq), BF),
            jax.ShapeDtypeStruct((1, seq, dim), BF),
            jax.ShapeDtypeStruct((1, 3 * local, 1), F32),
        ],
        compiler_params=pltpu.CompilerParams(vmem_limit_bytes=60 * MIB),
        name="attn_bwd",
    )(da, heads, qkv, lse, wp, wq)


def latents_kernel(*refs, lats):
    lat_ref, mod_ref = refs[:2]
    dh1_refs, dx1_refs, out_refs = [refs[2 + i * lats : 2 + (i + 1) * lats] for i in range(3)]
    grad_ref, stats_ref, out_ref = refs[2 + 3 * lats :]
    lat, step = pl.program_id(0), pl.program_id(1)
    n1, inv1 = norm_stats(lat_ref[0].astype(F32))
    for i in range(lats):

        @pl.when(lat == i)
        def _():
            dh1 = dh1_refs[i][0].astype(F32)
            back = norm_back(n1, inv1, dh1 * (1.0 + mod_ref[0, 1:2]))
            grad_ref[0] = (dx1_refs[i][0].astype(F32) + back).astype(BF)
            out_ref[0] = out_refs[i][0]
            pad = jnp.zeros((6, dh1.shape[1]), F32)
            sums = [jnp.sum(dh1, 0, keepdims=True), jnp.sum(dh1 * n1, 0, keepdims=True), pad]
            stats_ref[0] = jnp.where(step == 0, 0.0, stats_ref[0]) + jnp.concatenate(sums, 0)


def latents_back(dh1, dx1, outs, latents, mod, rows):
    lat, seq, dim = latents.shape
    steps = seq // rows
    tok = pl.BlockSpec((1, rows, dim), lambda l, t: (l, t, 0))
    at = lambda i: (lambda l, t: (0, jnp.where(l < i, 0, jnp.where(l == i, t, steps - 1)), 0))
    each = [pl.BlockSpec((1, rows, dim), at(i)) for i in range(lat)]
    return pl.pallas_call(
        functools.partial(latents_kernel, lats=lat),
        grid=(lat, steps),
        in_specs=[tok, pl.BlockSpec((1, 6, dim), lambda l, t: (l, 0, 0))] + each * 3,
        out_specs=[tok, pl.BlockSpec((1, 8, dim), lambda l, t: (l, 0, 0)), tok],
        out_shape=[
            jax.ShapeDtypeStruct((lat, seq, dim), BF),
            jax.ShapeDtypeStruct((lat, 8, dim), F32),
            jax.ShapeDtypeStruct((lat, seq, dim), BF),
        ],
        compiler_params=pltpu.CompilerParams(vmem_limit_bytes=63 * MIB),
        name="latents_back",
    )(latents, mod, *dh1, *dx1, *outs)


def per_device(
    n_dp,
    n_mp,
    latents,
    condition,
    cotangent,
    qkv_weight,
    qv_bias,
    proj_weight,
    proj_bias,
    fc1_weight,
    fc1_bias,
    fc2_weight,
    fc2_bias,
    ada_weight,
    ada_bias,
):
    lat, seq, dim = latents.shape
    local = qkv_weight.shape[2]
    n_heads = local // HEAD_DIM
    hid = fc1_weight.shape[1]
    cols = ada_weight.shape[1]
    mp_at = lax.axis_index("mp")
    dp_at = lax.axis_index("dp")
    me = jnp.full((1,), mp_at, jnp.int32)

    direct = n_mp == 4 and n_dp == 8
    bias_row = jnp.concatenate([qv_bias.reshape(-1), fc1_bias]).astype(F32)[None]
    ada_row = ada_bias.astype(F32)[None]
    wq_own = (
        qkv_weight.reshape(dim, 3, n_heads, HEAD_DIM).transpose(1, 2, 3, 0).reshape(3 * local, dim)
    )
    if direct:
        own = (wq_own, proj_weight, fc1_weight, fc2_weight)
        small_rows = jnp.concatenate([ada_row, bias_row], 0)
        heads, qkv, lse, h1, mod, b_fc1, cond_low, gathered = attn_gather(
            latents, condition, small_rows, ada_weight.T, own, n_mp
        )
        gathered = (gathered,) * 3
    else:
        cond_low = jax.nn.silu(condition).astype(BF)
        mod_part = mm(cond_low, ada_weight) + ada_row
        small = lax.all_gather(jnp.concatenate([mod_part, bias_row], 0), "mp", axis=0)
        mod = small[:, :lat].transpose(1, 0, 2).reshape(lat, 6, dim)
        b_fc1 = small[:, lat, 2 * local :].reshape(n_mp, 1, hid)
        qv_all = small[:, lat, : 2 * local].reshape(n_mp, 2, local)
        b_qkv = jnp.stack([qv_all[:, 0], jnp.zeros((n_mp, local), F32), qv_all[:, 1]], 1)
        b_qkv = b_qkv.reshape(n_mp, 1, 3 * local)

        def gather(weight):
            share = weight.shape[0] // n_dp
            mine = lax.dynamic_slice_in_dim(weight, dp_at * share, share, 0)
            whole = lax.all_gather(mine, ("dp", "mp"), axis=0)
            whole = whole.reshape(n_dp, n_mp, share, weight.shape[1]).transpose(1, 0, 2, 3)
            return whole.reshape(n_mp, weight.shape[0], weight.shape[1])

        gathered = (
            gather(jnp.concatenate([wq_own, proj_weight], 0)),
            gather(fc1_weight),
            gather(fc2_weight),
        )
        heads, qkv, lse, h1 = attn_fwd(me, latents, mod, gathered[0], b_qkv, n_mp)
    rows = min(256, seq)
    results, dqkv, dh1, bias_sums = [], [], [], []
    for i in range(lat):
        waiting = dqkv and direct
        outs = mlp_both(
            i,
            heads,
            latents,
            cotangent,
            mod,
            (proj_bias.astype(F32)[None], b_fc1, fc2_bias.astype(F32)[None]),
            (proj_weight, fc1_weight, fc2_weight),
            gathered,
            n_mp,
            rows,
            dh1_i if waiting else None,
        )
        if waiting:
            dh1.append(outs[-1])
        results.append(outs[:9])
        dqkv_i, dh1_i, sums_i = attn_bwd(
            outs[2], heads, qkv, lse, proj_weight, wq_own, i, min(512, seq)
        )
        dqkv.append(dqkv_i)
        bias_sums.append(sums_i)
        if not direct:
            dh1.append(lax.psum(dh1_i, "mp"))
    outs_by_kind = list(zip(*results))
    h2, dm, z, du = outs_by_kind[3:7]
    da = outs_by_kind[2]
    stats_two = jnp.concatenate(outs_by_kind[7], 0)
    grad_fc1_bias = sum(outs_by_kind[8])[0, 0]
    gate_one, gate_two = mod[:, 2], mod[:, 5]
    grad_fc2_bias = jnp.sum(gate_two * stats_two[:, 4], 0)
    grad_proj_bias = jnp.sum(gate_one * stats_two[:, 5], 0)
    bias_sums = sum(bias_sums).reshape(3, local)
    grad_qv_bias = jnp.stack([bias_sums[0], bias_sums[2]])
    if direct:
        bias_rows = jnp.stack(
            [
                grad_fc1_bias,
                grad_fc2_bias,
                grad_proj_bias,
                jnp.pad(grad_qv_bias.reshape(-1), (0, dim - 2 * local)),
            ]
        ).astype(BF)
        dh1_i, sums = tail_sums(dh1_i, bias_rows, heads, h1, (h2, du, z, dm, dqkv, da))
        dh1.append(dh1_i)
        grad_fc1, grad_fc2, grad_qkv, grad_proj, bias_rows = sums
        bias_rows = bias_rows[:4].astype(F32)
        grad_fc1_bias, grad_fc2_bias, grad_proj_bias = bias_rows[:3]
        grad_qv_bias = bias_rows[3, : 2 * local].reshape(2, local)
    else:
        flat = lambda parts: jnp.concatenate(parts, 0).reshape(lat * seq, -1)
        grad_fc2 = tn(flat(z), flat(dm))
        grad_fc1 = tn(flat(h2), flat(du))
        grad_qkv = sum(mm(dqkv[i][0], h1[i]) for i in range(lat))
        heads_own = lax.dynamic_index_in_dim(heads, mp_at, 0, keepdims=False)
        grad_proj = sum(mm(heads_own[i], da[i][0]) for i in range(lat))
        grads = [grad.astype(BF) for grad in (grad_fc1, grad_fc2, grad_qkv, grad_proj)]
        grad_fc1, grad_fc2, grad_qkv, grad_proj = lax.psum(grads, "dp")
        biases = lax.psum((grad_fc1_bias, grad_fc2_bias, grad_proj_bias, grad_qv_bias), "dp")
        grad_fc1_bias, grad_fc2_bias, grad_proj_bias, grad_qv_bias = biases

    latents_grad, stats_one, block_out = latents_back(
        dh1, outs_by_kind[1], outs_by_kind[0], latents, mod, rows
    )

    dmod = jnp.stack(
        [
            stats_one[:, 0],
            stats_one[:, 1],
            stats_two[:, 0],
            stats_two[:, 1],
            stats_two[:, 2],
            stats_two[:, 3],
        ],
        1,
    )
    dmod = dmod.reshape(lat, 6 * dim).astype(BF)
    dmod_own = lax.dynamic_slice_in_dim(dmod, mp_at * cols, cols, 1)
    both = jnp.concatenate([cond_low, dmod_own], 1)
    grad_act = nt(dmod_own, ada_weight)
    if direct:
        both = jnp.pad(both.reshape(5 * lat, -1), ((0, -5 * lat % 16), (0, 0)))
        grad_act = jnp.pad(grad_act, ((0, 8 - lat), (0, 0)))
        every, grad_act = rows_exchange(both, grad_act, n_dp, n_mp)
        every = every[:, : 5 * lat].reshape(n_dp * lat, dim + cols)
        grad_act = grad_act[:lat]
    else:
        every = lax.all_gather(both, "dp", axis=0, tiled=True)
        grad_act = lax.psum(grad_act, "mp")
    grad_ada = tn(every[:, :dim], every[:, dim:])
    grad_ada_bias = jnp.sum(every[:, dim:].astype(F32), 0)
    condition_grad = jax.vjp(jax.nn.silu, condition)[1](grad_act)[0]

    back = lambda v: v.astype(F32)
    return (
        block_out,
        latents_grad,
        condition_grad,
        back(grad_qkv).reshape(3, local, dim).transpose(2, 0, 1),
        grad_qv_bias,
        back(grad_proj),
        grad_proj_bias,
        back(grad_fc1),
        grad_fc1_bias,
        back(grad_fc2),
        grad_fc2_bias,
        grad_ada,
        grad_ada_bias,
    )


def solution(mesh):
    in_specs = (
        P("dp", None, None),
        P("dp", None),
        P("dp", None, None),
        P(None, None, "mp"),
        P(None, "mp"),
        P("mp", None),
        P(),
        P(None, "mp"),
        P("mp"),
        P("mp", None),
        P(),
        P(None, "mp"),
        P("mp"),
    )
    out_specs = (
        P("dp", None, None),
        P("dp", None, None),
        P("dp", None),
        P(None, None, "mp"),
        P(None, "mp"),
        P("mp", None),
        P(),
        P(None, "mp"),
        P("mp"),
        P("mp", None),
        P(),
        P(None, "mp"),
        P("mp"),
    )
    body = functools.partial(per_device, mesh.shape["dp"], mesh.shape["mp"])
    return jax.shard_map(body, mesh=mesh, in_specs=in_specs, out_specs=out_specs, check_vma=False)
```
